32 devices in a mesh: dp: 4 (over y, core), seq: 8 (over z, x).
Axes of the slice: x: 2, y: 2, z: 4, core: 2. Of those that a mesh axis runs over, the one named last changes fastest.
Arguments:
- queries: bfloat16 [4, 1024, 2048], P('dp', 'seq'), may hold values from -40 to 40, as said below
- keys: bfloat16 [4, 1024, 2048], P('dp', 'seq'), may hold values from -40 to 40, as said below
- values: bfloat16 [4, 1024, 2048], P('dp', 'seq'), may hold values from -40 to 40, as said below
- gain: float32 [2048], replicated, may hold values from 0.1 to 1.9
- cotangent: bfloat16 [4, 1024, 2048], P('dp', 'seq'), may hold values from -240 to 240, as said below
Outputs:
- output: bfloat16 [4, 1024, 2048], P('dp', 'seq')
- grad_query: bfloat16 [4, 1024, 2048], P('dp', 'seq')
- grad_key: bfloat16 [4, 1024, 2048], P('dp', 'seq')
- grad_value: bfloat16 [4, 1024, 2048], P('dp', 'seq')
- gain_grad: float32 [2048], replicated
The draws below stay inside these ranges and needn't reach their ends.
Inputs may be any that keep to these rules, and one draw needn't show every extreme that they name: queries: independent entries with row and feature scales. keys: independent entries with row and feature scales. values: independent entries with row and feature scales. cotangent: independent entries with row and feature scales.
All inputs are finite; a program needn't handle non-finite values.
Results may differ from the reference program's by a relative error of at most 0.0058.
Values may be sent and summed in bfloat16 or wider, within the bound.
No kernel may reach another device: no remote copies, remote signals or barrier semaphores. Data moves between devices by JAX's collectives and lax.ppermute only.
A program may use at most 64 MiB of HBM per device.

```python
import jax
import jax.numpy as jnp
from jax import lax

HEADS = 16
HEAD = 128
TOK_DEV = 128
FEATURES = 2048
SEQS = 4
LEN = 1024
N_SEQ = 8


def rough_field(key, rising):
    shape = (SEQS, LEN, HEADS * HEAD)
    key_base, key_rows, key_cols = jax.random.split(key, 3)
    base = jnp.clip(jax.random.normal(key_base, shape, jnp.float32), -4.0, 4.0)
    top = 10.0
    slope = 2.0
    row_scale = jnp.exp(jax.random.uniform(key_rows, (SEQS, LEN, 1), jnp.float32) * jnp.log(top)) / jnp.sqrt(top)
    col_scale = jnp.exp(jax.random.uniform(key_cols, (1, 1, shape[2]), jnp.float32) * jnp.log(top)) / jnp.sqrt(top)
    field = base * row_scale * col_scale
    if rising:
        position = jnp.arange(LEN).astype(jnp.float32) / max(LEN - 1, 1)
        field = field * (1.0 + slope * position)[None, :, None]
    return field


def draw_queries(key, part):
    return rough_field(jax.random.fold_in(key, 101), False).astype(jnp.bfloat16)


def draw_keys(key, part):
    return rough_field(jax.random.fold_in(key, 202), False).astype(jnp.bfloat16)


def draw_values(key, part):
    return rough_field(jax.random.fold_in(key, 303), False).astype(jnp.bfloat16)


def draw_cotangent(key, part):
    return rough_field(jax.random.fold_in(key, 404), True).astype(jnp.bfloat16)


def setup_inputs(seed: int = 0) -> dict:
    arg_keys = jax.random.split(jax.random.key(seed), 6)
    queries = draw_queries(jax.random.fold_in(arg_keys[5], 71), 0)
    keys = draw_keys(jax.random.fold_in(arg_keys[5], 71), 0)
    values = draw_values(jax.random.fold_in(arg_keys[5], 71), 0)
    gain = jnp.clip(1.0 + 0.18 * jax.random.normal(arg_keys[3], (FEATURES,), jnp.float32), 0.1, 1.9)
    cotangent = draw_cotangent(jax.random.fold_in(arg_keys[5], 71), 0)
    return {"queries": queries, "keys": keys, "values": values, "gain": gain, "cotangent": cotangent}


EPSILON = 1e-06

def to_blocks(matrix):
    return matrix.astype(jnp.float32).reshape(N_SEQ, TOK_DEV, HEADS, HEAD)

def rounded(tensor):
    return lax.optimization_barrier(tensor.astype(jnp.bfloat16)).astype(jnp.float32)

def reference(queries, keys, values, gain, cotangent):
    scaling = HEAD ** (-0.5)
    position = jnp.arange(TOK_DEV)
    causal_mask = (position[:, None] >= position[None, :]).astype(jnp.float32)

    def one_sequence(operands):
        query_seq, key_seq, value_seq, upstream_seq = operands
        query_blocks = to_blocks(query_seq)
        key_blocks = to_blocks(key_seq)
        value_blocks = to_blocks(value_seq)
        local_states = jnp.einsum('bthd,bthe->bhde', key_blocks, value_blocks)
        prefix_states = jnp.concatenate([jnp.zeros_like(local_states[:1]), jnp.cumsum(local_states[:-1], axis=0)], axis=0)
        prefix_half = rounded(prefix_states)
        scores = jnp.einsum('bthd,buhd->bhtu', query_blocks, key_blocks) * scaling * causal_mask
        score_half = rounded(scores)
        attended = jnp.einsum('bhtu,buhe->bthe', score_half, value_blocks)
        attended = attended + scaling * jnp.einsum('bthd,bhde->bthe', query_blocks, prefix_half)
        attended = attended.reshape(LEN, HEADS * HEAD)
        root_mean = jnp.sqrt(lax.optimization_barrier(jnp.mean(attended * attended, axis=-1, keepdims=True)) + EPSILON)
        normalized = attended / root_mean
        output = (gain * normalized).astype(jnp.bfloat16)
        upstream = upstream_seq.astype(jnp.float32)
        gain_part = lax.optimization_barrier(jnp.sum(upstream * normalized, axis=0))
        scaled = upstream * gain
        inner_mean = lax.optimization_barrier(jnp.mean(scaled * normalized, axis=-1, keepdims=True))
        grad_attn = rounded((scaled - normalized * inner_mean) / root_mean)
        grad_blocks = grad_attn.reshape(N_SEQ, TOK_DEV, HEADS, HEAD)
        local_grads = scaling * jnp.einsum('bthd,bthe->bhde', query_blocks, grad_blocks)
        inclusive = jnp.cumsum(local_grads[::-1], axis=0)[::-1]
        suffix_states = jnp.concatenate([inclusive[1:], jnp.zeros_like(local_grads[:1])], axis=0)
        suffix_half = rounded(suffix_states)
        grad_scores = rounded(jnp.einsum('bthe,buhe->bhtu', grad_blocks, value_blocks) * causal_mask)
        grad_query = scaling * (jnp.einsum('bhtu,buhd->bthd', grad_scores, key_blocks) + jnp.einsum('bthe,bhde->bthd', grad_blocks, prefix_half))
        grad_key = scaling * jnp.einsum('bhtu,bthd->buhd', grad_scores, query_blocks) + jnp.einsum('buhe,bhde->buhd', value_blocks, suffix_half)
        grad_value = jnp.einsum('bhtu,bthe->buhe', score_half, grad_blocks) + jnp.einsum('buhd,bhde->buhe', key_blocks, suffix_half)
        shape_out = (LEN, HEADS * HEAD)
        return (output, grad_query.reshape(shape_out).astype(jnp.bfloat16), grad_key.reshape(shape_out).astype(jnp.bfloat16), grad_value.reshape(shape_out).astype(jnp.bfloat16), gain_part)
    results = lax.map(one_sequence, (queries, keys, values, cotangent))
    gain_grad = lax.optimization_barrier(jnp.sum(results[4], axis=0)) / SEQS
    return (results[0], results[1], results[2], results[3], gain_grad)
```

```python
import functools

import jax
import jax.numpy as jnp
from jax import lax
from jax.experimental import pallas as pl
from jax.experimental.pallas import tpu as pltpu
from jax.sharding import PartitionSpec as P

HEADS = 16

EPSILON = 1e-06

F32 = jnp.float32
HALF = jnp.bfloat16


def dot(lhs, rhs, lhs_dim, rhs_dim):
    return lax.dot_general(
        lhs, rhs, (((lhs_dim,), (rhs_dim,)), ((), ())), preferred_element_type=F32
    )


def causal(size):
    rows = lax.broadcasted_iota(jnp.int32, (size, size), 0)
    columns = lax.broadcasted_iota(jnp.int32, (size, size), 1)
    return rows >= columns


def state_kernel(head, k_ref, v_ref, state_ref):
    for h in range(HEADS):
        part = slice(h * head, (h + 1) * head)
        state_ref[part, :] = dot(k_ref[:, part], v_ref[:, part], 0, 0).astype(HALF)


def local_kernel(head, q_ref, k_ref, v_ref, scores_ref, intra_ref):
    rows = q_ref.shape[0]
    mask = causal(rows)
    scaling = head ** (-0.5)
    for h in range(HEADS):
        part = slice(h * head, (h + 1) * head)
        scores = dot(q_ref[:, part], k_ref[:, part], 1, 1) * scaling
        scores = jnp.where(mask, scores, 0.0).astype(HALF)
        scores_ref[h * rows : (h + 1) * rows, :] = scores
        intra_ref[:, part] = dot(scores, v_ref[:, part], 1, 0)


def norm_kernel(
    head,
    replicas,
    q_ref,
    prefix_ref,
    intra_ref,
    gain_ref,
    cot_ref,
    out_ref,
    grad_ref,
    state_ref,
    gain_grad_ref,
    attended_ref,
):
    rows = q_ref.shape[0]
    scaling = head ** (-0.5)
    features = HEADS * head
    squares = jnp.zeros((rows, head), F32)
    inner = jnp.zeros((rows, head), F32)
    for h in range(HEADS):
        part = slice(h * head, (h + 1) * head)
        attended = intra_ref[:, part] + scaling * dot(
            q_ref[:, part], prefix_ref[part, :], 1, 0
        )
        attended_ref[:, part] = attended
        scaled = cot_ref[:, part].astype(F32) * gain_ref[:, part]
        squares += attended * attended
        inner += scaled * attended
    inverse = lax.rsqrt(
        jnp.sum(squares, axis=1, keepdims=True) * (1.0 / features) + EPSILON
    )
    inner_mean = jnp.sum(inner, axis=1, keepdims=True) * (1.0 / features) * inverse
    for h in range(HEADS):
        part = slice(h * head, (h + 1) * head)
        normalized = attended_ref[:, part] * inverse
        upstream = cot_ref[:, part].astype(F32)
        gain = gain_ref[:, part]
        out_ref[:, part] = (gain * normalized).astype(HALF)
        gain_grad_ref[:, part] = jnp.sum(
            upstream * normalized, axis=0, keepdims=True
        ) * (1.0 / replicas)
        grad = ((upstream * gain - normalized * inner_mean) * inverse).astype(HALF)
        grad_ref[:, part] = grad
        state_ref[part, :] = (scaling * dot(q_ref[:, part], grad, 0, 0)).astype(HALF)


def backward_kernel(
    head,
    q_ref,
    k_ref,
    v_ref,
    scores_ref,
    prefix_ref,
    grad_ref,
    grad_query_ref,
    key_part_ref,
    value_part_ref,
):
    rows = q_ref.shape[0]
    mask = causal(rows)
    scaling = head ** (-0.5)
    for h in range(HEADS):
        part = slice(h * head, (h + 1) * head)
        grad = grad_ref[:, part]
        grad_scores = dot(grad, v_ref[:, part], 1, 1)
        grad_scores = jnp.where(mask, grad_scores, 0.0).astype(HALF)
        grad_query = dot(grad_scores, k_ref[:, part], 1, 0) + dot(
            grad, prefix_ref[part, :], 1, 1
        )
        grad_query_ref[:, part] = (scaling * grad_query).astype(HALF)
        key_part_ref[:, part] = scaling * dot(grad_scores, q_ref[:, part], 0, 0)
        value_part_ref[:, part] = dot(
            scores_ref[h * rows : (h + 1) * rows, :], grad, 0, 0
        )


def final_kernel(
    head,
    k_ref,
    v_ref,
    suffix_ref,
    key_part_ref,
    value_part_ref,
    grad_key_ref,
    grad_value_ref,
):
    for h in range(HEADS):
        part = slice(h * head, (h + 1) * head)
        suffix = suffix_ref[part, :]
        grad_key_ref[:, part] = (
            key_part_ref[:, part] + dot(v_ref[:, part], suffix, 1, 1)
        ).astype(HALF)
        grad_value_ref[:, part] = (
            value_part_ref[:, part] + dot(k_ref[:, part], suffix, 1, 0)
        ).astype(HALF)


def scan_kernel(count, reverse, in_ref, out_ref):
    size = in_ref.shape[0] // count
    order = list(range(count))
    if reverse:
        order.reverse()
    total = jnp.zeros((size, in_ref.shape[1]), F32)
    for i in order:
        part = slice(i * size, (i + 1) * size)
        out_ref[part, :] = total.astype(HALF)
        total += in_ref[part, :].astype(F32)


def call(kernel, outs, args, matmuls, scratch=()):
    vmem = pl.BlockSpec(memory_space=pltpu.VMEM)
    size = sum(a.size * a.dtype.itemsize for a in args)
    size += sum(o.size * o.dtype.itemsize for o in outs)
    return pl.pallas_call(
        kernel,
        out_shape=tuple(outs),
        in_specs=[vmem] * len(args),
        out_specs=tuple([vmem] * len(outs)),
        scratch_shapes=list(scratch),
        compiler_params=pltpu.CompilerParams(vmem_limit_bytes=32 * 1024 * 1024),
        cost_estimate=pl.CostEstimate(
            flops=2 * 128 * 128 * 128 * HEADS * matmuls,
            bytes_accessed=size,
            transcendentals=0,
        ),
    )(*args)


def exclusive_scan(state, reverse):
    count = lax.axis_size("seq")
    columns = lax.all_to_all(state, "seq", split_axis=0, concat_axis=0, tiled=True)
    (summed,) = call(
        functools.partial(scan_kernel, count, reverse),
        [jax.ShapeDtypeStruct(state.shape, HALF)],
        [columns],
        0,
    )
    return lax.all_to_all(summed, "seq", split_axis=0, concat_axis=0, tiled=True)


def per_device(queries, keys, values, gain, cotangent):
    q, k, v, cot = queries[0], keys[0], values[0], cotangent[0]
    rows, features = q.shape
    head = features // HEADS
    wide = jax.ShapeDtypeStruct((rows, features), F32)
    half = jax.ShapeDtypeStruct((rows, features), HALF)
    state_shape = jax.ShapeDtypeStruct((features, head), HALF)
    scores_shape = jax.ShapeDtypeStruct((HEADS * rows, rows), HALF)
    part = functools.partial

    (state,) = call(part(state_kernel, head), [state_shape], [k, v], 1)
    prefix = exclusive_scan(state, False)
    scores, intra = call(part(local_kernel, head), [scores_shape, wide], [q, k, v], 2)
    output, grad, local_grad, gain_part = call(
        part(norm_kernel, head, lax.axis_size("dp")),
        [half, half, state_shape, jax.ShapeDtypeStruct((1, features), F32)],
        [q, prefix, intra, gain.reshape(1, features), cot],
        2,
        [pltpu.VMEM((rows, features), F32)],
    )
    suffix = exclusive_scan(local_grad, True)
    gain_grad = lax.psum(gain_part.reshape(features), ("dp", "seq"))
    grad_query, key_part, value_part = call(
        part(backward_kernel, head),
        [half, wide, wide],
        [q, k, v, scores, prefix, grad],
        5,
    )
    grad_key, grad_value = call(
        part(final_kernel, head),
        [half, half],
        [k, v, suffix, key_part, value_part],
        2,
    )
    return output[None], grad_query[None], grad_key[None], grad_value[None], gain_grad


def solution(mesh):
    spec = P("dp", "seq", None)
    return jax.shard_map(
        per_device,
        mesh=mesh,
        in_specs=(spec, spec, spec, P(), spec),
        out_specs=(spec, spec, spec, spec, P()),
        check_vma=False,
    )
```

```python
import functools

import jax
import jax.numpy as jnp
from jax import lax
from jax.experimental import pallas as pl
from jax.experimental.pallas import tpu as pltpu
from jax.sharding import PartitionSpec as P

HEADS = 16

EPSILON = 1e-06

F32 = jnp.float32
HALF = jnp.bfloat16


def dot(lhs, rhs, lhs_dim, rhs_dim):
    return lax.dot_general(
        lhs, rhs, (((lhs_dim,), (rhs_dim,)), ((), ())), preferred_element_type=F32
    )


def causal(size):
    rows = lax.broadcasted_iota(jnp.int32, (size, size), 0)
    columns = lax.broadcasted_iota(jnp.int32, (size, size), 1)
    return rows >= columns


def member_of(group):
    return lax.rem(lax.axis_index("seq"), group)


def features_of(member, chunk, i, size, head):
    start = (member ^ chunk) * size + i * head
    return pl.ds(pl.multiple_of(start, head), head)


def state_kernel(head, group, k_ref, v_ref, *piece_refs):
    member = member_of(group)
    size = piece_refs[0].shape[0]
    for chunk in range(group):
        for i in range(size // head):
            part = features_of(member, chunk, i, size, head)
            piece_refs[chunk][i * head : (i + 1) * head, :] = dot(
                k_ref[:, part], v_ref[:, part], 0, 0
            ).astype(HALF)


def local_kernel(head, q_ref, k_ref, v_ref, scores_ref, intra_ref):
    rows = q_ref.shape[0]
    mask = causal(rows)
    scaling = head ** (-0.5)
    for h in range(HEADS):
        part = slice(h * head, (h + 1) * head)
        scores = dot(q_ref[:, part], k_ref[:, part], 1, 1) * scaling
        scores = jnp.where(mask, scores, 0.0).astype(HALF)
        scores_ref[:, h * rows : (h + 1) * rows] = scores
        intra_ref[:, part] = dot(scores, v_ref[:, part], 1, 0)


def norm_kernel(head, group, replicas, *refs):
    q_ref, intra_ref, gain_ref, cot_ref = refs[:4]
    prefix_refs = refs[4 : 4 + group]
    out_ref, grad_ref, gain_grad_ref = refs[4 + group : 7 + group]
    piece_refs = refs[7 + group : 7 + 2 * group]
    attended_ref = refs[7 + 2 * group]
    member = member_of(group)
    rows = q_ref.shape[0]
    scaling = head ** (-0.5)
    features = HEADS * head
    size = features // group
    squares = jnp.zeros((rows, head), F32)
    inner = jnp.zeros((rows, head), F32)
    for chunk in range(group):
        for i in range(size // head):
            part = features_of(member, chunk, i, size, head)
            prefix = prefix_refs[chunk][i * head : (i + 1) * head, :]
            attended = intra_ref[:, part] + scaling * dot(q_ref[:, part], prefix, 1, 0)
            attended_ref[:, part] = attended
            scaled = cot_ref[:, part].astype(F32) * gain_ref[:, part]
            squares += attended * attended
            inner += scaled * attended
    inverse = lax.rsqrt(
        jnp.sum(squares, axis=1, keepdims=True) * (1.0 / features) + EPSILON
    )
    inner_mean = jnp.sum(inner, axis=1, keepdims=True) * (1.0 / features) * inverse
    for chunk in range(group):
        for i in range(size // head):
            part = features_of(member, chunk, i, size, head)
            normalized = attended_ref[:, part] * inverse
            upstream = cot_ref[:, part].astype(F32)
            gain = gain_ref[:, part]
            out_ref[:, part] = (gain * normalized).astype(HALF)
            gain_grad_ref[:, part] = jnp.sum(
                upstream * normalized, axis=0, keepdims=True
            ) * (1.0 / replicas)
            grad = ((upstream * gain - normalized * inner_mean) * inverse).astype(HALF)
            grad_ref[:, part] = grad
            piece_refs[chunk][i * head : (i + 1) * head, :] = (
                scaling * dot(q_ref[:, part], grad, 0, 0)
            ).astype(HALF)


def backward_kernel(head, group, *refs):
    q_ref, k_ref, v_ref, scores_ref, grad_ref = refs[:5]
    prefix_refs = refs[5 : 5 + group]
    grad_query_ref, key_part_ref, value_part_ref = refs[5 + group :]
    member = member_of(group)
    rows = q_ref.shape[0]
    mask = causal(rows)
    scaling = head ** (-0.5)
    size = prefix_refs[0].shape[0]
    for chunk in range(group):
        for i in range(size // head):
            part = features_of(member, chunk, i, size, head)
            prefix = prefix_refs[chunk][i * head : (i + 1) * head, :]
            grad = grad_ref[:, part]
            grad_scores = dot(grad, v_ref[:, part], 1, 1)
            grad_scores = jnp.where(mask, grad_scores, 0.0).astype(HALF)
            grad_query = dot(grad_scores, k_ref[:, part], 1, 0) + dot(grad, prefix, 1, 1)
            grad_query_ref[:, part] = (scaling * grad_query).astype(HALF)
            key_part_ref[:, part] = scaling * dot(grad_scores, q_ref[:, part], 0, 0)
            scores = scores_ref[:, features_of(member, chunk, i, size // head * rows, rows)]
            value_part_ref[:, part] = dot(scores, grad, 0, 0)


def final_kernel(head, group, *refs):
    k_ref, v_ref, key_part_ref, value_part_ref = refs[:4]
    suffix_refs = refs[4 : 4 + group]
    grad_key_ref, grad_value_ref = refs[4 + group :]
    member = member_of(group)
    size = suffix_refs[0].shape[0]
    for chunk in range(group):
        for i in range(size // head):
            part = features_of(member, chunk, i, size, head)
            suffix = suffix_refs[chunk][i * head : (i + 1) * head, :]
            grad_key_ref[:, part] = (
                key_part_ref[:, part] + dot(v_ref[:, part], suffix, 1, 1)
            ).astype(HALF)
            grad_value_ref[:, part] = (
                value_part_ref[:, part] + dot(k_ref[:, part], suffix, 1, 0)
            ).astype(HALF)


def total_kernel(*refs):
    total = refs[0][...].astype(F32)
    for ref in refs[1:-1]:
        total += ref[...].astype(F32)
    refs[-1][...] = total.astype(HALF)


def scan_kernel(group, reverse, *refs):
    member = member_of(group)
    carry = refs[0][...].astype(F32)
    blocks = [ref[...].astype(F32) for ref in refs[1 : 1 + group]]
    for j in range(group):
        total = carry
        for i in range(group):
            if i != j:
                earlier = (member ^ i) < (member ^ j)
                keep = jnp.where(earlier != reverse, 1.0, 0.0)
                total += keep * blocks[i]
        refs[1 + group + j][...] = total.astype(HALF)


def call(kernel, outs, args, matmuls, scratch=()):
    vmem = pl.BlockSpec(memory_space=pltpu.VMEM)
    size = sum(a.size * a.dtype.itemsize for a in args)
    size += sum(o.size * o.dtype.itemsize for o in outs)
    return pl.pallas_call(
        kernel,
        out_shape=tuple(outs),
        in_specs=[vmem] * len(args),
        out_specs=tuple([vmem] * len(outs)),
        scratch_shapes=list(scratch),
        compiler_params=pltpu.CompilerParams(vmem_limit_bytes=16 * 1024 * 1024),
        cost_estimate=pl.CostEstimate(
            flops=2 * 128 * 128 * 128 * HEADS * matmuls,
            bytes_accessed=size,
            transcendentals=0,
        ),
    )(*args)


def swap(array, axis, offset):
    count = lax.axis_size(axis)
    return lax.ppermute(array, axis, [(i, i ^ offset) for i in range(count)])


def exclusive_scan(pieces, reverse):
    group = len(pieces)
    count = lax.axis_size("seq")
    piece = jax.ShapeDtypeStruct(pieces[0].shape, HALF)
    blocks = [pieces[0]] + [swap(pieces[j], "seq", j) for j in range(1, group)]

    def shifted(array, distance):
        pairs = [(i, i + distance) for i in range(count - distance)]
        if reverse:
            pairs = [(b, a) for a, b in pairs]
        return lax.ppermute(array, "seq", pairs)

    (total,) = call(total_kernel, [piece], blocks, 0)
    carry = shifted(total, group)
    distance = group
    while distance < count - group:
        (carry,) = call(total_kernel, [piece], [carry, shifted(carry, distance)], 0)
        distance *= 2
    sums = call(
        functools.partial(scan_kernel, group, reverse),
        [piece] * group,
        [carry] + blocks,
        0,
    )
    return [sums[0]] + [swap(sums[j], "seq", j) for j in range(1, group)]


def small_sum(array):
    for axis in ("dp", "seq"):
        stride, count = 1, lax.axis_size(axis)
        while stride < count:
            width = 4 if count // stride % 4 == 0 else 2
            terms = [array] + [swap(array, axis, i * stride) for i in range(1, width)]
            array = terms[0] + terms[1]
            if width == 4:
                array = array + (terms[2] + terms[3])
            stride *= width
    return array


def per_device(queries, keys, values, gain, cotangent):
    q, k, v, cot = queries[0], keys[0], values[0], cotangent[0]
    rows, features = q.shape
    head = features // HEADS
    group = 4
    wide = jax.ShapeDtypeStruct((rows, features), F32)
    half = jax.ShapeDtypeStruct((rows, features), HALF)
    piece = jax.ShapeDtypeStruct((features // group, head), HALF)
    scores_shape = jax.ShapeDtypeStruct((rows, HEADS * rows), HALF)
    row = jax.ShapeDtypeStruct((1, features), F32)
    part = functools.partial

    pieces = call(part(state_kernel, head, group), [piece] * group, [k, v], 1)
    prefix = exclusive_scan(pieces, False)
    scores, intra = call(part(local_kernel, head), [scores_shape, wide], [q, k, v], 2)
    output, grad, gain_part, *pieces = call(
        part(norm_kernel, head, group, lax.axis_size("dp")),
        [half, half, row] + [piece] * group,
        [q, intra, gain.reshape(1, features), cot] + prefix,
        2,
        [pltpu.VMEM((rows, features), F32)],
    )
    suffix = exclusive_scan(pieces, True)
    gain_grad = small_sum(gain_part).reshape(features)
    grad_query, key_part, value_part = call(
        part(backward_kernel, head, group),
        [half, wide, wide],
        [q, k, v, scores, grad] + prefix,
        5,
    )
    grad_key, grad_value = call(
        part(final_kernel, head, group),
        [half, half],
        [k, v, key_part, value_part] + suffix,
        2,
    )
    return output[None], grad_query[None], grad_key[None], grad_value[None], gain_grad


def solution(mesh):
    spec = P("dp", "seq", None)
    return jax.shard_map(
        per_device,
        mesh=mesh,
        in_specs=(spec, spec, spec, P(), spec),
        out_specs=(spec, spec, spec, spec, P()),
        check_vma=False,
    )
```

```python
import functools

import jax
import jax.numpy as jnp
from jax import lax
from jax.experimental import pallas as pl
from jax.experimental.pallas import tpu as pltpu
from jax.sharding import PartitionSpec as P

HEADS = 16

EPSILON = 1e-06

STATE_LIMIT = 63 * 1024 * 1024

F32 = jnp.float32
HALF = jnp.bfloat16


def dot(lhs, rhs, lhs_dim, rhs_dim):
    return lax.dot_general(
        lhs, rhs, (((lhs_dim,), (rhs_dim,)), ((), ())), preferred_element_type=F32
    )


def causal(size):
    rows = lax.broadcasted_iota(jnp.int32, (size, size), 0)
    columns = lax.broadcasted_iota(jnp.int32, (size, size), 1)
    return rows >= columns


def member_of(group):
    return lax.rem(lax.axis_index("seq"), group)


def block_at(index, size):
    return pl.ds(pl.multiple_of(index * size, size), size)


def gathered(member, piece_refs, size, whole_ref):
    for j, ref in enumerate(piece_refs):
        whole_ref[block_at(member ^ j, size), :] = ref[0:size, :]


def scattered(member, whole_ref, size, piece_refs):
    for j, ref in enumerate(piece_refs):
        ref[...] = whole_ref[block_at(member ^ j, size), :]


def state_kernel(head, group, k_ref, v_ref, *refs):
    piece_refs = refs[:group]
    k_chunks, v_chunks, arrived = refs[group:]
    member = member_of(group)
    size = piece_refs[0].shape[0]
    copies = []
    for j in range(group):
        source = block_at(member ^ j, size)
        for i, (ref, chunks) in enumerate(((k_ref, k_chunks), (v_ref, v_chunks))):
            copy = pltpu.make_async_copy(
                ref.at[:, source], chunks.at[j], arrived.at[i, j]
            )
            copy.start()
            copies.append(copy)
    for j in range(group):
        copies[2 * j].wait()
        copies[2 * j + 1].wait()
        for i in range(size // head):
            part = slice(i * head, (i + 1) * head)
            piece_refs[j][part, :] = dot(
                k_chunks[j, :, part], v_chunks[j, :, part], 0, 0
            ).astype(HALF)


def local_kernel(head, q_ref, k_ref, v_ref, scores_ref, intra_ref):
    rows = q_ref.shape[0]
    mask = causal(rows)
    scaling = head ** (-0.5)
    for h in range(HEADS):
        part = slice(h * head, (h + 1) * head)
        scores = dot(q_ref[:, part], k_ref[:, part], 1, 1) * scaling
        scores = jnp.where(mask, scores, 0.0).astype(HALF)
        scores_ref[h * rows : (h + 1) * rows, :] = scores
        intra_ref[:, part] = dot(scores, v_ref[:, part], 1, 0)


def norm_kernel(head, group, replicas, *refs):
    q_ref, intra_ref, gain_ref, cot_ref = refs[:4]
    prefix_refs = refs[4 : 4 + group]
    attended_ref, inverse_ref, grad_ref, gain_grad_ref = refs[4 + group : 8 + group]
    piece_refs = refs[8 + group : 8 + 2 * group]
    whole_ref = refs[8 + 2 * group]
    member = member_of(group)
    rows = q_ref.shape[0]
    scaling = head ** (-0.5)
    features = HEADS * head
    size = features // group
    gathered(member, prefix_refs, size, whole_ref)
    squares = jnp.zeros((rows, head), F32)
    inner = jnp.zeros((rows, head), F32)
    for h in range(HEADS):
        part = slice(h * head, (h + 1) * head)
        attended = intra_ref[:, part] + scaling * dot(
            q_ref[:, part], whole_ref[part, :], 1, 0
        )
        attended_ref[:, part] = attended
        scaled = cot_ref[:, part].astype(F32) * gain_ref[h : h + 1, :]
        squares += attended * attended
        inner += scaled * attended
    inverse = lax.rsqrt(
        jnp.sum(squares, axis=1, keepdims=True) * (1.0 / features) + EPSILON
    )
    inner_mean = jnp.sum(inner, axis=1, keepdims=True) * (1.0 / features) * inverse
    inverse_ref[...] = jnp.broadcast_to(inverse, inverse_ref.shape)
    for h in range(HEADS):
        part = slice(h * head, (h + 1) * head)
        normalized = attended_ref[:, part] * inverse
        upstream = cot_ref[:, part].astype(F32)
        gain = gain_ref[h : h + 1, :]
        gain_grad_ref[h : h + 1, :] = jnp.sum(
            upstream * normalized, axis=0, keepdims=True
        ) * (1.0 / replicas)
        grad = ((upstream * gain - normalized * inner_mean) * inverse).astype(HALF)
        grad_ref[:, part] = grad
        whole_ref[part, :] = (scaling * dot(q_ref[:, part], grad, 0, 0)).astype(HALF)
    scattered(member, whole_ref, size, piece_refs)


def backward_kernel(head, group, *refs):
    q_ref, k_ref, v_ref, scores_ref, grad_ref = refs[:5]
    attended_ref, inverse_ref, gain_ref = refs[5:8]
    prefix_refs = refs[8 : 8 + group]
    out_ref, grad_query_ref, key_part_ref, value_part_ref, token_ref = refs[
        8 + group : 13 + group
    ]
    whole_ref = refs[13 + group]
    rows = q_ref.shape[0]
    mask = causal(rows)
    scaling = head ** (-0.5)
    gathered(member_of(group), prefix_refs, prefix_refs[0].shape[0], whole_ref)
    inverse = inverse_ref[...]
    for h in range(HEADS):
        part = slice(h * head, (h + 1) * head)
        out_ref[:, part] = (
            gain_ref[h : h + 1, :] * (attended_ref[:, part] * inverse)
        ).astype(HALF)
        grad = grad_ref[:, part]
        grad_scores = dot(grad, v_ref[:, part], 1, 1)
        grad_scores = jnp.where(mask, grad_scores, 0.0).astype(HALF)
        grad_query = dot(grad_scores, k_ref[:, part], 1, 0) + dot(
            grad, whole_ref[part, :], 1, 1
        )
        grad_query_ref[:, part] = (scaling * grad_query).astype(HALF)
        key_part_ref[:, part] = scaling * dot(grad_scores, q_ref[:, part], 0, 0)
        value_part_ref[:, part] = dot(
            scores_ref[h * rows : (h + 1) * rows, :], grad, 0, 0
        )
    token_ref[...] = jnp.zeros_like(token_ref)


def final_kernel(head, group, *refs):
    k_ref, v_ref, key_part_ref, value_part_ref = refs[:4]
    suffix_refs = refs[4 : 4 + group]
    grad_key_ref, grad_value_ref, gain_grad_ref = refs[4 + group : 7 + group]
    whole_ref, key_buffer, value_buffer, written = refs[7 + group :]
    size = whole_ref.shape[0] // group
    gathered(member_of(group), suffix_refs, size, whole_ref)
    copies = []
    for chunk in range(group):
        for i in range(size // head):
            start = chunk * size + i * head
            part = slice(start, start + head)
            suffix = whole_ref[part, :]
            key_buffer[:, part] = (
                key_part_ref[:, part] + dot(v_ref[:, part], suffix, 1, 1)
            ).astype(HALF)
            value_buffer[:, part] = (
                value_part_ref[:, part] + dot(k_ref[:, part], suffix, 1, 0)
            ).astype(HALF)
        part = slice(chunk * size, (chunk + 1) * size)
        for i, (buffer, ref) in enumerate(
            ((key_buffer, grad_key_ref), (value_buffer, grad_value_ref))
        ):
            copy = pltpu.make_async_copy(
                buffer.at[:, part], ref.at[:, part], written.at[i, chunk]
            )
            copy.start()
            copies.append(copy)
    terms = []
    for ref in suffix_refs:
        rows = (ref.shape[0] - size) // 2
        high, low = ref[size : size + rows, :], ref[size + rows : size + 2 * rows, :]
        terms.append(high.astype(F32) + low.astype(F32))
    while len(terms) > 1:
        terms = [a + b for a, b in zip(terms[::2], terms[1::2])]
    gain_grad_ref[...] = terms[0]
    for copy in copies:
        copy.wait()


def total_kernel(*refs):
    total = refs[0][...].astype(F32)
    for ref in refs[1:-1]:
        total += ref[...].astype(F32)
    refs[-1][...] = total.astype(HALF)


def group_flag(group, reverse, distance):
    index = lax.axis_index("seq") // group
    last = lax.axis_size("seq") // group - 1
    known = index + distance <= last if reverse else index >= distance
    return jnp.where(known, 1.0, 0.0)


def carry_kernel(group, reverse, distance, first, own_ref, moved_ref, out_ref):
    own = own_ref[...].astype(F32)
    if first:
        own = own * group_flag(group, reverse, 1)
    moved = moved_ref[...].astype(F32) * group_flag(group, reverse, distance)
    out_ref[...] = (own + moved).astype(HALF)


def scan_kernel(group, reverse, masked, sums, *refs):
    member = member_of(group)
    carry = refs[0][...].astype(F32)
    if masked:
        carry = carry * group_flag(group, reverse, 1)
    blocks = [ref[...].astype(F32) for ref in refs[1 : 1 + group]]
    out_refs = refs[-group:]
    size = blocks[0].shape[0]
    for j in range(group):
        total = carry
        for i in range(group):
            if i != j:
                earlier = (member ^ i) < (member ^ j)
                keep = jnp.where(earlier != reverse, 1.0, 0.0)
                total += keep * blocks[i]
        out_refs[j][0:size, :] = total.astype(HALF)
    if sums:
        total = refs[1 + group][...]
        for ref in refs[2 + group : 1 + group + sums]:
            total = total + ref[...]
        high = total.astype(HALF)
        low = (total - high.astype(F32)).astype(HALF)
        rows = total.shape[0]
        for ref in out_refs:
            ref[size : size + rows, :] = high
            ref[size + rows : size + 2 * rows, :] = low


VMEM = pl.BlockSpec(memory_space=pltpu.VMEM)
ANY = pl.BlockSpec(memory_space=pl.ANY)
HBM = pl.BlockSpec(memory_space=pltpu.HBM)


def call(
    kernel,
    outs,
    args,
    matmuls,
    scratch=(),
    in_any=(),
    out_any=(),
    in_hbm=(),
    limit=16 * 1024 * 1024,
):
    size = sum(a.size * a.dtype.itemsize for a in args)
    size += sum(o.size * o.dtype.itemsize for o in outs)
    return pl.pallas_call(
        kernel,
        out_shape=tuple(outs),
        in_specs=[
            HBM if i in in_hbm else ANY if i in in_any else VMEM
            for i in range(len(args))
        ],
        out_specs=tuple(HBM if i in out_any else VMEM for i in range(len(outs))),
        scratch_shapes=list(scratch),
        compiler_params=pltpu.CompilerParams(vmem_limit_bytes=limit),
        cost_estimate=pl.CostEstimate(
            flops=2 * 128 * 128 * 128 * HEADS * matmuls,
            bytes_accessed=size,
            transcendentals=0,
        ),
    )(*args)


def swap(array, axis, offset):
    count = lax.axis_size(axis)
    return lax.ppermute(array, axis, [(i, i ^ offset) for i in range(count)])


def own_and_swapped(pieces):
    order = sorted(range(1, len(pieces)), key=lambda j: -bin(j).count("1"))
    moved = {j: swap(pieces[j], "seq", j) for j in order}
    return [pieces[0]] + [moved[j] for j in range(1, len(pieces))]


def exclusive_scan(pieces, reverse, token, gain_part=None):
    group = len(pieces)
    count = lax.axis_size("seq")
    piece = jax.ShapeDtypeStruct(pieces[0].shape, HALF)
    blocks = own_and_swapped(pieces)

    def shifted(array, distance):
        step = -distance if reverse else distance
        pairs = [(i, (i + step) % count) for i in range(count)]
        return lax.ppermute(array, "seq", pairs)

    (total,) = call(total_kernel, [piece], blocks, 0)
    carry = shifted(total, group)
    distance = 1
    while distance < count // group - 1:
        kernel = functools.partial(
            carry_kernel, group, reverse, distance + (distance == 1), distance == 1
        )
        (carry,) = call(kernel, [piece], [carry, shifted(carry, distance * group)], 0)
        distance *= 2
    gains = gain_terms(gain_part, group) if gain_part is not None else []
    rows = piece.shape[0] + 2 * (gain_part.shape[0] if gains else 0)
    inputs = [carry] + blocks + gains + [token]
    sums = call(
        functools.partial(scan_kernel, group, reverse, distance == 1, len(gains)),
        [jax.ShapeDtypeStruct((rows, piece.shape[1]), HALF)] * group,
        inputs,
        0,
        in_any=(len(inputs) - 1,),
    )
    return own_and_swapped(sums)


def gain_terms(array, group):
    for axis, stride in (("dp", 1), ("seq", group)):
        count = lax.axis_size(axis)
        terms = [array]
        while stride < count:
            array = functools.reduce(jnp.add, terms)
            width = 4 if count // stride % 4 == 0 else 2
            terms = [array] + [swap(array, axis, i * stride) for i in range(1, width)]
            if width == 4:
                terms = [terms[0] + terms[1], terms[2] + terms[3]]
            stride *= width
        array = functools.reduce(jnp.add, terms) if axis == "dp" else array
    return terms


def per_device(queries, keys, values, gain, cotangent):
    q, k, v, cot = queries[0], keys[0], values[0], cotangent[0]
    rows, features = q.shape
    head = features // HEADS
    group = 4
    size = features // group
    part = functools.partial
    wide = jax.ShapeDtypeStruct((rows, features), F32)
    half = jax.ShapeDtypeStruct((rows, features), HALF)
    square = jax.ShapeDtypeStruct((rows, head), F32)
    piece = jax.ShapeDtypeStruct((size, head), HALF)
    scores_shape = jax.ShapeDtypeStruct((HEADS * rows, rows), HALF)
    gain_shape = jax.ShapeDtypeStruct((HEADS, head), F32)
    token_shape = jax.ShapeDtypeStruct((8, head), F32)
    whole = pltpu.VMEM((features, head), HALF)
    gain_rows = gain.reshape(HEADS, head)

    pieces = call(
        part(state_kernel, head, group),
        [piece] * group,
        [k, v],
        1,
        [pltpu.VMEM((group, rows, size), HALF)] * 2
        + [pltpu.SemaphoreType.DMA((2, group))],
        in_hbm=(0, 1),
        limit=STATE_LIMIT,
    )
    scores, intra = call(part(local_kernel, head), [scores_shape, wide], [q, k, v], 2)
    prefix = exclusive_scan(pieces, False, intra)
    attended, inverse, grad, gain_part, *pieces = call(
        part(norm_kernel, head, group, lax.axis_size("dp")),
        [wide, square, half, gain_shape] + [piece] * group,
        [q, intra, gain_rows, cot] + prefix,
        2,
        [whole],
    )
    output, grad_query, key_part, value_part, token = call(
        part(backward_kernel, head, group),
        [half, half, wide, wide, token_shape],
        [q, k, v, scores, grad, attended, inverse, gain_rows] + prefix,
        5,
        [whole],
    )
    suffix = exclusive_scan(pieces, True, token, gain_part)
    grad_key, grad_value, gain_grad = call(
        part(final_kernel, head, group),
        [half, half, gain_shape],
        [k, v, key_part, value_part] + suffix,
        2,
        [
            whole,
            pltpu.VMEM((rows, features), HALF),
            pltpu.VMEM((rows, features), HALF),
            pltpu.SemaphoreType.DMA((2, group)),
        ],
        out_any=(0, 1),
    )
    return (
        output[None],
        grad_query[None],
        grad_key[None],
        grad_value[None],
        gain_grad.reshape(features),
    )


def solution(mesh):
    spec = P("dp", "seq", None)
    return jax.shard_map(
        per_device,
        mesh=mesh,
        in_specs=(spec, spec, spec, P(), spec),
        out_specs=(spec, spec, spec, spec, P()),
        check_vma=False,
    )
```

```python
import functools

import jax
import jax.numpy as jnp
from jax import lax
from jax.experimental import pallas as pl
from jax.experimental.pallas import tpu as pltpu
from jax.sharding import PartitionSpec as P

HEADS = 16

EPSILON = 1e-06

F32 = jnp.float32
HALF = jnp.bfloat16


def dot(lhs, rhs, lhs_dim, rhs_dim):
    return lax.dot_general(
        lhs, rhs, (((lhs_dim,), (rhs_dim,)), ((), ())), preferred_element_type=F32
    )


def causal(size):
    rows = lax.broadcasted_iota(jnp.int32, (size, size), 0)
    columns = lax.broadcasted_iota(jnp.int32, (size, size), 1)
    return rows >= columns


def member_of(group):
    return lax.rem(lax.axis_index("seq"), group)


def block_at(index, size):
    return pl.ds(pl.multiple_of(index * size, size), size)


def gathered(member, piece_refs, size, whole_ref):
    for j, ref in enumerate(piece_refs):
        whole_ref[block_at(member ^ j, size), :] = ref[0:size, :]


def scattered(member, whole_ref, size, piece_refs):
    for j, ref in enumerate(piece_refs):
        ref[...] = whole_ref[block_at(member ^ j, size), :]


def columns(first, count):
    return slice(first, first + count)


def loading_state_kernel(head, group, first, k_ref, v_ref, *refs):
    piece_refs = refs[:group]
    whole_ref, k_buffer, v_buffer, arrived = refs[group:]
    rows, width = k_buffer.shape
    step = rows // arrived.shape[1]
    copies = []
    for i in range(arrived.shape[1]):
        part = columns(i * step, step)
        for n, (ref, buffer) in enumerate(((k_ref, k_buffer), (v_ref, v_buffer))):
            copy = pltpu.make_async_copy(
                ref.at[part, columns(first * head, width)],
                buffer.at[part, :],
                arrived.at[n, i],
            )
            copy.start()
            copies.append(copy)
    for copy in copies:
        copy.wait()
    for h in range(width // head):
        part = columns(h * head, head)
        whole_ref[part, :] = dot(k_buffer[:, part], v_buffer[:, part], 0, 0).astype(HALF)
    scattered(member_of(group), whole_ref, piece_refs[0].shape[0], piece_refs)


def state_kernel(head, group, first, k_ref, v_ref, *refs):
    piece_refs = refs[:group]
    whole_ref = refs[group]
    for h in range(whole_ref.shape[0] // head):
        part = columns((first + h) * head, head)
        whole_ref[columns(h * head, head), :] = dot(
            k_ref[:, part], v_ref[:, part], 0, 0
        ).astype(HALF)
    scattered(member_of(group), whole_ref, piece_refs[0].shape[0], piece_refs)


def local_kernel(head, q_ref, k_ref, v_ref, scores_ref, intra_ref):
    rows = q_ref.shape[0]
    mask = causal(rows)
    scaling = head ** (-0.5)
    for h in range(HEADS):
        part = columns(h * head, head)
        scores = dot(q_ref[:, part], k_ref[:, part], 1, 1) * scaling
        scores = jnp.where(mask, scores, 0.0).astype(HALF)
        scores_ref[columns(h * rows, rows), :] = scores
        intra_ref[:, part] = dot(scores, v_ref[:, part], 1, 0)


def norm_kernel(head, group, replicas, streams, *refs):
    q_ref, intra_ref, gain_ref, cot_ref = refs[:4]
    pieces = streams * group
    prefix_refs = refs[4 : 4 + pieces]
    attended_ref, inverse_ref, grad_ref, gain_grad_ref = refs[4 + pieces : 8 + pieces]
    piece_refs = refs[8 + pieces : 8 + 2 * pieces]
    whole_refs = refs[8 + 2 * pieces :]
    member = member_of(group)
    rows = q_ref.shape[0]
    scaling = head ** (-0.5)
    features = HEADS * head
    size = features // pieces
    for s in range(streams):
        gathered(member, prefix_refs[s * group : (s + 1) * group], size, whole_refs[s])
    per_stream = HEADS // streams
    squares = jnp.zeros((rows, head), F32)
    inner = jnp.zeros((rows, head), F32)
    for h in range(HEADS):
        part = columns(h * head, head)
        prefix = whole_refs[h // per_stream][columns(h % per_stream * head, head), :]
        attended = intra_ref[:, part] + scaling * dot(q_ref[:, part], prefix, 1, 0)
        attended_ref[:, part] = attended
        scaled = cot_ref[:, part].astype(F32) * gain_ref[h : h + 1, :]
        squares += attended * attended
        inner += scaled * attended
    inverse = lax.rsqrt(
        jnp.sum(squares, axis=1, keepdims=True) * (1.0 / features) + EPSILON
    )
    inner_mean = jnp.sum(inner, axis=1, keepdims=True) * (1.0 / features) * inverse
    inverse_ref[...] = jnp.broadcast_to(inverse, inverse_ref.shape)
    for h in range(HEADS):
        part = columns(h * head, head)
        normalized = attended_ref[:, part] * inverse
        upstream = cot_ref[:, part].astype(F32)
        gain = gain_ref[h : h + 1, :]
        gain_grad_ref[h : h + 1, :] = jnp.sum(
            upstream * normalized, axis=0, keepdims=True
        ) * (1.0 / replicas)
        grad = ((upstream * gain - normalized * inner_mean) * inverse).astype(HALF)
        grad_ref[:, part] = grad
        whole_refs[h // per_stream][columns(h % per_stream * head, head), :] = (
            scaling * dot(q_ref[:, part], grad, 0, 0)
        ).astype(HALF)
    for s in range(streams):
        scattered(member, whole_refs[s], size, piece_refs[s * group : (s + 1) * group])


def backward_kernel(head, group, first, *refs):
    q_ref, k_ref, v_ref, scores_ref, grad_ref = refs[:5]
    prefix_refs = refs[5 : 5 + group]
    grad_query_ref, key_part_ref, value_part_ref, whole_ref = refs[5 + group :]
    rows = q_ref.shape[0]
    mask = causal(rows)
    scaling = head ** (-0.5)
    gathered(member_of(group), prefix_refs, prefix_refs[0].shape[0], whole_ref)
    for h in range(whole_ref.shape[0] // head):
        part = columns((first + h) * head, head)
        local = columns(h * head, head)
        grad = grad_ref[:, part]
        grad_scores = dot(grad, v_ref[:, part], 1, 1)
        grad_scores = jnp.where(mask, grad_scores, 0.0).astype(HALF)
        grad_query = dot(grad_scores, k_ref[:, part], 1, 0) + dot(
            grad, whole_ref[local, :], 1, 1
        )
        grad_query_ref[:, local] = (scaling * grad_query).astype(HALF)
        key_part_ref[:, local] = scaling * dot(grad_scores, q_ref[:, part], 0, 0)
        value_part_ref[:, local] = dot(
            scores_ref[columns((first + h) * rows, rows), :], grad, 0, 0
        )


def output_kernel(head, *refs):
    attended_ref, inverse_ref, gain_ref = refs[:3]
    query_refs = refs[3:-2]
    out_ref, grad_query_ref = refs[-2:]
    inverse = inverse_ref[...]
    for h in range(HEADS):
        part = columns(h * head, head)
        out_ref[:, part] = (
            gain_ref[h : h + 1, :] * (attended_ref[:, part] * inverse)
        ).astype(HALF)
    width = grad_query_ref.shape[1] // len(query_refs)
    for i, ref in enumerate(query_refs):
        grad_query_ref[:, columns(i * width, width)] = ref[...]


def final_kernel(head, group, first, last, refs):
    k_ref, v_ref, key_part_ref, value_part_ref = refs[:4]
    suffix_refs = refs[4 : 4 + group]
    refs = refs[4 + group + (2 if first else 0) :]
    out_refs, refs = refs[:2], refs[2:]
    if last:
        gain_grad_ref, refs = refs[0], refs[1:]
    whole_ref, key_buffer, value_buffer, written = refs
    gathered(member_of(group), suffix_refs, whole_ref.shape[0] // group, whole_ref)
    chunks = written.shape[1]
    per_chunk = whole_ref.shape[0] // head // chunks
    copies = []
    for chunk in range(chunks):
        for h in range(chunk * per_chunk, (chunk + 1) * per_chunk):
            part = columns((first + h) * head, head)
            local = columns(h * head, head)
            suffix = whole_ref[local, :]
            key_buffer[:, local] = (
                key_part_ref[:, local] + dot(v_ref[:, part], suffix, 1, 1)
            ).astype(HALF)
            value_buffer[:, local] = (
                value_part_ref[:, local] + dot(k_ref[:, part], suffix, 1, 0)
            ).astype(HALF)
        width = per_chunk * head
        for i, buffer in enumerate((key_buffer, value_buffer)):
            copy = pltpu.make_async_copy(
                buffer.at[:, columns(chunk * width, width)],
                out_refs[i].at[:, columns(first * head + chunk * width, width)],
                written.at[i, chunk],
            )
            copy.start()
            copies.append(copy)
    if last:
        terms = [wide_rows(ref, whole_ref.shape[0] // group) for ref in suffix_refs]
        while len(terms) > 1:
            terms = [a + b for a, b in zip(terms[::2], terms[1::2])]
        gain_grad_ref[...] = terms[0]
    for copy in copies:
        copy.wait()


def wide_rows(ref, start):
    rows = (ref.shape[0] - start) // 2
    high = ref[columns(start, rows), :].astype(F32)
    return high + ref[columns(start + rows, rows), :].astype(F32)


def put_wide_rows(ref, start, value):
    rows = value.shape[0]
    high = value.astype(HALF)
    ref[columns(start, rows), :] = high
    ref[columns(start + rows, rows), :] = (value - high.astype(F32)).astype(HALF)


def total_kernel(group, *refs):
    total = refs[0][...].astype(F32)
    for ref in refs[1:group]:
        total += ref[...].astype(F32)
    out_ref = refs[-1]
    size = total.shape[0]
    out_ref[0:size, :] = total.astype(HALF)
    gains = [ref[...] for ref in refs[group:-1]]
    if gains:
        put_wide_rows(out_ref, size, functools.reduce(jnp.add, gains))


def group_flag(group, reverse, distance):
    index = lax.axis_index("seq") // group
    last = lax.axis_size("seq") // group - 1
    known = index + distance <= last if reverse else index >= distance
    return jnp.where(known, 1.0, 0.0)


def carry_kernel(group, reverse, distance, first, own_ref, moved_ref, out_ref):
    own = own_ref[...].astype(F32)
    if first:
        own = own * group_flag(group, reverse, 1)
    moved = moved_ref[...].astype(F32) * group_flag(group, reverse, distance)
    out_ref[...] = (own + moved).astype(HALF)


def scan_kernel(group, reverse, masked, extra, *refs):
    member = member_of(group)
    size = refs[1].shape[0]
    carry = refs[0][0:size, :].astype(F32)
    if masked:
        carry = carry * group_flag(group, reverse, 1)
    blocks = [ref[...].astype(F32) for ref in refs[1 : 1 + group]]
    out_refs = refs[-group:]
    for j in range(group):
        total = carry
        for i in range(group):
            if i != j:
                earlier = (member ^ i) < (member ^ j)
                keep = jnp.where(earlier != reverse, 1.0, 0.0)
                total += keep * blocks[i]
        out_refs[j][0:size, :] = total.astype(HALF)
    if extra == "message":
        total = wide_rows(refs[0], size) + wide_rows(refs[1 + group], size)
    elif extra:
        total = functools.reduce(
            jnp.add, [ref[...] for ref in refs[1 + group : 1 + group + extra]]
        )
    if extra:
        for ref in out_refs:
            put_wide_rows(ref, size, total)


VMEM = pl.BlockSpec(memory_space=pltpu.VMEM)
ANY = pl.BlockSpec(memory_space=pl.ANY)
HBM = pl.BlockSpec(memory_space=pltpu.HBM)


def call(kernel, outs, args, matmuls, scratch=(), ins=None, out_specs=None, aliases=None):
    size = sum(a.size * a.dtype.itemsize for a in args)
    size += sum(o.size * o.dtype.itemsize for o in outs)
    ins = ins or {}
    out_specs = out_specs or {}
    return pl.pallas_call(
        kernel,
        out_shape=tuple(outs),
        in_specs=[ins.get(i, VMEM) for i in range(len(args))],
        out_specs=tuple(out_specs.get(i, VMEM) for i in range(len(outs))),
        scratch_shapes=list(scratch),
        input_output_aliases=aliases or {},
        compiler_params=pltpu.CompilerParams(vmem_limit_bytes=16 * 1024 * 1024),
        cost_estimate=pl.CostEstimate(
            flops=2 * 128 * 128 * 128 * HEADS * matmuls,
            bytes_accessed=size,
            transcendentals=0,
        ),
    )(*args)


def swap(array, axis, offset):
    count = lax.axis_size(axis)
    return lax.ppermute(array, axis, [(i, i ^ offset) for i in range(count)])


def own_and_swapped(pieces):
    order = sorted(range(1, len(pieces)), key=lambda j: -bin(j).count("1"))
    moved = {j: swap(pieces[j], "seq", j) for j in order}
    return [pieces[0]] + [moved[j] for j in range(1, len(pieces))]


def exclusive_scan(streams, reverse, tokens, gain_part=None):
    group = len(streams[0])
    count = lax.axis_size("seq")
    groups = count // group
    part = functools.partial

    def shaped(array, more=0):
        return jax.ShapeDtypeStruct((array.shape[0] + more, array.shape[1]), HALF)

    def shifted(array, distance):
        step = -distance if reverse else distance
        pairs = [(i, (i + step) % count) for i in range(count)]
        return lax.ppermute(array, "seq", pairs)

    blocks = [own_and_swapped(pieces) for pieces in streams]
    gains, rows = [], 0
    if gain_part is not None:
        gains = summed_over("dp", 1, gain_part)
        rows = 2 * gain_part.shape[0]
        if groups != 2:
            gains = summed_over("seq", group, functools.reduce(jnp.add, gains))
    totals, carries = [], []
    for s, received in enumerate(blocks):
        more = gains if s == len(blocks) - 1 and groups == 2 else []
        (total,) = call(
            part(total_kernel, group),
            [shaped(received[0], rows if more else 0)],
            received + more,
            0,
        )
        carry = shifted(total, group)
        distance = 1
        while distance < groups - 1:
            moved = shifted(carry, distance * group)
            kernel = part(
                carry_kernel, group, reverse, distance + (distance == 1), distance == 1
            )
            (carry,) = call(kernel, [shaped(total)], [carry, moved], 0)
            distance *= 2
        totals.append(total)
        carries.append(carry)
    results = []
    for s, received in enumerate(blocks):
        more, extra = [], 0
        if gains and s == len(blocks) - 1:
            more, extra = ([totals[s]], "message") if groups == 2 else (gains, len(gains))
        inputs = [carries[s]] + received + more + tokens[s]
        free = range(len(inputs) - len(tokens[s]), len(inputs))
        sums = call(
            part(scan_kernel, group, reverse, groups <= 2, extra),
            [shaped(received[0], rows if more else 0)] * group,
            inputs,
            0,
            ins={i: ANY for i in free},
        )
        results.append(own_and_swapped(sums))
    return results


def summed_over(axis, stride, array):
    count = lax.axis_size(axis)
    terms = [array]
    while stride < count:
        array = functools.reduce(jnp.add, terms)
        width = 4 if count // stride % 4 == 0 else 2
        terms = [array] + [swap(array, axis, i * stride) for i in range(1, width)]
        if width == 4:
            terms = [terms[0] + terms[1], terms[2] + terms[3]]
        stride *= width
    return terms


def per_device(queries, keys, values, gain, cotangent):
    q, k, v, cot = queries[0], keys[0], values[0], cotangent[0]
    rows, features = q.shape
    head = features // HEADS
    group, streams = 4, 2
    width = features // streams
    heads = HEADS // streams
    part = functools.partial
    wide = jax.ShapeDtypeStruct((rows, features), F32)
    half = jax.ShapeDtypeStruct((rows, features), HALF)
    narrow = jax.ShapeDtypeStruct((rows, width), F32)
    narrow_half = jax.ShapeDtypeStruct((rows, width), HALF)
    square = jax.ShapeDtypeStruct((rows, head), F32)
    piece = jax.ShapeDtypeStruct((width // group, head), HALF)
    scores_shape = jax.ShapeDtypeStruct((HEADS * rows, rows), HALF)
    gain_shape = jax.ShapeDtypeStruct((HEADS, head), F32)
    whole = pltpu.VMEM((width, head), HALF)
    gain_rows = gain.reshape(HEADS, head)

    states = []
    for s in range(streams):
        if s == 0:
            states.append(
                call(
                    part(loading_state_kernel, head, group, 0),
                    [piece] * group,
                    [pltpu.with_memory_space_constraint(a, pltpu.HBM) for a in (k, v)],
                    1,
                    [whole]
                    + [pltpu.VMEM((rows, width), HALF)] * 2
                    + [pltpu.SemaphoreType.DMA((2, 2))],
                    ins={0: HBM, 1: HBM},
                )
            )
        else:
            states.append(
                call(
                    part(state_kernel, head, group, s * heads),
                    [piece] * group,
                    [k, v],
                    1,
                    [whole],
                )
            )
    scores, intra = call(part(local_kernel, head), [scores_shape, wide], [q, k, v], 2)
    prefix = exclusive_scan(states, False, [[intra]] + [[]] * (streams - 1))
    attended, inverse, grad, gain_part, *pieces = call(
        part(norm_kernel, head, group, lax.axis_size("dp"), streams),
        [wide, square, half, gain_shape] + [piece] * (streams * group),
        [q, intra, gain_rows, cot] + sum(prefix, []),
        2,
        [whole] * streams,
    )
    queries_out, key_parts, value_parts = [], [], []
    for s in range(streams):
        grad_query, key_part, value_part = call(
            part(backward_kernel, head, group, s * heads),
            [narrow_half, narrow, narrow],
            [q, k, v, scores, grad] + list(prefix[s]),
            3,
            [whole],
        )
        queries_out.append(grad_query)
        key_parts.append(key_part)
        value_parts.append(value_part)
    output, grad_query = call(
        part(output_kernel, head),
        [half, half],
        [attended, inverse, gain_rows] + queries_out,
        0,
    )
    local = [pieces[s * group : (s + 1) * group] for s in range(streams)]
    tokens = [[key_parts[0]]] + [[]] * (streams - 1)
    suffix = exclusive_scan(local, True, tokens, gain_part)
    outs = []
    for s in range(streams):
        last = s == streams - 1
        inputs = [k, v, key_parts[s], value_parts[s]] + list(suffix[s]) + outs
        known = len(inputs) - len(outs)
        kernel = part(final_kernel, head, group, s * heads, last)
        results = call(
            lambda *refs, kernel=kernel: kernel(refs),
            [half, half] + ([gain_shape] if last else []),
            inputs,
            2,
            [
                whole,
                pltpu.VMEM((rows, width), HALF),
                pltpu.VMEM((rows, width), HALF),
                pltpu.SemaphoreType.DMA((2, 2)),
            ],
            ins={known + i: HBM for i in range(len(outs))},
            out_specs={0: HBM, 1: HBM},
            aliases={known + i: i for i in range(len(outs))},
        )
        outs = list(results[:2])
    grad_key, grad_value = outs
    return (
        output[None],
        grad_query[None],
        grad_key[None],
        grad_value[None],
        results[2].reshape(features),
    )


def solution(mesh):
    spec = P("dp", "seq", None)
    return jax.shard_map(
        per_device,
        mesh=mesh,
        in_specs=(spec, spec, spec, P(), spec),
        out_specs=(spec, spec, spec, spec, P()),
        check_vma=False,
    )
```

```python
import functools

import jax
import jax.numpy as jnp
from jax import lax
from jax.experimental import pallas as pl
from jax.experimental.pallas import tpu as pltpu
from jax.sharding import PartitionSpec as P

HEADS = 16

EPSILON = 1e-06

F32 = jnp.float32
HALF = jnp.bfloat16


def dot(lhs, rhs, lhs_dim, rhs_dim):
    return lax.dot_general(
        lhs, rhs, (((lhs_dim,), (rhs_dim,)), ((), ())), preferred_element_type=F32
    )


def causal(size):
    rows = lax.broadcasted_iota(jnp.int32, (size, size), 0)
    columns = lax.broadcasted_iota(jnp.int32, (size, size), 1)
    return rows >= columns


def member_of(group):
    return lax.rem(lax.axis_index("seq"), group)


def block_at(index, size):
    return pl.ds(pl.multiple_of(index * size, size), size)


def gathered(member, piece_refs, size, whole_ref):
    for j, ref in enumerate(piece_refs):
        whole_ref[block_at(member ^ j, size), :] = ref[0:size, :]


def scattered(member, whole_ref, size, piece_refs):
    for j, ref in enumerate(piece_refs):
        ref[...] = whole_ref[block_at(member ^ j, size), :]


def columns(first, count):
    return slice(first, first + count)


def state_kernel(head, group, k_ref, v_ref, *refs):
    piece_refs = refs[:group]
    whole_ref, k_buffer, v_buffer, arrived = refs[group:]
    copies = [
        pltpu.make_async_copy(k_ref, k_buffer, arrived.at[0]),
        pltpu.make_async_copy(v_ref, v_buffer, arrived.at[1]),
    ]
    for copy in copies:
        copy.start()
    for copy in copies:
        copy.wait()
    for h in range(HEADS):
        part = columns(h * head, head)
        whole_ref[part, :] = dot(k_buffer[:, part], v_buffer[:, part], 0, 0).astype(HALF)
    scattered(member_of(group), whole_ref, piece_refs[0].shape[0], piece_refs)


def local_kernel(head, q_ref, k_ref, v_ref, scores_ref, intra_ref):
    rows = q_ref.shape[0]
    mask = causal(rows)
    scaling = head ** (-0.5)
    for h in range(HEADS):
        part = columns(h * head, head)
        scores = dot(q_ref[:, part], k_ref[:, part], 1, 1) * scaling
        scores = jnp.where(mask, scores, 0.0).astype(HALF)
        scores_ref[columns(h * rows, rows), :] = scores
        intra_ref[:, part] = dot(scores, v_ref[:, part], 1, 0)


def norm_kernel(head, group, replicas, *refs):
    q_ref, intra_ref, gain_ref, cot_ref = refs[:4]
    prefix_refs = refs[4 : 4 + group]
    attended_ref, inverse_ref, grad_ref, gain_grad_ref = refs[4 + group : 8 + group]
    piece_refs = refs[8 + group : 8 + 2 * group]
    whole_ref = refs[8 + 2 * group]
    member = member_of(group)
    rows = q_ref.shape[0]
    scaling = head ** (-0.5)
    features = HEADS * head
    size = features // group
    gathered(member, prefix_refs, size, whole_ref)
    squares = jnp.zeros((rows, head), F32)
    inner = jnp.zeros((rows, head), F32)
    for h in range(HEADS):
        part = columns(h * head, head)
        attended = intra_ref[:, part] + scaling * dot(
            q_ref[:, part], whole_ref[part, :], 1, 0
        )
        attended_ref[:, part] = attended
        scaled = cot_ref[:, part].astype(F32) * gain_ref[h : h + 1, :]
        squares += attended * attended
        inner += scaled * attended
    inverse = lax.rsqrt(
        jnp.sum(squares, axis=1, keepdims=True) * (1.0 / features) + EPSILON
    )
    inner_mean = jnp.sum(inner, axis=1, keepdims=True) * (1.0 / features) * inverse
    inverse_ref[...] = jnp.broadcast_to(inverse, inverse_ref.shape)
    for h in range(HEADS):
        part = columns(h * head, head)
        normalized = attended_ref[:, part] * inverse
        upstream = cot_ref[:, part].astype(F32)
        gain = gain_ref[h : h + 1, :]
        gain_grad_ref[h : h + 1, :] = jnp.sum(
            upstream * normalized, axis=0, keepdims=True
        ) * (1.0 / replicas)
        grad = ((upstream * gain - normalized * inner_mean) * inverse).astype(HALF)
        grad_ref[:, part] = grad
        whole_ref[part, :] = (scaling * dot(q_ref[:, part], grad, 0, 0)).astype(HALF)
    scattered(member, whole_ref, size, piece_refs)


def backward_kernel(head, group, *refs):
    q_ref, k_ref, v_ref, scores_ref, grad_ref = refs[:5]
    attended_ref, inverse_ref, gain_ref = refs[5:8]
    prefix_refs = refs[8 : 8 + group]
    out_ref, grad_query_ref, key_part_ref, value_part_ref, token_ref = refs[
        8 + group : 13 + group
    ]
    whole_ref = refs[13 + group]
    rows = q_ref.shape[0]
    mask = causal(rows)
    scaling = head ** (-0.5)
    gathered(member_of(group), prefix_refs, prefix_refs[0].shape[0], whole_ref)
    inverse = inverse_ref[...]
    for h in range(HEADS):
        part = columns(h * head, head)
        out_ref[:, part] = (
            gain_ref[h : h + 1, :] * (attended_ref[:, part] * inverse)
        ).astype(HALF)
        grad = grad_ref[:, part]
        grad_scores = dot(grad, v_ref[:, part], 1, 1)
        grad_scores = jnp.where(mask, grad_scores, 0.0).astype(HALF)
        grad_query = dot(grad_scores, k_ref[:, part], 1, 0) + dot(
            grad, whole_ref[part, :], 1, 1
        )
        grad_query_ref[:, part] = (scaling * grad_query).astype(HALF)
        key_part_ref[:, part] = scaling * dot(grad_scores, q_ref[:, part], 0, 0)
        value_part_ref[:, part] = dot(
            scores_ref[columns(h * rows, rows), :], grad, 0, 0
        )
    token_ref[...] = jnp.zeros_like(token_ref)


def final_kernel(head, group, chunks, last, *refs):
    k_ref, v_ref, key_part_ref, value_part_ref = refs[:4]
    suffix_refs = refs[4 : 4 + (group if last else len(chunks))]
    refs = refs[4 + len(suffix_refs) + (2 if last else 0) :]
    out_refs, refs = refs[:2], refs[2:]
    if last:
        gain_grad_ref, refs = refs[0], refs[1:]
    key_buffer, value_buffer, written = refs
    member = member_of(group)
    width = key_buffer.shape[2]
    copies = []
    for n, chunk in enumerate(chunks):
        suffix_ref = suffix_refs[chunk if last else n]
        start = (member ^ chunk) * width
        for i in range(width // head):
            part = pl.ds(pl.multiple_of(start + i * head, head), head)
            local = columns(i * head, head)
            suffix = suffix_ref[local, :]
            key_buffer[n, :, local] = (
                key_part_ref[:, part] + dot(v_ref[:, part], suffix, 1, 1)
            ).astype(HALF)
            value_buffer[n, :, local] = (
                value_part_ref[:, part] + dot(k_ref[:, part], suffix, 1, 0)
            ).astype(HALF)
        for i, buffer in enumerate((key_buffer, value_buffer)):
            copy = pltpu.make_async_copy(
                buffer.at[n],
                out_refs[i].at[:, block_at(member ^ chunk, width)],
                written.at[i, n],
            )
            copy.start()
            copies.append(copy)
    if last:
        terms = [wide_rows(ref, width) for ref in suffix_refs]
        while len(terms) > 1:
            terms = [a + b for a, b in zip(terms[::2], terms[1::2])]
        gain_grad_ref[...] = terms[0]
    for copy in copies:
        copy.wait()


def wide_rows(ref, start):
    rows = (ref.shape[0] - start) // 2
    high = ref[columns(start, rows), :].astype(F32)
    return high + ref[columns(start + rows, rows), :].astype(F32)


def put_wide_rows(ref, start, value):
    rows = value.shape[0]
    high = value.astype(HALF)
    ref[columns(start, rows), :] = high
    ref[columns(start + rows, rows), :] = (value - high.astype(F32)).astype(HALF)


def total_kernel(group, *refs):
    total = refs[0][...].astype(F32)
    for ref in refs[1:group]:
        total += ref[...].astype(F32)
    out_ref = refs[-1]
    size = total.shape[0]
    out_ref[0:size, :] = total.astype(HALF)
    gains = [ref[...] for ref in refs[group:-1]]
    if gains:
        put_wide_rows(out_ref, size, functools.reduce(jnp.add, gains))


def group_flag(group, reverse, distance):
    index = lax.axis_index("seq") // group
    last = lax.axis_size("seq") // group - 1
    known = index + distance <= last if reverse else index >= distance
    return jnp.where(known, 1.0, 0.0)


def carry_kernel(group, reverse, distance, first, own_ref, moved_ref, out_ref):
    own = own_ref[...].astype(F32)
    if first:
        own = own * group_flag(group, reverse, 1)
    moved = moved_ref[...].astype(F32) * group_flag(group, reverse, distance)
    out_ref[...] = (own + moved).astype(HALF)


def scan_kernel(group, reverse, masked, extra, *refs):
    member = member_of(group)
    size = refs[1].shape[0]
    carry = refs[0][0:size, :].astype(F32)
    if masked:
        carry = carry * group_flag(group, reverse, 1)
    blocks = [ref[...].astype(F32) for ref in refs[1 : 1 + group]]
    out_refs = refs[-group:]
    for j in range(group):
        total = carry
        for i in range(group):
            if i != j:
                earlier = (member ^ i) < (member ^ j)
                keep = jnp.where(earlier != reverse, 1.0, 0.0)
                total += keep * blocks[i]
        out_refs[j][0:size, :] = total.astype(HALF)
    if extra == "message":
        total = wide_rows(refs[0], size) + wide_rows(refs[1 + group], size)
    elif extra:
        total = functools.reduce(
            jnp.add, [ref[...] for ref in refs[1 + group : 1 + group + extra]]
        )
    if extra:
        for ref in out_refs:
            put_wide_rows(ref, size, total)


VMEM = pl.BlockSpec(memory_space=pltpu.VMEM)
ANY = pl.BlockSpec(memory_space=pl.ANY)
HBM = pl.BlockSpec(memory_space=pltpu.HBM)


def call(kernel, outs, args, matmuls, scratch=(), ins=None, out_specs=None, aliases=None):
    size = sum(a.size * a.dtype.itemsize for a in args)
    size += sum(o.size * o.dtype.itemsize for o in outs)
    ins = ins or {}
    out_specs = out_specs or {}
    return pl.pallas_call(
        kernel,
        out_shape=tuple(outs),
        in_specs=[ins.get(i, VMEM) for i in range(len(args))],
        out_specs=tuple(out_specs.get(i, VMEM) for i in range(len(outs))),
        scratch_shapes=list(scratch),
        input_output_aliases=aliases or {},
        compiler_params=pltpu.CompilerParams(vmem_limit_bytes=16 * 1024 * 1024),
        cost_estimate=pl.CostEstimate(
            flops=2 * 128 * 128 * 128 * HEADS * matmuls,
            bytes_accessed=size,
            transcendentals=0,
        ),
    )(*args)


def swap(array, axis, offset):
    count = lax.axis_size(axis)
    return lax.ppermute(array, axis, [(i, i ^ offset) for i in range(count)])


def own_and_swapped(pieces):
    order = sorted(range(1, len(pieces)), key=lambda j: -bin(j).count("1"))
    moved = {j: swap(pieces[j], "seq", j) for j in order}
    return [pieces[0]] + [moved[j] for j in range(1, len(pieces))]


def exclusive_scan(pieces, reverse, token, gain_part=None):
    group = len(pieces)
    count = lax.axis_size("seq")
    groups = count // group
    part = functools.partial

    def shaped(more=0):
        return jax.ShapeDtypeStruct((pieces[0].shape[0] + more, pieces[0].shape[1]), HALF)

    def shifted(array, distance):
        step = -distance if reverse else distance
        pairs = [(i, (i + step) % count) for i in range(count)]
        return lax.ppermute(array, "seq", pairs)

    received = own_and_swapped(pieces)
    gains, rows = [], 0
    if gain_part is not None:
        gains = summed_over("dp", 1, gain_part)
        rows = 2 * gain_part.shape[0]
        if groups != 2:
            gains = summed_over("seq", group, functools.reduce(jnp.add, gains))
    riding = gains if groups == 2 else []
    (total,) = call(
        part(total_kernel, group), [shaped(rows if riding else 0)], received + riding, 0
    )
    carry = shifted(total, group)
    distance = 1
    while distance < groups - 1:
        moved = shifted(carry, distance * group)
        kernel = part(
            carry_kernel, group, reverse, distance + (distance == 1), distance == 1
        )
        (carry,) = call(kernel, [shaped()], [carry, moved], 0)
        distance *= 2
    more, extra = [], 0
    if gains:
        more, extra = ([total], "message") if riding else (gains, len(gains))
    inputs = [carry] + received + more + [token]
    sums = call(
        part(scan_kernel, group, reverse, groups <= 2, extra),
        [shaped(rows)] * group,
        inputs,
        0,
        ins={len(inputs) - 1: ANY},
    )
    return own_and_swapped(sums)


def summed_over(axis, stride, array):
    count = lax.axis_size(axis)
    terms = [array]
    while stride < count:
        array = functools.reduce(jnp.add, terms)
        width = 4 if count // stride % 4 == 0 else 2
        terms = [array] + [swap(array, axis, i * stride) for i in range(1, width)]
        if width == 4:
            terms = [terms[0] + terms[1], terms[2] + terms[3]]
        stride *= width
    return terms


def per_device(queries, keys, values, gain, cotangent):
    q, k, v, cot = queries[0], keys[0], values[0], cotangent[0]
    rows, features = q.shape
    head = features // HEADS
    group = 4
    width = features // group
    part = functools.partial
    wide = jax.ShapeDtypeStruct((rows, features), F32)
    half = jax.ShapeDtypeStruct((rows, features), HALF)
    square = jax.ShapeDtypeStruct((rows, head), F32)
    piece = jax.ShapeDtypeStruct((width, head), HALF)
    scores_shape = jax.ShapeDtypeStruct((HEADS * rows, rows), HALF)
    gain_shape = jax.ShapeDtypeStruct((HEADS, head), F32)
    token_shape = jax.ShapeDtypeStruct((8, head), F32)
    whole = pltpu.VMEM((features, head), HALF)
    gain_rows = gain.reshape(HEADS, head)

    pieces = call(
        part(state_kernel, head, group),
        [piece] * group,
        [pltpu.with_memory_space_constraint(a, pltpu.HBM) for a in (k, v)],
        1,
        [whole]
        + [pltpu.VMEM((rows, features), HALF)] * 2
        + [pltpu.SemaphoreType.DMA((2,))],
        ins={0: HBM, 1: HBM},
    )
    scores, intra = call(part(local_kernel, head), [scores_shape, wide], [q, k, v], 2)
    prefix = exclusive_scan(pieces, False, intra)
    attended, inverse, grad, gain_part, *pieces = call(
        part(norm_kernel, head, group, lax.axis_size("dp")),
        [wide, square, half, gain_shape] + [piece] * group,
        [q, intra, gain_rows, cot] + prefix,
        2,
        [whole],
    )
    output, grad_query, key_part, value_part, token = call(
        part(backward_kernel, head, group),
        [half, half, wide, wide, token_shape],
        [q, k, v, scores, grad, attended, inverse, gain_rows] + prefix,
        5,
        [whole],
    )
    suffix = exclusive_scan(pieces, True, token, gain_part)
    inputs = [k, v, key_part, value_part]
    early, late = [0, 3, 1], [2]

    def buffers(count):
        return [pltpu.VMEM((count, rows, width), HALF)] * 2 + [
            pltpu.SemaphoreType.DMA((2, count))
        ]

    first = call(
        part(final_kernel, head, group, early, False),
        [half, half],
        inputs + [suffix[j] for j in early],
        1,
        buffers(len(early)),
        out_specs={0: HBM, 1: HBM},
    )
    at = len(inputs) + group
    grad_key, grad_value, gain_grad = call(
        part(final_kernel, head, group, late, True),
        [half, half, gain_shape],
        inputs + suffix + list(first),
        1,
        buffers(len(late)),
        ins={at: HBM, at + 1: HBM},
        out_specs={0: HBM, 1: HBM},
        aliases={at: 0, at + 1: 1},
    )
    return (
        output[None],
        grad_query[None],
        grad_key[None],
        grad_value[None],
        gain_grad.reshape(features),
    )


def solution(mesh):
    spec = P("dp", "seq", None)
    return jax.shard_map(
        per_device,
        mesh=mesh,
        in_specs=(spec, spec, spec, P(), spec),
        out_specs=(spec, spec, spec, spec, P()),
        check_vma=False,
    )
```

```python
import functools

import jax
import jax.numpy as jnp
from jax import lax
from jax.experimental import pallas as pl
from jax.experimental.pallas import tpu as pltpu
from jax.sharding import PartitionSpec as P

HEADS = 16

EPSILON = 1e-06

F32 = jnp.float32
HALF = jnp.bfloat16


def dot(lhs, rhs, lhs_dim, rhs_dim):
    return lax.dot_general(
        lhs, rhs, (((lhs_dim,), (rhs_dim,)), ((), ())), preferred_element_type=F32
    )


def causal(size):
    rows = lax.broadcasted_iota(jnp.int32, (size, size), 0)
    columns = lax.broadcasted_iota(jnp.int32, (size, size), 1)
    return rows >= columns


def member_of(group):
    return lax.rem(lax.axis_index("seq"), group)


def block_at(index, size):
    return pl.ds(pl.multiple_of(index * size, size), size)


def gathered(member, piece_refs, size, whole_ref):
    for j, ref in enumerate(piece_refs):
        whole_ref[block_at(member ^ j, size), :] = ref[0:size, :]


def scattered(member, whole_ref, size, piece_refs):
    for j, ref in enumerate(piece_refs):
        ref[0:size, :] = whole_ref[block_at(member ^ j, size), :]


def columns(first, count):
    return slice(first, first + count)


def state_kernel(head, group, k_ref, v_ref, *refs):
    piece_refs = refs[:group]
    whole_ref, k_buffer, v_buffer, arrived = refs[group:]
    copies = [
        pltpu.make_async_copy(k_ref, k_buffer, arrived.at[0]),
        pltpu.make_async_copy(v_ref, v_buffer, arrived.at[1]),
    ]
    for copy in copies:
        copy.start()
    for copy in copies:
        copy.wait()
    for h in range(HEADS):
        part = columns(h * head, head)
        whole_ref[part, :] = dot(k_buffer[:, part], v_buffer[:, part], 0, 0).astype(HALF)
    scattered(member_of(group), whole_ref, piece_refs[0].shape[0], piece_refs)


def local_kernel(head, q_ref, k_ref, v_ref, scores_ref, intra_ref):
    rows = q_ref.shape[0]
    mask = causal(rows)
    scaling = head ** (-0.5)
    for h in range(HEADS):
        part = columns(h * head, head)
        scores = dot(q_ref[:, part], k_ref[:, part], 1, 1) * scaling
        scores = jnp.where(mask, scores, 0.0).astype(HALF)
        scores_ref[columns(h * rows, rows), :] = scores
        intra_ref[:, part] = dot(scores, v_ref[:, part], 1, 0)


def norm_kernel(head, group, replicas, *refs):
    q_ref, intra_ref, gain_ref, cot_ref = refs[:4]
    prefix_refs = refs[4 : 4 + group]
    attended_ref, inverse_ref, grad_ref = refs[4 + group : 7 + group]
    piece_refs = refs[7 + group : 7 + 2 * group]
    whole_ref, gain_grad_ref = refs[7 + 2 * group :]
    member = member_of(group)
    rows = q_ref.shape[0]
    scaling = head ** (-0.5)
    features = HEADS * head
    size = features // group
    gathered(member, prefix_refs, size, whole_ref)
    squares = jnp.zeros((rows, head), F32)
    inner = jnp.zeros((rows, head), F32)
    for h in range(HEADS):
        part = columns(h * head, head)
        attended = intra_ref[:, part] + scaling * dot(
            q_ref[:, part], whole_ref[part, :], 1, 0
        )
        attended_ref[:, part] = attended
        scaled = cot_ref[:, part].astype(F32) * gain_ref[h : h + 1, :]
        squares += attended * attended
        inner += scaled * attended
    inverse = lax.rsqrt(
        jnp.sum(squares, axis=1, keepdims=True) * (1.0 / features) + EPSILON
    )
    inner_mean = jnp.sum(inner, axis=1, keepdims=True) * (1.0 / features) * inverse
    inverse_ref[...] = jnp.broadcast_to(inverse, inverse_ref.shape)
    for h in range(HEADS):
        part = columns(h * head, head)
        normalized = attended_ref[:, part] * inverse
        upstream = cot_ref[:, part].astype(F32)
        gain = gain_ref[h : h + 1, :]
        gain_grad_ref[h : h + 1, :] = jnp.sum(
            upstream * normalized, axis=0, keepdims=True
        ) * (1.0 / replicas)
        grad = ((upstream * gain - normalized * inner_mean) * inverse).astype(HALF)
        grad_ref[:, part] = grad
        whole_ref[part, :] = (scaling * dot(q_ref[:, part], grad, 0, 0)).astype(HALF)
    scattered(member, whole_ref, size, piece_refs)
    for ref in piece_refs:
        put_wide_rows(ref, size, gain_grad_ref[...])


def backward_kernel(head, group, *refs):
    q_ref, k_ref, v_ref, scores_ref, grad_ref = refs[:5]
    attended_ref, inverse_ref, gain_ref = refs[5:8]
    prefix_refs = refs[8 : 8 + group]
    out_ref, grad_query_ref, key_part_ref, value_part_ref, token_ref = refs[
        8 + group : 13 + group
    ]
    whole_ref = refs[13 + group]
    rows = q_ref.shape[0]
    mask = causal(rows)
    scaling = head ** (-0.5)
    gathered(member_of(group), prefix_refs, prefix_refs[0].shape[0], whole_ref)
    inverse = inverse_ref[...]
    for h in range(HEADS):
        part = columns(h * head, head)
        out_ref[:, part] = (
            gain_ref[h : h + 1, :] * (attended_ref[:, part] * inverse)
        ).astype(HALF)
        grad = grad_ref[:, part]
        grad_scores = dot(grad, v_ref[:, part], 1, 1)
        grad_scores = jnp.where(mask, grad_scores, 0.0).astype(HALF)
        grad_query = dot(grad_scores, k_ref[:, part], 1, 0) + dot(
            grad, whole_ref[part, :], 1, 1
        )
        grad_query_ref[:, part] = (scaling * grad_query).astype(HALF)
        key_part_ref[:, part] = scaling * dot(grad_scores, q_ref[:, part], 0, 0)
        value_part_ref[:, part] = dot(
            scores_ref[columns(h * rows, rows), :], grad, 0, 0
        )
    token_ref[...] = jnp.zeros_like(token_ref)


def final_kernel(head, group, chunks, last, *refs):
    k_ref, v_ref, key_part_ref, value_part_ref = refs[:4]
    suffix_refs = refs[4 : 4 + len(chunks)]
    refs = refs[4 + len(suffix_refs) :]
    copies = []
    if last:
        gain_grad_ref, total_ref, gain_written = refs[-6], refs[-2], refs[-1]
        total_ref[...] = tree_sum([ref[...] for ref in refs[2:-8]])
        copies.append(pltpu.make_async_copy(total_ref, gain_grad_ref, gain_written))
        copies[0].start()
        out_refs, refs = refs[-8:-6], refs[-5:-2]
    else:
        out_refs, refs = refs[:2], refs[2:]
    key_buffer, value_buffer, written = refs
    member = member_of(group)
    width = key_buffer.shape[2]
    for n, chunk in enumerate(chunks):
        suffix_ref = suffix_refs[n]
        start = (member ^ chunk) * width
        for i in range(width // head):
            part = pl.ds(pl.multiple_of(start + i * head, head), head)
            local = columns(i * head, head)
            suffix = suffix_ref[local, :]
            key_buffer[n, :, local] = (
                key_part_ref[:, part] + dot(v_ref[:, part], suffix, 1, 1)
            ).astype(HALF)
            value_buffer[n, :, local] = (
                value_part_ref[:, part] + dot(k_ref[:, part], suffix, 1, 0)
            ).astype(HALF)
        for i, buffer in enumerate((key_buffer, value_buffer)):
            copy = pltpu.make_async_copy(
                buffer.at[n],
                out_refs[i].at[:, block_at(member ^ chunk, width)],
                written.at[i, n],
            )
            copy.start()
            copies.append(copy)
    for copy in copies:
        copy.wait()


def tree_sum(terms):
    while len(terms) > 1:
        terms = [a + b for a, b in zip(terms[::2], terms[1::2])]
    return terms[0]


def wide_rows(ref, start):
    rows = (ref.shape[0] - start) // 2
    high = ref[columns(start, rows), :].astype(F32)
    return high + ref[columns(start + rows, rows), :].astype(F32)


def put_wide_rows(ref, start, value):
    rows = value.shape[0]
    high = value.astype(HALF)
    ref[columns(start, rows), :] = high
    ref[columns(start + rows, rows), :] = (value - high.astype(F32)).astype(HALF)


def total_kernel(size, *refs):
    out_ref = refs[-1]
    total = refs[0][0:size, :].astype(F32)
    for ref in refs[1:-1]:
        total += ref[0:size, :].astype(F32)
    out_ref[0:size, :] = total.astype(HALF)
    if out_ref.shape[0] > size:
        put_wide_rows(out_ref, size, tree_sum([wide_rows(ref, size) for ref in refs[:-1]]))


def group_flag(group, reverse, distance):
    index = lax.axis_index("seq") // group
    last = lax.axis_size("seq") // group - 1
    known = index + distance <= last if reverse else index >= distance
    return jnp.where(known, 1.0, 0.0)


def carry_kernel(group, reverse, distance, first, own_ref, moved_ref, out_ref):
    own = own_ref[...].astype(F32)
    if first:
        own = own * group_flag(group, reverse, 1)
    moved = moved_ref[...].astype(F32) * group_flag(group, reverse, distance)
    out_ref[...] = (own + moved).astype(HALF)


def scan_kernel(group, reverse, masked, size, riding, *refs):
    member = member_of(group)
    carry = refs[0][0:size, :].astype(F32)
    if masked:
        carry = carry * group_flag(group, reverse, 1)
    blocks = [ref[0:size, :].astype(F32) for ref in refs[1 : 1 + group]]
    out_refs = refs[-group - riding :][:group]
    for j in range(group):
        total = carry
        for i in range(group):
            if i != j:
                earlier = (member ^ i) < (member ^ j)
                keep = jnp.where(earlier != reverse, 1.0, 0.0)
                total += keep * blocks[i]
        out_refs[j][...] = total.astype(HALF)
    if riding:
        refs[-1][...] = wide_rows(refs[0], size) + wide_rows(refs[1 + group], size)


VMEM = pl.BlockSpec(memory_space=pltpu.VMEM)
ANY = pl.BlockSpec(memory_space=pl.ANY)
HBM = pl.BlockSpec(memory_space=pltpu.HBM)


def call(kernel, outs, args, matmuls, scratch=(), ins=None, out_specs=None, aliases=None):
    size = sum(a.size * a.dtype.itemsize for a in args)
    size += sum(o.size * o.dtype.itemsize for o in outs)
    ins = ins or {}
    out_specs = out_specs or {}
    return pl.pallas_call(
        kernel,
        out_shape=tuple(outs),
        in_specs=[ins.get(i, VMEM) for i in range(len(args))],
        out_specs=tuple(out_specs.get(i, VMEM) for i in range(len(outs))),
        scratch_shapes=list(scratch),
        input_output_aliases=aliases or {},
        compiler_params=pltpu.CompilerParams(vmem_limit_bytes=16 * 1024 * 1024),
        cost_estimate=pl.CostEstimate(
            flops=2 * 128 * 128 * 128 * HEADS * matmuls,
            bytes_accessed=size,
            transcendentals=0,
        ),
    )(*args)


def swap(array, axis, offset):
    count = lax.axis_size(axis)
    return lax.ppermute(array, axis, [(i, i ^ offset) for i in range(count)])


def own_and_swapped(pieces):
    order = sorted(range(1, len(pieces)), key=lambda j: -bin(j).count("1"))
    moved = {j: swap(pieces[j], "seq", j) for j in order}
    return [pieces[0]] + [moved[j] for j in range(1, len(pieces))]


def exclusive_scan(pieces, size, reverse, token):
    group = len(pieces)
    count = lax.axis_size("seq")
    groups = count // group
    part = functools.partial
    lanes = pieces[0].shape[1]
    extra = pieces[0].shape[0] - size
    piece = jax.ShapeDtypeStruct((size, lanes), HALF)
    gain_shape = jax.ShapeDtypeStruct((extra // 2, lanes), F32)

    def shifted(array, distance):
        step = -distance if reverse else distance
        pairs = [(i, (i + step) % count) for i in range(count)]
        return lax.ppermute(array, "seq", pairs)

    received = own_and_swapped(pieces)
    (total,) = call(
        part(total_kernel, size),
        [jax.ShapeDtypeStruct(pieces[0].shape, HALF)],
        received,
        0,
    )
    riding = int(extra > 0 and groups == 2)
    gain = None
    if extra and not riding:
        gain = total[size : size + extra // 2].astype(F32) + total[size + extra // 2 :]
        gain = tree_sum(summed_over("seq", group, gain))
        total = total[:size]
    carry = shifted(total, group)
    distance = 1
    while distance < groups - 1:
        moved = shifted(carry, distance * group)
        kernel = part(
            carry_kernel, group, reverse, distance + (distance == 1), distance == 1
        )
        (carry,) = call(kernel, [piece], [carry, moved], 0)
        distance *= 2
    inputs = [carry] + received + ([total] if riding else []) + [token]
    sums = call(
        part(scan_kernel, group, reverse, groups <= 2, size, riding),
        [piece] * group + [gain_shape] * riding,
        inputs,
        0,
        ins={len(inputs) - 1: ANY},
    )
    results = own_and_swapped(sums[:group])
    return results, (sums[-1] if riding else gain)


def summed_over(axis, stride, array):
    count = lax.axis_size(axis)
    terms = [array]
    while stride < count:
        array = tree_sum(terms)
        width = 4 if count // stride % 4 == 0 else 2
        terms = [array] + [swap(array, axis, i * stride) for i in range(1, width)]
        stride *= width
    return terms


def per_device(queries, keys, values, gain, cotangent):
    q, k, v, cot = queries[0], keys[0], values[0], cotangent[0]
    rows, features = q.shape
    head = features // HEADS
    group = 4
    width = features // group
    part = functools.partial
    wide = jax.ShapeDtypeStruct((rows, features), F32)
    half = jax.ShapeDtypeStruct((rows, features), HALF)
    square = jax.ShapeDtypeStruct((rows, head), F32)
    piece = jax.ShapeDtypeStruct((width, head), HALF)
    scores_shape = jax.ShapeDtypeStruct((HEADS * rows, rows), HALF)
    gain_shape = jax.ShapeDtypeStruct((HEADS, head), F32)
    token_shape = jax.ShapeDtypeStruct((8, head), F32)
    whole = pltpu.VMEM((features, head), HALF)
    gain_rows = gain.reshape(HEADS, head)

    pieces = call(
        part(state_kernel, head, group),
        [piece] * group,
        [pltpu.with_memory_space_constraint(a, pltpu.HBM) for a in (k, v)],
        1,
        [whole]
        + [pltpu.VMEM((rows, features), HALF)] * 2
        + [pltpu.SemaphoreType.DMA((2,))],
        ins={0: HBM, 1: HBM},
    )
    scores, intra = call(part(local_kernel, head), [scores_shape, wide], [q, k, v], 2)
    prefix, _ = exclusive_scan(pieces, width, False, intra)
    message = jax.ShapeDtypeStruct((width + 2 * HEADS, head), HALF)
    attended, inverse, grad, *pieces = call(
        part(norm_kernel, head, group, lax.axis_size("dp")),
        [wide, square, half] + [message] * group,
        [q, intra, gain_rows, cot] + prefix,
        2,
        [whole, pltpu.VMEM((HEADS, head), F32)],
    )
    output, grad_query, key_part, value_part, token = call(
        part(backward_kernel, head, group),
        [half, half, wide, wide, token_shape],
        [q, k, v, scores, grad, attended, inverse, gain_rows] + prefix,
        5,
        [whole],
    )
    suffix, gain_grad = exclusive_scan(pieces, width, True, token)
    gains = summed_over("dp", 1, gain_grad)
    inputs = [k, v, key_part, value_part]
    early, late = [0, 3, 1], [2]

    def buffers(count):
        return [pltpu.VMEM((count, rows, width), HALF)] * 2 + [
            pltpu.SemaphoreType.DMA((2, count))
        ]

    first = call(
        part(final_kernel, head, group, early, False),
        [half, half],
        inputs + [suffix[j] for j in early],
        1,
        buffers(len(early)),
        out_specs={0: HBM, 1: HBM},
    )
    at = len(inputs) + len(late)
    grad_key, grad_value, gain_grad = call(
        part(final_kernel, head, group, late, True),
        [half, half, gain_shape],
        inputs + [suffix[j] for j in late] + list(first) + gains,
        1,
        buffers(len(late))
        + [pltpu.VMEM((HEADS, head), F32), pltpu.SemaphoreType.DMA(())],
        ins={at: HBM, at + 1: HBM},
        out_specs={0: HBM, 1: HBM, 2: HBM},
        aliases={at: 0, at + 1: 1},
    )
    return (
        output[None],
        grad_query[None],
        grad_key[None],
        grad_value[None],
        gain_grad.reshape(features),
    )


def solution(mesh):
    spec = P("dp", "seq", None)
    return jax.shard_map(
        per_device,
        mesh=mesh,
        in_specs=(spec, spec, spec, P(), spec),
        out_specs=(spec, spec, spec, spec, P()),
        check_vma=False,
    )
```

```python
import functools

import jax
import jax.numpy as jnp
from jax import lax
from jax.experimental import pallas as pl
from jax.experimental.pallas import tpu as pltpu
from jax.sharding import PartitionSpec as P

HEADS = 16

EPSILON = 1e-06

F32 = jnp.float32
HALF = jnp.bfloat16


def dot(lhs, rhs, lhs_dim, rhs_dim):
    return lax.dot_general(
        lhs, rhs, (((lhs_dim,), (rhs_dim,)), ((), ())), preferred_element_type=F32
    )


def causal(size):
    rows = lax.broadcasted_iota(jnp.int32, (size, size), 0)
    columns = lax.broadcasted_iota(jnp.int32, (size, size), 1)
    return rows >= columns


def member_of(group):
    return lax.rem(lax.axis_index("seq"), group)


def block_at(index, size):
    return pl.ds(pl.multiple_of(index * size, size), size)


def gathered(member, piece_refs, size, whole_ref):
    for j, ref in enumerate(piece_refs):
        whole_ref[block_at(member ^ j, size), :] = ref[0:size, :]


def scattered(member, whole_ref, size, piece_refs):
    for j, ref in enumerate(piece_refs):
        ref[0:size, :] = whole_ref[block_at(member ^ j, size), :]


def columns(first, count):
    return slice(first, first + count)


def second_core():
    return lax.rem(lax.axis_index("dp"), 2) == 1


def state_kernel(head, group, k_ref, v_ref, q_ref, *refs):
    piece_refs = refs[:group]
    scores_ref, intra_ref = refs[group : 2 + group]
    whole_ref, k_buffer, v_buffer, q_buffer, arrived = refs[2 + group :]
    pairs = ((k_ref, k_buffer), (v_ref, v_buffer), (q_ref, q_buffer))
    copies = [
        pltpu.make_async_copy(ref, buffer, arrived.at[i])
        for i, (ref, buffer) in enumerate(pairs)
    ]
    for copy in copies:
        copy.start()
    for copy in copies[:2]:
        copy.wait()
    for h in range(HEADS):
        part = columns(h * head, head)
        whole_ref[part, :] = dot(k_buffer[:, part], v_buffer[:, part], 0, 0).astype(HALF)
    scattered(member_of(group), whole_ref, piece_refs[0].shape[0], piece_refs)
    copies[2].wait()

    @pl.when(second_core())
    def _():
        local_attention(head, q_buffer, k_buffer, v_buffer, scores_ref, intra_ref)


def local_attention(head, q_ref, k_ref, v_ref, scores_ref, intra_ref):
    rows = q_ref.shape[0]
    mask = causal(rows)
    scaling = head ** (-0.5)
    for h in range(HEADS):
        part = columns(h * head, head)
        scores = dot(q_ref[:, part], k_ref[:, part], 1, 1) * scaling
        scores = jnp.where(mask, scores, 0.0).astype(HALF)
        scores_ref[columns(h * rows, rows), :] = scores
        intra_ref[:, part] = dot(scores, v_ref[:, part], 1, 0)


def local_kernel(head, q_ref, k_ref, v_ref, scores_in, intra_in, scores_ref, intra_ref):
    @pl.when(jnp.logical_not(second_core()))
    def _():
        local_attention(head, q_ref, k_ref, v_ref, scores_ref, intra_ref)

    @pl.when(second_core())
    def _():
        scores_ref[...] = scores_in[...]
        intra_ref[...] = intra_in[...]


def norm_kernel(head, group, replicas, *refs):
    q_ref, intra_ref, gain_ref, cot_ref = refs[:4]
    prefix_refs = refs[4 : 4 + group]
    attended_ref, inverse_ref, grad_ref = refs[4 + group : 7 + group]
    piece_refs = refs[7 + group : 7 + 2 * group]
    whole_ref, gain_grad_ref = refs[7 + 2 * group :]
    member = member_of(group)
    rows = q_ref.shape[0]
    scaling = head ** (-0.5)
    features = HEADS * head
    size = features // group
    gathered(member, prefix_refs, size, whole_ref)
    squares = jnp.zeros((rows, head), F32)
    inner = jnp.zeros((rows, head), F32)
    for h in range(HEADS):
        part = columns(h * head, head)
        attended = intra_ref[:, part] + scaling * dot(
            q_ref[:, part], whole_ref[part, :], 1, 0
        )
        attended_ref[:, part] = attended
        scaled = cot_ref[:, part].astype(F32) * gain_ref[h : h + 1, :]
        squares += attended * attended
        inner += scaled * attended
    inverse = lax.rsqrt(
        jnp.sum(squares, axis=1, keepdims=True) * (1.0 / features) + EPSILON
    )
    inner_mean = jnp.sum(inner, axis=1, keepdims=True) * (1.0 / features) * inverse
    inverse_ref[...] = jnp.broadcast_to(inverse, inverse_ref.shape)
    for h in range(HEADS):
        part = columns(h * head, head)
        normalized = attended_ref[:, part] * inverse
        upstream = cot_ref[:, part].astype(F32)
        gain = gain_ref[h : h + 1, :]
        gain_grad_ref[h : h + 1, :] = jnp.sum(
            upstream * normalized, axis=0, keepdims=True
        ) * (1.0 / replicas)
        grad = ((upstream * gain - normalized * inner_mean) * inverse).astype(HALF)
        grad_ref[:, part] = grad
        whole_ref[part, :] = (scaling * dot(q_ref[:, part], grad, 0, 0)).astype(HALF)
    scattered(member, whole_ref, size, piece_refs)
    for ref in piece_refs:
        put_wide_rows(ref, size, gain_grad_ref[...])


def backward_kernel(head, group, *refs):
    q_ref, k_ref, v_ref, scores_ref, grad_ref = refs[:5]
    attended_ref, inverse_ref, gain_ref = refs[5:8]
    prefix_refs = refs[8 : 8 + group]
    out_ref, grad_query_ref, key_part_ref, value_part_ref, token_ref = refs[
        8 + group : 13 + group
    ]
    whole_ref = refs[13 + group]
    rows = q_ref.shape[0]
    mask = causal(rows)
    scaling = head ** (-0.5)
    gathered(member_of(group), prefix_refs, prefix_refs[0].shape[0], whole_ref)
    inverse = inverse_ref[...]
    for h in range(HEADS):
        part = columns(h * head, head)
        out_ref[:, part] = (
            gain_ref[h : h + 1, :] * (attended_ref[:, part] * inverse)
        ).astype(HALF)
        grad = grad_ref[:, part]
        grad_scores = dot(grad, v_ref[:, part], 1, 1)
        grad_scores = jnp.where(mask, grad_scores, 0.0).astype(HALF)
        grad_query = dot(grad_scores, k_ref[:, part], 1, 0) + dot(
            grad, whole_ref[part, :], 1, 1
        )
        grad_query_ref[:, part] = (scaling * grad_query).astype(HALF)
        key_part_ref[:, part] = scaling * dot(grad_scores, q_ref[:, part], 0, 0)
        value_part_ref[:, part] = dot(
            scores_ref[columns(h * rows, rows), :], grad, 0, 0
        )
    token_ref[...] = jnp.zeros_like(token_ref)


def final_kernel(head, group, chunks, last, *refs):
    k_ref, v_ref, key_part_ref, value_part_ref = refs[:4]
    suffix_refs = refs[4 : 4 + len(chunks)]
    refs = refs[4 + len(suffix_refs) :]
    copies = []
    if last:
        gain_grad_ref, total_ref, gain_written = refs[-6], refs[-2], refs[-1]
        total_ref[...] = tree_sum([ref[...] for ref in refs[2:-8]])
        copies.append(pltpu.make_async_copy(total_ref, gain_grad_ref, gain_written))
        copies[0].start()
        out_refs, refs = refs[-8:-6], refs[-5:-2]
    else:
        out_refs, refs = refs[:2], refs[2:]
    key_buffer, value_buffer, written = refs
    member = member_of(group)
    width = key_buffer.shape[2]
    for n, chunk in enumerate(chunks):
        suffix_ref = suffix_refs[n]
        start = (member ^ chunk) * width
        for i in range(width // head):
            part = pl.ds(pl.multiple_of(start + i * head, head), head)
            local = columns(i * head, head)
            suffix = suffix_ref[local, :]
            key_buffer[n, :, local] = (
                key_part_ref[:, part] + dot(v_ref[:, part], suffix, 1, 1)
            ).astype(HALF)
            value_buffer[n, :, local] = (
                value_part_ref[:, part] + dot(k_ref[:, part], suffix, 1, 0)
            ).astype(HALF)
        for i, buffer in enumerate((key_buffer, value_buffer)):
            copy = pltpu.make_async_copy(
                buffer.at[n],
                out_refs[i].at[:, block_at(member ^ chunk, width)],
                written.at[i, n],
            )
            copy.start()
            copies.append(copy)
    for copy in copies:
        copy.wait()


def tree_sum(terms):
    while len(terms) > 1:
        terms = [a + b for a, b in zip(terms[::2], terms[1::2])]
    return terms[0]


def wide_rows(ref, start):
    rows = (ref.shape[0] - start) // 2
    high = ref[columns(start, rows), :].astype(F32)
    return high + ref[columns(start + rows, rows), :].astype(F32)


def put_wide_rows(ref, start, value):
    rows = value.shape[0]
    high = value.astype(HALF)
    ref[columns(start, rows), :] = high
    ref[columns(start + rows, rows), :] = (value - high.astype(F32)).astype(HALF)


def total_kernel(size, *refs):
    out_ref = refs[-1]
    total = refs[0][0:size, :].astype(F32)
    for ref in refs[1:-1]:
        total += ref[0:size, :].astype(F32)
    out_ref[0:size, :] = total.astype(HALF)
    if out_ref.shape[0] > size:
        put_wide_rows(out_ref, size, tree_sum([wide_rows(ref, size) for ref in refs[:-1]]))


def group_flag(group, reverse, distance):
    index = lax.axis_index("seq") // group
    last = lax.axis_size("seq") // group - 1
    known = index + distance <= last if reverse else index >= distance
    return jnp.where(known, 1.0, 0.0)


def carry_kernel(group, reverse, distance, first, own_ref, moved_ref, out_ref):
    own = own_ref[...].astype(F32)
    if first:
        own = own * group_flag(group, reverse, 1)
    moved = moved_ref[...].astype(F32) * group_flag(group, reverse, distance)
    out_ref[...] = (own + moved).astype(HALF)


def scan_kernel(group, reverse, masked, size, riding, *refs):
    member = member_of(group)
    carry = refs[0][0:size, :].astype(F32)
    if masked:
        carry = carry * group_flag(group, reverse, 1)
    blocks = [ref[0:size, :].astype(F32) for ref in refs[1 : 1 + group]]
    out_refs = refs[-group - riding :][:group]
    for j in range(group):
        total = carry
        for i in range(group):
            if i != j:
                earlier = (member ^ i) < (member ^ j)
                keep = jnp.where(earlier != reverse, 1.0, 0.0)
                total += keep * blocks[i]
        out_refs[j][...] = total.astype(HALF)
    if riding:
        refs[-1][...] = wide_rows(refs[0], size) + wide_rows(refs[1 + group], size)


VMEM = pl.BlockSpec(memory_space=pltpu.VMEM)
ANY = pl.BlockSpec(memory_space=pl.ANY)
HBM = pl.BlockSpec(memory_space=pltpu.HBM)


def call(kernel, outs, args, matmuls, scratch=(), ins=None, out_specs=None, aliases=None):
    size = sum(a.size * a.dtype.itemsize for a in args)
    size += sum(o.size * o.dtype.itemsize for o in outs)
    ins = ins or {}
    out_specs = out_specs or {}
    return pl.pallas_call(
        kernel,
        out_shape=tuple(outs),
        in_specs=[ins.get(i, VMEM) for i in range(len(args))],
        out_specs=tuple(out_specs.get(i, VMEM) for i in range(len(outs))),
        scratch_shapes=list(scratch),
        input_output_aliases=aliases or {},
        compiler_params=pltpu.CompilerParams(vmem_limit_bytes=16 * 1024 * 1024),
        cost_estimate=pl.CostEstimate(
            flops=2 * 128 * 128 * 128 * HEADS * matmuls,
            bytes_accessed=size,
            transcendentals=0,
        ),
    )(*args)


def swap(array, axis, offset):
    count = lax.axis_size(axis)
    return lax.ppermute(array, axis, [(i, i ^ offset) for i in range(count)])


def own_and_swapped(pieces):
    order = sorted(range(1, len(pieces)), key=lambda j: -bin(j).count("1"))
    moved = {j: swap(pieces[j], "seq", j) for j in order}
    return [pieces[0]] + [moved[j] for j in range(1, len(pieces))]


def exclusive_scan(pieces, size, reverse, token):
    group = len(pieces)
    count = lax.axis_size("seq")
    groups = count // group
    part = functools.partial
    lanes = pieces[0].shape[1]
    extra = pieces[0].shape[0] - size
    piece = jax.ShapeDtypeStruct((size, lanes), HALF)
    gain_shape = jax.ShapeDtypeStruct((extra // 2, lanes), F32)

    def shifted(array, distance):
        step = -distance if reverse else distance
        pairs = [(i, (i + step) % count) for i in range(count)]
        return lax.ppermute(array, "seq", pairs)

    received = own_and_swapped(pieces)
    (total,) = call(
        part(total_kernel, size),
        [jax.ShapeDtypeStruct(pieces[0].shape, HALF)],
        received,
        0,
    )
    riding = int(extra > 0 and groups == 2)
    gain = None
    if extra and not riding:
        gain = total[size : size + extra // 2].astype(F32) + total[size + extra // 2 :]
        gain = tree_sum(summed_over("seq", group, gain))
        total = total[:size]
    carry = shifted(total, group)
    distance = 1
    while distance < groups - 1:
        moved = shifted(carry, distance * group)
        kernel = part(
            carry_kernel, group, reverse, distance + (distance == 1), distance == 1
        )
        (carry,) = call(kernel, [piece], [carry, moved], 0)
        distance *= 2
    inputs = [carry] + received + ([total] if riding else []) + [token]
    sums = call(
        part(scan_kernel, group, reverse, groups <= 2, size, riding),
        [piece] * group + [gain_shape] * riding,
        inputs,
        0,
        ins={len(inputs) - 1: ANY},
    )
    results = own_and_swapped(sums[:group])
    return results, (sums[-1] if riding else gain)


def summed_over(axis, stride, array):
    count = lax.axis_size(axis)
    terms = [array]
    while stride < count:
        array = tree_sum(terms)
        width = 4 if count // stride % 4 == 0 else 2
        order = sorted(range(1, width), key=lambda i: i % 2)
        moved = {i: swap(array, axis, i * stride) for i in order}
        terms = [array] + [moved[i] for i in range(1, width)]
        stride *= width
    return terms


def per_device(queries, keys, values, gain, cotangent):
    q, k, v, cot = queries[0], keys[0], values[0], cotangent[0]
    rows, features = q.shape
    head = features // HEADS
    group = 4
    width = features // group
    part = functools.partial
    wide = jax.ShapeDtypeStruct((rows, features), F32)
    half = jax.ShapeDtypeStruct((rows, features), HALF)
    square = jax.ShapeDtypeStruct((rows, head), F32)
    piece = jax.ShapeDtypeStruct((width, head), HALF)
    scores_shape = jax.ShapeDtypeStruct((HEADS * rows, rows), HALF)
    gain_shape = jax.ShapeDtypeStruct((HEADS, head), F32)
    token_shape = jax.ShapeDtypeStruct((8, head), F32)
    whole = pltpu.VMEM((features, head), HALF)
    gain_rows = gain.reshape(HEADS, head)

    *pieces, scores, intra = call(
        part(state_kernel, head, group),
        [piece] * group + [scores_shape, wide],
        [pltpu.with_memory_space_constraint(a, pltpu.HBM) for a in (k, v, q)],
        1,
        [whole]
        + [pltpu.VMEM((rows, features), HALF)] * 3
        + [pltpu.SemaphoreType.DMA((3,))],
        ins={0: HBM, 1: HBM, 2: HBM},
    )
    scores, intra = call(
        part(local_kernel, head),
        [scores_shape, wide],
        [q, k, v, scores, intra],
        2,
        aliases={3: 0, 4: 1},
    )
    prefix, _ = exclusive_scan(pieces, width, False, intra)
    message = jax.ShapeDtypeStruct((width + 2 * HEADS, head), HALF)
    attended, inverse, grad, *pieces = call(
        part(norm_kernel, head, group, lax.axis_size("dp")),
        [wide, square, half] + [message] * group,
        [q, intra, gain_rows, cot] + prefix,
        2,
        [whole, pltpu.VMEM((HEADS, head), F32)],
    )
    output, grad_query, key_part, value_part, token = call(
        part(backward_kernel, head, group),
        [half, half, wide, wide, token_shape],
        [q, k, v, scores, grad, attended, inverse, gain_rows] + prefix,
        5,
        [whole],
    )
    suffix, gain_grad = exclusive_scan(pieces, width, True, token)
    gains = summed_over("dp", 1, gain_grad)
    inputs = [k, v, key_part, value_part]
    early, late = [0, 3, 1], [2]

    def buffers(count):
        return [pltpu.VMEM((count, rows, width), HALF)] * 2 + [
            pltpu.SemaphoreType.DMA((2, count))
        ]

    first = call(
        part(final_kernel, head, group, early, False),
        [half, half],
        inputs + [suffix[j] for j in early],
        1,
        buffers(len(early)),
        out_specs={0: HBM, 1: HBM},
    )
    at = len(inputs) + len(late)
    grad_key, grad_value, gain_grad = call(
        part(final_kernel, head, group, late, True),
        [half, half, gain_shape],
        inputs + [suffix[j] for j in late] + list(first) + gains,
        1,
        buffers(len(late))
        + [pltpu.VMEM((HEADS, head), F32), pltpu.SemaphoreType.DMA(())],
        ins={at: HBM, at + 1: HBM},
        out_specs={0: HBM, 1: HBM, 2: HBM},
        aliases={at: 0, at + 1: 1},
    )
    return (
        output[None],
        grad_query[None],
        grad_key[None],
        grad_value[None],
        gain_grad.reshape(features),
    )


def solution(mesh):
    spec = P("dp", "seq", None)
    return jax.shard_map(
        per_device,
        mesh=mesh,
        in_specs=(spec, spec, spec, P(), spec),
        out_specs=(spec, spec, spec, spec, P()),
        check_vma=False,
    )
```

```python
import functools

import jax
import jax.numpy as jnp
from jax import lax
from jax.experimental import pallas as pl
from jax.experimental.pallas import tpu as pltpu
from jax.sharding import PartitionSpec as P

HEADS = 16

EPSILON = 1e-06

F32 = jnp.float32
HALF = jnp.bfloat16


def dot(lhs, rhs, lhs_dim, rhs_dim):
    return lax.dot_general(
        lhs, rhs, (((lhs_dim,), (rhs_dim,)), ((), ())), preferred_element_type=F32
    )


def causal(size):
    rows = lax.broadcasted_iota(jnp.int32, (size, size), 0)
    columns = lax.broadcasted_iota(jnp.int32, (size, size), 1)
    return rows >= columns


def member_of(group):
    return lax.rem(lax.axis_index("seq"), group)


def block_at(index, size):
    return pl.ds(pl.multiple_of(index * size, size), size)


def gathered(member, piece_refs, size, whole_ref):
    for j, ref in enumerate(piece_refs):
        whole_ref[block_at(member ^ j, size), :] = ref[0:size, :]


def scattered(member, whole_ref, size, piece_refs):
    for j, ref in enumerate(piece_refs):
        ref[0:size, :] = whole_ref[block_at(member ^ j, size), :]


def columns(first, count):
    return slice(first, first + count)


def late_core():
    return lax.rem(lax.axis_index("dp"), 2) == 0


def state_kernel(head, group, k_ref, v_ref, q_ref, *refs):
    piece_refs = refs[:group]
    scores_ref, intra_ref = refs[group : 2 + group]
    whole_ref, k_buffer, v_buffer, q_buffer, arrived = refs[2 + group :]
    pairs = ((k_ref, k_buffer), (v_ref, v_buffer), (q_ref, q_buffer))
    copies = [
        pltpu.make_async_copy(ref, buffer, arrived.at[i])
        for i, (ref, buffer) in enumerate(pairs)
    ]
    for copy in copies:
        copy.start()
    for copy in copies[:2]:
        copy.wait()
    for h in range(HEADS):
        part = columns(h * head, head)
        whole_ref[part, :] = dot(k_buffer[:, part], v_buffer[:, part], 0, 0).astype(HALF)
    scattered(member_of(group), whole_ref, piece_refs[0].shape[0], piece_refs)
    copies[2].wait()

    @pl.when(late_core())
    def _():
        local_attention(head, q_buffer, k_buffer, v_buffer, scores_ref, intra_ref)


def local_attention(head, q_ref, k_ref, v_ref, scores_ref, intra_ref):
    rows = q_ref.shape[0]
    mask = causal(rows)
    scaling = head ** (-0.5)
    for h in range(HEADS):
        part = columns(h * head, head)
        scores = dot(q_ref[:, part], k_ref[:, part], 1, 1) * scaling
        scores = jnp.where(mask, scores, 0.0).astype(HALF)
        scores_ref[columns(h * rows, rows), :] = scores
        intra_ref[:, part] = dot(scores, v_ref[:, part], 1, 0)


def local_kernel(head, q_ref, k_ref, v_ref, scores_in, intra_in, scores_ref, intra_ref):
    @pl.when(jnp.logical_not(late_core()))
    def _():
        local_attention(head, q_ref, k_ref, v_ref, scores_ref, intra_ref)

    @pl.when(late_core())
    def _():
        scores_ref[...] = scores_in[...]
        intra_ref[...] = intra_in[...]


def norm_kernel(head, group, replicas, *refs):
    q_ref, intra_ref, gain_ref, cot_ref = refs[:4]
    prefix_refs = refs[4 : 4 + group]
    attended_ref, inverse_ref, grad_ref = refs[4 + group : 7 + group]
    piece_refs = refs[7 + group : 7 + 2 * group]
    whole_ref, gain_grad_ref = refs[7 + 2 * group :]
    member = member_of(group)
    rows = q_ref.shape[0]
    scaling = head ** (-0.5)
    features = HEADS * head
    size = features // group
    gathered(member, prefix_refs, size, whole_ref)
    squares = jnp.zeros((rows, head), F32)
    inner = jnp.zeros((rows, head), F32)
    for h in range(HEADS):
        part = columns(h * head, head)
        attended = intra_ref[:, part] + scaling * dot(
            q_ref[:, part], whole_ref[part, :], 1, 0
        )
        attended_ref[:, part] = attended
        scaled = cot_ref[:, part].astype(F32) * gain_ref[h : h + 1, :]
        squares += attended * attended
        inner += scaled * attended
    inverse = lax.rsqrt(
        jnp.sum(squares, axis=1, keepdims=True) * (1.0 / features) + EPSILON
    )
    inner_mean = jnp.sum(inner, axis=1, keepdims=True) * (1.0 / features) * inverse
    inverse_ref[...] = jnp.broadcast_to(inverse, inverse_ref.shape)
    for h in range(HEADS):
        part = columns(h * head, head)
        normalized = attended_ref[:, part] * inverse
        upstream = cot_ref[:, part].astype(F32)
        gain = gain_ref[h : h + 1, :]
        gain_grad_ref[h : h + 1, :] = jnp.sum(
            upstream * normalized, axis=0, keepdims=True
        ) * (1.0 / replicas)
        grad = ((upstream * gain - normalized * inner_mean) * inverse).astype(HALF)
        grad_ref[:, part] = grad
        whole_ref[part, :] = (scaling * dot(q_ref[:, part], grad, 0, 0)).astype(HALF)
    scattered(member, whole_ref, size, piece_refs)
    for ref in piece_refs:
        put_wide_rows(ref, size, gain_grad_ref[...])


def backward_kernel(head, group, *refs):
    q_ref, k_ref, v_ref, scores_ref, grad_ref = refs[:5]
    attended_ref, inverse_ref, gain_ref = refs[5:8]
    prefix_refs = refs[8 : 8 + group]
    out_ref, grad_query_ref, key_part_ref, value_part_ref, token_ref = refs[
        8 + group : 13 + group
    ]
    whole_ref = refs[13 + group]
    rows = q_ref.shape[0]
    mask = causal(rows)
    scaling = head ** (-0.5)
    gathered(member_of(group), prefix_refs, prefix_refs[0].shape[0], whole_ref)
    inverse = inverse_ref[...]
    for h in range(HEADS):
        part = columns(h * head, head)
        out_ref[:, part] = (
            gain_ref[h : h + 1, :] * (attended_ref[:, part] * inverse)
        ).astype(HALF)
        grad = grad_ref[:, part]
        grad_scores = dot(grad, v_ref[:, part], 1, 1)
        grad_scores = jnp.where(mask, grad_scores, 0.0).astype(HALF)
        grad_query = dot(grad_scores, k_ref[:, part], 1, 0) + dot(
            grad, whole_ref[part, :], 1, 1
        )
        grad_query_ref[:, part] = (scaling * grad_query).astype(HALF)
        key_part_ref[:, part] = scaling * dot(grad_scores, q_ref[:, part], 0, 0)
        value_part_ref[:, part] = dot(
            scores_ref[columns(h * rows, rows), :], grad, 0, 0
        )
    token_ref[...] = jnp.zeros_like(token_ref)


def final_kernel(head, group, chunks, last, *refs):
    k_ref, v_ref, key_part_ref, value_part_ref = refs[:4]
    suffix_refs = refs[4 : 4 + len(chunks)]
    refs = refs[4 + len(suffix_refs) :]
    copies = []
    if last:
        gain_grad_ref, total_ref, gain_written = refs[-6], refs[-2], refs[-1]
        total_ref[...] = tree_sum([ref[...] for ref in refs[2:-8]])
        copies.append(pltpu.make_async_copy(total_ref, gain_grad_ref, gain_written))
        copies[0].start()
        out_refs, refs = refs[-8:-6], refs[-5:-2]
    else:
        out_refs, refs = refs[:2], refs[2:]
    key_buffer, value_buffer, written = refs
    member = member_of(group)
    width = key_buffer.shape[2]
    for n, chunk in enumerate(chunks):
        suffix_ref = suffix_refs[n]
        start = (member ^ chunk) * width
        for i in range(width // head):
            part = pl.ds(pl.multiple_of(start + i * head, head), head)
            local = columns(i * head, head)
            suffix = suffix_ref[local, :]
            key_buffer[n, :, local] = (
                key_part_ref[:, part] + dot(v_ref[:, part], suffix, 1, 1)
            ).astype(HALF)
            value_buffer[n, :, local] = (
                value_part_ref[:, part] + dot(k_ref[:, part], suffix, 1, 0)
            ).astype(HALF)
        for i, buffer in enumerate((key_buffer, value_buffer)):
            copy = pltpu.make_async_copy(
                buffer.at[n],
                out_refs[i].at[:, block_at(member ^ chunk, width)],
                written.at[i, n],
            )
            copy.start()
            copies.append(copy)
    for copy in copies:
        copy.wait()


def tree_sum(terms):
    while len(terms) > 1:
        terms = [a + b for a, b in zip(terms[::2], terms[1::2])]
    return terms[0]


def wide_rows(ref, start):
    rows = (ref.shape[0] - start) // 2
    high = ref[columns(start, rows), :].astype(F32)
    return high + ref[columns(start + rows, rows), :].astype(F32)


def put_wide_rows(ref, start, value):
    rows = value.shape[0]
    high = value.astype(HALF)
    ref[columns(start, rows), :] = high
    ref[columns(start + rows, rows), :] = (value - high.astype(F32)).astype(HALF)


def total_kernel(size, *refs):
    out_ref = refs[-1]
    total = refs[0][0:size, :].astype(F32)
    for ref in refs[1:-1]:
        total += ref[0:size, :].astype(F32)
    out_ref[0:size, :] = total.astype(HALF)
    if out_ref.shape[0] > size:
        put_wide_rows(out_ref, size, tree_sum([wide_rows(ref, size) for ref in refs[:-1]]))


def group_flag(group, reverse, distance):
    index = lax.axis_index("seq") // group
    last = lax.axis_size("seq") // group - 1
    known = index + distance <= last if reverse else index >= distance
    return jnp.where(known, 1.0, 0.0)


def carry_kernel(group, reverse, distance, first, own_ref, moved_ref, out_ref):
    own = own_ref[...].astype(F32)
    if first:
        own = own * group_flag(group, reverse, 1)
    moved = moved_ref[...].astype(F32) * group_flag(group, reverse, distance)
    out_ref[...] = (own + moved).astype(HALF)


def scan_kernel(group, reverse, masked, size, riding, *refs):
    member = member_of(group)
    carry = refs[0][0:size, :].astype(F32)
    if masked:
        carry = carry * group_flag(group, reverse, 1)
    blocks = [ref[0:size, :].astype(F32) for ref in refs[1 : 1 + group]]
    out_refs = refs[-group - riding :][:group]
    for j in range(group):
        total = carry
        for i in range(group):
            if i != j:
                earlier = (member ^ i) < (member ^ j)
                keep = jnp.where(earlier != reverse, 1.0, 0.0)
                total += keep * blocks[i]
        out_refs[j][...] = total.astype(HALF)
    if riding:
        refs[-1][...] = wide_rows(refs[0], size) + wide_rows(refs[1 + group], size)


VMEM = pl.BlockSpec(memory_space=pltpu.VMEM)
ANY = pl.BlockSpec(memory_space=pl.ANY)
HBM = pl.BlockSpec(memory_space=pltpu.HBM)


def call(kernel, outs, args, matmuls, scratch=(), ins=None, out_specs=None, aliases=None):
    size = sum(a.size * a.dtype.itemsize for a in args)
    size += sum(o.size * o.dtype.itemsize for o in outs)
    ins = ins or {}
    out_specs = out_specs or {}
    return pl.pallas_call(
        kernel,
        out_shape=tuple(outs),
        in_specs=[ins.get(i, VMEM) for i in range(len(args))],
        out_specs=tuple(out_specs.get(i, VMEM) for i in range(len(outs))),
        scratch_shapes=list(scratch),
        input_output_aliases=aliases or {},
        compiler_params=pltpu.CompilerParams(vmem_limit_bytes=16 * 1024 * 1024),
        cost_estimate=pl.CostEstimate(
            flops=2 * 128 * 128 * 128 * HEADS * matmuls,
            bytes_accessed=size,
            transcendentals=0,
        ),
    )(*args)


def swap(array, axis, offset):
    count = lax.axis_size(axis)
    return lax.ppermute(array, axis, [(i, i ^ offset) for i in range(count)])


def own_and_swapped(pieces):
    order = sorted(range(1, len(pieces)), key=lambda j: -bin(j).count("1"))
    moved = {j: swap(pieces[j], "seq", j) for j in order}
    return [pieces[0]] + [moved[j] for j in range(1, len(pieces))]


def exclusive_scan(pieces, size, reverse, token):
    group = len(pieces)
    count = lax.axis_size("seq")
    groups = count // group
    part = functools.partial
    lanes = pieces[0].shape[1]
    extra = pieces[0].shape[0] - size
    piece = jax.ShapeDtypeStruct((size, lanes), HALF)
    gain_shape = jax.ShapeDtypeStruct((extra // 2, lanes), F32)

    def shifted(array, distance):
        step = -distance if reverse else distance
        pairs = [(i, (i + step) % count) for i in range(count)]
        return lax.ppermute(array, "seq", pairs)

    received = own_and_swapped(pieces)
    (total,) = call(
        part(total_kernel, size),
        [jax.ShapeDtypeStruct(pieces[0].shape, HALF)],
        received,
        0,
    )
    riding = int(extra > 0 and groups == 2)
    gain = None
    if extra and not riding:
        gain = total[size : size + extra // 2].astype(F32) + total[size + extra // 2 :]
        gain = tree_sum(summed_over("seq", group, gain))
        total = total[:size]
    carry = shifted(total, group)
    distance = 1
    while distance < groups - 1:
        moved = shifted(carry, distance * group)
        kernel = part(
            carry_kernel, group, reverse, distance + (distance == 1), distance == 1
        )
        (carry,) = call(kernel, [piece], [carry, moved], 0)
        distance *= 2
    inputs = [carry] + received + ([total] if riding else []) + [token]
    sums = call(
        part(scan_kernel, group, reverse, groups <= 2, size, riding),
        [piece] * group + [gain_shape] * riding,
        inputs,
        0,
        ins={len(inputs) - 1: ANY},
    )
    results = own_and_swapped(sums[:group])
    return results, (sums[-1] if riding else gain)


def summed_over(axis, stride, array):
    count = lax.axis_size(axis)
    terms = [array]
    while stride < count:
        array = tree_sum(terms)
        width = 4 if count // stride % 4 == 0 else 2
        order = sorted(range(1, width), key=lambda i: i % 2)
        moved = {i: swap(array, axis, i * stride) for i in order}
        terms = [array] + [moved[i] for i in range(1, width)]
        stride *= width
    return terms


def per_device(queries, keys, values, gain, cotangent):
    q, k, v, cot = queries[0], keys[0], values[0], cotangent[0]
    rows, features = q.shape
    head = features // HEADS
    group = 4
    width = features // group
    part = functools.partial
    wide = jax.ShapeDtypeStruct((rows, features), F32)
    half = jax.ShapeDtypeStruct((rows, features), HALF)
    square = jax.ShapeDtypeStruct((rows, head), F32)
    piece = jax.ShapeDtypeStruct((width, head), HALF)
    scores_shape = jax.ShapeDtypeStruct((HEADS * rows, rows), HALF)
    gain_shape = jax.ShapeDtypeStruct((HEADS, head), F32)
    token_shape = jax.ShapeDtypeStruct((8, head), F32)
    whole = pltpu.VMEM((features, head), HALF)
    gain_rows = gain.reshape(HEADS, head)

    *pieces, scores, intra = call(
        part(state_kernel, head, group),
        [piece] * group + [scores_shape, wide],
        [pltpu.with_memory_space_constraint(a, pltpu.HBM) for a in (k, v, q)],
        1,
        [whole]
        + [pltpu.VMEM((rows, features), HALF)] * 3
        + [pltpu.SemaphoreType.DMA((3,))],
        ins={0: HBM, 1: HBM, 2: HBM},
    )
    scores, intra = call(
        part(local_kernel, head),
        [scores_shape, wide],
        [q, k, v, scores, intra],
        2,
        aliases={3: 0, 4: 1},
    )
    prefix, _ = exclusive_scan(pieces, width, False, intra)
    message = jax.ShapeDtypeStruct((width + 2 * HEADS, head), HALF)
    attended, inverse, grad, *pieces = call(
        part(norm_kernel, head, group, lax.axis_size("dp")),
        [wide, square, half] + [message] * group,
        [q, intra, gain_rows, cot] + prefix,
        2,
        [whole, pltpu.VMEM((HEADS, head), F32)],
    )
    output, grad_query, key_part, value_part, token = call(
        part(backward_kernel, head, group),
        [half, half, wide, wide, token_shape],
        [q, k, v, scores, grad, attended, inverse, gain_rows] + prefix,
        5,
        [whole],
    )
    suffix, gain_grad = exclusive_scan(pieces, width, True, token)
    gains = summed_over("dp", 1, gain_grad)
    inputs = [k, v, key_part, value_part]
    early, late = [0, 3, 1], [2]

    def buffers(count):
        return [pltpu.VMEM((count, rows, width), HALF)] * 2 + [
            pltpu.SemaphoreType.DMA((2, count))
        ]

    first = call(
        part(final_kernel, head, group, early, False),
        [half, half],
        inputs + [suffix[j] for j in early],
        1,
        buffers(len(early)),
        out_specs={0: HBM, 1: HBM},
    )
    at = len(inputs) + len(late)
    grad_key, grad_value, gain_grad = call(
        part(final_kernel, head, group, late, True),
        [half, half, gain_shape],
        inputs + [suffix[j] for j in late] + list(first) + gains,
        1,
        buffers(len(late))
        + [pltpu.VMEM((HEADS, head), F32), pltpu.SemaphoreType.DMA(())],
        ins={at: HBM, at + 1: HBM},
        out_specs={0: HBM, 1: HBM, 2: HBM},
        aliases={at: 0, at + 1: 1},
    )
    return (
        output[None],
        grad_query[None],
        grad_key[None],
        grad_value[None],
        gain_grad.reshape(features),
    )


def solution(mesh):
    spec = P("dp", "seq", None)
    return jax.shard_map(
        per_device,
        mesh=mesh,
        in_specs=(spec, spec, spec, P(), spec),
        out_specs=(spec, spec, spec, spec, P()),
        check_vma=False,
    )
```

```python
import functools

import jax
import jax.numpy as jnp
from jax import lax
from jax.experimental import pallas as pl
from jax.experimental.pallas import tpu as pltpu
from jax.sharding import PartitionSpec as P

HEADS = 16

EPSILON = 1e-06

F32 = jnp.float32
HALF = jnp.bfloat16


def dot(lhs, rhs, lhs_dim, rhs_dim):
    return lax.dot_general(
        lhs, rhs, (((lhs_dim,), (rhs_dim,)), ((), ())), preferred_element_type=F32
    )


def causal(size):
    rows = lax.broadcasted_iota(jnp.int32, (size, size), 0)
    columns = lax.broadcasted_iota(jnp.int32, (size, size), 1)
    return rows >= columns


def member_of(group):
    return lax.rem(lax.axis_index("seq"), group)


def partner_of(group, slot):
    if slot in (1, 2):
        odd = lax.rem(lax.axis_index("dp"), 2) == 1
        slot = jnp.where(odd, 3 - slot, slot)
    return member_of(group) ^ slot


def block_at(index, size):
    return pl.ds(pl.multiple_of(index * size, size), size)


def gathered(piece_refs, size, whole_ref):
    for j, ref in enumerate(piece_refs):
        whole_ref[block_at(partner_of(len(piece_refs), j), size), :] = ref[0:size, :]


def scattered(whole_ref, size, piece_refs):
    for j, ref in enumerate(piece_refs):
        ref[0:size, :] = whole_ref[block_at(partner_of(len(piece_refs), j), size), :]


def columns(first, count):
    return slice(first, first + count)


def state_kernel(head, group, k_ref, v_ref, *refs):
    piece_refs = refs[:group]
    whole_ref, k_buffer, v_buffer, arrived = refs[group:]
    copies = [
        pltpu.make_async_copy(k_ref, k_buffer, arrived.at[0]),
        pltpu.make_async_copy(v_ref, v_buffer, arrived.at[1]),
    ]
    for copy in copies:
        copy.start()
    for copy in copies:
        copy.wait()
    for h in range(HEADS):
        part = columns(h * head, head)
        whole_ref[part, :] = dot(k_buffer[:, part], v_buffer[:, part], 0, 0).astype(HALF)
    scattered(whole_ref, piece_refs[0].shape[0], piece_refs)


def local_kernel(head, q_ref, k_ref, v_ref, scores_ref, intra_ref):
    rows = q_ref.shape[0]
    mask = causal(rows)
    scaling = head ** (-0.5)
    for h in range(HEADS):
        part = columns(h * head, head)
        scores = dot(q_ref[:, part], k_ref[:, part], 1, 1) * scaling
        scores = jnp.where(mask, scores, 0.0).astype(HALF)
        scores_ref[columns(h * rows, rows), :] = scores
        intra_ref[:, part] = dot(scores, v_ref[:, part], 1, 0)


def norm_kernel(head, group, replicas, *refs):
    q_ref, intra_ref, gain_ref, cot_ref = refs[:4]
    prefix_refs = refs[4 : 4 + group]
    attended_ref, inverse_ref, grad_ref = refs[4 + group : 7 + group]
    piece_refs = refs[7 + group : 7 + 2 * group]
    whole_ref, gain_grad_ref = refs[7 + 2 * group :]
    rows = q_ref.shape[0]
    scaling = head ** (-0.5)
    features = HEADS * head
    size = features // group
    gathered(prefix_refs, size, whole_ref)
    squares = jnp.zeros((rows, head), F32)
    inner = jnp.zeros((rows, head), F32)
    for h in range(HEADS):
        part = columns(h * head, head)
        attended = intra_ref[:, part] + scaling * dot(
            q_ref[:, part], whole_ref[part, :], 1, 0
        )
        attended_ref[:, part] = attended
        scaled = cot_ref[:, part].astype(F32) * gain_ref[h : h + 1, :]
        squares += attended * attended
        inner += scaled * attended
    inverse = lax.rsqrt(
        jnp.sum(squares, axis=1, keepdims=True) * (1.0 / features) + EPSILON
    )
    inner_mean = jnp.sum(inner, axis=1, keepdims=True) * (1.0 / features) * inverse
    inverse_ref[...] = jnp.broadcast_to(inverse, inverse_ref.shape)
    for h in range(HEADS):
        part = columns(h * head, head)
        normalized = attended_ref[:, part] * inverse
        upstream = cot_ref[:, part].astype(F32)
        gain = gain_ref[h : h + 1, :]
        gain_grad_ref[h : h + 1, :] = jnp.sum(
            upstream * normalized, axis=0, keepdims=True
        ) * (1.0 / replicas)
        grad = ((upstream * gain - normalized * inner_mean) * inverse).astype(HALF)
        grad_ref[:, part] = grad
        whole_ref[part, :] = (scaling * dot(q_ref[:, part], grad, 0, 0)).astype(HALF)
    scattered(whole_ref, size, piece_refs)
    for ref in piece_refs:
        put_wide_rows(ref, size, gain_grad_ref[...])


def backward_kernel(head, group, *refs):
    q_ref, k_ref, v_ref, scores_ref, grad_ref = refs[:5]
    attended_ref, inverse_ref, gain_ref = refs[5:8]
    prefix_refs = refs[8 : 8 + group]
    out_ref, grad_query_ref, key_part_ref, value_part_ref, token_ref = refs[
        8 + group : 13 + group
    ]
    whole_ref = refs[13 + group]
    rows = q_ref.shape[0]
    mask = causal(rows)
    scaling = head ** (-0.5)
    gathered(prefix_refs, prefix_refs[0].shape[0], whole_ref)
    inverse = inverse_ref[...]
    for h in range(HEADS):
        part = columns(h * head, head)
        out_ref[:, part] = (
            gain_ref[h : h + 1, :] * (attended_ref[:, part] * inverse)
        ).astype(HALF)
        grad = grad_ref[:, part]
        grad_scores = dot(grad, v_ref[:, part], 1, 1)
        grad_scores = jnp.where(mask, grad_scores, 0.0).astype(HALF)
        grad_query = dot(grad_scores, k_ref[:, part], 1, 0) + dot(
            grad, whole_ref[part, :], 1, 1
        )
        grad_query_ref[:, part] = (scaling * grad_query).astype(HALF)
        key_part_ref[:, part] = scaling * dot(grad_scores, q_ref[:, part], 0, 0)
        value_part_ref[:, part] = dot(
            scores_ref[columns(h * rows, rows), :], grad, 0, 0
        )
    token_ref[...] = jnp.zeros_like(token_ref)


def final_kernel(head, group, chunks, *refs):
    k_ref, v_ref, key_part_ref, value_part_ref = refs[:4]
    suffix_refs = refs[4 : 4 + len(chunks)]
    refs = refs[4 + len(suffix_refs) :]
    out_refs, token_ref = refs[-6:-4], refs[-4]
    key_buffer, value_buffer, written = refs[-3:]
    token_ref[...] = jnp.zeros_like(token_ref)
    copies = []
    width = key_buffer.shape[2]
    for n, chunk in enumerate(chunks):
        suffix_ref = suffix_refs[n]
        start = partner_of(group, chunk) * width
        for i in range(width // head):
            part = pl.ds(pl.multiple_of(start + i * head, head), head)
            local = columns(i * head, head)
            suffix = suffix_ref[local, :]
            key_buffer[n, :, local] = (
                key_part_ref[:, part] + dot(v_ref[:, part], suffix, 1, 1)
            ).astype(HALF)
            value_buffer[n, :, local] = (
                value_part_ref[:, part] + dot(k_ref[:, part], suffix, 1, 0)
            ).astype(HALF)
        for i, buffer in enumerate((key_buffer, value_buffer)):
            copy = pltpu.make_async_copy(
                buffer.at[n],
                out_refs[i].at[:, block_at(partner_of(group, chunk), width)],
                written.at[i, n],
            )
            copy.start()
            copies.append(copy)
    for copy in copies:
        copy.wait()


def gain_kernel(token_ref, *refs):
    del token_ref
    refs[-1][...] = tree_sum([ref[...] for ref in refs[:-1]])


def tree_sum(terms):
    while len(terms) > 1:
        terms = [a + b for a, b in zip(terms[::2], terms[1::2])]
    return terms[0]


def wide_rows(ref, start):
    rows = (ref.shape[0] - start) // 2
    high = ref[columns(start, rows), :].astype(F32)
    return high + ref[columns(start + rows, rows), :].astype(F32)


def put_wide_rows(ref, start, value):
    rows = value.shape[0]
    high = value.astype(HALF)
    ref[columns(start, rows), :] = high
    ref[columns(start + rows, rows), :] = (value - high.astype(F32)).astype(HALF)


def total_kernel(size, *refs):
    out_ref = refs[-1]
    total = refs[0][0:size, :].astype(F32)
    for ref in refs[1:-1]:
        total += ref[0:size, :].astype(F32)
    out_ref[0:size, :] = total.astype(HALF)
    if out_ref.shape[0] > size:
        put_wide_rows(out_ref, size, tree_sum([wide_rows(ref, size) for ref in refs[:-1]]))


def group_flag(group, reverse, distance):
    index = lax.axis_index("seq") // group
    last = lax.axis_size("seq") // group - 1
    known = index + distance <= last if reverse else index >= distance
    return jnp.where(known, 1.0, 0.0)


def carry_kernel(group, reverse, distance, first, own_ref, moved_ref, out_ref):
    own = own_ref[...].astype(F32)
    if first:
        own = own * group_flag(group, reverse, 1)
    moved = moved_ref[...].astype(F32) * group_flag(group, reverse, distance)
    out_ref[...] = (own + moved).astype(HALF)


def scan_kernel(group, reverse, masked, size, riding, *refs):
    members = [partner_of(group, j) for j in range(group)]
    carry = refs[0][0:size, :].astype(F32)
    if masked:
        carry = carry * group_flag(group, reverse, 1)
    blocks = [ref[0:size, :].astype(F32) for ref in refs[1 : 1 + group]]
    out_refs = refs[-group - riding :][:group]
    for j in range(group):
        total = carry
        for i in range(group):
            if i != j:
                earlier = members[i] < members[j]
                keep = jnp.where(earlier != reverse, 1.0, 0.0)
                total += keep * blocks[i]
        out_refs[j][...] = total.astype(HALF)
    if riding:
        refs[-1][...] = wide_rows(refs[0], size) + wide_rows(refs[1 + group], size)


VMEM = pl.BlockSpec(memory_space=pltpu.VMEM)
ANY = pl.BlockSpec(memory_space=pl.ANY)
HBM = pl.BlockSpec(memory_space=pltpu.HBM)


def call(kernel, outs, args, matmuls, scratch=(), ins=None, out_specs=None, aliases=None):
    size = sum(a.size * a.dtype.itemsize for a in args)
    size += sum(o.size * o.dtype.itemsize for o in outs)
    ins = ins or {}
    out_specs = out_specs or {}
    return pl.pallas_call(
        kernel,
        out_shape=tuple(outs),
        in_specs=[ins.get(i, VMEM) for i in range(len(args))],
        out_specs=tuple(out_specs.get(i, VMEM) for i in range(len(outs))),
        scratch_shapes=list(scratch),
        input_output_aliases=aliases or {},
        compiler_params=pltpu.CompilerParams(vmem_limit_bytes=16 * 1024 * 1024),
        cost_estimate=pl.CostEstimate(
            flops=2 * 128 * 128 * 128 * HEADS * matmuls,
            bytes_accessed=size,
            transcendentals=0,
        ),
    )(*args)


def swap(array, axis, offset):
    count = lax.axis_size(axis)
    return lax.ppermute(array, axis, [(i, i ^ offset) for i in range(count)])


def own_and_swapped(pieces):
    count = lax.axis_size("seq")
    results = [pieces[0]]
    for slot in range(1, len(pieces)):
        pairs = []
        for row in range(lax.axis_size("dp")):
            offset = 3 - slot if slot in (1, 2) and row % 2 else slot
            pairs += [(row * count + i, row * count + (i ^ offset)) for i in range(count)]
        results.append(lax.ppermute(pieces[slot], ("dp", "seq"), pairs))
    return results


def exclusive_scan(pieces, size, reverse, token):
    group = len(pieces)
    count = lax.axis_size("seq")
    groups = count // group
    part = functools.partial
    lanes = pieces[0].shape[1]
    extra = pieces[0].shape[0] - size
    piece = jax.ShapeDtypeStruct((size, lanes), HALF)
    gain_shape = jax.ShapeDtypeStruct((extra // 2, lanes), F32)

    def shifted(array, distance):
        step = -distance if reverse else distance
        pairs = [(i, (i + step) % count) for i in range(count)]
        return lax.ppermute(array, "seq", pairs)

    received = own_and_swapped(pieces)
    (total,) = call(
        part(total_kernel, size),
        [jax.ShapeDtypeStruct(pieces[0].shape, HALF)],
        received,
        0,
    )
    riding = int(extra > 0 and groups == 2)
    gain = None
    if extra and not riding:
        gain = total[size : size + extra // 2].astype(F32) + total[size + extra // 2 :]
        gain = tree_sum(summed_over("seq", group, gain))
        total = total[:size]
    carry = shifted(total, group)
    distance = 1
    while distance < groups - 1:
        moved = shifted(carry, distance * group)
        kernel = part(
            carry_kernel, group, reverse, distance + (distance == 1), distance == 1
        )
        (carry,) = call(kernel, [piece], [carry, moved], 0)
        distance *= 2
    inputs = [carry] + received + ([total] if riding else []) + [token]
    sums = call(
        part(scan_kernel, group, reverse, groups <= 2, size, riding),
        [piece] * group + [gain_shape] * riding,
        inputs,
        0,
        ins={len(inputs) - 1: ANY},
    )
    results = own_and_swapped(sums[:group])
    return results, (sums[-1] if riding else gain)


def summed_over(axis, stride, array):
    count = lax.axis_size(axis)
    terms = [array]
    while stride < count:
        array = tree_sum(terms)
        width = 4 if count // stride % 4 == 0 else 2
        order = sorted(range(1, width), key=lambda i: i % 2)
        moved = {i: swap(array, axis, i * stride) for i in order}
        terms = [array] + [moved[i] for i in range(1, width)]
        stride *= width
    return terms


def per_device(queries, keys, values, gain, cotangent):
    q, k, v, cot = queries[0], keys[0], values[0], cotangent[0]
    rows, features = q.shape
    head = features // HEADS
    group = 4
    width = features // group
    part = functools.partial
    wide = jax.ShapeDtypeStruct((rows, features), F32)
    half = jax.ShapeDtypeStruct((rows, features), HALF)
    square = jax.ShapeDtypeStruct((rows, head), F32)
    piece = jax.ShapeDtypeStruct((width, head), HALF)
    scores_shape = jax.ShapeDtypeStruct((HEADS * rows, rows), HALF)
    gain_shape = jax.ShapeDtypeStruct((HEADS, head), F32)
    token_shape = jax.ShapeDtypeStruct((8, head), F32)
    whole = pltpu.VMEM((features, head), HALF)
    gain_rows = gain.reshape(HEADS, head)

    pieces = call(
        part(state_kernel, head, group),
        [piece] * group,
        [pltpu.with_memory_space_constraint(a, pltpu.HBM) for a in (k, v)],
        1,
        [whole]
        + [pltpu.VMEM((rows, features), HALF)] * 2
        + [pltpu.SemaphoreType.DMA((2,))],
        ins={0: HBM, 1: HBM},
    )
    scores, intra = call(part(local_kernel, head), [scores_shape, wide], [q, k, v], 2)
    prefix, _ = exclusive_scan(pieces, width, False, intra)
    message = jax.ShapeDtypeStruct((width + 2 * HEADS, head), HALF)
    attended, inverse, grad, *pieces = call(
        part(norm_kernel, head, group, lax.axis_size("dp")),
        [wide, square, half] + [message] * group,
        [q, intra, gain_rows, cot] + prefix,
        2,
        [whole, pltpu.VMEM((HEADS, head), F32)],
    )
    output, grad_query, key_part, value_part, token = call(
        part(backward_kernel, head, group),
        [half, half, wide, wide, token_shape],
        [q, k, v, scores, grad, attended, inverse, gain_rows] + prefix,
        5,
        [whole],
    )
    suffix, gain_grad = exclusive_scan(pieces, width, True, token)
    gains = summed_over("dp", 1, gain_grad)
    inputs = [k, v, key_part, value_part]
    early, late = [0, 1, 2], [3]

    def buffers(count):
        return [pltpu.VMEM((count, rows, width), HALF)] * 2 + [
            pltpu.SemaphoreType.DMA((2, count))
        ]

    *first, _ = call(
        part(final_kernel, head, group, early),
        [half, half, token_shape],
        inputs + [suffix[j] for j in early],
        1,
        buffers(len(early)),
        out_specs={0: HBM, 1: HBM},
    )
    at = len(inputs) + len(late)
    grad_key, grad_value, token = call(
        part(final_kernel, head, group, late),
        [half, half, token_shape],
        inputs + [suffix[j] for j in late] + first,
        1,
        buffers(len(late)),
        ins={at: HBM, at + 1: HBM},
        out_specs={0: HBM, 1: HBM},
        aliases={at: 0, at + 1: 1},
    )
    (gain_grad,) = call(gain_kernel, [gain_shape], [token] + gains, 0, ins={0: ANY})
    return (
        output[None],
        grad_query[None],
        grad_key[None],
        grad_value[None],
        gain_grad.reshape(features),
    )


def solution(mesh):
    spec = P("dp", "seq", None)
    return jax.shard_map(
        per_device,
        mesh=mesh,
        in_specs=(spec, spec, spec, P(), spec),
        out_specs=(spec, spec, spec, spec, P()),
        check_vma=False,
    )
```

```python
import functools

import jax
import jax.numpy as jnp
from jax import lax
from jax.experimental import pallas as pl
from jax.experimental.pallas import tpu as pltpu
from jax.sharding import PartitionSpec as P

HEADS = 16

EPSILON = 1e-06

F32 = jnp.float32
HALF = jnp.bfloat16


def dot(lhs, rhs, lhs_dim, rhs_dim):
    return lax.dot_general(
        lhs, rhs, (((lhs_dim,), (rhs_dim,)), ((), ())), preferred_element_type=F32
    )


def causal(size):
    rows = lax.broadcasted_iota(jnp.int32, (size, size), 0)
    columns = lax.broadcasted_iota(jnp.int32, (size, size), 1)
    return rows >= columns


def member_of(group):
    return lax.rem(lax.axis_index("seq"), group)


CROSSED = ((0, 1, 2, 3), (0, 2, 1, 3))
DIAGONAL_FIRST = ((0, 3, 1, 2), (0, 3, 1, 2))


def partner_of(order, slot):
    even, odd = order[0][slot], order[1][slot]
    offset = even
    if even != odd:
        offset = jnp.where(lax.rem(lax.axis_index("dp"), 2) == 1, odd, even)
    return member_of(len(order[0])) ^ offset


def block_at(index, size):
    return pl.ds(pl.multiple_of(index * size, size), size)


def gathered(order, piece_refs, size, whole_ref):
    for j, ref in enumerate(piece_refs):
        whole_ref[block_at(partner_of(order, j), size), :] = ref[0:size, :]


def scattered(order, whole_ref, size, piece_refs):
    for j, ref in enumerate(piece_refs):
        ref[0:size, :] = whole_ref[block_at(partner_of(order, j), size), :]


def columns(first, count):
    return slice(first, first + count)


def state_kernel(head, group, k_ref, v_ref, *refs):
    piece_refs = refs[:group]
    whole_ref, k_buffer, v_buffer, arrived = refs[group:]
    copies = [
        pltpu.make_async_copy(k_ref, k_buffer, arrived.at[0]),
        pltpu.make_async_copy(v_ref, v_buffer, arrived.at[1]),
    ]
    for copy in copies:
        copy.start()
    for copy in copies:
        copy.wait()
    for h in range(HEADS):
        part = columns(h * head, head)
        whole_ref[part, :] = dot(k_buffer[:, part], v_buffer[:, part], 0, 0).astype(HALF)
    scattered(CROSSED, whole_ref, piece_refs[0].shape[0], piece_refs)


def local_kernel(head, q_ref, k_ref, v_ref, scores_ref, intra_ref):
    rows = q_ref.shape[0]
    mask = causal(rows)
    scaling = head ** (-0.5)
    for h in range(HEADS):
        part = columns(h * head, head)
        scores = dot(q_ref[:, part], k_ref[:, part], 1, 1) * scaling
        scores = jnp.where(mask, scores, 0.0).astype(HALF)
        scores_ref[columns(h * rows, rows), :] = scores
        intra_ref[:, part] = dot(scores, v_ref[:, part], 1, 0)


def norm_kernel(head, group, replicas, *refs):
    q_ref, intra_ref, gain_ref, cot_ref = refs[:4]
    prefix_refs = refs[4 : 4 + group]
    attended_ref, inverse_ref, grad_ref = refs[4 + group : 7 + group]
    piece_refs = refs[7 + group : 7 + 2 * group]
    whole_ref, gain_grad_ref = refs[7 + 2 * group :]
    rows = q_ref.shape[0]
    scaling = head ** (-0.5)
    features = HEADS * head
    size = features // group
    gathered(CROSSED, prefix_refs, size, whole_ref)
    squares = jnp.zeros((rows, head), F32)
    inner = jnp.zeros((rows, head), F32)
    for h in range(HEADS):
        part = columns(h * head, head)
        attended = intra_ref[:, part] + scaling * dot(
            q_ref[:, part], whole_ref[part, :], 1, 0
        )
        attended_ref[:, part] = attended
        scaled = cot_ref[:, part].astype(F32) * gain_ref[h : h + 1, :]
        squares += attended * attended
        inner += scaled * attended
    inverse = lax.rsqrt(
        jnp.sum(squares, axis=1, keepdims=True) * (1.0 / features) + EPSILON
    )
    inner_mean = jnp.sum(inner, axis=1, keepdims=True) * (1.0 / features) * inverse
    inverse_ref[...] = jnp.broadcast_to(inverse, inverse_ref.shape)
    for h in range(HEADS):
        part = columns(h * head, head)
        normalized = attended_ref[:, part] * inverse
        upstream = cot_ref[:, part].astype(F32)
        gain = gain_ref[h : h + 1, :]
        gain_grad_ref[h : h + 1, :] = jnp.sum(
            upstream * normalized, axis=0, keepdims=True
        ) * (1.0 / replicas)
        grad = ((upstream * gain - normalized * inner_mean) * inverse).astype(HALF)
        grad_ref[:, part] = grad
        whole_ref[part, :] = (scaling * dot(q_ref[:, part], grad, 0, 0)).astype(HALF)
    scattered(DIAGONAL_FIRST, whole_ref, size, piece_refs)
    for ref in piece_refs:
        put_wide_rows(ref, size, gain_grad_ref[...])


def backward_kernel(head, group, *refs):
    q_ref, k_ref, v_ref, scores_ref, grad_ref = refs[:5]
    attended_ref, inverse_ref, gain_ref = refs[5:8]
    prefix_refs = refs[8 : 8 + group]
    out_ref, grad_query_ref, key_part_ref, value_part_ref, token_ref = refs[
        8 + group : 13 + group
    ]
    whole_ref = refs[13 + group]
    rows = q_ref.shape[0]
    mask = causal(rows)
    scaling = head ** (-0.5)
    gathered(CROSSED, prefix_refs, prefix_refs[0].shape[0], whole_ref)
    inverse = inverse_ref[...]
    for h in range(HEADS):
        part = columns(h * head, head)
        out_ref[:, part] = (
            gain_ref[h : h + 1, :] * (attended_ref[:, part] * inverse)
        ).astype(HALF)
        grad = grad_ref[:, part]
        grad_scores = dot(grad, v_ref[:, part], 1, 1)
        grad_scores = jnp.where(mask, grad_scores, 0.0).astype(HALF)
        grad_query = dot(grad_scores, k_ref[:, part], 1, 0) + dot(
            grad, whole_ref[part, :], 1, 1
        )
        grad_query_ref[:, part] = (scaling * grad_query).astype(HALF)
        key_part_ref[:, part] = scaling * dot(grad_scores, q_ref[:, part], 0, 0)
        value_part_ref[:, part] = dot(
            scores_ref[columns(h * rows, rows), :], grad, 0, 0
        )
    token_ref[...] = jnp.zeros_like(token_ref)


def final_kernel(head, chunks, last, *refs):
    k_ref, v_ref, key_part_ref, value_part_ref = refs[:4]
    suffix_refs = refs[4 : 4 + len(chunks)]
    refs = refs[4 + len(suffix_refs) :]
    copies = []
    if last:
        gain_grad_ref, total_ref, gain_written = refs[-6], refs[-2], refs[-1]
        total_ref[...] = tree_sum([ref[...] for ref in refs[2:-8]])
        copies.append(pltpu.make_async_copy(total_ref, gain_grad_ref, gain_written))
        copies[0].start()
        out_refs, refs = refs[-8:-6], refs[-5:-2]
    else:
        out_refs, refs = refs[:2], refs[2:]
    key_buffer, value_buffer, written = refs
    width = key_buffer.shape[2]
    for n, chunk in enumerate(chunks):
        suffix_ref = suffix_refs[n]
        start = partner_of(DIAGONAL_FIRST, chunk) * width
        for i in range(width // head):
            part = pl.ds(pl.multiple_of(start + i * head, head), head)
            local = columns(i * head, head)
            suffix = suffix_ref[local, :]
            key_buffer[n, :, local] = (
                key_part_ref[:, part] + dot(v_ref[:, part], suffix, 1, 1)
            ).astype(HALF)
            value_buffer[n, :, local] = (
                value_part_ref[:, part] + dot(k_ref[:, part], suffix, 1, 0)
            ).astype(HALF)
        for i, buffer in enumerate((key_buffer, value_buffer)):
            copy = pltpu.make_async_copy(
                buffer.at[n],
                out_refs[i].at[:, block_at(partner_of(DIAGONAL_FIRST, chunk), width)],
                written.at[i, n],
            )
            copy.start()
            copies.append(copy)
    for copy in copies:
        copy.wait()


def tree_sum(terms):
    while len(terms) > 1:
        terms = [a + b for a, b in zip(terms[::2], terms[1::2])]
    return terms[0]


def wide_rows(ref, start):
    rows = (ref.shape[0] - start) // 2
    high = ref[columns(start, rows), :].astype(F32)
    return high + ref[columns(start + rows, rows), :].astype(F32)


def put_wide_rows(ref, start, value):
    rows = value.shape[0]
    high = value.astype(HALF)
    ref[columns(start, rows), :] = high
    ref[columns(start + rows, rows), :] = (value - high.astype(F32)).astype(HALF)


def total_kernel(size, *refs):
    out_ref = refs[-1]
    total = refs[0][0:size, :].astype(F32)
    for ref in refs[1:-1]:
        total += ref[0:size, :].astype(F32)
    out_ref[0:size, :] = total.astype(HALF)
    if out_ref.shape[0] > size:
        put_wide_rows(out_ref, size, tree_sum([wide_rows(ref, size) for ref in refs[:-1]]))


def group_flag(group, reverse, distance):
    index = lax.axis_index("seq") // group
    last = lax.axis_size("seq") // group - 1
    known = index + distance <= last if reverse else index >= distance
    return jnp.where(known, 1.0, 0.0)


def carry_kernel(group, reverse, distance, first, own_ref, moved_ref, out_ref):
    own = own_ref[...].astype(F32)
    if first:
        own = own * group_flag(group, reverse, 1)
    moved = moved_ref[...].astype(F32) * group_flag(group, reverse, distance)
    out_ref[...] = (own + moved).astype(HALF)


def scan_kernel(group, order, reverse, masked, size, riding, *refs):
    members = [partner_of(order, j) for j in range(group)]
    carry = refs[0][0:size, :].astype(F32)
    if masked:
        carry = carry * group_flag(group, reverse, 1)
    blocks = [ref[0:size, :].astype(F32) for ref in refs[1 : 1 + group]]
    out_refs = refs[-group - riding :][:group]
    for j in range(group):
        total = carry
        for i in range(group):
            if i != j:
                earlier = members[i] < members[j]
                keep = jnp.where(earlier != reverse, 1.0, 0.0)
                total += keep * blocks[i]
        out_refs[j][...] = total.astype(HALF)
    if riding:
        refs[-1][...] = wide_rows(refs[0], size) + wide_rows(refs[1 + group], size)


VMEM = pl.BlockSpec(memory_space=pltpu.VMEM)
ANY = pl.BlockSpec(memory_space=pl.ANY)
HBM = pl.BlockSpec(memory_space=pltpu.HBM)


def call(kernel, outs, args, matmuls, scratch=(), ins=None, out_specs=None, aliases=None):
    size = sum(a.size * a.dtype.itemsize for a in args)
    size += sum(o.size * o.dtype.itemsize for o in outs)
    ins = ins or {}
    out_specs = out_specs or {}
    return pl.pallas_call(
        kernel,
        out_shape=tuple(outs),
        in_specs=[ins.get(i, VMEM) for i in range(len(args))],
        out_specs=tuple(out_specs.get(i, VMEM) for i in range(len(outs))),
        scratch_shapes=list(scratch),
        input_output_aliases=aliases or {},
        compiler_params=pltpu.CompilerParams(vmem_limit_bytes=16 * 1024 * 1024),
        cost_estimate=pl.CostEstimate(
            flops=2 * 128 * 128 * 128 * HEADS * matmuls,
            bytes_accessed=size,
            transcendentals=0,
        ),
    )(*args)


def swap(array, axis, offset):
    count = lax.axis_size(axis)
    return lax.ppermute(array, axis, [(i, i ^ offset) for i in range(count)])


def own_and_swapped(pieces, order):
    count = lax.axis_size("seq")
    results = [pieces[0]]
    for slot in range(1, len(pieces)):
        pairs = []
        for row in range(lax.axis_size("dp")):
            offset = order[row % 2][slot]
            pairs += [(row * count + i, row * count + (i ^ offset)) for i in range(count)]
        results.append(lax.ppermute(pieces[slot], ("dp", "seq"), pairs))
    return results


def exclusive_scan(pieces, order, size, reverse, token):
    group = len(pieces)
    count = lax.axis_size("seq")
    groups = count // group
    part = functools.partial
    lanes = pieces[0].shape[1]
    extra = pieces[0].shape[0] - size
    piece = jax.ShapeDtypeStruct((size, lanes), HALF)
    gain_shape = jax.ShapeDtypeStruct((extra // 2, lanes), F32)

    def shifted(array, distance):
        step = -distance if reverse else distance
        pairs = [(i, (i + step) % count) for i in range(count)]
        return lax.ppermute(array, "seq", pairs)

    received = own_and_swapped(pieces, order)
    (total,) = call(
        part(total_kernel, size),
        [jax.ShapeDtypeStruct(pieces[0].shape, HALF)],
        received,
        0,
    )
    riding = int(extra > 0 and groups == 2)
    gain = None
    if extra and not riding:
        gain = total[size : size + extra // 2].astype(F32) + total[size + extra // 2 :]
        gain = tree_sum(summed_over("seq", group, gain))
        total = total[:size]
    carry = shifted(total, group)
    distance = 1
    while distance < groups - 1:
        moved = shifted(carry, distance * group)
        kernel = part(
            carry_kernel, group, reverse, distance + (distance == 1), distance == 1
        )
        (carry,) = call(kernel, [piece], [carry, moved], 0)
        distance *= 2
    inputs = [carry] + received + ([total] if riding else []) + [token]
    sums = call(
        part(scan_kernel, group, order, reverse, groups <= 2, size, riding),
        [piece] * group + [gain_shape] * riding,
        inputs,
        0,
        ins={len(inputs) - 1: ANY},
    )
    results = own_and_swapped(sums[:group], order)
    return results, (sums[-1] if riding else gain)


def summed_over(axis, stride, array):
    count = lax.axis_size(axis)
    terms = [array]
    while stride < count:
        array = tree_sum(terms)
        width = 4 if count // stride % 4 == 0 else 2
        order = sorted(range(1, width), key=lambda i: i % 2)
        moved = {i: swap(array, axis, i * stride) for i in order}
        terms = [array] + [moved[i] for i in range(1, width)]
        stride *= width
    return terms


def per_device(queries, keys, values, gain, cotangent):
    q, k, v, cot = queries[0], keys[0], values[0], cotangent[0]
    rows, features = q.shape
    head = features // HEADS
    group = 4
    width = features // group
    part = functools.partial
    wide = jax.ShapeDtypeStruct((rows, features), F32)
    half = jax.ShapeDtypeStruct((rows, features), HALF)
    square = jax.ShapeDtypeStruct((rows, head), F32)
    piece = jax.ShapeDtypeStruct((width, head), HALF)
    scores_shape = jax.ShapeDtypeStruct((HEADS * rows, rows), HALF)
    gain_shape = jax.ShapeDtypeStruct((HEADS, head), F32)
    token_shape = jax.ShapeDtypeStruct((8, head), F32)
    whole = pltpu.VMEM((features, head), HALF)
    gain_rows = gain.reshape(HEADS, head)

    pieces = call(
        part(state_kernel, head, group),
        [piece] * group,
        [pltpu.with_memory_space_constraint(a, pltpu.HBM) for a in (k, v)],
        1,
        [whole]
        + [pltpu.VMEM((rows, features), HALF)] * 2
        + [pltpu.SemaphoreType.DMA((2,))],
        ins={0: HBM, 1: HBM},
    )
    scores, intra = call(part(local_kernel, head), [scores_shape, wide], [q, k, v], 2)
    prefix, _ = exclusive_scan(pieces, CROSSED, width, False, intra)
    message = jax.ShapeDtypeStruct((width + 2 * HEADS, head), HALF)
    attended, inverse, grad, *pieces = call(
        part(norm_kernel, head, group, lax.axis_size("dp")),
        [wide, square, half] + [message] * group,
        [q, intra, gain_rows, cot] + prefix,
        2,
        [whole, pltpu.VMEM((HEADS, head), F32)],
    )
    output, grad_query, key_part, value_part, token = call(
        part(backward_kernel, head, group),
        [half, half, wide, wide, token_shape],
        [q, k, v, scores, grad, attended, inverse, gain_rows] + prefix,
        5,
        [whole],
    )
    suffix, gain_grad = exclusive_scan(pieces, DIAGONAL_FIRST, width, True, token)
    gains = summed_over("dp", 1, gain_grad)
    inputs = [k, v, key_part, value_part]
    early, late = [0, 1, 2], [3]

    def buffers(count):
        return [pltpu.VMEM((count, rows, width), HALF)] * 2 + [
            pltpu.SemaphoreType.DMA((2, count))
        ]

    first = call(
        part(final_kernel, head, early, False),
        [half, half],
        inputs + [suffix[j] for j in early],
        1,
        buffers(len(early)),
        out_specs={0: HBM, 1: HBM},
    )
    at = len(inputs) + len(late)
    grad_key, grad_value, gain_grad = call(
        part(final_kernel, head, late, True),
        [half, half, gain_shape],
        inputs + [suffix[j] for j in late] + list(first) + gains,
        1,
        buffers(len(late))
        + [pltpu.VMEM((HEADS, head), F32), pltpu.SemaphoreType.DMA(())],
        ins={at: HBM, at + 1: HBM},
        out_specs={0: HBM, 1: HBM, 2: HBM},
        aliases={at: 0, at + 1: 1},
    )
    return (
        output[None],
        grad_query[None],
        grad_key[None],
        grad_value[None],
        gain_grad.reshape(features),
    )


def solution(mesh):
    spec = P("dp", "seq", None)
    return jax.shard_map(
        per_device,
        mesh=mesh,
        in_specs=(spec, spec, spec, P(), spec),
        out_specs=(spec, spec, spec, spec, P()),
        check_vma=False,
    )
```

```python
import functools

import jax
import jax.numpy as jnp
from jax import lax
from jax.experimental import pallas as pl
from jax.experimental.pallas import tpu as pltpu
from jax.sharding import PartitionSpec as P

HEADS = 16

EPSILON = 1e-06

F32 = jnp.float32
HALF = jnp.bfloat16


def dot(lhs, rhs, lhs_dim, rhs_dim):
    return lax.dot_general(
        lhs, rhs, (((lhs_dim,), (rhs_dim,)), ((), ())), preferred_element_type=F32
    )


def causal(size):
    rows = lax.broadcasted_iota(jnp.int32, (size, size), 0)
    columns = lax.broadcasted_iota(jnp.int32, (size, size), 1)
    return rows >= columns


def member_of(group):
    return lax.rem(lax.axis_index("seq"), group)


CROSSED = ((0, 1, 2, 3), (0, 2, 1, 3))
DIAGONAL_FIRST = ((0, 3, 1, 2), (0, 3, 1, 2))


def partner_of(order, slot):
    even, odd = order[0][slot], order[1][slot]
    offset = even
    if even != odd:
        offset = jnp.where(lax.rem(lax.axis_index("dp"), 2) == 1, odd, even)
    return member_of(len(order[0])) ^ offset


def block_at(index, size):
    return pl.ds(pl.multiple_of(index * size, size), size)


def gathered(order, piece_refs, size, whole_ref):
    for j, ref in enumerate(piece_refs):
        whole_ref[block_at(partner_of(order, j), size), :] = ref[0:size, :]


def scattered(order, whole_ref, size, piece_refs):
    for j, ref in enumerate(piece_refs):
        ref[0:size, :] = whole_ref[block_at(partner_of(order, j), size), :]


def columns(first, count):
    return slice(first, first + count)


def state_kernel(head, group, k_ref, v_ref, *refs):
    piece_refs = refs[:group]
    whole_ref, k_buffer, v_buffer, arrived = refs[group:]
    copies = [
        pltpu.make_async_copy(k_ref, k_buffer, arrived.at[0]),
        pltpu.make_async_copy(v_ref, v_buffer, arrived.at[1]),
    ]
    for copy in copies:
        copy.start()
    for copy in copies:
        copy.wait()
    for h in range(HEADS):
        part = columns(h * head, head)
        whole_ref[part, :] = dot(k_buffer[:, part], v_buffer[:, part], 0, 0).astype(HALF)
    scattered(CROSSED, whole_ref, piece_refs[0].shape[0], piece_refs)


def local_kernel(head, q_ref, k_ref, v_ref, scores_ref, intra_ref):
    rows = q_ref.shape[0]
    mask = causal(rows)
    scaling = head ** (-0.5)
    for h in range(HEADS):
        part = columns(h * head, head)
        scores = dot(q_ref[:, part], k_ref[:, part], 1, 1) * scaling
        scores = jnp.where(mask, scores, 0.0).astype(HALF)
        scores_ref[columns(h * rows, rows), :] = scores
        intra_ref[:, part] = dot(scores, v_ref[:, part], 1, 0)


def norm_kernel(head, group, replicas, *refs):
    q_ref, intra_ref, gain_ref, cot_ref = refs[:4]
    prefix_refs = refs[4 : 4 + group]
    attended_ref, inverse_ref, grad_ref = refs[4 + group : 7 + group]
    piece_refs = refs[7 + group : 7 + 2 * group]
    whole_ref, gain_grad_ref = refs[7 + 2 * group :]
    rows = q_ref.shape[0]
    scaling = head ** (-0.5)
    features = HEADS * head
    size = features // group
    gathered(CROSSED, prefix_refs, size, whole_ref)
    squares = jnp.zeros((rows, head), F32)
    inner = jnp.zeros((rows, head), F32)
    for h in range(HEADS):
        part = columns(h * head, head)
        attended = intra_ref[:, part] + scaling * dot(
            q_ref[:, part], whole_ref[part, :], 1, 0
        )
        attended_ref[:, part] = attended
        scaled = cot_ref[:, part].astype(F32) * gain_ref[h : h + 1, :]
        squares += attended * attended
        inner += scaled * attended
    inverse = lax.rsqrt(
        jnp.sum(squares, axis=1, keepdims=True) * (1.0 / features) + EPSILON
    )
    inner_mean = jnp.sum(inner, axis=1, keepdims=True) * (1.0 / features) * inverse
    inverse_ref[...] = jnp.broadcast_to(inverse, inverse_ref.shape)
    for h in range(HEADS):
        part = columns(h * head, head)
        normalized = attended_ref[:, part] * inverse
        upstream = cot_ref[:, part].astype(F32)
        gain = gain_ref[h : h + 1, :]
        gain_grad_ref[h : h + 1, :] = jnp.sum(
            upstream * normalized, axis=0, keepdims=True
        ) * (1.0 / replicas)
        grad = ((upstream * gain - normalized * inner_mean) * inverse).astype(HALF)
        grad_ref[:, part] = grad
        whole_ref[part, :] = (scaling * dot(q_ref[:, part], grad, 0, 0)).astype(HALF)
    scattered(DIAGONAL_FIRST, whole_ref, size, piece_refs)
    for ref in piece_refs:
        put_wide_rows(ref, size, gain_grad_ref[...])


def backward_kernel(head, group, *refs):
    q_ref, k_ref, v_ref, scores_ref, grad_ref = refs[:5]
    attended_ref, inverse_ref, gain_ref = refs[5:8]
    prefix_refs = refs[8 : 8 + group]
    out_ref, grad_query_ref, key_part_ref, value_part_ref, token_ref = refs[
        8 + group : 13 + group
    ]
    whole_ref = refs[13 + group]
    rows = q_ref.shape[0]
    mask = causal(rows)
    scaling = head ** (-0.5)
    gathered(CROSSED, prefix_refs, prefix_refs[0].shape[0], whole_ref)
    inverse = inverse_ref[...]
    for h in range(HEADS):
        part = columns(h * head, head)
        out_ref[:, part] = (
            gain_ref[h : h + 1, :] * (attended_ref[:, part] * inverse)
        ).astype(HALF)
        grad = grad_ref[:, part]
        grad_scores = dot(grad, v_ref[:, part], 1, 1)
        grad_scores = jnp.where(mask, grad_scores, 0.0).astype(HALF)
        grad_query = dot(grad_scores, k_ref[:, part], 1, 0) + dot(
            grad, whole_ref[part, :], 1, 1
        )
        grad_query_ref[:, part] = (scaling * grad_query).astype(HALF)
        key_part_ref[:, part] = scaling * dot(grad_scores, q_ref[:, part], 0, 0)
        value_part_ref[:, part] = dot(
            scores_ref[columns(h * rows, rows), :], grad, 0, 0
        )
    token_ref[...] = jnp.zeros_like(token_ref)


def final_kernel(head, chunks, last, *refs):
    k_ref, v_ref, key_part_ref, value_part_ref = refs[:4]
    suffix_refs = refs[4 : 4 + len(chunks)]
    refs = refs[4 + len(suffix_refs) :]
    copies = []
    if last:
        gain_grad_ref, total_ref, gain_written = refs[-6], refs[-2], refs[-1]
        total_ref[...] = tree_sum([ref[...] for ref in refs[2:-8]])
        copies.append(pltpu.make_async_copy(total_ref, gain_grad_ref, gain_written))
        copies[0].start()
        out_refs, refs = refs[-8:-6], refs[-5:-2]
    else:
        out_refs, refs = refs[:2], refs[2:]
    key_buffer, value_buffer, written = refs
    width = key_buffer.shape[2]
    for n, chunk in enumerate(chunks):
        suffix_ref = suffix_refs[n]
        start = partner_of(DIAGONAL_FIRST, chunk) * width
        for i in range(width // head):
            part = pl.ds(pl.multiple_of(start + i * head, head), head)
            local = columns(i * head, head)
            suffix = suffix_ref[local, :]
            key_buffer[n, :, local] = (
                key_part_ref[:, part] + dot(v_ref[:, part], suffix, 1, 1)
            ).astype(HALF)
            value_buffer[n, :, local] = (
                value_part_ref[:, part] + dot(k_ref[:, part], suffix, 1, 0)
            ).astype(HALF)
        for i, buffer in enumerate((key_buffer, value_buffer)):
            copy = pltpu.make_async_copy(
                buffer.at[n],
                out_refs[i].at[:, block_at(partner_of(DIAGONAL_FIRST, chunk), width)],
                written.at[i, n],
            )
            copy.start()
            copies.append(copy)
    for copy in copies:
        copy.wait()


def tree_sum(terms):
    while len(terms) > 1:
        terms = [a + b for a, b in zip(terms[::2], terms[1::2])]
    return terms[0]


def wide_rows(ref, start):
    rows = (ref.shape[0] - start) // 2
    high = ref[columns(start, rows), :].astype(F32)
    return high + ref[columns(start + rows, rows), :].astype(F32)


def put_wide_rows(ref, start, value):
    rows = value.shape[0]
    high = value.astype(HALF)
    ref[columns(start, rows), :] = high
    ref[columns(start + rows, rows), :] = (value - high.astype(F32)).astype(HALF)


def total_kernel(size, count, *refs):
    refs, out_refs = refs[:count], refs[count + 1 :]
    total = refs[0][0:size, :].astype(F32)
    for ref in refs[1:]:
        total += ref[0:size, :].astype(F32)
    out_refs[0][0:size, :] = total.astype(HALF)
    if len(out_refs) > 1:
        gain = tree_sum([wide_rows(ref, size) for ref in refs])
        put_wide_rows(out_refs[0], size, gain)
        out_refs[1][...] = wide_rows(out_refs[0], size)


def group_flag(group, reverse, distance):
    index = lax.axis_index("seq") // group
    last = lax.axis_size("seq") // group - 1
    known = index + distance <= last if reverse else index >= distance
    return jnp.where(known, 1.0, 0.0)


def carry_kernel(group, reverse, distance, first, own_ref, moved_ref, out_ref):
    own = own_ref[...].astype(F32)
    if first:
        own = own * group_flag(group, reverse, 1)
    moved = moved_ref[...].astype(F32) * group_flag(group, reverse, distance)
    out_ref[...] = (own + moved).astype(HALF)


def scan_kernel(group, order, reverse, masked, size, riding, *refs):
    members = [partner_of(order, j) for j in range(group)]
    carry = refs[0][0:size, :].astype(F32)
    if masked:
        carry = carry * group_flag(group, reverse, 1)
    blocks = [ref[0:size, :].astype(F32) for ref in refs[1 : 1 + group]]
    out_refs = refs[-group - riding :][:group]
    for j in range(group):
        total = carry
        for i in range(group):
            if i != j:
                earlier = members[i] < members[j]
                keep = jnp.where(earlier != reverse, 1.0, 0.0)
                total += keep * blocks[i]
        out_refs[j][...] = total.astype(HALF)
    if riding:
        terms = [refs[1 + group][...], wide_rows(refs[0], size)]
        terms += [ref[...] for ref in refs[2 + group : -group - 1]]
        refs[-1][...] = tree_sum(terms)


VMEM = pl.BlockSpec(memory_space=pltpu.VMEM)
ANY = pl.BlockSpec(memory_space=pl.ANY)
HBM = pl.BlockSpec(memory_space=pltpu.HBM)


def call(kernel, outs, args, matmuls, scratch=(), ins=None, out_specs=None, aliases=None):
    size = sum(a.size * a.dtype.itemsize for a in args)
    size += sum(o.size * o.dtype.itemsize for o in outs)
    ins = ins or {}
    out_specs = out_specs or {}
    return pl.pallas_call(
        kernel,
        out_shape=tuple(outs),
        in_specs=[ins.get(i, VMEM) for i in range(len(args))],
        out_specs=tuple(out_specs.get(i, VMEM) for i in range(len(outs))),
        scratch_shapes=list(scratch),
        input_output_aliases=aliases or {},
        compiler_params=pltpu.CompilerParams(vmem_limit_bytes=16 * 1024 * 1024),
        cost_estimate=pl.CostEstimate(
            flops=2 * 128 * 128 * 128 * HEADS * matmuls,
            bytes_accessed=size,
            transcendentals=0,
        ),
    )(*args)


def swap(array, axis, offset):
    count = lax.axis_size(axis)
    return lax.ppermute(array, axis, [(i, i ^ offset) for i in range(count)])


def own_and_swapped(pieces, order):
    count = lax.axis_size("seq")
    results = [pieces[0]]
    for slot in range(1, len(pieces)):
        pairs = []
        for row in range(lax.axis_size("dp")):
            offset = order[row % 2][slot]
            pairs += [(row * count + i, row * count + (i ^ offset)) for i in range(count)]
        results.append(lax.ppermute(pieces[slot], ("dp", "seq"), pairs))
    return results


def exclusive_scan(pieces, order, size, reverse, token):
    group = len(pieces)
    count, rows = lax.axis_size("seq"), lax.axis_size("dp")
    groups = count // group
    part = functools.partial
    lanes = pieces[0].shape[1]
    extra = pieces[0].shape[0] - size
    piece = jax.ShapeDtypeStruct((size, lanes), HALF)
    gain_shape = jax.ShapeDtypeStruct((extra // 2, lanes), F32)

    def shifted(array, distance):
        step = -distance if reverse else distance
        pairs = [(i, (i + step) % count) for i in range(count)]
        return lax.ppermute(array, "seq", pairs)

    received = own_and_swapped(pieces, order)
    totals = call(
        part(total_kernel, size, group),
        [jax.ShapeDtypeStruct(pieces[0].shape, HALF)] + [gain_shape] * (extra > 0),
        received + [token],
        0,
        ins={group: ANY},
    )
    total, gains = totals[0], list(totals[1:])
    riding = int(extra > 0 and groups == 2 and rows == 4)
    carry = shifted(total if riding else total[:size], group)
    if riding:
        for offset in (0, group):
            pairs = [
                (row * count + i, (row ^ 2) * count + (i ^ offset))
                for row in range(rows)
                for i in range(count)
            ]
            gains.append(lax.ppermute(gains[0], ("dp", "seq"), pairs))
    elif extra:
        gains = [tree_sum(summed_over("seq", group, gains[0]))]
        gains = [tree_sum(summed_over("dp", 2, gains[0]))]
    distance = 1
    while distance < groups - 1:
        moved = shifted(carry, distance * group)
        kernel = part(
            carry_kernel, group, reverse, distance + (distance == 1), distance == 1
        )
        (carry,) = call(kernel, [piece], [carry, moved], 0)
        distance *= 2
    sums = call(
        part(scan_kernel, group, order, reverse, groups <= 2, size, riding),
        [piece] * group + [gain_shape] * riding,
        [carry] + received + (gains if riding else []),
        0,
    )
    results = own_and_swapped(sums[:group], order)
    return results, (sums[-1] if riding else gains[0] if gains else None)


def summed_over(axis, stride, array):
    count = lax.axis_size(axis)
    terms = [array]
    while stride < count:
        array = tree_sum(terms)
        width = 4 if count // stride % 4 == 0 else 2
        terms = [array] + [swap(array, axis, i * stride) for i in range(1, width)]
        stride *= width
    return terms


def per_device(queries, keys, values, gain, cotangent):
    q, k, v, cot = queries[0], keys[0], values[0], cotangent[0]
    rows, features = q.shape
    head = features // HEADS
    group = 4
    width = features // group
    part = functools.partial
    wide = jax.ShapeDtypeStruct((rows, features), F32)
    half = jax.ShapeDtypeStruct((rows, features), HALF)
    square = jax.ShapeDtypeStruct((rows, head), F32)
    piece = jax.ShapeDtypeStruct((width, head), HALF)
    scores_shape = jax.ShapeDtypeStruct((HEADS * rows, rows), HALF)
    gain_shape = jax.ShapeDtypeStruct((HEADS, head), F32)
    token_shape = jax.ShapeDtypeStruct((8, head), F32)
    whole = pltpu.VMEM((features, head), HALF)
    gain_rows = gain.reshape(HEADS, head)

    pieces = call(
        part(state_kernel, head, group),
        [piece] * group,
        [pltpu.with_memory_space_constraint(a, pltpu.HBM) for a in (k, v)],
        1,
        [whole]
        + [pltpu.VMEM((rows, features), HALF)] * 2
        + [pltpu.SemaphoreType.DMA((2,))],
        ins={0: HBM, 1: HBM},
    )
    scores, intra = call(part(local_kernel, head), [scores_shape, wide], [q, k, v], 2)
    prefix, _ = exclusive_scan(pieces, CROSSED, width, False, intra)
    message = jax.ShapeDtypeStruct((width + 2 * HEADS, head), HALF)
    attended, inverse, grad, *pieces = call(
        part(norm_kernel, head, group, lax.axis_size("dp")),
        [wide, square, half] + [message] * group,
        [q, intra, gain_rows, cot] + prefix,
        2,
        [whole, pltpu.VMEM((HEADS, head), F32)],
    )
    output, grad_query, key_part, value_part, token = call(
        part(backward_kernel, head, group),
        [half, half, wide, wide, token_shape],
        [q, k, v, scores, grad, attended, inverse, gain_rows] + prefix,
        5,
        [whole],
    )
    suffix, gain_grad = exclusive_scan(pieces, DIAGONAL_FIRST, width, True, token)
    gains = [gain_grad, swap(gain_grad, "dp", 1)]
    inputs = [k, v, key_part, value_part]
    early, late = [0, 1, 2], [3]

    def buffers(count):
        return [pltpu.VMEM((count, rows, width), HALF)] * 2 + [
            pltpu.SemaphoreType.DMA((2, count))
        ]

    first = call(
        part(final_kernel, head, early, False),
        [half, half],
        inputs + [suffix[j] for j in early],
        1,
        buffers(len(early)),
        out_specs={0: HBM, 1: HBM},
    )
    at = len(inputs) + len(late)
    grad_key, grad_value, gain_grad = call(
        part(final_kernel, head, late, True),
        [half, half, gain_shape],
        inputs + [suffix[j] for j in late] + list(first) + gains,
        1,
        buffers(len(late))
        + [pltpu.VMEM((HEADS, head), F32), pltpu.SemaphoreType.DMA(())],
        ins={at: HBM, at + 1: HBM},
        out_specs={0: HBM, 1: HBM, 2: HBM},
        aliases={at: 0, at + 1: 1},
    )
    return (
        output[None],
        grad_query[None],
        grad_key[None],
        grad_value[None],
        gain_grad.reshape(features),
    )


def solution(mesh):
    spec = P("dp", "seq", None)
    return jax.shard_map(
        per_device,
        mesh=mesh,
        in_specs=(spec, spec, spec, P(), spec),
        out_specs=(spec, spec, spec, spec, P()),
        check_vma=False,
    )
```

```python
import functools

import jax
import jax.numpy as jnp
from jax import lax
from jax.experimental import pallas as pl
from jax.experimental.pallas import tpu as pltpu
from jax.sharding import PartitionSpec as P

HEADS = 16

EPSILON = 1e-06

F32 = jnp.float32
HALF = jnp.bfloat16


def dot(lhs, rhs, lhs_dim, rhs_dim):
    return lax.dot_general(
        lhs, rhs, (((lhs_dim,), (rhs_dim,)), ((), ())), preferred_element_type=F32
    )


def causal(size):
    rows = lax.broadcasted_iota(jnp.int32, (size, size), 0)
    columns = lax.broadcasted_iota(jnp.int32, (size, size), 1)
    return rows >= columns


def member_of(group):
    return lax.rem(lax.axis_index("seq"), group)


CROSSED = ((0, 1, 2, 3), (0, 2, 1, 3))
DIAGONAL_FIRST = ((0, 3, 1, 2), (0, 3, 1, 2))


def partner_of(order, slot):
    even, odd = order[0][slot], order[1][slot]
    offset = even
    if even != odd:
        offset = jnp.where(lax.rem(lax.axis_index("dp"), 2) == 1, odd, even)
    return member_of(len(order[0])) ^ offset


def block_at(index, size):
    return pl.ds(pl.multiple_of(index * size, size), size)


def gathered(order, piece_refs, size, whole_ref):
    for j, ref in enumerate(piece_refs):
        whole_ref[block_at(partner_of(order, j), size), :] = ref[0:size, :]


def scattered(order, whole_ref, size, piece_refs):
    for j, ref in enumerate(piece_refs):
        ref[0:size, :] = whole_ref[block_at(partner_of(order, j), size), :]


def columns(first, count):
    return slice(first, first + count)


def state_kernel(head, group, k_ref, v_ref, *refs):
    piece_refs = refs[:group]
    whole_ref, k_buffer, v_buffer, arrived = refs[group:]
    step = k_buffer.shape[0] // arrived.shape[1]
    copies = []
    for i in range(arrived.shape[1]):
        part = columns(i * step, step)
        for n, (ref, buffer) in enumerate(((k_ref, k_buffer), (v_ref, v_buffer))):
            copy = pltpu.make_async_copy(
                ref.at[part, :], buffer.at[part, :], arrived.at[n, i]
            )
            copy.start()
            copies.append(copy)
    for copy in copies:
        copy.wait()
    for h in range(HEADS):
        part = columns(h * head, head)
        whole_ref[part, :] = dot(k_buffer[:, part], v_buffer[:, part], 0, 0).astype(HALF)
    scattered(CROSSED, whole_ref, piece_refs[0].shape[0], piece_refs)


def local_kernel(head, q_ref, k_ref, v_ref, scores_ref, intra_ref):
    rows = q_ref.shape[0]
    mask = causal(rows)
    scaling = head ** (-0.5)
    for h in range(HEADS):
        part = columns(h * head, head)
        scores = dot(q_ref[:, part], k_ref[:, part], 1, 1) * scaling
        scores = jnp.where(mask, scores, 0.0).astype(HALF)
        scores_ref[columns(h * rows, rows), :] = scores
        intra_ref[:, part] = dot(scores, v_ref[:, part], 1, 0)


def features_at(order, slot, i, width, head):
    start = partner_of(order, slot) * width + i * head
    return pl.ds(pl.multiple_of(start, head), head)


def attend(head, order, slot, refs, prefix_ref, attended_ref, at, squares, inner):
    q_ref, intra_ref, gain_ref, cot_ref = refs
    scaling = head ** (-0.5)
    width = prefix_ref.shape[0]
    for i in range(width // head):
        part = features_at(order, slot, i, width, head)
        prefix = prefix_ref[columns(i * head, head), :]
        attended = intra_ref[:, part] + scaling * dot(q_ref[:, part], prefix, 1, 0)
        attended_ref[:, part if at is None else columns(i * head, head)] = attended
        scaled = cot_ref[:, part].astype(F32) * gain_ref[:, part]
        squares += attended * attended
        inner += scaled * attended
    return squares, inner


def early_norm_kernel(head, order, *refs):
    prefix_refs, (attended_ref, squares_ref, inner_ref) = refs[4:-3], refs[-3:]
    squares = jnp.zeros(squares_ref.shape, F32)
    inner = jnp.zeros(squares_ref.shape, F32)
    for slot, prefix_ref in enumerate(prefix_refs):
        squares, inner = attend(
            head, order, slot, refs[:4], prefix_ref, attended_ref, None, squares, inner
        )
    squares_ref[...] = squares
    inner_ref[...] = inner


def norm_kernel(head, group, orders, replicas, *refs):
    q_ref, _, gain_ref, cot_ref = refs[:4]
    early_ref, squares_ref, inner_ref, prefix_ref = refs[4:8]
    late_ref, inverse_ref, grad_ref = refs[8:11]
    piece_refs = refs[11 : 11 + group]
    gain_grad_ref, gain_rows_ref = refs[11 + group :]
    features = q_ref.shape[1]
    width = features // group
    last = orders[0][0][group - 1]
    squares, inner = attend(
        head,
        orders[0],
        group - 1,
        refs[:4],
        prefix_ref,
        late_ref,
        0,
        squares_ref[...],
        inner_ref[...],
    )
    inverse = lax.rsqrt(
        jnp.sum(squares, axis=1, keepdims=True) * (1.0 / features) + EPSILON
    )
    inner_mean = jnp.sum(inner, axis=1, keepdims=True) * (1.0 / features) * inverse
    inverse_ref[...] = jnp.broadcast_to(inverse, inverse_ref.shape)
    scaling = head ** (-0.5)
    for slot in range(group):
        for i in range(width // head):
            part = features_at(orders[1], slot, i, width, head)
            local = columns(i * head, head)
            if orders[1][0][slot] == last:
                attended = late_ref[:, local]
            else:
                attended = early_ref[:, part]
            normalized = attended * inverse
            upstream = cot_ref[:, part].astype(F32)
            gain_grad_ref[:, part] = jnp.sum(
                upstream * normalized, axis=0, keepdims=True
            ) * (1.0 / replicas)
            scaled = upstream * gain_ref[:, part]
            grad = ((scaled - normalized * inner_mean) * inverse).astype(HALF)
            grad_ref[:, part] = grad
            piece_refs[slot][local, :] = (
                scaling * dot(q_ref[:, part], grad, 0, 0)
            ).astype(HALF)
    for h in range(HEADS):
        gain_rows_ref[h : h + 1, :] = gain_grad_ref[:, columns(h * head, head)]
    for ref in piece_refs:
        put_wide_rows(ref, width, gain_rows_ref[...])


def backward_kernel(head, group, *refs):
    q_ref, k_ref, v_ref, scores_ref, grad_ref = refs[:5]
    early_ref, late_ref, inverse_ref, gain_ref = refs[5:9]
    prefix_refs = refs[9 : 9 + group]
    out_ref, grad_query_ref, key_part_ref, value_part_ref, token_ref = refs[
        9 + group : 14 + group
    ]
    whole_ref = refs[14 + group]
    rows = q_ref.shape[0]
    mask = causal(rows)
    scaling = head ** (-0.5)
    gathered(CROSSED, prefix_refs, prefix_refs[0].shape[0], whole_ref)
    inverse = inverse_ref[...]
    width = late_ref.shape[1]
    for slot in range(group):
        for i in range(width // head):
            part = features_at(CROSSED, slot, i, width, head)
            if slot == group - 1:
                attended = late_ref[:, columns(i * head, head)]
            else:
                attended = early_ref[:, part]
            out_ref[:, part] = (gain_ref[:, part] * (attended * inverse)).astype(HALF)
    for h in range(HEADS):
        part = columns(h * head, head)
        grad = grad_ref[:, part]
        grad_scores = dot(grad, v_ref[:, part], 1, 1)
        grad_scores = jnp.where(mask, grad_scores, 0.0).astype(HALF)
        grad_query = dot(grad_scores, k_ref[:, part], 1, 0) + dot(
            grad, whole_ref[part, :], 1, 1
        )
        grad_query_ref[:, part] = (scaling * grad_query).astype(HALF)
        key_part_ref[:, part] = scaling * dot(grad_scores, q_ref[:, part], 0, 0)
        value_part_ref[:, part] = dot(
            scores_ref[columns(h * rows, rows), :], grad, 0, 0
        )
    token_ref[...] = jnp.zeros_like(token_ref)


def final_kernel(head, slot, last, *refs):
    k_ref, v_ref, key_part_ref, value_part_ref, suffix_ref = refs[:5]
    copies = []
    if last:
        gain_grad_ref, total_ref, gain_written = refs[-6], refs[-2], refs[-1]
        total_ref[...] = tree_sum([ref[...] for ref in refs[7:-8]])
        copies.append(pltpu.make_async_copy(total_ref, gain_grad_ref, gain_written))
        copies[0].start()
        out_refs, refs = refs[-8:-6], refs[-5:-2]
    else:
        out_refs, refs = refs[-5:-3], refs[-3:]
    buffers, written = refs[:2], refs[2]
    rows, width = buffers[0].shape
    for i in range(width // head):
        part = features_at(DIAGONAL_FIRST, slot, i, width, head)
        local = columns(i * head, head)
        suffix = suffix_ref[local, :]
        buffers[0][:, local] = (
            key_part_ref[:, part] + dot(v_ref[:, part], suffix, 1, 1)
        ).astype(HALF)
        buffers[1][:, local] = (
            value_part_ref[:, part] + dot(k_ref[:, part], suffix, 1, 0)
        ).astype(HALF)
    block = block_at(partner_of(DIAGONAL_FIRST, slot), width)
    step = rows // written.shape[1]
    for n in range(written.shape[1]):
        part = columns(n * step, step)
        for i in range(2):
            copy = pltpu.make_async_copy(
                buffers[i].at[part, :], out_refs[i].at[part, block], written.at[i, n]
            )
            copy.start()
            copies.append(copy)
    for copy in copies:
        copy.wait()


def tree_sum(terms):
    while len(terms) > 1:
        terms = [a + b for a, b in zip(terms[::2], terms[1::2])]
    return terms[0]


def wide_rows(ref, start):
    rows = (ref.shape[0] - start) // 2
    high = ref[columns(start, rows), :].astype(F32)
    return high + ref[columns(start + rows, rows), :].astype(F32)


def put_wide_rows(ref, start, value):
    rows = value.shape[0]
    high = value.astype(HALF)
    ref[columns(start, rows), :] = high
    ref[columns(start + rows, rows), :] = (value - high.astype(F32)).astype(HALF)


def total_kernel(size, *refs):
    out_ref = refs[-1]
    total = refs[0][0:size, :].astype(F32)
    for ref in refs[1:-1]:
        total += ref[0:size, :].astype(F32)
    out_ref[0:size, :] = total.astype(HALF)
    if out_ref.shape[0] > size:
        put_wide_rows(out_ref, size, tree_sum([wide_rows(ref, size) for ref in refs[:-1]]))


def group_flag(group, reverse, distance):
    index = lax.axis_index("seq") // group
    last = lax.axis_size("seq") // group - 1
    known = index + distance <= last if reverse else index >= distance
    return jnp.where(known, 1.0, 0.0)


def carry_kernel(group, reverse, distance, first, own_ref, moved_ref, out_ref):
    own = own_ref[...].astype(F32)
    if first:
        own = own * group_flag(group, reverse, 1)
    moved = moved_ref[...].astype(F32) * group_flag(group, reverse, distance)
    out_ref[...] = (own + moved).astype(HALF)


def scan_kernel(group, order, reverse, masked, size, riding, *refs):
    members = [partner_of(order, j) for j in range(group)]
    carry = refs[0][0:size, :].astype(F32)
    if masked:
        carry = carry * group_flag(group, reverse, 1)
    blocks = [ref[0:size, :].astype(F32) for ref in refs[1 : 1 + group]]
    out_refs = refs[-group - riding :][:group]
    for j in range(group):
        total = carry
        for i in range(group):
            if i != j:
                earlier = members[i] < members[j]
                keep = jnp.where(earlier != reverse, 1.0, 0.0)
                total += keep * blocks[i]
        out_refs[j][...] = total.astype(HALF)
    if riding:
        refs[-1][...] = wide_rows(refs[0], size) + wide_rows(refs[1 + group], size)


VMEM = pl.BlockSpec(memory_space=pltpu.VMEM)
ANY = pl.BlockSpec(memory_space=pl.ANY)
HBM = pl.BlockSpec(memory_space=pltpu.HBM)


def call(kernel, outs, args, matmuls, scratch=(), ins=None, out_specs=None, aliases=None):
    size = sum(a.size * a.dtype.itemsize for a in args)
    size += sum(o.size * o.dtype.itemsize for o in outs)
    ins = ins or {}
    out_specs = out_specs or {}
    return pl.pallas_call(
        kernel,
        out_shape=tuple(outs),
        in_specs=[ins.get(i, VMEM) for i in range(len(args))],
        out_specs=tuple(out_specs.get(i, VMEM) for i in range(len(outs))),
        scratch_shapes=list(scratch),
        input_output_aliases=aliases or {},
        compiler_params=pltpu.CompilerParams(vmem_limit_bytes=16 * 1024 * 1024),
        cost_estimate=pl.CostEstimate(
            flops=2 * 128 * 128 * 128 * HEADS * matmuls,
            bytes_accessed=size,
            transcendentals=0,
        ),
    )(*args)


def swap(array, axis, offset):
    count = lax.axis_size(axis)
    return lax.ppermute(array, axis, [(i, i ^ offset) for i in range(count)])


def own_and_swapped(pieces, order):
    count = lax.axis_size("seq")
    results = [pieces[0]]
    for slot in range(1, len(pieces)):
        pairs = []
        for row in range(lax.axis_size("dp")):
            offset = order[row % 2][slot]
            pairs += [(row * count + i, row * count + (i ^ offset)) for i in range(count)]
        results.append(lax.ppermute(pieces[slot], ("dp", "seq"), pairs))
    return results


def exclusive_scan(pieces, order, size, reverse, token):
    group = len(pieces)
    count = lax.axis_size("seq")
    groups = count // group
    part = functools.partial
    lanes = pieces[0].shape[1]
    extra = pieces[0].shape[0] - size
    piece = jax.ShapeDtypeStruct((size, lanes), HALF)
    gain_shape = jax.ShapeDtypeStruct((extra // 2, lanes), F32)

    def shifted(array, distance):
        step = -distance if reverse else distance
        pairs = [(i, (i + step) % count) for i in range(count)]
        return lax.ppermute(array, "seq", pairs)

    received = own_and_swapped(pieces, order)
    (total,) = call(
        part(total_kernel, size),
        [jax.ShapeDtypeStruct(pieces[0].shape, HALF)],
        received,
        0,
    )
    riding = int(extra > 0 and groups == 2)
    gain = None
    if extra and not riding:
        gain = total[size : size + extra // 2].astype(F32) + total[size + extra // 2 :]
        gain = tree_sum(summed_over("seq", group, gain))
        total = total[:size]
    carry = shifted(total, group)
    distance = 1
    while distance < groups - 1:
        moved = shifted(carry, distance * group)
        kernel = part(
            carry_kernel, group, reverse, distance + (distance == 1), distance == 1
        )
        (carry,) = call(kernel, [piece], [carry, moved], 0)
        distance *= 2
    inputs = [carry] + received + ([total] if riding else []) + [token]
    sums = call(
        part(scan_kernel, group, order, reverse, groups <= 2, size, riding),
        [piece] * group + [gain_shape] * riding,
        inputs,
        0,
        ins={len(inputs) - 1: ANY},
    )
    results = own_and_swapped(sums[:group], order)
    return results, (sums[-1] if riding else gain)


def summed_over(axis, stride, array):
    count = lax.axis_size(axis)
    terms = [array]
    while stride < count:
        array = tree_sum(terms)
        width = 4 if count // stride % 4 == 0 else 2
        order = sorted(range(1, width), key=lambda i: i % 2)
        moved = {i: swap(array, axis, i * stride) for i in order}
        terms = [array] + [moved[i] for i in range(1, width)]
        stride *= width
    return terms


def per_device(queries, keys, values, gain, cotangent):
    q, k, v, cot = queries[0], keys[0], values[0], cotangent[0]
    rows, features = q.shape
    head = features // HEADS
    group = 4
    width = features // group
    part = functools.partial
    wide = jax.ShapeDtypeStruct((rows, features), F32)
    half = jax.ShapeDtypeStruct((rows, features), HALF)
    square = jax.ShapeDtypeStruct((rows, head), F32)
    piece = jax.ShapeDtypeStruct((width, head), HALF)
    scores_shape = jax.ShapeDtypeStruct((HEADS * rows, rows), HALF)
    gain_shape = jax.ShapeDtypeStruct((HEADS, head), F32)
    token_shape = jax.ShapeDtypeStruct((8, head), F32)
    whole = pltpu.VMEM((features, head), HALF)
    gain_row = gain.reshape(1, features)

    pieces = call(
        part(state_kernel, head, group),
        [piece] * group,
        [pltpu.with_memory_space_constraint(a, pltpu.HBM) for a in (k, v)],
        1,
        [whole]
        + [pltpu.VMEM((rows, features), HALF)] * 2
        + [pltpu.SemaphoreType.DMA((2, 4))],
        ins={0: HBM, 1: HBM},
    )
    scores, intra = call(part(local_kernel, head), [scores_shape, wide], [q, k, v], 2)
    prefix, _ = exclusive_scan(pieces, CROSSED, width, False, intra)
    message = jax.ShapeDtypeStruct((width + 2 * HEADS, head), HALF)
    sources = [q, intra, gain_row, cot]
    early, squares, inner = call(
        part(early_norm_kernel, head, CROSSED),
        [wide, square, square],
        sources + prefix[:-1],
        1,
    )
    late, inverse, grad, *pieces = call(
        part(norm_kernel, head, group, (CROSSED, DIAGONAL_FIRST), lax.axis_size("dp")),
        [jax.ShapeDtypeStruct((rows, width), F32), square, half] + [message] * group,
        sources + [early, squares, inner, prefix[-1]],
        2,
        [pltpu.VMEM((1, features), F32), pltpu.VMEM((HEADS, head), F32)],
    )
    output, grad_query, key_part, value_part, token = call(
        part(backward_kernel, head, group),
        [half, half, wide, wide, token_shape],
        [q, k, v, scores, grad, early, late, inverse, gain_row] + prefix,
        5,
        [whole],
    )
    suffix, gain_grad = exclusive_scan(pieces, DIAGONAL_FIRST, width, True, token)
    gains = summed_over("dp", 1, gain_grad)
    inputs = [k, v, key_part, value_part]
    outs = []
    for slot in range(group):
        last = slot == group - 1
        args = inputs + [suffix[slot]] + outs + (gains if last else [])
        at = len(inputs) + 1
        *outs, gain_grad = call(
            part(final_kernel, head, slot, last),
            [half, half] + [gain_shape] * last,
            args,
            1,
            [pltpu.VMEM((rows, width), HALF)] * 2
            + [pltpu.SemaphoreType.DMA((2, 2))]
            + [pltpu.VMEM((HEADS, head), F32), pltpu.SemaphoreType.DMA(())] * last,
            ins={at + i: HBM for i in range(len(outs))},
            out_specs={0: HBM, 1: HBM, 2: HBM},
            aliases={at + i: i for i in range(len(outs))},
        ) + (() if last else (None,))
    grad_key, grad_value = outs
    return (
        output[None],
        grad_query[None],
        grad_key[None],
        grad_value[None],
        gain_grad.reshape(features),
    )


def solution(mesh):
    spec = P("dp", "seq", None)
    return jax.shard_map(
        per_device,
        mesh=mesh,
        in_specs=(spec, spec, spec, P(), spec),
        out_specs=(spec, spec, spec, spec, P()),
        check_vma=False,
    )
```

```python
import functools

import jax
import jax.numpy as jnp
from jax import lax
from jax.experimental import pallas as pl
from jax.experimental.pallas import tpu as pltpu
from jax.sharding import PartitionSpec as P

HEADS = 16

EPSILON = 1e-06

F32 = jnp.float32
HALF = jnp.bfloat16


def dot(lhs, rhs, lhs_dim, rhs_dim):
    return lax.dot_general(
        lhs, rhs, (((lhs_dim,), (rhs_dim,)), ((), ())), preferred_element_type=F32
    )


def causal(size):
    rows = lax.broadcasted_iota(jnp.int32, (size, size), 0)
    columns = lax.broadcasted_iota(jnp.int32, (size, size), 1)
    return rows >= columns


def member_of(group):
    return lax.rem(lax.axis_index("seq"), group)


CROSSED = ((0, 1, 2, 3), (0, 2, 1, 3))
DIAGONAL_FIRST = ((0, 3, 1, 2), (0, 3, 1, 2))
X_FIRST = ((0, 1, 2, 3), (0, 1, 2, 3))
STATE_ORDERS = (CROSSED, X_FIRST)
GRAD_ORDERS = (DIAGONAL_FIRST, DIAGONAL_FIRST)
NORM_ORDERS = (STATE_ORDERS[1], GRAD_ORDERS[0])


def partner_of(order, slot):
    even, odd = order[0][slot], order[1][slot]
    offset = even
    if even != odd:
        offset = jnp.where(lax.rem(lax.axis_index("dp"), 2) == 1, odd, even)
    return member_of(len(order[0])) ^ offset


def block_at(index, size):
    return pl.ds(pl.multiple_of(index * size, size), size)


def gathered(order, piece_refs, size, whole_ref):
    for j, ref in enumerate(piece_refs):
        whole_ref[block_at(partner_of(order, j), size), :] = ref[0:size, :]


def scattered(order, whole_ref, size, piece_refs):
    for j, ref in enumerate(piece_refs):
        ref[0:size, :] = whole_ref[block_at(partner_of(order, j), size), :]


def columns(first, count):
    return slice(first, first + count)


def state_kernel(head, group, k_ref, v_ref, *refs):
    piece_refs = refs[:group]
    whole_ref, k_buffer, v_buffer, arrived = refs[group:]
    copies = [
        pltpu.make_async_copy(k_ref, k_buffer, arrived.at[0]),
        pltpu.make_async_copy(v_ref, v_buffer, arrived.at[1]),
    ]
    for copy in copies:
        copy.start()
    for copy in copies:
        copy.wait()
    for h in range(HEADS):
        part = columns(h * head, head)
        whole_ref[part, :] = dot(k_buffer[:, part], v_buffer[:, part], 0, 0).astype(HALF)
    scattered(STATE_ORDERS[0], whole_ref, piece_refs[0].shape[0], piece_refs)


def local_kernel(head, q_ref, k_ref, v_ref, scores_ref, intra_ref):
    rows = q_ref.shape[0]
    mask = causal(rows)
    scaling = head ** (-0.5)
    for h in range(HEADS):
        part = columns(h * head, head)
        scores = dot(q_ref[:, part], k_ref[:, part], 1, 1) * scaling
        scores = jnp.where(mask, scores, 0.0).astype(HALF)
        scores_ref[columns(h * rows, rows), :] = scores
        intra_ref[:, part] = dot(scores, v_ref[:, part], 1, 0)


def features_at(order, slot, i, width, head):
    start = partner_of(order, slot) * width + i * head
    return pl.ds(pl.multiple_of(start, head), head)


def attend(head, order, slot, refs, prefix_ref, attended_ref, at, squares, inner):
    q_ref, intra_ref, gain_ref, cot_ref = refs
    scaling = head ** (-0.5)
    width = prefix_ref.shape[0]
    for i in range(width // head):
        part = features_at(order, slot, i, width, head)
        prefix = prefix_ref[columns(i * head, head), :]
        attended = intra_ref[:, part] + scaling * dot(q_ref[:, part], prefix, 1, 0)
        attended_ref[:, part if at is None else columns(i * head, head)] = attended
        scaled = cot_ref[:, part].astype(F32) * gain_ref[:, part]
        squares += attended * attended
        inner += scaled * attended
    return squares, inner


def early_norm_kernel(head, order, *refs):
    prefix_refs, (attended_ref, squares_ref, inner_ref) = refs[4:-3], refs[-3:]
    squares = jnp.zeros(squares_ref.shape, F32)
    inner = jnp.zeros(squares_ref.shape, F32)
    for slot, prefix_ref in enumerate(prefix_refs):
        squares, inner = attend(
            head, order, slot, refs[:4], prefix_ref, attended_ref, None, squares, inner
        )
    squares_ref[...] = squares
    inner_ref[...] = inner


def norm_kernel(head, group, orders, replicas, *refs):
    q_ref, _, gain_ref, cot_ref = refs[:4]
    early_ref, squares_ref, inner_ref, prefix_ref = refs[4:8]
    late_ref, inverse_ref, grad_ref = refs[8:11]
    piece_refs = refs[11 : 11 + group]
    gain_grad_ref, gain_rows_ref = refs[11 + group :]
    features = q_ref.shape[1]
    width = features // group
    last = orders[0][0][group - 1]
    squares, inner = attend(
        head,
        orders[0],
        group - 1,
        refs[:4],
        prefix_ref,
        late_ref,
        0,
        squares_ref[...],
        inner_ref[...],
    )
    inverse = lax.rsqrt(
        jnp.sum(squares, axis=1, keepdims=True) * (1.0 / features) + EPSILON
    )
    inner_mean = jnp.sum(inner, axis=1, keepdims=True) * (1.0 / features) * inverse
    inverse_ref[...] = jnp.broadcast_to(inverse, inverse_ref.shape)
    scaling = head ** (-0.5)
    for slot in range(group):
        for i in range(width // head):
            part = features_at(orders[1], slot, i, width, head)
            local = columns(i * head, head)
            if orders[1][0][slot] == last:
                attended = late_ref[:, local]
            else:
                attended = early_ref[:, part]
            normalized = attended * inverse
            upstream = cot_ref[:, part].astype(F32)
            gain_grad_ref[:, part] = jnp.sum(
                upstream * normalized, axis=0, keepdims=True
            ) * (1.0 / replicas)
            scaled = upstream * gain_ref[:, part]
            grad = ((scaled - normalized * inner_mean) * inverse).astype(HALF)
            grad_ref[:, part] = grad
            piece_refs[slot][local, :] = (
                scaling * dot(q_ref[:, part], grad, 0, 0)
            ).astype(HALF)
    for h in range(HEADS):
        gain_rows_ref[h : h + 1, :] = gain_grad_ref[:, columns(h * head, head)]
    for ref in piece_refs:
        put_wide_rows(ref, width, gain_rows_ref[...])


def backward_kernel(head, group, *refs):
    q_ref, k_ref, v_ref, scores_ref, grad_ref = refs[:5]
    early_ref, late_ref, inverse_ref, gain_ref = refs[5:9]
    prefix_refs = refs[9 : 9 + group]
    out_ref, grad_query_ref, key_part_ref, value_part_ref, token_ref = refs[
        9 + group : 14 + group
    ]
    whole_ref = refs[14 + group]
    rows = q_ref.shape[0]
    mask = causal(rows)
    scaling = head ** (-0.5)
    gathered(STATE_ORDERS[1], prefix_refs, prefix_refs[0].shape[0], whole_ref)
    inverse = inverse_ref[...]
    width = late_ref.shape[1]
    for slot in range(group):
        for i in range(width // head):
            part = features_at(STATE_ORDERS[1], slot, i, width, head)
            if slot == group - 1:
                attended = late_ref[:, columns(i * head, head)]
            else:
                attended = early_ref[:, part]
            out_ref[:, part] = (gain_ref[:, part] * (attended * inverse)).astype(HALF)
    for h in range(HEADS):
        part = columns(h * head, head)
        grad = grad_ref[:, part]
        grad_scores = dot(grad, v_ref[:, part], 1, 1)
        grad_scores = jnp.where(mask, grad_scores, 0.0).astype(HALF)
        grad_query = dot(grad_scores, k_ref[:, part], 1, 0) + dot(
            grad, whole_ref[part, :], 1, 1
        )
        grad_query_ref[:, part] = (scaling * grad_query).astype(HALF)
        key_part_ref[:, part] = scaling * dot(grad_scores, q_ref[:, part], 0, 0)
        value_part_ref[:, part] = dot(
            scores_ref[columns(h * rows, rows), :], grad, 0, 0
        )
    token_ref[...] = jnp.zeros_like(token_ref)


def final_kernel(head, slots, last, *refs):
    k_ref, v_ref, key_part_ref, value_part_ref = refs[:4]
    suffix_refs = refs[4 : 4 + len(slots)]
    refs = refs[4 + len(slots) :]
    copies = []
    if last:
        gain_grad_ref, total_ref, gain_written = refs[-6], refs[-2], refs[-1]
        total_ref[...] = tree_sum([ref[...] for ref in refs[2:-8]])
        copies.append(pltpu.make_async_copy(total_ref, gain_grad_ref, gain_written))
        copies[0].start()
        out_refs, refs = refs[-8:-6], refs[-5:-2]
    else:
        out_refs, refs = refs[:2], refs[2:]
    key_buffer, value_buffer, written = refs
    width = key_buffer.shape[2]
    for n, slot in enumerate(slots):
        for i in range(width // head):
            part = features_at(GRAD_ORDERS[1], slot, i, width, head)
            local = columns(i * head, head)
            suffix = suffix_refs[n][local, :]
            key_buffer[n, :, local] = (
                key_part_ref[:, part] + dot(v_ref[:, part], suffix, 1, 1)
            ).astype(HALF)
            value_buffer[n, :, local] = (
                value_part_ref[:, part] + dot(k_ref[:, part], suffix, 1, 0)
            ).astype(HALF)
        for i, buffer in enumerate((key_buffer, value_buffer)):
            copy = pltpu.make_async_copy(
                buffer.at[n],
                out_refs[i].at[:, block_at(partner_of(GRAD_ORDERS[1], slot), width)],
                written.at[i, n],
            )
            copy.start()
            copies.append(copy)
    for copy in copies:
        copy.wait()


def tree_sum(terms):
    while len(terms) > 1:
        terms = [a + b for a, b in zip(terms[::2], terms[1::2])]
    return terms[0]


def wide_rows(ref, start):
    rows = (ref.shape[0] - start) // 2
    high = ref[columns(start, rows), :].astype(F32)
    return high + ref[columns(start + rows, rows), :].astype(F32)


def put_wide_rows(ref, start, value):
    rows = value.shape[0]
    high = value.astype(HALF)
    ref[columns(start, rows), :] = high
    ref[columns(start + rows, rows), :] = (value - high.astype(F32)).astype(HALF)


def total_kernel(size, count, *refs):
    refs, out_refs = refs[:count], refs[count + 1 :]
    total = refs[0][0:size, :].astype(F32)
    for ref in refs[1:]:
        total += ref[0:size, :].astype(F32)
    out_refs[0][0:size, :] = total.astype(HALF)
    if len(out_refs) > 1:
        gain = tree_sum([wide_rows(ref, size) for ref in refs])
        put_wide_rows(out_refs[0], size, gain)
        out_refs[1][...] = wide_rows(out_refs[0], size)


def group_flag(group, reverse, distance):
    index = lax.axis_index("seq") // group
    last = lax.axis_size("seq") // group - 1
    known = index + distance <= last if reverse else index >= distance
    return jnp.where(known, 1.0, 0.0)


def carry_kernel(group, reverse, distance, first, own_ref, moved_ref, out_ref):
    own = own_ref[...].astype(F32)
    if first:
        own = own * group_flag(group, reverse, 1)
    moved = moved_ref[...].astype(F32) * group_flag(group, reverse, distance)
    out_ref[...] = (own + moved).astype(HALF)


def scan_kernel(group, orders, reverse, masked, size, riding, *refs):
    sources = [partner_of(orders[0], j) for j in range(group)]
    targets = [partner_of(orders[1], j) for j in range(group)]
    carry = refs[0][0:size, :].astype(F32)
    if masked:
        carry = carry * group_flag(group, reverse, 1)
    blocks = [ref[0:size, :].astype(F32) for ref in refs[1 : 1 + group]]
    out_refs = refs[-group - riding :][:group]
    for j in range(group):
        total = carry
        for i in range(group):
            earlier = sources[i] < targets[j]
            later = sources[i] > targets[j]
            total += jnp.where(later if reverse else earlier, 1.0, 0.0) * blocks[i]
        out_refs[j][...] = total.astype(HALF)
    if riding:
        refs[-1][...] = refs[1 + group][...] + wide_rows(refs[0], size)


VMEM = pl.BlockSpec(memory_space=pltpu.VMEM)
ANY = pl.BlockSpec(memory_space=pl.ANY)
HBM = pl.BlockSpec(memory_space=pltpu.HBM)


def call(kernel, outs, args, matmuls, scratch=(), ins=None, out_specs=None, aliases=None):
    size = sum(a.size * a.dtype.itemsize for a in args)
    size += sum(o.size * o.dtype.itemsize for o in outs)
    ins = ins or {}
    out_specs = out_specs or {}
    return pl.pallas_call(
        kernel,
        out_shape=tuple(outs),
        in_specs=[ins.get(i, VMEM) for i in range(len(args))],
        out_specs=tuple(out_specs.get(i, VMEM) for i in range(len(outs))),
        scratch_shapes=list(scratch),
        input_output_aliases=aliases or {},
        compiler_params=pltpu.CompilerParams(vmem_limit_bytes=16 * 1024 * 1024),
        cost_estimate=pl.CostEstimate(
            flops=2 * 128 * 128 * 128 * HEADS * matmuls,
            bytes_accessed=size,
            transcendentals=0,
        ),
    )(*args)


def swap(array, axis, offset):
    count = lax.axis_size(axis)
    return lax.ppermute(array, axis, [(i, i ^ offset) for i in range(count)])


def own_and_swapped(pieces, order):
    count = lax.axis_size("seq")
    results = [pieces[0]]
    for slot in range(1, len(pieces)):
        pairs = []
        for row in range(lax.axis_size("dp")):
            offset = order[row % 2][slot]
            pairs += [(row * count + i, row * count + (i ^ offset)) for i in range(count)]
        results.append(lax.ppermute(pieces[slot], ("dp", "seq"), pairs))
    return results


def exclusive_scan(pieces, orders, size, reverse, token):
    group = len(pieces)
    count, rows = lax.axis_size("seq"), lax.axis_size("dp")
    groups = count // group
    part = functools.partial
    lanes = pieces[0].shape[1]
    extra = pieces[0].shape[0] - size
    piece = jax.ShapeDtypeStruct((size, lanes), HALF)
    gain_shape = jax.ShapeDtypeStruct((extra // 2, lanes), F32)

    def shifted(array, distance):
        step = -distance if reverse else distance
        pairs = [(i, (i + step) % count) for i in range(count)]
        return lax.ppermute(array, "seq", pairs)

    received = own_and_swapped(pieces, orders[0])
    totals = call(
        part(total_kernel, size, group),
        [jax.ShapeDtypeStruct(pieces[0].shape, HALF)] + [gain_shape] * (extra > 0),
        received + [token],
        0,
        ins={group: ANY},
    )
    total, gains = totals[0], list(totals[1:])
    riding = int(extra > 0 and groups == 2 and rows == 4)
    carry = shifted(total if riding else total[:size], group)
    if riding:
        for offset in (0, group):
            pairs = [
                (row * count + i, (row ^ 2) * count + (i ^ offset))
                for row in range(rows)
                for i in range(count)
            ]
            gains.append(lax.ppermute(gains[0], ("dp", "seq"), pairs))
    elif extra:
        gains = [tree_sum(summed_over("seq", group, gains[0]))]
        gains = [tree_sum(summed_over("dp", 2, gains[0]))]
    distance = 1
    while distance < groups - 1:
        moved = shifted(carry, distance * group)
        kernel = part(
            carry_kernel, group, reverse, distance + (distance == 1), distance == 1
        )
        (carry,) = call(kernel, [piece], [carry, moved], 0)
        distance *= 2
    sums = call(
        part(scan_kernel, group, orders, reverse, groups <= 2, size, riding),
        [piece] * group + [gain_shape] * riding,
        [carry] + received + (gains[:1] if riding else []),
        0,
    )
    results = own_and_swapped(sums[:group], orders[1])
    if riding:
        gains = [sums[-1] + (gains[1] + gains[2])]
    return results, (gains[0] if gains else None)


def summed_over(axis, stride, array):
    count = lax.axis_size(axis)
    terms = [array]
    while stride < count:
        array = tree_sum(terms)
        width = 4 if count // stride % 4 == 0 else 2
        order = sorted(range(1, width), key=lambda i: i % 2)
        moved = {i: swap(array, axis, i * stride) for i in order}
        terms = [array] + [moved[i] for i in range(1, width)]
        stride *= width
    return terms


def per_device(queries, keys, values, gain, cotangent):
    q, k, v, cot = queries[0], keys[0], values[0], cotangent[0]
    rows, features = q.shape
    head = features // HEADS
    group = 4
    width = features // group
    part = functools.partial
    wide = jax.ShapeDtypeStruct((rows, features), F32)
    half = jax.ShapeDtypeStruct((rows, features), HALF)
    square = jax.ShapeDtypeStruct((rows, head), F32)
    piece = jax.ShapeDtypeStruct((width, head), HALF)
    scores_shape = jax.ShapeDtypeStruct((HEADS * rows, rows), HALF)
    gain_shape = jax.ShapeDtypeStruct((HEADS, head), F32)
    token_shape = jax.ShapeDtypeStruct((8, head), F32)
    whole = pltpu.VMEM((features, head), HALF)
    gain_row = gain.reshape(1, features)

    pieces = call(
        part(state_kernel, head, group),
        [piece] * group,
        [pltpu.with_memory_space_constraint(a, pltpu.HBM) for a in (k, v)],
        1,
        [whole]
        + [pltpu.VMEM((rows, features), HALF)] * 2
        + [pltpu.SemaphoreType.DMA((2,))],
        ins={0: HBM, 1: HBM},
    )
    scores, intra = call(part(local_kernel, head), [scores_shape, wide], [q, k, v], 2)
    prefix, _ = exclusive_scan(pieces, STATE_ORDERS, width, False, intra)
    message = jax.ShapeDtypeStruct((width + 2 * HEADS, head), HALF)
    sources = [q, intra, gain_row, cot]
    early, squares, inner = call(
        part(early_norm_kernel, head, STATE_ORDERS[1]),
        [wide, square, square],
        sources + prefix[:-1],
        1,
    )
    late, inverse, grad, *pieces = call(
        part(norm_kernel, head, group, NORM_ORDERS, lax.axis_size("dp")),
        [jax.ShapeDtypeStruct((rows, width), F32), square, half] + [message] * group,
        sources + [early, squares, inner, prefix[-1]],
        2,
        [pltpu.VMEM((1, features), F32), pltpu.VMEM((HEADS, head), F32)],
    )
    output, grad_query, key_part, value_part, token = call(
        part(backward_kernel, head, group),
        [half, half, wide, wide, token_shape],
        [q, k, v, scores, grad, early, late, inverse, gain_row] + prefix,
        5,
        [whole],
    )
    suffix, gain_grad = exclusive_scan(pieces, GRAD_ORDERS, width, True, token)
    gains = [gain_grad, swap(gain_grad, "dp", 1)]
    inputs = [k, v, key_part, value_part]
    outs = []
    for slots in ((0, 1, 2), (3,)):
        last = group - 1 in slots
        at = len(inputs) + len(slots)
        results = call(
            part(final_kernel, head, slots, last),
            [half, half] + [gain_shape] * last,
            inputs + [suffix[slot] for slot in slots] + outs + (gains if last else []),
            1,
            [pltpu.VMEM((len(slots), rows, width), HALF)] * 2
            + [pltpu.SemaphoreType.DMA((2, len(slots)))]
            + [pltpu.VMEM((HEADS, head), F32), pltpu.SemaphoreType.DMA(())] * last,
            ins={at + i: HBM for i in range(len(outs))},
            out_specs={0: HBM, 1: HBM, 2: HBM},
            aliases={at + i: i for i in range(len(outs))},
        )
        outs = list(results[:2])
    grad_key, grad_value, gain_grad = results
    return (
        output[None],
        grad_query[None],
        grad_key[None],
        grad_value[None],
        gain_grad.reshape(features),
    )


def solution(mesh):
    spec = P("dp", "seq", None)
    return jax.shard_map(
        per_device,
        mesh=mesh,
        in_specs=(spec, spec, spec, P(), spec),
        out_specs=(spec, spec, spec, spec, P()),
        check_vma=False,
    )
```

```python
import functools

import jax
import jax.numpy as jnp
from jax import lax
from jax.experimental import pallas as pl
from jax.experimental.pallas import tpu as pltpu
from jax.sharding import PartitionSpec as P

HEADS = 16

EPSILON = 1e-06

F32 = jnp.float32
HALF = jnp.bfloat16


def dot(lhs, rhs, lhs_dim, rhs_dim):
    return lax.dot_general(
        lhs, rhs, (((lhs_dim,), (rhs_dim,)), ((), ())), preferred_element_type=F32
    )


def causal(size):
    rows = lax.broadcasted_iota(jnp.int32, (size, size), 0)
    columns = lax.broadcasted_iota(jnp.int32, (size, size), 1)
    return rows >= columns


def member_of(group):
    return lax.rem(lax.axis_index("seq"), group)


CROSSED = ((0, 1, 2, 3), (0, 2, 1, 3))
DIAGONAL_FIRST = ((0, 3, 1, 2), (0, 3, 1, 2))
X_FIRST = ((0, 1, 2, 3), (0, 1, 2, 3))
STATE_ORDERS = (CROSSED, X_FIRST)
GRAD_ORDERS = (DIAGONAL_FIRST, DIAGONAL_FIRST)
NORM_ORDERS = (STATE_ORDERS[1], GRAD_ORDERS[0])


def partner_of(order, slot):
    even, odd = order[0][slot], order[1][slot]
    offset = even
    if even != odd:
        offset = jnp.where(lax.rem(lax.axis_index("dp"), 2) == 1, odd, even)
    return member_of(len(order[0])) ^ offset


def block_at(index, size):
    return pl.ds(pl.multiple_of(index * size, size), size)


def gathered(order, piece_refs, size, whole_ref):
    for j, ref in enumerate(piece_refs):
        whole_ref[block_at(partner_of(order, j), size), :] = ref[0:size, :]


def scattered(order, whole_ref, size, piece_refs):
    for j, ref in enumerate(piece_refs):
        ref[0:size, :] = whole_ref[block_at(partner_of(order, j), size), :]


def columns(first, count):
    return slice(first, first + count)


def state_kernel(head, group, k_ref, v_ref, *refs):
    piece_refs = refs[:group]
    whole_ref, k_buffer, v_buffer, arrived = refs[group:]
    copies = [
        pltpu.make_async_copy(k_ref, k_buffer, arrived.at[0]),
        pltpu.make_async_copy(v_ref, v_buffer, arrived.at[1]),
    ]
    for copy in copies:
        copy.start()
    for copy in copies:
        copy.wait()
    for h in range(HEADS):
        part = columns(h * head, head)
        whole_ref[part, :] = dot(k_buffer[:, part], v_buffer[:, part], 0, 0).astype(HALF)
    scattered(STATE_ORDERS[0], whole_ref, piece_refs[0].shape[0], piece_refs)


def local_kernel(head, q_ref, k_ref, v_ref, scores_ref, intra_ref):
    rows = q_ref.shape[0]
    mask = causal(rows)
    scaling = head ** (-0.5)
    for h in range(HEADS):
        part = columns(h * head, head)
        scores = dot(q_ref[:, part], k_ref[:, part], 1, 1) * scaling
        scores = jnp.where(mask, scores, 0.0).astype(HALF)
        scores_ref[columns(h * rows, rows), :] = scores
        intra_ref[:, part] = dot(scores, v_ref[:, part], 1, 0)


def features_at(order, slot, i, width, head):
    start = partner_of(order, slot) * width + i * head
    return pl.ds(pl.multiple_of(start, head), head)


def attend(head, order, slot, refs, prefix_ref, attended_ref, at, squares, inner):
    q_ref, intra_ref, gain_ref, cot_ref = refs
    scaling = head ** (-0.5)
    width = prefix_ref.shape[0]
    for i in range(width // head):
        part = features_at(order, slot, i, width, head)
        prefix = prefix_ref[columns(i * head, head), :]
        attended = intra_ref[:, part] + scaling * dot(q_ref[:, part], prefix, 1, 0)
        attended_ref[:, part if at is None else columns(i * head, head)] = attended
        scaled = cot_ref[:, part].astype(F32) * gain_ref[:, part]
        squares += attended * attended
        inner += scaled * attended
    return squares, inner


def early_norm_kernel(head, order, *refs):
    prefix_refs, (attended_ref, squares_ref, inner_ref) = refs[4:-3], refs[-3:]
    squares = jnp.zeros(squares_ref.shape, F32)
    inner = jnp.zeros(squares_ref.shape, F32)
    for slot, prefix_ref in enumerate(prefix_refs):
        squares, inner = attend(
            head, order, slot, refs[:4], prefix_ref, attended_ref, None, squares, inner
        )
    squares_ref[...] = squares
    inner_ref[...] = inner


def norm_kernel(head, group, orders, replicas, *refs):
    q_ref, _, gain_ref, cot_ref = refs[:4]
    early_ref, squares_ref, inner_ref, prefix_ref = refs[4:8]
    late_ref, inverse_ref, grad_ref = refs[8:11]
    piece_refs = refs[11 : 11 + group]
    gain_grad_ref, gain_rows_ref = refs[11 + group :]
    features = q_ref.shape[1]
    width = features // group
    last = orders[0][0][group - 1]
    squares, inner = attend(
        head,
        orders[0],
        group - 1,
        refs[:4],
        prefix_ref,
        late_ref,
        0,
        squares_ref[...],
        inner_ref[...],
    )
    inverse = lax.rsqrt(
        jnp.sum(squares, axis=1, keepdims=True) * (1.0 / features) + EPSILON
    )
    inner_mean = jnp.sum(inner, axis=1, keepdims=True) * (1.0 / features) * inverse
    inverse_ref[...] = jnp.broadcast_to(inverse, inverse_ref.shape)
    scaling = head ** (-0.5)
    for slot in range(group):
        for i in range(width // head):
            part = features_at(orders[1], slot, i, width, head)
            local = columns(i * head, head)
            if orders[1][0][slot] == last:
                attended = late_ref[:, local]
            else:
                attended = early_ref[:, part]
            normalized = attended * inverse
            upstream = cot_ref[:, part].astype(F32)
            gain_grad_ref[:, part] = jnp.sum(
                upstream * normalized, axis=0, keepdims=True
            ) * (1.0 / replicas)
            scaled = upstream * gain_ref[:, part]
            grad = ((scaled - normalized * inner_mean) * inverse).astype(HALF)
            grad_ref[:, part] = grad
            piece_refs[slot][local, :] = (
                scaling * dot(q_ref[:, part], grad, 0, 0)
            ).astype(HALF)
    for h in range(HEADS):
        gain_rows_ref[h : h + 1, :] = gain_grad_ref[:, columns(h * head, head)]
    for ref in piece_refs:
        put_wide_rows(ref, width, gain_rows_ref[...])


def backward_kernel(head, group, *refs):
    q_ref, k_ref, v_ref, scores_ref, grad_ref = refs[:5]
    early_ref, late_ref, inverse_ref, gain_ref = refs[5:9]
    prefix_refs = refs[9 : 9 + group]
    out_ref, grad_query_ref, key_part_ref, value_part_ref, token_ref = refs[
        9 + group : 14 + group
    ]
    whole_ref = refs[14 + group]
    rows = q_ref.shape[0]
    mask = causal(rows)
    scaling = head ** (-0.5)
    gathered(STATE_ORDERS[1], prefix_refs, prefix_refs[0].shape[0], whole_ref)
    inverse = inverse_ref[...]
    width = late_ref.shape[1]
    for slot in range(group):
        for i in range(width // head):
            part = features_at(STATE_ORDERS[1], slot, i, width, head)
            if slot == group - 1:
                attended = late_ref[:, columns(i * head, head)]
            else:
                attended = early_ref[:, part]
            out_ref[:, part] = (gain_ref[:, part] * (attended * inverse)).astype(HALF)
    for h in range(HEADS):
        part = columns(h * head, head)
        grad = grad_ref[:, part]
        grad_scores = dot(grad, v_ref[:, part], 1, 1)
        grad_scores = jnp.where(mask, grad_scores, 0.0).astype(HALF)
        grad_query = dot(grad_scores, k_ref[:, part], 1, 0) + dot(
            grad, whole_ref[part, :], 1, 1
        )
        grad_query_ref[:, part] = (scaling * grad_query).astype(HALF)
        key_part_ref[:, part] = scaling * dot(grad_scores, q_ref[:, part], 0, 0)
        value_part_ref[:, part] = dot(
            scores_ref[columns(h * rows, rows), :], grad, 0, 0
        )
    token_ref[...] = jnp.zeros_like(token_ref)


def final_kernel(head, slots, last, *refs):
    k_ref, v_ref, key_part_ref, value_part_ref = refs[:4]
    suffix_refs = refs[4 : 4 + len(slots)]
    refs = refs[4 + len(slots) :]
    copies = []
    if last:
        gain_grad_ref, total_ref, gain_written = refs[-6], refs[-2], refs[-1]
        total_ref[...] = tree_sum([ref[...] for ref in refs[2:-8]])
        copies.append(pltpu.make_async_copy(total_ref, gain_grad_ref, gain_written))
        copies[0].start()
        out_refs, refs = refs[-8:-6], refs[-5:-2]
    else:
        out_refs, refs = refs[:2], refs[2:]
    key_buffer, value_buffer, written = refs
    width = key_buffer.shape[2]
    for n, slot in enumerate(slots):
        for i in range(width // head):
            part = features_at(GRAD_ORDERS[1], slot, i, width, head)
            local = columns(i * head, head)
            suffix = suffix_refs[n][local, :]
            key_buffer[n, :, local] = (
                key_part_ref[:, part] + dot(v_ref[:, part], suffix, 1, 1)
            ).astype(HALF)
            value_buffer[n, :, local] = (
                value_part_ref[:, part] + dot(k_ref[:, part], suffix, 1, 0)
            ).astype(HALF)
        for i, buffer in enumerate((key_buffer, value_buffer)):
            copy = pltpu.make_async_copy(
                buffer.at[n],
                out_refs[i].at[:, block_at(partner_of(GRAD_ORDERS[1], slot), width)],
                written.at[i, n],
            )
            copy.start()
            copies.append(copy)
    for copy in copies:
        copy.wait()


def tree_sum(terms):
    while len(terms) > 1:
        terms = [a + b for a, b in zip(terms[::2], terms[1::2])]
    return terms[0]


def wide_rows(ref, start):
    rows = (ref.shape[0] - start) // 2
    high = ref[columns(start, rows), :].astype(F32)
    return high + ref[columns(start + rows, rows), :].astype(F32)


def put_wide_rows(ref, start, value):
    rows = value.shape[0]
    high = value.astype(HALF)
    ref[columns(start, rows), :] = high
    ref[columns(start + rows, rows), :] = (value - high.astype(F32)).astype(HALF)


def total_kernel(size, count, *refs):
    refs, out_refs = refs[:count], refs[count + 1 :]
    total = refs[0][0:size, :].astype(F32)
    for ref in refs[1:]:
        total += ref[0:size, :].astype(F32)
    out_refs[0][0:size, :] = total.astype(HALF)
    if len(out_refs) > 1:
        gain = tree_sum([wide_rows(ref, size) for ref in refs])
        put_wide_rows(out_refs[0], size, gain)
        out_refs[1][...] = wide_rows(out_refs[0], size)


def group_flag(group, reverse, distance):
    index = lax.axis_index("seq") // group
    last = lax.axis_size("seq") // group - 1
    known = index + distance <= last if reverse else index >= distance
    return jnp.where(known, 1.0, 0.0)


def carry_kernel(group, reverse, distance, first, own_ref, moved_ref, out_ref):
    own = own_ref[...].astype(F32)
    if first:
        own = own * group_flag(group, reverse, 1)
    moved = moved_ref[...].astype(F32) * group_flag(group, reverse, distance)
    out_ref[...] = (own + moved).astype(HALF)


def scan_kernel(group, orders, slots, reverse, masked, size, riding, *refs):
    sources = [partner_of(orders[0], j) for j in range(group)]
    carry = refs[0][0:size, :].astype(F32)
    if masked:
        carry = carry * group_flag(group, reverse, 1)
    blocks = [ref[0:size, :].astype(F32) for ref in refs[1 : 1 + group]]
    out_refs = refs[-len(slots) - riding :][: len(slots)]
    for slot, out_ref in zip(slots, out_refs):
        target = partner_of(orders[1], slot)
        total = carry
        for i in range(group):
            known = sources[i] > target if reverse else sources[i] < target
            total += jnp.where(known, 1.0, 0.0) * blocks[i]
        out_ref[...] = total.astype(HALF)
    if riding:
        refs[-1][...] = refs[1 + group][...] + wide_rows(refs[0], size)


VMEM = pl.BlockSpec(memory_space=pltpu.VMEM)
ANY = pl.BlockSpec(memory_space=pl.ANY)
HBM = pl.BlockSpec(memory_space=pltpu.HBM)


def call(kernel, outs, args, matmuls, scratch=(), ins=None, out_specs=None, aliases=None):
    size = sum(a.size * a.dtype.itemsize for a in args)
    size += sum(o.size * o.dtype.itemsize for o in outs)
    ins = ins or {}
    out_specs = out_specs or {}
    return pl.pallas_call(
        kernel,
        out_shape=tuple(outs),
        in_specs=[ins.get(i, VMEM) for i in range(len(args))],
        out_specs=tuple(out_specs.get(i, VMEM) for i in range(len(outs))),
        scratch_shapes=list(scratch),
        input_output_aliases=aliases or {},
        compiler_params=pltpu.CompilerParams(vmem_limit_bytes=16 * 1024 * 1024),
        cost_estimate=pl.CostEstimate(
            flops=2 * 128 * 128 * 128 * HEADS * matmuls,
            bytes_accessed=size,
            transcendentals=0,
        ),
    )(*args)


def swap(array, axis, offset):
    count = lax.axis_size(axis)
    return lax.ppermute(array, axis, [(i, i ^ offset) for i in range(count)])


def own_and_swapped(pieces, order):
    count = lax.axis_size("seq")
    results = [pieces[0]]
    for slot in range(1, len(pieces)):
        pairs = []
        for row in range(lax.axis_size("dp")):
            offset = order[row % 2][slot]
            pairs += [(row * count + i, row * count + (i ^ offset)) for i in range(count)]
        results.append(lax.ppermute(pieces[slot], ("dp", "seq"), pairs))
    return results


def exclusive_scan(pieces, orders, size, reverse, token):
    group = len(pieces)
    count, rows = lax.axis_size("seq"), lax.axis_size("dp")
    groups = count // group
    part = functools.partial
    lanes = pieces[0].shape[1]
    extra = pieces[0].shape[0] - size
    piece = jax.ShapeDtypeStruct((size, lanes), HALF)
    gain_shape = jax.ShapeDtypeStruct((extra // 2, lanes), F32)

    def shifted(array, distance):
        step = -distance if reverse else distance
        pairs = [(i, (i + step) % count) for i in range(count)]
        return lax.ppermute(array, "seq", pairs)

    received = own_and_swapped(pieces, orders[0])
    totals = call(
        part(total_kernel, size, group),
        [jax.ShapeDtypeStruct(pieces[0].shape, HALF)] + [gain_shape] * (extra > 0),
        received + [token],
        0,
        ins={group: ANY},
    )
    total, gains = totals[0], list(totals[1:])
    riding = int(extra > 0 and groups == 2 and rows == 4)
    carry = shifted(total if riding else total[:size], group)
    if riding:
        for offset in (0, group):
            pairs = [
                (row * count + i, (row ^ 2) * count + (i ^ offset))
                for row in range(rows)
                for i in range(count)
            ]
            gains.append(lax.ppermute(gains[0], ("dp", "seq"), pairs))
    elif extra:
        gains = [tree_sum(summed_over("seq", group, gains[0]))]
        gains = [tree_sum(summed_over("dp", 2, gains[0]))]
    distance = 1
    while distance < groups - 1:
        moved = shifted(carry, distance * group)
        kernel = part(
            carry_kernel, group, reverse, distance + (distance == 1), distance == 1
        )
        (carry,) = call(kernel, [piece], [carry, moved], 0)
        distance *= 2
    pieces, after = {}, []
    for slots in ((1,), (2,), (3, 0)):
        adding = riding if 0 in slots else 0
        inputs = [carry] + received + gains[:adding] + after
        sums = call(
            part(scan_kernel, group, orders, slots, reverse, groups <= 2, size, adding),
            [piece] * len(slots) + [gain_shape] * adding,
            inputs,
            0,
            ins={len(inputs) - 1: ANY} if after else {},
        )
        pieces.update(zip(slots, sums))
        after = [sums[0]]
    results = own_and_swapped([pieces[slot] for slot in range(group)], orders[1])
    if riding:
        gains = [sums[-1] + (gains[1] + gains[2])]
    return results, (gains[0] if gains else None)


def summed_over(axis, stride, array):
    count = lax.axis_size(axis)
    terms = [array]
    while stride < count:
        array = tree_sum(terms)
        width = 4 if count // stride % 4 == 0 else 2
        order = sorted(range(1, width), key=lambda i: i % 2)
        moved = {i: swap(array, axis, i * stride) for i in order}
        terms = [array] + [moved[i] for i in range(1, width)]
        stride *= width
    return terms


def per_device(queries, keys, values, gain, cotangent):
    q, k, v, cot = queries[0], keys[0], values[0], cotangent[0]
    rows, features = q.shape
    head = features // HEADS
    group = 4
    width = features // group
    part = functools.partial
    wide = jax.ShapeDtypeStruct((rows, features), F32)
    half = jax.ShapeDtypeStruct((rows, features), HALF)
    square = jax.ShapeDtypeStruct((rows, head), F32)
    piece = jax.ShapeDtypeStruct((width, head), HALF)
    scores_shape = jax.ShapeDtypeStruct((HEADS * rows, rows), HALF)
    gain_shape = jax.ShapeDtypeStruct((HEADS, head), F32)
    token_shape = jax.ShapeDtypeStruct((8, head), F32)
    whole = pltpu.VMEM((features, head), HALF)
    gain_row = gain.reshape(1, features)

    pieces = call(
        part(state_kernel, head, group),
        [piece] * group,
        [pltpu.with_memory_space_constraint(a, pltpu.HBM) for a in (k, v)],
        1,
        [whole]
        + [pltpu.VMEM((rows, features), HALF)] * 2
        + [pltpu.SemaphoreType.DMA((2,))],
        ins={0: HBM, 1: HBM},
    )
    scores, intra = call(part(local_kernel, head), [scores_shape, wide], [q, k, v], 2)
    prefix, _ = exclusive_scan(pieces, STATE_ORDERS, width, False, intra)
    message = jax.ShapeDtypeStruct((width + 2 * HEADS, head), HALF)
    sources = [q, intra, gain_row, cot]
    early, squares, inner = call(
        part(early_norm_kernel, head, STATE_ORDERS[1]),
        [wide, square, square],
        sources + prefix[:-1],
        1,
    )
    late, inverse, grad, *pieces = call(
        part(norm_kernel, head, group, NORM_ORDERS, lax.axis_size("dp")),
        [jax.ShapeDtypeStruct((rows, width), F32), square, half] + [message] * group,
        sources + [early, squares, inner, prefix[-1]],
        2,
        [pltpu.VMEM((1, features), F32), pltpu.VMEM((HEADS, head), F32)],
    )
    output, grad_query, key_part, value_part, token = call(
        part(backward_kernel, head, group),
        [half, half, wide, wide, token_shape],
        [q, k, v, scores, grad, early, late, inverse, gain_row] + prefix,
        5,
        [whole],
    )
    suffix, gain_grad = exclusive_scan(pieces, GRAD_ORDERS, width, True, token)
    gains = [gain_grad, swap(gain_grad, "dp", 1)]
    inputs = [k, v, key_part, value_part]
    outs = []
    for slots in ((0, 1, 2), (3,)):
        last = group - 1 in slots
        at = len(inputs) + len(slots)
        results = call(
            part(final_kernel, head, slots, last),
            [half, half] + [gain_shape] * last,
            inputs + [suffix[slot] for slot in slots] + outs + (gains if last else []),
            1,
            [pltpu.VMEM((len(slots), rows, width), HALF)] * 2
            + [pltpu.SemaphoreType.DMA((2, len(slots)))]
            + [pltpu.VMEM((HEADS, head), F32), pltpu.SemaphoreType.DMA(())] * last,
            ins={at + i: HBM for i in range(len(outs))},
            out_specs={0: HBM, 1: HBM, 2: HBM},
            aliases={at + i: i for i in range(len(outs))},
        )
        outs = list(results[:2])
    grad_key, grad_value, gain_grad = results
    return (
        output[None],
        grad_query[None],
        grad_key[None],
        grad_value[None],
        gain_grad.reshape(features),
    )


def solution(mesh):
    spec = P("dp", "seq", None)
    return jax.shard_map(
        per_device,
        mesh=mesh,
        in_specs=(spec, spec, spec, P(), spec),
        out_specs=(spec, spec, spec, spec, P()),
        check_vma=False,
    )
```

```python
import functools

import jax
import jax.numpy as jnp
from jax import lax
from jax.experimental import pallas as pl
from jax.experimental.pallas import tpu as pltpu
from jax.sharding import PartitionSpec as P

HEADS = 16

EPSILON = 1e-06

F32 = jnp.float32
HALF = jnp.bfloat16


def dot(lhs, rhs, lhs_dim, rhs_dim):
    return lax.dot_general(
        lhs, rhs, (((lhs_dim,), (rhs_dim,)), ((), ())), preferred_element_type=F32
    )


def causal(size):
    rows = lax.broadcasted_iota(jnp.int32, (size, size), 0)
    columns = lax.broadcasted_iota(jnp.int32, (size, size), 1)
    return rows >= columns


def member_of(group):
    return lax.rem(lax.axis_index("seq"), group)


CROSSED = ((0, 2, 1, 3), (0, 1, 2, 3))
DIAGONAL_FIRST = ((0, 3, 1, 2), (0, 3, 1, 2))


def partner_of(order, slot):
    even, odd = order[0][slot], order[1][slot]
    offset = even
    if even != odd:
        offset = jnp.where(lax.rem(lax.axis_index("dp"), 2) == 1, odd, even)
    return member_of(len(order[0])) ^ offset


def block_at(index, size):
    return pl.ds(pl.multiple_of(index * size, size), size)


def gathered(order, piece_refs, size, whole_ref):
    for j, ref in enumerate(piece_refs):
        whole_ref[block_at(partner_of(order, j), size), :] = ref[0:size, :]


def scattered(order, whole_ref, size, piece_refs):
    for j, ref in enumerate(piece_refs):
        ref[0:size, :] = whole_ref[block_at(partner_of(order, j), size), :]


def columns(first, count):
    return slice(first, first + count)


def state_kernel(head, group, k_ref, v_ref, *refs):
    piece_refs = refs[:group]
    whole_ref, k_buffer, v_buffer, arrived = refs[group:]
    copies = [
        pltpu.make_async_copy(k_ref, k_buffer, arrived.at[0]),
        pltpu.make_async_copy(v_ref, v_buffer, arrived.at[1]),
    ]
    for copy in copies:
        copy.start()
    for copy in copies:
        copy.wait()
    for h in range(HEADS):
        part = columns(h * head, head)
        whole_ref[part, :] = dot(k_buffer[:, part], v_buffer[:, part], 0, 0).astype(HALF)
    scattered(CROSSED, whole_ref, piece_refs[0].shape[0], piece_refs)


def local_kernel(head, q_ref, k_ref, v_ref, scores_ref, intra_ref):
    rows = q_ref.shape[0]
    mask = causal(rows)
    scaling = head ** (-0.5)
    for h in range(HEADS):
        part = columns(h * head, head)
        scores = dot(q_ref[:, part], k_ref[:, part], 1, 1) * scaling
        scores = jnp.where(mask, scores, 0.0).astype(HALF)
        scores_ref[columns(h * rows, rows), :] = scores
        intra_ref[:, part] = dot(scores, v_ref[:, part], 1, 0)


def features_at(order, slot, i, width, head):
    start = partner_of(order, slot) * width + i * head
    return pl.ds(pl.multiple_of(start, head), head)


def attend(head, order, slot, refs, prefix_ref, attended_ref, at, squares, inner):
    q_ref, intra_ref, gain_ref, cot_ref = refs
    scaling = head ** (-0.5)
    width = prefix_ref.shape[0]
    for i in range(width // head):
        part = features_at(order, slot, i, width, head)
        prefix = prefix_ref[columns(i * head, head), :]
        attended = intra_ref[:, part] + scaling * dot(q_ref[:, part], prefix, 1, 0)
        attended_ref[:, part if at is None else columns(i * head, head)] = attended
        scaled = cot_ref[:, part].astype(F32) * gain_ref[:, part]
        squares += attended * attended
        inner += scaled * attended
    return squares, inner


def early_norm_kernel(head, order, *refs):
    prefix_refs, (attended_ref, squares_ref, inner_ref) = refs[4:-3], refs[-3:]
    squares = jnp.zeros(squares_ref.shape, F32)
    inner = jnp.zeros(squares_ref.shape, F32)
    for slot, prefix_ref in enumerate(prefix_refs):
        squares, inner = attend(
            head, order, slot, refs[:4], prefix_ref, attended_ref, None, squares, inner
        )
    squares_ref[...] = squares
    inner_ref[...] = inner


def norm_kernel(head, group, orders, replicas, *refs):
    q_ref, _, gain_ref, cot_ref = refs[:4]
    early_ref, squares_ref, inner_ref, prefix_ref = refs[4:8]
    late_ref, inverse_ref, grad_ref = refs[8:11]
    piece_refs = refs[11 : 11 + group]
    gain_grad_ref, gain_rows_ref = refs[11 + group :]
    features = q_ref.shape[1]
    width = features // group
    last = orders[0][0][group - 1]
    squares, inner = attend(
        head,
        orders[0],
        group - 1,
        refs[:4],
        prefix_ref,
        late_ref,
        0,
        squares_ref[...],
        inner_ref[...],
    )
    inverse = lax.rsqrt(
        jnp.sum(squares, axis=1, keepdims=True) * (1.0 / features) + EPSILON
    )
    inner_mean = jnp.sum(inner, axis=1, keepdims=True) * (1.0 / features) * inverse
    inverse_ref[...] = jnp.broadcast_to(inverse, inverse_ref.shape)
    scaling = head ** (-0.5)
    for slot in range(group):
        for i in range(width // head):
            part = features_at(orders[1], slot, i, width, head)
            local = columns(i * head, head)
            if orders[1][0][slot] == last:
                attended = late_ref[:, local]
            else:
                attended = early_ref[:, part]
            normalized = attended * inverse
            upstream = cot_ref[:, part].astype(F32)
            gain_grad_ref[:, part] = jnp.sum(
                upstream * normalized, axis=0, keepdims=True
            ) * (1.0 / replicas)
            scaled = upstream * gain_ref[:, part]
            grad = ((scaled - normalized * inner_mean) * inverse).astype(HALF)
            grad_ref[:, part] = grad
            piece_refs[slot][local, :] = (
                scaling * dot(q_ref[:, part], grad, 0, 0)
            ).astype(HALF)
    for h in range(HEADS):
        gain_rows_ref[h : h + 1, :] = gain_grad_ref[:, columns(h * head, head)]
    for ref in piece_refs:
        put_wide_rows(ref, width, gain_rows_ref[...])


def backward_kernel(head, group, *refs):
    q_ref, k_ref, v_ref, scores_ref, grad_ref = refs[:5]
    early_ref, late_ref, inverse_ref, gain_ref = refs[5:9]
    prefix_refs = refs[9 : 9 + group]
    out_ref, grad_query_ref, key_part_ref, value_part_ref, token_ref = refs[
        9 + group : 14 + group
    ]
    whole_ref = refs[14 + group]
    rows = q_ref.shape[0]
    mask = causal(rows)
    scaling = head ** (-0.5)
    gathered(CROSSED, prefix_refs, prefix_refs[0].shape[0], whole_ref)
    inverse = inverse_ref[...]
    width = late_ref.shape[1]
    for slot in range(group):
        for i in range(width // head):
            part = features_at(CROSSED, slot, i, width, head)
            if slot == group - 1:
                attended = late_ref[:, columns(i * head, head)]
            else:
                attended = early_ref[:, part]
            out_ref[:, part] = (gain_ref[:, part] * (attended * inverse)).astype(HALF)
    for h in range(HEADS):
        part = columns(h * head, head)
        grad = grad_ref[:, part]
        grad_scores = dot(grad, v_ref[:, part], 1, 1)
        grad_scores = jnp.where(mask, grad_scores, 0.0).astype(HALF)
        grad_query = dot(grad_scores, k_ref[:, part], 1, 0) + dot(
            grad, whole_ref[part, :], 1, 1
        )
        grad_query_ref[:, part] = (scaling * grad_query).astype(HALF)
        key_part_ref[:, part] = scaling * dot(grad_scores, q_ref[:, part], 0, 0)
        value_part_ref[:, part] = dot(
            scores_ref[columns(h * rows, rows), :], grad, 0, 0
        )
    token_ref[...] = jnp.zeros_like(token_ref)


def final_kernel(head, slots, last, *refs):
    k_ref, v_ref, key_part_ref, value_part_ref = refs[:4]
    suffix_refs = refs[4 : 4 + len(slots)]
    refs = refs[4 + len(slots) :]
    copies = []
    if last:
        gain_grad_ref, total_ref, gain_written = refs[-6], refs[-2], refs[-1]
        total_ref[...] = tree_sum([ref[...] for ref in refs[2:-8]])
        copies.append(pltpu.make_async_copy(total_ref, gain_grad_ref, gain_written))
        copies[0].start()
        out_refs, refs = refs[-8:-6], refs[-5:-2]
    else:
        out_refs, refs = refs[:2], refs[2:]
    key_buffer, value_buffer, written = refs
    width = key_buffer.shape[2]
    for n, slot in enumerate(slots):
        for i in range(width // head):
            part = features_at(DIAGONAL_FIRST, slot, i, width, head)
            local = columns(i * head, head)
            suffix = suffix_refs[n][local, :]
            key_buffer[n, :, local] = (
                key_part_ref[:, part] + dot(v_ref[:, part], suffix, 1, 1)
            ).astype(HALF)
            value_buffer[n, :, local] = (
                value_part_ref[:, part] + dot(k_ref[:, part], suffix, 1, 0)
            ).astype(HALF)
        for i, buffer in enumerate((key_buffer, value_buffer)):
            copy = pltpu.make_async_copy(
                buffer.at[n],
                out_refs[i].at[:, block_at(partner_of(DIAGONAL_FIRST, slot), width)],
                written.at[i, n],
            )
            copy.start()
            copies.append(copy)
    for copy in copies:
        copy.wait()


def tree_sum(terms):
    while len(terms) > 1:
        terms = [a + b for a, b in zip(terms[::2], terms[1::2])]
    return terms[0]


def wide_rows(ref, start):
    rows = (ref.shape[0] - start) // 2
    high = ref[columns(start, rows), :].astype(F32)
    return high + ref[columns(start + rows, rows), :].astype(F32)


def put_wide_rows(ref, start, value):
    rows = value.shape[0]
    high = value.astype(HALF)
    ref[columns(start, rows), :] = high
    ref[columns(start + rows, rows), :] = (value - high.astype(F32)).astype(HALF)


def total_kernel(size, *refs):
    out_ref = refs[-1]
    total = refs[0][0:size, :].astype(F32)
    for ref in refs[1:-1]:
        total += ref[0:size, :].astype(F32)
    out_ref[0:size, :] = total.astype(HALF)
    if out_ref.shape[0] > size:
        put_wide_rows(out_ref, size, tree_sum([wide_rows(ref, size) for ref in refs[:-1]]))


def group_flag(group, reverse, distance):
    index = lax.axis_index("seq") // group
    last = lax.axis_size("seq") // group - 1
    known = index + distance <= last if reverse else index >= distance
    return jnp.where(known, 1.0, 0.0)


def carry_kernel(group, reverse, distance, first, own_ref, moved_ref, out_ref):
    own = own_ref[...].astype(F32)
    if first:
        own = own * group_flag(group, reverse, 1)
    moved = moved_ref[...].astype(F32) * group_flag(group, reverse, distance)
    out_ref[...] = (own + moved).astype(HALF)


def scan_kernel(group, order, reverse, masked, size, riding, *refs):
    members = [partner_of(order, j) for j in range(group)]
    carry = refs[0][0:size, :].astype(F32)
    if masked:
        carry = carry * group_flag(group, reverse, 1)
    blocks = [ref[0:size, :].astype(F32) for ref in refs[1 : 1 + group]]
    out_refs = refs[-group - riding :][:group]
    for j in range(group):
        total = carry
        for i in range(group):
            if i != j:
                earlier = members[i] < members[j]
                keep = jnp.where(earlier != reverse, 1.0, 0.0)
                total += keep * blocks[i]
        out_refs[j][...] = total.astype(HALF)
    if riding:
        refs[-1][...] = wide_rows(refs[0], size) + wide_rows(refs[1 + group], size)


VMEM = pl.BlockSpec(memory_space=pltpu.VMEM)
ANY = pl.BlockSpec(memory_space=pl.ANY)
HBM = pl.BlockSpec(memory_space=pltpu.HBM)


def call(kernel, outs, args, matmuls, scratch=(), ins=None, out_specs=None, aliases=None):
    size = sum(a.size * a.dtype.itemsize for a in args)
    size += sum(o.size * o.dtype.itemsize for o in outs)
    ins = ins or {}
    out_specs = out_specs or {}
    return pl.pallas_call(
        kernel,
        out_shape=tuple(outs),
        in_specs=[ins.get(i, VMEM) for i in range(len(args))],
        out_specs=tuple(out_specs.get(i, VMEM) for i in range(len(outs))),
        scratch_shapes=list(scratch),
        input_output_aliases=aliases or {},
        compiler_params=pltpu.CompilerParams(vmem_limit_bytes=16 * 1024 * 1024),
        cost_estimate=pl.CostEstimate(
            flops=2 * 128 * 128 * 128 * HEADS * matmuls,
            bytes_accessed=size,
            transcendentals=0,
        ),
    )(*args)


def swap(array, axis, offset):
    count = lax.axis_size(axis)
    return lax.ppermute(array, axis, [(i, i ^ offset) for i in range(count)])


def own_and_swapped(pieces, order):
    count = lax.axis_size("seq")
    results = [pieces[0]]
    for slot in range(1, len(pieces)):
        pairs = []
        for row in range(lax.axis_size("dp")):
            offset = order[row % 2][slot]
            pairs += [(row * count + i, row * count + (i ^ offset)) for i in range(count)]
        results.append(lax.ppermute(pieces[slot], ("dp", "seq"), pairs))
    return results


def exclusive_scan(pieces, order, size, reverse, token):
    group = len(pieces)
    count = lax.axis_size("seq")
    groups = count // group
    part = functools.partial
    lanes = pieces[0].shape[1]
    extra = pieces[0].shape[0] - size
    piece = jax.ShapeDtypeStruct((size, lanes), HALF)
    gain_shape = jax.ShapeDtypeStruct((extra // 2, lanes), F32)

    def shifted(array, distance):
        step = -distance if reverse else distance
        pairs = [(i, (i + step) % count) for i in range(count)]
        return lax.ppermute(array, "seq", pairs)

    received = own_and_swapped(pieces, order)
    (total,) = call(
        part(total_kernel, size),
        [jax.ShapeDtypeStruct(pieces[0].shape, HALF)],
        received,
        0,
    )
    riding = int(extra > 0 and groups == 2)
    gain = None
    if extra and not riding:
        gain = total[size : size + extra // 2].astype(F32) + total[size + extra // 2 :]
        gain = tree_sum(summed_over("seq", group, gain))
        total = total[:size]
    carry = shifted(total, group)
    distance = 1
    while distance < groups - 1:
        moved = shifted(carry, distance * group)
        kernel = part(
            carry_kernel, group, reverse, distance + (distance == 1), distance == 1
        )
        (carry,) = call(kernel, [piece], [carry, moved], 0)
        distance *= 2
    inputs = [carry] + received + ([total] if riding else []) + [token]
    sums = call(
        part(scan_kernel, group, order, reverse, groups <= 2, size, riding),
        [piece] * group + [gain_shape] * riding,
        inputs,
        0,
        ins={len(inputs) - 1: ANY},
    )
    results = own_and_swapped(sums[:group], order)
    return results, (sums[-1] if riding else gain)


def summed_over(axis, stride, array):
    count = lax.axis_size(axis)
    terms = [array]
    while stride < count:
        array = tree_sum(terms)
        width = 4 if count // stride % 4 == 0 else 2
        order = sorted(range(1, width), key=lambda i: i % 2)
        moved = {i: swap(array, axis, i * stride) for i in order}
        terms = [array] + [moved[i] for i in range(1, width)]
        stride *= width
    return terms


def per_device(queries, keys, values, gain, cotangent):
    q, k, v, cot = queries[0], keys[0], values[0], cotangent[0]
    rows, features = q.shape
    head = features // HEADS
    group = 4
    width = features // group
    part = functools.partial
    wide = jax.ShapeDtypeStruct((rows, features), F32)
    half = jax.ShapeDtypeStruct((rows, features), HALF)
    square = jax.ShapeDtypeStruct((rows, head), F32)
    piece = jax.ShapeDtypeStruct((width, head), HALF)
    scores_shape = jax.ShapeDtypeStruct((HEADS * rows, rows), HALF)
    gain_shape = jax.ShapeDtypeStruct((HEADS, head), F32)
    token_shape = jax.ShapeDtypeStruct((8, head), F32)
    whole = pltpu.VMEM((features, head), HALF)
    gain_row = gain.reshape(1, features)

    pieces = call(
        part(state_kernel, head, group),
        [piece] * group,
        [pltpu.with_memory_space_constraint(a, pltpu.HBM) for a in (k, v)],
        1,
        [whole]
        + [pltpu.VMEM((rows, features), HALF)] * 2
        + [pltpu.SemaphoreType.DMA((2,))],
        ins={0: HBM, 1: HBM},
    )
    scores, intra = call(part(local_kernel, head), [scores_shape, wide], [q, k, v], 2)
    prefix, _ = exclusive_scan(pieces, CROSSED, width, False, intra)
    message = jax.ShapeDtypeStruct((width + 2 * HEADS, head), HALF)
    sources = [q, intra, gain_row, cot]
    early, squares, inner = call(
        part(early_norm_kernel, head, CROSSED),
        [wide, square, square],
        sources + prefix[:-1],
        1,
    )
    late, inverse, grad, *pieces = call(
        part(norm_kernel, head, group, (CROSSED, DIAGONAL_FIRST), lax.axis_size("dp")),
        [jax.ShapeDtypeStruct((rows, width), F32), square, half] + [message] * group,
        sources + [early, squares, inner, prefix[-1]],
        2,
        [pltpu.VMEM((1, features), F32), pltpu.VMEM((HEADS, head), F32)],
    )
    output, grad_query, key_part, value_part, token = call(
        part(backward_kernel, head, group),
        [half, half, wide, wide, token_shape],
        [q, k, v, scores, grad, early, late, inverse, gain_row] + prefix,
        5,
        [whole],
    )
    suffix, gain_grad = exclusive_scan(pieces, DIAGONAL_FIRST, width, True, token)
    gains = summed_over("dp", 1, gain_grad)
    inputs = [k, v, key_part, value_part]
    outs = []
    for slots in ((0, 1, 2), (3,)):
        last = group - 1 in slots
        at = len(inputs) + len(slots)
        results = call(
            part(final_kernel, head, slots, last),
            [half, half] + [gain_shape] * last,
            inputs + [suffix[slot] for slot in slots] + outs + (gains if last else []),
            1,
            [pltpu.VMEM((len(slots), rows, width), HALF)] * 2
            + [pltpu.SemaphoreType.DMA((2, len(slots)))]
            + [pltpu.VMEM((HEADS, head), F32), pltpu.SemaphoreType.DMA(())] * last,
            ins={at + i: HBM for i in range(len(outs))},
            out_specs={0: HBM, 1: HBM, 2: HBM},
            aliases={at + i: i for i in range(len(outs))},
        )
        outs = list(results[:2])
    grad_key, grad_value, gain_grad = results
    return (
        output[None],
        grad_query[None],
        grad_key[None],
        grad_value[None],
        gain_grad.reshape(features),
    )


def solution(mesh):
    spec = P("dp", "seq", None)
    return jax.shard_map(
        per_device,
        mesh=mesh,
        in_specs=(spec, spec, spec, P(), spec),
        out_specs=(spec, spec, spec, spec, P()),
        check_vma=False,
    )
```

```python
import functools

import jax
import jax.numpy as jnp
from jax import lax
from jax.experimental import pallas as pl
from jax.experimental.pallas import tpu as pltpu
from jax.sharding import PartitionSpec as P

HEADS = 16

EPSILON = 1e-06

F32 = jnp.float32
HALF = jnp.bfloat16


def dot(lhs, rhs, lhs_dim, rhs_dim):
    return lax.dot_general(
        lhs, rhs, (((lhs_dim,), (rhs_dim,)), ((), ())), preferred_element_type=F32
    )


def causal(size):
    rows = lax.broadcasted_iota(jnp.int32, (size, size), 0)
    columns = lax.broadcasted_iota(jnp.int32, (size, size), 1)
    return rows >= columns


def member_of(group):
    return lax.rem(lax.axis_index("seq"), group)


STATE_ORDERS = (((0, 1, 2, 3), (0, 2, 1, 3)), ((0, 1, 2, 3), (0, 1, 2, 3)))
GRAD_ORDERS = (((0, 2, 3, 1), (0, 2, 3, 1)), ((0, 3, 1, 2), (0, 1, 3, 2)))
NORM_ORDERS = (STATE_ORDERS[1], GRAD_ORDERS[0])


def partner_of(order, slot):
    even, odd = order[0][slot], order[1][slot]
    offset = even
    if even != odd:
        offset = jnp.where(lax.rem(lax.axis_index("dp"), 2) == 1, odd, even)
    return member_of(len(order[0])) ^ offset


def block_at(index, size):
    return pl.ds(pl.multiple_of(index * size, size), size)


def gathered(order, piece_refs, size, whole_ref):
    for j, ref in enumerate(piece_refs):
        whole_ref[block_at(partner_of(order, j), size), :] = ref[0:size, :]


def scattered(order, whole_ref, size, piece_refs):
    for j, ref in enumerate(piece_refs):
        ref[0:size, :] = whole_ref[block_at(partner_of(order, j), size), :]


def columns(first, count):
    return slice(first, first + count)


def state_kernel(head, group, k_ref, v_ref, *refs):
    piece_refs = refs[:group]
    whole_ref, k_buffer, v_buffer, arrived = refs[group:]
    copies = [
        pltpu.make_async_copy(k_ref, k_buffer, arrived.at[0]),
        pltpu.make_async_copy(v_ref, v_buffer, arrived.at[1]),
    ]
    for copy in copies:
        copy.start()
    for copy in copies:
        copy.wait()
    for h in range(HEADS):
        part = columns(h * head, head)
        whole_ref[part, :] = dot(k_buffer[:, part], v_buffer[:, part], 0, 0).astype(HALF)
    scattered(STATE_ORDERS[0], whole_ref, piece_refs[0].shape[0], piece_refs)


def local_kernel(head, q_ref, k_ref, v_ref, scores_ref, intra_ref):
    rows = q_ref.shape[0]
    mask = causal(rows)
    scaling = head ** (-0.5)
    for h in range(HEADS):
        part = columns(h * head, head)
        scores = dot(q_ref[:, part], k_ref[:, part], 1, 1) * scaling
        scores = jnp.where(mask, scores, 0.0).astype(HALF)
        scores_ref[columns(h * rows, rows), :] = scores
        intra_ref[:, part] = dot(scores, v_ref[:, part], 1, 0)


def features_at(order, slot, i, width, head):
    start = partner_of(order, slot) * width + i * head
    return pl.ds(pl.multiple_of(start, head), head)


def attend(head, order, slot, refs, prefix_ref, attended_ref, at, squares, inner):
    q_ref, intra_ref, gain_ref, cot_ref = refs
    scaling = head ** (-0.5)
    width = prefix_ref.shape[0]
    for i in range(width // head):
        part = features_at(order, slot, i, width, head)
        prefix = prefix_ref[columns(i * head, head), :]
        attended = intra_ref[:, part] + scaling * dot(q_ref[:, part], prefix, 1, 0)
        attended_ref[:, part if at is None else columns(i * head, head)] = attended
        scaled = cot_ref[:, part].astype(F32) * gain_ref[:, part]
        squares += attended * attended
        inner += scaled * attended
    return squares, inner


def early_norm_kernel(head, order, *refs):
    prefix_refs, (attended_ref, squares_ref, inner_ref) = refs[4:-3], refs[-3:]
    squares = jnp.zeros(squares_ref.shape, F32)
    inner = jnp.zeros(squares_ref.shape, F32)
    for slot, prefix_ref in enumerate(prefix_refs):
        squares, inner = attend(
            head, order, slot, refs[:4], prefix_ref, attended_ref, None, squares, inner
        )
    squares_ref[...] = squares
    inner_ref[...] = inner


def norm_kernel(head, group, orders, replicas, *refs):
    q_ref, _, gain_ref, cot_ref = refs[:4]
    early_ref, squares_ref, inner_ref, prefix_ref = refs[4:8]
    late_ref, inverse_ref, grad_ref = refs[8:11]
    piece_refs = refs[11 : 11 + group]
    gain_grad_ref, gain_rows_ref = refs[11 + group :]
    features = q_ref.shape[1]
    width = features // group
    last = orders[0][0][group - 1]
    squares, inner = attend(
        head,
        orders[0],
        group - 1,
        refs[:4],
        prefix_ref,
        late_ref,
        0,
        squares_ref[...],
        inner_ref[...],
    )
    inverse = lax.rsqrt(
        jnp.sum(squares, axis=1, keepdims=True) * (1.0 / features) + EPSILON
    )
    inner_mean = jnp.sum(inner, axis=1, keepdims=True) * (1.0 / features) * inverse
    inverse_ref[...] = jnp.broadcast_to(inverse, inverse_ref.shape)
    scaling = head ** (-0.5)
    for slot in range(group):
        for i in range(width // head):
            part = features_at(orders[1], slot, i, width, head)
            local = columns(i * head, head)
            if orders[1][0][slot] == last:
                attended = late_ref[:, local]
            else:
                attended = early_ref[:, part]
            normalized = attended * inverse
            upstream = cot_ref[:, part].astype(F32)
            gain_grad_ref[:, part] = jnp.sum(
                upstream * normalized, axis=0, keepdims=True
            ) * (1.0 / replicas)
            scaled = upstream * gain_ref[:, part]
            grad = ((scaled - normalized * inner_mean) * inverse).astype(HALF)
            grad_ref[:, part] = grad
            piece_refs[slot][local, :] = (
                scaling * dot(q_ref[:, part], grad, 0, 0)
            ).astype(HALF)
    for h in range(HEADS):
        gain_rows_ref[h : h + 1, :] = gain_grad_ref[:, columns(h * head, head)]
    for ref in piece_refs:
        put_wide_rows(ref, width, gain_rows_ref[...])


def backward_kernel(head, group, *refs):
    q_ref, k_ref, v_ref, scores_ref, grad_ref = refs[:5]
    early_ref, late_ref, inverse_ref, gain_ref = refs[5:9]
    prefix_refs = refs[9 : 9 + group]
    out_ref, grad_query_ref, key_part_ref, value_part_ref, token_ref = refs[
        9 + group : 14 + group
    ]
    whole_ref = refs[14 + group]
    rows = q_ref.shape[0]
    mask = causal(rows)
    scaling = head ** (-0.5)
    gathered(STATE_ORDERS[1], prefix_refs, prefix_refs[0].shape[0], whole_ref)
    inverse = inverse_ref[...]
    width = late_ref.shape[1]
    for slot in range(group):
        for i in range(width // head):
            part = features_at(STATE_ORDERS[1], slot, i, width, head)
            if slot == group - 1:
                attended = late_ref[:, columns(i * head, head)]
            else:
                attended = early_ref[:, part]
            out_ref[:, part] = (gain_ref[:, part] * (attended * inverse)).astype(HALF)
    for h in range(HEADS):
        part = columns(h * head, head)
        grad = grad_ref[:, part]
        grad_scores = dot(grad, v_ref[:, part], 1, 1)
        grad_scores = jnp.where(mask, grad_scores, 0.0).astype(HALF)
        grad_query = dot(grad_scores, k_ref[:, part], 1, 0) + dot(
            grad, whole_ref[part, :], 1, 1
        )
        grad_query_ref[:, part] = (scaling * grad_query).astype(HALF)
        key_part_ref[:, part] = scaling * dot(grad_scores, q_ref[:, part], 0, 0)
        value_part_ref[:, part] = dot(
            scores_ref[columns(h * rows, rows), :], grad, 0, 0
        )
    token_ref[...] = jnp.zeros_like(token_ref)


def final_kernel(head, slots, last, *refs):
    k_ref, v_ref, key_part_ref, value_part_ref = refs[:4]
    suffix_refs = refs[4 : 4 + len(slots)]
    refs = refs[4 + len(slots) :]
    copies = []
    if last:
        gain_grad_ref, total_ref, gain_written = refs[-6], refs[-2], refs[-1]
        total_ref[...] = tree_sum([ref[...] for ref in refs[2:-8]])
        copies.append(pltpu.make_async_copy(total_ref, gain_grad_ref, gain_written))
        copies[0].start()
        out_refs, refs = refs[-8:-6], refs[-5:-2]
    else:
        out_refs, refs = refs[:2], refs[2:]
    key_buffer, value_buffer, written = refs
    width = key_buffer.shape[2]
    for n, slot in enumerate(slots):
        for i in range(width // head):
            part = features_at(GRAD_ORDERS[1], slot, i, width, head)
            local = columns(i * head, head)
            suffix = suffix_refs[n][local, :]
            key_buffer[n, :, local] = (
                key_part_ref[:, part] + dot(v_ref[:, part], suffix, 1, 1)
            ).astype(HALF)
            value_buffer[n, :, local] = (
                value_part_ref[:, part] + dot(k_ref[:, part], suffix, 1, 0)
            ).astype(HALF)
        for i, buffer in enumerate((key_buffer, value_buffer)):
            copy = pltpu.make_async_copy(
                buffer.at[n],
                out_refs[i].at[:, block_at(partner_of(GRAD_ORDERS[1], slot), width)],
                written.at[i, n],
            )
            copy.start()
            copies.append(copy)
    for copy in copies:
        copy.wait()


def tree_sum(terms):
    while len(terms) > 1:
        terms = [a + b for a, b in zip(terms[::2], terms[1::2])]
    return terms[0]


def wide_rows(ref, start):
    rows = (ref.shape[0] - start) // 2
    high = ref[columns(start, rows), :].astype(F32)
    return high + ref[columns(start + rows, rows), :].astype(F32)


def put_wide_rows(ref, start, value):
    rows = value.shape[0]
    high = value.astype(HALF)
    ref[columns(start, rows), :] = high
    ref[columns(start + rows, rows), :] = (value - high.astype(F32)).astype(HALF)


def total_kernel(size, *refs):
    out_ref = refs[-1]
    total = refs[0][0:size, :].astype(F32)
    for ref in refs[1:-1]:
        total += ref[0:size, :].astype(F32)
    out_ref[0:size, :] = total.astype(HALF)
    if out_ref.shape[0] > size:
        put_wide_rows(out_ref, size, tree_sum([wide_rows(ref, size) for ref in refs[:-1]]))


def group_flag(group, reverse, distance):
    index = lax.axis_index("seq") // group
    last = lax.axis_size("seq") // group - 1
    known = index + distance <= last if reverse else index >= distance
    return jnp.where(known, 1.0, 0.0)


def carry_kernel(group, reverse, distance, first, own_ref, moved_ref, out_ref):
    own = own_ref[...].astype(F32)
    if first:
        own = own * group_flag(group, reverse, 1)
    moved = moved_ref[...].astype(F32) * group_flag(group, reverse, distance)
    out_ref[...] = (own + moved).astype(HALF)


def scan_kernel(group, orders, reverse, masked, size, riding, *refs):
    sources = [partner_of(orders[0], j) for j in range(group)]
    targets = [partner_of(orders[1], j) for j in range(group)]
    carry = refs[0][0:size, :].astype(F32)
    if masked:
        carry = carry * group_flag(group, reverse, 1)
    blocks = [ref[0:size, :].astype(F32) for ref in refs[1 : 1 + group]]
    out_refs = refs[-group - riding :][:group]
    for j in range(group):
        total = carry
        for i in range(group):
            earlier = sources[i] < targets[j]
            later = sources[i] > targets[j]
            total += jnp.where(later if reverse else earlier, 1.0, 0.0) * blocks[i]
        out_refs[j][...] = total.astype(HALF)
    if riding:
        refs[-1][...] = wide_rows(refs[0], size) + wide_rows(refs[1 + group], size)


VMEM = pl.BlockSpec(memory_space=pltpu.VMEM)
ANY = pl.BlockSpec(memory_space=pl.ANY)
HBM = pl.BlockSpec(memory_space=pltpu.HBM)


def call(kernel, outs, args, matmuls, scratch=(), ins=None, out_specs=None, aliases=None):
    size = sum(a.size * a.dtype.itemsize for a in args)
    size += sum(o.size * o.dtype.itemsize for o in outs)
    ins = ins or {}
    out_specs = out_specs or {}
    return pl.pallas_call(
        kernel,
        out_shape=tuple(outs),
        in_specs=[ins.get(i, VMEM) for i in range(len(args))],
        out_specs=tuple(out_specs.get(i, VMEM) for i in range(len(outs))),
        scratch_shapes=list(scratch),
        input_output_aliases=aliases or {},
        compiler_params=pltpu.CompilerParams(vmem_limit_bytes=16 * 1024 * 1024),
        cost_estimate=pl.CostEstimate(
            flops=2 * 128 * 128 * 128 * HEADS * matmuls,
            bytes_accessed=size,
            transcendentals=0,
        ),
    )(*args)


def swap(array, axis, offset):
    count = lax.axis_size(axis)
    return lax.ppermute(array, axis, [(i, i ^ offset) for i in range(count)])


def own_and_swapped(pieces, order):
    count = lax.axis_size("seq")
    results = [pieces[0]]
    for slot in range(1, len(pieces)):
        pairs = []
        for row in range(lax.axis_size("dp")):
            offset = order[row % 2][slot]
            pairs += [(row * count + i, row * count + (i ^ offset)) for i in range(count)]
        results.append(lax.ppermute(pieces[slot], ("dp", "seq"), pairs))
    return results


def exclusive_scan(pieces, orders, size, reverse, token):
    group = len(pieces)
    count = lax.axis_size("seq")
    groups = count // group
    part = functools.partial
    lanes = pieces[0].shape[1]
    extra = pieces[0].shape[0] - size
    piece = jax.ShapeDtypeStruct((size, lanes), HALF)
    gain_shape = jax.ShapeDtypeStruct((extra // 2, lanes), F32)

    def shifted(array, distance):
        step = -distance if reverse else distance
        pairs = [(i, (i + step) % count) for i in range(count)]
        return lax.ppermute(array, "seq", pairs)

    received = own_and_swapped(pieces, orders[0])
    (total,) = call(
        part(total_kernel, size),
        [jax.ShapeDtypeStruct(pieces[0].shape, HALF)],
        received,
        0,
    )
    riding = int(extra > 0 and groups == 2)
    gain = None
    if extra and not riding:
        gain = total[size : size + extra // 2].astype(F32) + total[size + extra // 2 :]
        gain = tree_sum(summed_over("seq", group, gain))
        total = total[:size]
    carry = shifted(total, group)
    distance = 1
    while distance < groups - 1:
        moved = shifted(carry, distance * group)
        kernel = part(
            carry_kernel, group, reverse, distance + (distance == 1), distance == 1
        )
        (carry,) = call(kernel, [piece], [carry, moved], 0)
        distance *= 2
    inputs = [carry] + received + ([total] if riding else []) + [token]
    sums = call(
        part(scan_kernel, group, orders, reverse, groups <= 2, size, riding),
        [piece] * group + [gain_shape] * riding,
        inputs,
        0,
        ins={len(inputs) - 1: ANY},
    )
    results = own_and_swapped(sums[:group], orders[1])
    return results, (sums[-1] if riding else gain)


def summed_over(axis, stride, array):
    count = lax.axis_size(axis)
    terms = [array]
    while stride < count:
        array = tree_sum(terms)
        width = 4 if count // stride % 4 == 0 else 2
        order = sorted(range(1, width), key=lambda i: i % 2)
        moved = {i: swap(array, axis, i * stride) for i in order}
        terms = [array] + [moved[i] for i in range(1, width)]
        stride *= width
    return terms


def per_device(queries, keys, values, gain, cotangent):
    q, k, v, cot = queries[0], keys[0], values[0], cotangent[0]
    rows, features = q.shape
    head = features // HEADS
    group = 4
    width = features // group
    part = functools.partial
    wide = jax.ShapeDtypeStruct((rows, features), F32)
    half = jax.ShapeDtypeStruct((rows, features), HALF)
    square = jax.ShapeDtypeStruct((rows, head), F32)
    piece = jax.ShapeDtypeStruct((width, head), HALF)
    scores_shape = jax.ShapeDtypeStruct((HEADS * rows, rows), HALF)
    gain_shape = jax.ShapeDtypeStruct((HEADS, head), F32)
    token_shape = jax.ShapeDtypeStruct((8, head), F32)
    whole = pltpu.VMEM((features, head), HALF)
    gain_row = gain.reshape(1, features)

    pieces = call(
        part(state_kernel, head, group),
        [piece] * group,
        [pltpu.with_memory_space_constraint(a, pltpu.HBM) for a in (k, v)],
        1,
        [whole]
        + [pltpu.VMEM((rows, features), HALF)] * 2
        + [pltpu.SemaphoreType.DMA((2,))],
        ins={0: HBM, 1: HBM},
    )
    scores, intra = call(part(local_kernel, head), [scores_shape, wide], [q, k, v], 2)
    prefix, _ = exclusive_scan(pieces, STATE_ORDERS, width, False, intra)
    message = jax.ShapeDtypeStruct((width + 2 * HEADS, head), HALF)
    sources = [q, intra, gain_row, cot]
    early, squares, inner = call(
        part(early_norm_kernel, head, STATE_ORDERS[1]),
        [wide, square, square],
        sources + prefix[:-1],
        1,
    )
    late, inverse, grad, *pieces = call(
        part(norm_kernel, head, group, NORM_ORDERS, lax.axis_size("dp")),
        [jax.ShapeDtypeStruct((rows, width), F32), square, half] + [message] * group,
        sources + [early, squares, inner, prefix[-1]],
        2,
        [pltpu.VMEM((1, features), F32), pltpu.VMEM((HEADS, head), F32)],
    )
    output, grad_query, key_part, value_part, token = call(
        part(backward_kernel, head, group),
        [half, half, wide, wide, token_shape],
        [q, k, v, scores, grad, early, late, inverse, gain_row] + prefix,
        5,
        [whole],
    )
    suffix, gain_grad = exclusive_scan(pieces, GRAD_ORDERS, width, True, token)
    gains = summed_over("dp", 1, gain_grad)
    inputs = [k, v, key_part, value_part]
    outs = []
    for slots in ((0, 1, 2), (3,)):
        last = group - 1 in slots
        at = len(inputs) + len(slots)
        results = call(
            part(final_kernel, head, slots, last),
            [half, half] + [gain_shape] * last,
            inputs + [suffix[slot] for slot in slots] + outs + (gains if last else []),
            1,
            [pltpu.VMEM((len(slots), rows, width), HALF)] * 2
            + [pltpu.SemaphoreType.DMA((2, len(slots)))]
            + [pltpu.VMEM((HEADS, head), F32), pltpu.SemaphoreType.DMA(())] * last,
            ins={at + i: HBM for i in range(len(outs))},
            out_specs={0: HBM, 1: HBM, 2: HBM},
            aliases={at + i: i for i in range(len(outs))},
        )
        outs = list(results[:2])
    grad_key, grad_value, gain_grad = results
    return (
        output[None],
        grad_query[None],
        grad_key[None],
        grad_value[None],
        gain_grad.reshape(features),
    )


def solution(mesh):
    spec = P("dp", "seq", None)
    return jax.shard_map(
        per_device,
        mesh=mesh,
        in_specs=(spec, spec, spec, P(), spec),
        out_specs=(spec, spec, spec, spec, P()),
        check_vma=False,
    )
```

```python
import functools

import jax
import jax.numpy as jnp
from jax import lax
from jax.experimental import pallas as pl
from jax.experimental.pallas import tpu as pltpu
from jax.sharding import PartitionSpec as P

HEADS = 16

EPSILON = 1e-06

F32 = jnp.float32
HALF = jnp.bfloat16


def dot(lhs, rhs, lhs_dim, rhs_dim):
    return lax.dot_general(
        lhs, rhs, (((lhs_dim,), (rhs_dim,)), ((), ())), preferred_element_type=F32
    )


def causal(size):
    rows = lax.broadcasted_iota(jnp.int32, (size, size), 0)
    columns = lax.broadcasted_iota(jnp.int32, (size, size), 1)
    return rows >= columns


def member_of(group):
    return lax.rem(lax.axis_index("seq"), group)


STATE_ORDERS = (((0, 1, 2, 3), (0, 2, 1, 3)), ((0, 1, 2, 3), (0, 1, 2, 3)))
GRAD_ORDERS = (((0, 2, 3, 1), (0, 3, 1, 2)), ((0, 3, 1, 2), (0, 1, 3, 2)))
NORM_ORDERS = (STATE_ORDERS[1], GRAD_ORDERS[0])


def partner_of(order, slot):
    even, odd = order[0][slot], order[1][slot]
    offset = even
    if even != odd:
        offset = jnp.where(lax.rem(lax.axis_index("dp"), 2) == 1, odd, even)
    return member_of(len(order[0])) ^ offset


def block_at(index, size):
    return pl.ds(pl.multiple_of(index * size, size), size)


def gathered(order, piece_refs, size, whole_ref):
    for j, ref in enumerate(piece_refs):
        whole_ref[block_at(partner_of(order, j), size), :] = ref[0:size, :]


def scattered(order, whole_ref, size, piece_refs):
    for j, ref in enumerate(piece_refs):
        ref[0:size, :] = whole_ref[block_at(partner_of(order, j), size), :]


def columns(first, count):
    return slice(first, first + count)


def state_kernel(head, group, k_ref, v_ref, *refs):
    piece_refs = refs[:group]
    whole_ref, k_buffer, v_buffer, arrived = refs[group:]
    copies = [
        pltpu.make_async_copy(k_ref, k_buffer, arrived.at[0]),
        pltpu.make_async_copy(v_ref, v_buffer, arrived.at[1]),
    ]
    for copy in copies:
        copy.start()
    for copy in copies:
        copy.wait()
    for h in range(HEADS):
        part = columns(h * head, head)
        whole_ref[part, :] = dot(k_buffer[:, part], v_buffer[:, part], 0, 0).astype(HALF)
    scattered(STATE_ORDERS[0], whole_ref, piece_refs[0].shape[0], piece_refs)


def local_kernel(head, q_ref, k_ref, v_ref, scores_ref, intra_ref):
    rows = q_ref.shape[0]
    mask = causal(rows)
    scaling = head ** (-0.5)
    for h in range(HEADS):
        part = columns(h * head, head)
        scores = dot(q_ref[:, part], k_ref[:, part], 1, 1) * scaling
        scores = jnp.where(mask, scores, 0.0).astype(HALF)
        scores_ref[columns(h * rows, rows), :] = scores
        intra_ref[:, part] = dot(scores, v_ref[:, part], 1, 0)


def features_at(order, slot, i, width, head):
    start = partner_of(order, slot) * width + i * head
    return pl.ds(pl.multiple_of(start, head), head)


def attend(head, order, slot, refs, prefix_ref, attended_ref, at, squares, inner):
    q_ref, intra_ref, gain_ref, cot_ref = refs
    scaling = head ** (-0.5)
    width = prefix_ref.shape[0]
    for i in range(width // head):
        part = features_at(order, slot, i, width, head)
        prefix = prefix_ref[columns(i * head, head), :]
        attended = intra_ref[:, part] + scaling * dot(q_ref[:, part], prefix, 1, 0)
        attended_ref[:, part if at is None else columns(i * head, head)] = attended
        scaled = cot_ref[:, part].astype(F32) * gain_ref[:, part]
        squares += attended * attended
        inner += scaled * attended
    return squares, inner


def early_norm_kernel(head, order, *refs):
    prefix_refs, (attended_ref, squares_ref, inner_ref) = refs[4:-3], refs[-3:]
    squares = jnp.zeros(squares_ref.shape, F32)
    inner = jnp.zeros(squares_ref.shape, F32)
    for slot, prefix_ref in enumerate(prefix_refs):
        squares, inner = attend(
            head, order, slot, refs[:4], prefix_ref, attended_ref, None, squares, inner
        )
    squares_ref[...] = squares
    inner_ref[...] = inner


def norm_kernel(head, group, orders, replicas, *refs):
    q_ref, _, gain_ref, cot_ref = refs[:4]
    early_ref, squares_ref, inner_ref, prefix_ref = refs[4:8]
    late_ref, inverse_ref, grad_ref = refs[8:11]
    piece_refs = refs[11 : 11 + group]
    gain_grad_ref, gain_rows_ref = refs[11 + group :]
    features = q_ref.shape[1]
    width = features // group
    last = orders[0][0][group - 1]
    odd = lax.rem(lax.axis_index("dp"), 2) == 1
    squares, inner = attend(
        head,
        orders[0],
        group - 1,
        refs[:4],
        prefix_ref,
        late_ref,
        0,
        squares_ref[...],
        inner_ref[...],
    )
    inverse = lax.rsqrt(
        jnp.sum(squares, axis=1, keepdims=True) * (1.0 / features) + EPSILON
    )
    inner_mean = jnp.sum(inner, axis=1, keepdims=True) * (1.0 / features) * inverse
    inverse_ref[...] = jnp.broadcast_to(inverse, inverse_ref.shape)
    scaling = head ** (-0.5)
    for slot in range(group):
        for i in range(width // head):
            part = features_at(orders[1], slot, i, width, head)
            local = columns(i * head, head)
            late = [order[slot] == last for order in orders[1]]
            attended = late_ref[:, local] if late[0] else early_ref[:, part]
            if late[0] != late[1]:
                other = late_ref[:, local] if late[1] else early_ref[:, part]
                attended = jnp.where(odd, other, attended)
            normalized = attended * inverse
            upstream = cot_ref[:, part].astype(F32)
            gain_grad_ref[:, part] = jnp.sum(
                upstream * normalized, axis=0, keepdims=True
            ) * (1.0 / replicas)
            scaled = upstream * gain_ref[:, part]
            grad = ((scaled - normalized * inner_mean) * inverse).astype(HALF)
            grad_ref[:, part] = grad
            piece_refs[slot][local, :] = (
                scaling * dot(q_ref[:, part], grad, 0, 0)
            ).astype(HALF)
    for h in range(HEADS):
        gain_rows_ref[h : h + 1, :] = gain_grad_ref[:, columns(h * head, head)]
    for ref in piece_refs:
        put_wide_rows(ref, width, gain_rows_ref[...])


def backward_kernel(head, group, *refs):
    q_ref, k_ref, v_ref, scores_ref, grad_ref = refs[:5]
    early_ref, late_ref, inverse_ref, gain_ref = refs[5:9]
    prefix_refs = refs[9 : 9 + group]
    out_ref, grad_query_ref, key_part_ref, value_part_ref, token_ref = refs[
        9 + group : 14 + group
    ]
    whole_ref = refs[14 + group]
    rows = q_ref.shape[0]
    mask = causal(rows)
    scaling = head ** (-0.5)
    gathered(STATE_ORDERS[1], prefix_refs, prefix_refs[0].shape[0], whole_ref)
    inverse = inverse_ref[...]
    width = late_ref.shape[1]
    for slot in range(group):
        for i in range(width // head):
            part = features_at(STATE_ORDERS[1], slot, i, width, head)
            if slot == group - 1:
                attended = late_ref[:, columns(i * head, head)]
            else:
                attended = early_ref[:, part]
            out_ref[:, part] = (gain_ref[:, part] * (attended * inverse)).astype(HALF)
    for h in range(HEADS):
        part = columns(h * head, head)
        grad = grad_ref[:, part]
        grad_scores = dot(grad, v_ref[:, part], 1, 1)
        grad_scores = jnp.where(mask, grad_scores, 0.0).astype(HALF)
        grad_query = dot(grad_scores, k_ref[:, part], 1, 0) + dot(
            grad, whole_ref[part, :], 1, 1
        )
        grad_query_ref[:, part] = (scaling * grad_query).astype(HALF)
        key_part_ref[:, part] = scaling * dot(grad_scores, q_ref[:, part], 0, 0)
        value_part_ref[:, part] = dot(
            scores_ref[columns(h * rows, rows), :], grad, 0, 0
        )
    token_ref[...] = jnp.zeros_like(token_ref)


def final_kernel(head, slots, last, *refs):
    k_ref, v_ref, key_part_ref, value_part_ref = refs[:4]
    suffix_refs = refs[4 : 4 + len(slots)]
    refs = refs[4 + len(slots) :]
    copies = []
    if last:
        gain_grad_ref, total_ref, gain_written = refs[-6], refs[-2], refs[-1]
        total_ref[...] = tree_sum([ref[...] for ref in refs[2:-8]])
        copies.append(pltpu.make_async_copy(total_ref, gain_grad_ref, gain_written))
        copies[0].start()
        out_refs, refs = refs[-8:-6], refs[-5:-2]
    else:
        out_refs, refs = refs[:2], refs[2:]
    key_buffer, value_buffer, written = refs
    width = key_buffer.shape[2]
    for n, slot in enumerate(slots):
        for i in range(width // head):
            part = features_at(GRAD_ORDERS[1], slot, i, width, head)
            local = columns(i * head, head)
            suffix = suffix_refs[n][local, :]
            key_buffer[n, :, local] = (
                key_part_ref[:, part] + dot(v_ref[:, part], suffix, 1, 1)
            ).astype(HALF)
            value_buffer[n, :, local] = (
                value_part_ref[:, part] + dot(k_ref[:, part], suffix, 1, 0)
            ).astype(HALF)
        for i, buffer in enumerate((key_buffer, value_buffer)):
            copy = pltpu.make_async_copy(
                buffer.at[n],
                out_refs[i].at[:, block_at(partner_of(GRAD_ORDERS[1], slot), width)],
                written.at[i, n],
            )
            copy.start()
            copies.append(copy)
    for copy in copies:
        copy.wait()


def tree_sum(terms):
    while len(terms) > 1:
        terms = [a + b for a, b in zip(terms[::2], terms[1::2])]
    return terms[0]


def wide_rows(ref, start):
    rows = (ref.shape[0] - start) // 2
    high = ref[columns(start, rows), :].astype(F32)
    return high + ref[columns(start + rows, rows), :].astype(F32)


def put_wide_rows(ref, start, value):
    rows = value.shape[0]
    high = value.astype(HALF)
    ref[columns(start, rows), :] = high
    ref[columns(start + rows, rows), :] = (value - high.astype(F32)).astype(HALF)


def total_kernel(size, count, *refs):
    refs, out_refs = refs[:count], refs[count + 1 :]
    total = refs[0][0:size, :].astype(F32)
    for ref in refs[1:]:
        total += ref[0:size, :].astype(F32)
    out_refs[0][0:size, :] = total.astype(HALF)
    if len(out_refs) > 1:
        gain = tree_sum([wide_rows(ref, size) for ref in refs])
        put_wide_rows(out_refs[0], size, gain)
        out_refs[1][...] = wide_rows(out_refs[0], size)


def group_flag(group, reverse, distance):
    index = lax.axis_index("seq") // group
    last = lax.axis_size("seq") // group - 1
    known = index + distance <= last if reverse else index >= distance
    return jnp.where(known, 1.0, 0.0)


def carry_kernel(group, reverse, distance, first, own_ref, moved_ref, out_ref):
    own = own_ref[...].astype(F32)
    if first:
        own = own * group_flag(group, reverse, 1)
    moved = moved_ref[...].astype(F32) * group_flag(group, reverse, distance)
    out_ref[...] = (own + moved).astype(HALF)


def scan_kernel(group, orders, slots, reverse, masked, size, riding, *refs):
    sources = [partner_of(orders[0], j) for j in range(group)]
    carry = refs[0][0:size, :].astype(F32)
    if masked:
        carry = carry * group_flag(group, reverse, 1)
    blocks = [ref[0:size, :].astype(F32) for ref in refs[1 : 1 + group]]
    out_refs = refs[-len(slots) - riding :][: len(slots)]
    for slot, out_ref in zip(slots, out_refs):
        target = partner_of(orders[1], slot)
        total = carry
        for i in range(group):
            known = sources[i] > target if reverse else sources[i] < target
            total += jnp.where(known, 1.0, 0.0) * blocks[i]
        out_ref[...] = total.astype(HALF)
    if riding:
        refs[-1][...] = refs[1 + group][...] + wide_rows(refs[0], size)


VMEM = pl.BlockSpec(memory_space=pltpu.VMEM)
ANY = pl.BlockSpec(memory_space=pl.ANY)
HBM = pl.BlockSpec(memory_space=pltpu.HBM)


def call(kernel, outs, args, matmuls, scratch=(), ins=None, out_specs=None, aliases=None):
    size = sum(a.size * a.dtype.itemsize for a in args)
    size += sum(o.size * o.dtype.itemsize for o in outs)
    ins = ins or {}
    out_specs = out_specs or {}
    return pl.pallas_call(
        kernel,
        out_shape=tuple(outs),
        in_specs=[ins.get(i, VMEM) for i in range(len(args))],
        out_specs=tuple(out_specs.get(i, VMEM) for i in range(len(outs))),
        scratch_shapes=list(scratch),
        input_output_aliases=aliases or {},
        compiler_params=pltpu.CompilerParams(vmem_limit_bytes=16 * 1024 * 1024),
        cost_estimate=pl.CostEstimate(
            flops=2 * 128 * 128 * 128 * HEADS * matmuls,
            bytes_accessed=size,
            transcendentals=0,
        ),
    )(*args)


def swap(array, axis, offset):
    count = lax.axis_size(axis)
    return lax.ppermute(array, axis, [(i, i ^ offset) for i in range(count)])


def own_and_swapped(pieces, order):
    count = lax.axis_size("seq")
    results = [pieces[0]]
    for slot in range(1, len(pieces)):
        pairs = []
        for row in range(lax.axis_size("dp")):
            offset = order[row % 2][slot]
            pairs += [(row * count + i, row * count + (i ^ offset)) for i in range(count)]
        results.append(lax.ppermute(pieces[slot], ("dp", "seq"), pairs))
    return results


def exclusive_scan(pieces, orders, size, reverse, token):
    group = len(pieces)
    count, rows = lax.axis_size("seq"), lax.axis_size("dp")
    groups = count // group
    part = functools.partial
    lanes = pieces[0].shape[1]
    extra = pieces[0].shape[0] - size
    piece = jax.ShapeDtypeStruct((size, lanes), HALF)
    gain_shape = jax.ShapeDtypeStruct((extra // 2, lanes), F32)

    def shifted(array, distance):
        step = -distance if reverse else distance
        pairs = [(i, (i + step) % count) for i in range(count)]
        return lax.ppermute(array, "seq", pairs)

    received = own_and_swapped(pieces, orders[0])
    totals = call(
        part(total_kernel, size, group),
        [jax.ShapeDtypeStruct(pieces[0].shape, HALF)] + [gain_shape] * (extra > 0),
        received + [token],
        0,
        ins={group: ANY},
    )
    total, gains = totals[0], list(totals[1:])
    riding = int(extra > 0 and groups == 2 and rows == 4)
    carry = shifted(total if riding else total[:size], group)
    if riding:
        for offset in (0, group):
            pairs = [
                (row * count + i, (row ^ 2) * count + (i ^ offset))
                for row in range(rows)
                for i in range(count)
            ]
            gains.append(lax.ppermute(gains[0], ("dp", "seq"), pairs))
    elif extra:
        gains = [tree_sum(summed_over("seq", group, gains[0]))]
        gains = [tree_sum(summed_over("dp", 2, gains[0]))]
    distance = 1
    while distance < groups - 1:
        moved = shifted(carry, distance * group)
        kernel = part(
            carry_kernel, group, reverse, distance + (distance == 1), distance == 1
        )
        (carry,) = call(kernel, [piece], [carry, moved], 0)
        distance *= 2
    pieces, after = {}, []
    for slots in ((1,), (2,), (3, 0)):
        adding = riding if 0 in slots else 0
        inputs = [carry] + received + gains[:adding] + after
        sums = call(
            part(scan_kernel, group, orders, slots, reverse, groups <= 2, size, adding),
            [piece] * len(slots) + [gain_shape] * adding,
            inputs,
            0,
            ins={len(inputs) - 1: ANY} if after else {},
        )
        pieces.update(zip(slots, sums))
        after = [sums[0]]
    results = own_and_swapped([pieces[slot] for slot in range(group)], orders[1])
    if riding:
        gains = [sums[-1] + (gains[1] + gains[2])]
    return results, (gains[0] if gains else None)


def summed_over(axis, stride, array):
    count = lax.axis_size(axis)
    terms = [array]
    while stride < count:
        array = tree_sum(terms)
        width = 4 if count // stride % 4 == 0 else 2
        order = sorted(range(1, width), key=lambda i: i % 2)
        moved = {i: swap(array, axis, i * stride) for i in order}
        terms = [array] + [moved[i] for i in range(1, width)]
        stride *= width
    return terms


def per_device(queries, keys, values, gain, cotangent):
    q, k, v, cot = queries[0], keys[0], values[0], cotangent[0]
    rows, features = q.shape
    head = features // HEADS
    group = 4
    width = features // group
    part = functools.partial
    wide = jax.ShapeDtypeStruct((rows, features), F32)
    half = jax.ShapeDtypeStruct((rows, features), HALF)
    square = jax.ShapeDtypeStruct((rows, head), F32)
    piece = jax.ShapeDtypeStruct((width, head), HALF)
    scores_shape = jax.ShapeDtypeStruct((HEADS * rows, rows), HALF)
    gain_shape = jax.ShapeDtypeStruct((HEADS, head), F32)
    token_shape = jax.ShapeDtypeStruct((8, head), F32)
    whole = pltpu.VMEM((features, head), HALF)
    gain_row = gain.reshape(1, features)

    pieces = call(
        part(state_kernel, head, group),
        [piece] * group,
        [pltpu.with_memory_space_constraint(a, pltpu.HBM) for a in (k, v)],
        1,
        [whole]
        + [pltpu.VMEM((rows, features), HALF)] * 2
        + [pltpu.SemaphoreType.DMA((2,))],
        ins={0: HBM, 1: HBM},
    )
    scores, intra = call(part(local_kernel, head), [scores_shape, wide], [q, k, v], 2)
    prefix, _ = exclusive_scan(pieces, STATE_ORDERS, width, False, intra)
    message = jax.ShapeDtypeStruct((width + 2 * HEADS, head), HALF)
    sources = [q, intra, gain_row, cot]
    early, squares, inner = call(
        part(early_norm_kernel, head, STATE_ORDERS[1]),
        [wide, square, square],
        sources + prefix[:-1],
        1,
    )
    late, inverse, grad, *pieces = call(
        part(norm_kernel, head, group, NORM_ORDERS, lax.axis_size("dp")),
        [jax.ShapeDtypeStruct((rows, width), F32), square, half] + [message] * group,
        sources + [early, squares, inner, prefix[-1]],
        2,
        [pltpu.VMEM((1, features), F32), pltpu.VMEM((HEADS, head), F32)],
    )
    output, grad_query, key_part, value_part, token = call(
        part(backward_kernel, head, group),
        [half, half, wide, wide, token_shape],
        [q, k, v, scores, grad, early, late, inverse, gain_row] + prefix,
        5,
        [whole],
    )
    suffix, gain_grad = exclusive_scan(pieces, GRAD_ORDERS, width, True, token)
    gains = [gain_grad, swap(gain_grad, "dp", 1)]
    inputs = [k, v, key_part, value_part]
    outs = []
    for slots in ((0, 1, 2), (3,)):
        last = group - 1 in slots
        at = len(inputs) + len(slots)
        results = call(
            part(final_kernel, head, slots, last),
            [half, half] + [gain_shape] * last,
            inputs + [suffix[slot] for slot in slots] + outs + (gains if last else []),
            1,
            [pltpu.VMEM((len(slots), rows, width), HALF)] * 2
            + [pltpu.SemaphoreType.DMA((2, len(slots)))]
            + [pltpu.VMEM((HEADS, head), F32), pltpu.SemaphoreType.DMA(())] * last,
            ins={at + i: HBM for i in range(len(outs))},
            out_specs={0: HBM, 1: HBM, 2: HBM},
            aliases={at + i: i for i in range(len(outs))},
        )
        outs = list(results[:2])
    grad_key, grad_value, gain_grad = results
    return (
        output[None],
        grad_query[None],
        grad_key[None],
        grad_value[None],
        gain_grad.reshape(features),
    )


def solution(mesh):
    spec = P("dp", "seq", None)
    return jax.shard_map(
        per_device,
        mesh=mesh,
        in_specs=(spec, spec, spec, P(), spec),
        out_specs=(spec, spec, spec, spec, P()),
        check_vma=False,
    )
```

```python
import functools

import jax
import jax.numpy as jnp
from jax import lax
from jax.experimental import pallas as pl
from jax.experimental.pallas import tpu as pltpu
from jax.sharding import PartitionSpec as P

HEADS = 16

EPSILON = 1e-06

F32 = jnp.float32
HALF = jnp.bfloat16


def dot(lhs, rhs, lhs_dim, rhs_dim):
    return lax.dot_general(
        lhs, rhs, (((lhs_dim,), (rhs_dim,)), ((), ())), preferred_element_type=F32
    )


def causal(size):
    rows = lax.broadcasted_iota(jnp.int32, (size, size), 0)
    columns = lax.broadcasted_iota(jnp.int32, (size, size), 1)
    return rows >= columns


def member_of(group):
    return lax.rem(lax.axis_index("seq"), group)


CROSSED = ((0, 1, 2, 3), (0, 2, 1, 3))
DIAGONAL_FIRST = ((0, 3, 1, 2), (0, 3, 1, 2))


def partner_of(order, slot):
    even, odd = order[0][slot], order[1][slot]
    offset = even
    if even != odd:
        offset = jnp.where(lax.rem(lax.axis_index("dp"), 2) == 1, odd, even)
    return member_of(len(order[0])) ^ offset


def block_at(index, size):
    return pl.ds(pl.multiple_of(index * size, size), size)


def gathered(order, piece_refs, size, whole_ref):
    for j, ref in enumerate(piece_refs):
        whole_ref[block_at(partner_of(order, j), size), :] = ref[0:size, :]


def scattered(order, whole_ref, size, piece_refs):
    for j, ref in enumerate(piece_refs):
        ref[0:size, :] = whole_ref[block_at(partner_of(order, j), size), :]


def columns(first, count):
    return slice(first, first + count)


def state_kernel(head, group, k_ref, v_ref, *refs):
    piece_refs = refs[:group]
    whole_ref, k_buffer, v_buffer, arrived = refs[group:]
    copies = [
        pltpu.make_async_copy(k_ref, k_buffer, arrived.at[0]),
        pltpu.make_async_copy(v_ref, v_buffer, arrived.at[1]),
    ]
    for copy in copies:
        copy.start()
    for copy in copies:
        copy.wait()
    for h in range(HEADS):
        part = columns(h * head, head)
        whole_ref[part, :] = dot(k_buffer[:, part], v_buffer[:, part], 0, 0).astype(HALF)
    scattered(CROSSED, whole_ref, piece_refs[0].shape[0], piece_refs)


def local_kernel(head, q_ref, k_ref, v_ref, scores_ref, intra_ref):
    rows = q_ref.shape[0]
    mask = causal(rows)
    scaling = head ** (-0.5)
    for h in range(HEADS):
        part = columns(h * head, head)
        scores = dot(q_ref[:, part], k_ref[:, part], 1, 1) * scaling
        scores = jnp.where(mask, scores, 0.0).astype(HALF)
        scores_ref[columns(h * rows, rows), :] = scores
        intra_ref[:, part] = dot(scores, v_ref[:, part], 1, 0)


def features_at(order, slot, i, width, head):
    start = partner_of(order, slot) * width + i * head
    return pl.ds(pl.multiple_of(start, head), head)


def attend(head, order, slot, refs, prefix_ref, attended_ref, at, squares, inner):
    q_ref, intra_ref, gain_ref, cot_ref = refs
    scaling = head ** (-0.5)
    width = prefix_ref.shape[0]
    for i in range(width // head):
        part = features_at(order, slot, i, width, head)
        prefix = prefix_ref[columns(i * head, head), :]
        attended = intra_ref[:, part] + scaling * dot(q_ref[:, part], prefix, 1, 0)
        attended_ref[:, part if at is None else columns(i * head, head)] = attended
        scaled = cot_ref[:, part].astype(F32) * gain_ref[:, part]
        squares += attended * attended
        inner += scaled * attended
    return squares, inner


def early_norm_kernel(head, order, *refs):
    prefix_refs, (attended_ref, squares_ref, inner_ref) = refs[4:-3], refs[-3:]
    squares = jnp.zeros(squares_ref.shape, F32)
    inner = jnp.zeros(squares_ref.shape, F32)
    for slot, prefix_ref in enumerate(prefix_refs):
        squares, inner = attend(
            head, order, slot, refs[:4], prefix_ref, attended_ref, None, squares, inner
        )
    squares_ref[...] = squares
    inner_ref[...] = inner


def norm_kernel(head, group, orders, replicas, *refs):
    q_ref, _, gain_ref, cot_ref = refs[:4]
    early_ref, squares_ref, inner_ref, prefix_ref = refs[4:8]
    late_ref, inverse_ref, grad_ref = refs[8:11]
    piece_refs = refs[11 : 11 + group]
    gain_grad_ref, gain_rows_ref = refs[11 + group :]
    features = q_ref.shape[1]
    width = features // group
    last = orders[0][0][group - 1]
    squares, inner = attend(
        head,
        orders[0],
        group - 1,
        refs[:4],
        prefix_ref,
        late_ref,
        0,
        squares_ref[...],
        inner_ref[...],
    )
    inverse = lax.rsqrt(
        jnp.sum(squares, axis=1, keepdims=True) * (1.0 / features) + EPSILON
    )
    inner_mean = jnp.sum(inner, axis=1, keepdims=True) * (1.0 / features) * inverse
    inverse_ref[...] = jnp.broadcast_to(inverse, inverse_ref.shape)
    scaling = head ** (-0.5)
    for slot in range(group):
        for i in range(width // head):
            part = features_at(orders[1], slot, i, width, head)
            local = columns(i * head, head)
            if orders[1][0][slot] == last:
                attended = late_ref[:, local]
            else:
                attended = early_ref[:, part]
            normalized = attended * inverse
            upstream = cot_ref[:, part].astype(F32)
            gain_grad_ref[:, part] = jnp.sum(
                upstream * normalized, axis=0, keepdims=True
            ) * (1.0 / replicas)
            scaled = upstream * gain_ref[:, part]
            grad = ((scaled - normalized * inner_mean) * inverse).astype(HALF)
            grad_ref[:, part] = grad
            piece_refs[slot][local, :] = (
                scaling * dot(q_ref[:, part], grad, 0, 0)
            ).astype(HALF)
    for h in range(HEADS):
        gain_rows_ref[h : h + 1, :] = gain_grad_ref[:, columns(h * head, head)]
    for ref in piece_refs:
        put_wide_rows(ref, width, gain_rows_ref[...])


def backward_kernel(head, group, *refs):
    q_ref, k_ref, v_ref, scores_ref, grad_ref = refs[:5]
    early_ref, late_ref, inverse_ref, gain_ref = refs[5:9]
    prefix_refs = refs[9 : 9 + group]
    out_ref, grad_query_ref, key_part_ref, value_part_ref, token_ref = refs[
        9 + group : 14 + group
    ]
    whole_ref = refs[14 + group]
    rows = q_ref.shape[0]
    mask = causal(rows)
    scaling = head ** (-0.5)
    gathered(CROSSED, prefix_refs, prefix_refs[0].shape[0], whole_ref)
    inverse = inverse_ref[...]
    width = late_ref.shape[1]
    for slot in range(group):
        for i in range(width // head):
            part = features_at(CROSSED, slot, i, width, head)
            if slot == group - 1:
                attended = late_ref[:, columns(i * head, head)]
            else:
                attended = early_ref[:, part]
            out_ref[:, part] = (gain_ref[:, part] * (attended * inverse)).astype(HALF)
    for h in range(HEADS):
        part = columns(h * head, head)
        grad = grad_ref[:, part]
        grad_scores = dot(grad, v_ref[:, part], 1, 1)
        grad_scores = jnp.where(mask, grad_scores, 0.0).astype(HALF)
        grad_query = dot(grad_scores, k_ref[:, part], 1, 0) + dot(
            grad, whole_ref[part, :], 1, 1
        )
        grad_query_ref[:, part] = (scaling * grad_query).astype(HALF)
        key_part_ref[:, part] = scaling * dot(grad_scores, q_ref[:, part], 0, 0)
        value_part_ref[:, part] = dot(
            scores_ref[columns(h * rows, rows), :], grad, 0, 0
        )
    token_ref[...] = jnp.zeros_like(token_ref)


def final_kernel(head, slots, last, *refs):
    k_ref, v_ref, key_part_ref, value_part_ref = refs[:4]
    suffix_refs = refs[4 : 4 + len(slots)]
    refs = refs[4 + len(slots) :]
    copies = []
    if last:
        gain_grad_ref, total_ref, gain_written = refs[-6], refs[-2], refs[-1]
        total_ref[...] = tree_sum([ref[...] for ref in refs[2:-8]])
        copies.append(pltpu.make_async_copy(total_ref, gain_grad_ref, gain_written))
        copies[0].start()
        out_refs, refs = refs[-8:-6], refs[-5:-2]
    else:
        out_refs, refs = refs[:2], refs[2:]
    key_buffer, value_buffer, written = refs
    width = key_buffer.shape[2]
    for n, slot in enumerate(slots):
        for i in range(width // head):
            part = features_at(DIAGONAL_FIRST, slot, i, width, head)
            local = columns(i * head, head)
            suffix = suffix_refs[n][local, :]
            key_buffer[n, :, local] = (
                key_part_ref[:, part] + dot(v_ref[:, part], suffix, 1, 1)
            ).astype(HALF)
            value_buffer[n, :, local] = (
                value_part_ref[:, part] + dot(k_ref[:, part], suffix, 1, 0)
            ).astype(HALF)
        for i, buffer in enumerate((key_buffer, value_buffer)):
            copy = pltpu.make_async_copy(
                buffer.at[n],
                out_refs[i].at[:, block_at(partner_of(DIAGONAL_FIRST, slot), width)],
                written.at[i, n],
            )
            copy.start()
            copies.append(copy)
    for copy in copies:
        copy.wait()


def tree_sum(terms):
    while len(terms) > 1:
        terms = [a + b for a, b in zip(terms[::2], terms[1::2])]
    return terms[0]


def wide_rows(ref, start):
    rows = (ref.shape[0] - start) // 2
    high = ref[columns(start, rows), :].astype(F32)
    return high + ref[columns(start + rows, rows), :].astype(F32)


def put_wide_rows(ref, start, value):
    rows = value.shape[0]
    high = value.astype(HALF)
    ref[columns(start, rows), :] = high
    ref[columns(start + rows, rows), :] = (value - high.astype(F32)).astype(HALF)


def total_kernel(size, *refs):
    out_ref = refs[-1]
    total = refs[0][0:size, :].astype(F32)
    for ref in refs[1:-1]:
        total += ref[0:size, :].astype(F32)
    out_ref[0:size, :] = total.astype(HALF)
    if out_ref.shape[0] > size:
        put_wide_rows(out_ref, size, tree_sum([wide_rows(ref, size) for ref in refs[:-1]]))


def group_flag(group, reverse, distance):
    index = lax.axis_index("seq") // group
    last = lax.axis_size("seq") // group - 1
    known = index + distance <= last if reverse else index >= distance
    return jnp.where(known, 1.0, 0.0)


def carry_kernel(group, reverse, distance, first, own_ref, moved_ref, out_ref):
    own = own_ref[...].astype(F32)
    if first:
        own = own * group_flag(group, reverse, 1)
    moved = moved_ref[...].astype(F32) * group_flag(group, reverse, distance)
    out_ref[...] = (own + moved).astype(HALF)


def scan_kernel(group, order, reverse, masked, size, riding, *refs):
    members = [partner_of(order, j) for j in range(group)]
    carry = refs[0][0:size, :].astype(F32)
    if masked:
        carry = carry * group_flag(group, reverse, 1)
    blocks = [ref[0:size, :].astype(F32) for ref in refs[1 : 1 + group]]
    out_refs = refs[-group - riding :][:group]
    for j in range(group):
        total = carry
        for i in range(group):
            if i != j:
                earlier = members[i] < members[j]
                keep = jnp.where(earlier != reverse, 1.0, 0.0)
                total += keep * blocks[i]
        out_refs[j][...] = total.astype(HALF)
    if riding:
        refs[-1][...] = wide_rows(refs[0], size) + wide_rows(refs[1 + group], size)


VMEM = pl.BlockSpec(memory_space=pltpu.VMEM)
ANY = pl.BlockSpec(memory_space=pl.ANY)
HBM = pl.BlockSpec(memory_space=pltpu.HBM)


def call(kernel, outs, args, matmuls, scratch=(), ins=None, out_specs=None, aliases=None):
    size = sum(a.size * a.dtype.itemsize for a in args)
    size += sum(o.size * o.dtype.itemsize for o in outs)
    ins = ins or {}
    out_specs = out_specs or {}
    return pl.pallas_call(
        kernel,
        out_shape=tuple(outs),
        in_specs=[ins.get(i, VMEM) for i in range(len(args))],
        out_specs=tuple(out_specs.get(i, VMEM) for i in range(len(outs))),
        scratch_shapes=list(scratch),
        input_output_aliases=aliases or {},
        compiler_params=pltpu.CompilerParams(vmem_limit_bytes=16 * 1024 * 1024),
        cost_estimate=pl.CostEstimate(
            flops=2 * 128 * 128 * 128 * HEADS * matmuls,
            bytes_accessed=size,
            transcendentals=0,
        ),
    )(*args)


def swap(array, axis, offset):
    count = lax.axis_size(axis)
    return lax.ppermute(array, axis, [(i, i ^ offset) for i in range(count)])


def own_and_swapped(pieces, order):
    count = lax.axis_size("seq")
    results = [pieces[0]]
    for slot in range(1, len(pieces)):
        pairs = []
        for row in range(lax.axis_size("dp")):
            offset = order[row % 2][slot]
            pairs += [(row * count + i, row * count + (i ^ offset)) for i in range(count)]
        results.append(lax.ppermute(pieces[slot], ("dp", "seq"), pairs))
    return results


def exclusive_scan(pieces, order, size, reverse, token):
    group = len(pieces)
    count = lax.axis_size("seq")
    groups = count // group
    part = functools.partial
    lanes = pieces[0].shape[1]
    extra = pieces[0].shape[0] - size
    piece = jax.ShapeDtypeStruct((size, lanes), HALF)
    gain_shape = jax.ShapeDtypeStruct((extra // 2, lanes), F32)

    def shifted(array, distance):
        step = -distance if reverse else distance
        pairs = [(i, (i + step) % count) for i in range(count)]
        return lax.ppermute(array, "seq", pairs)

    received = own_and_swapped(pieces, order)
    (total,) = call(
        part(total_kernel, size),
        [jax.ShapeDtypeStruct(pieces[0].shape, HALF)],
        received,
        0,
    )
    riding = int(extra > 0 and groups == 2)
    gain = None
    if extra and not riding:
        gain = total[size : size + extra // 2].astype(F32) + total[size + extra // 2 :]
        gain = tree_sum(summed_over("seq", group, gain))
        total = total[:size]
    carry = shifted(total, group)
    distance = 1
    while distance < groups - 1:
        moved = shifted(carry, distance * group)
        kernel = part(
            carry_kernel, group, reverse, distance + (distance == 1), distance == 1
        )
        (carry,) = call(kernel, [piece], [carry, moved], 0)
        distance *= 2
    inputs = [carry] + received + ([total] if riding else []) + [token]
    sums = call(
        part(scan_kernel, group, order, reverse, groups <= 2, size, riding),
        [piece] * group + [gain_shape] * riding,
        inputs,
        0,
        ins={len(inputs) - 1: ANY},
    )
    results = own_and_swapped(sums[:group], order)
    return results, (sums[-1] if riding else gain)


def summed_over(axis, stride, array):
    count = lax.axis_size(axis)
    terms = [array]
    while stride < count:
        array = tree_sum(terms)
        width = 4 if count // stride % 4 == 0 else 2
        order = sorted(range(1, width), key=lambda i: i % 2)
        moved = {i: swap(array, axis, i * stride) for i in order}
        terms = [array] + [moved[i] for i in range(1, width)]
        stride *= width
    return terms


def per_device(queries, keys, values, gain, cotangent):
    q, k, v, cot = queries[0], keys[0], values[0], cotangent[0]
    rows, features = q.shape
    head = features // HEADS
    group = 4
    width = features // group
    part = functools.partial
    wide = jax.ShapeDtypeStruct((rows, features), F32)
    half = jax.ShapeDtypeStruct((rows, features), HALF)
    square = jax.ShapeDtypeStruct((rows, head), F32)
    piece = jax.ShapeDtypeStruct((width, head), HALF)
    scores_shape = jax.ShapeDtypeStruct((HEADS * rows, rows), HALF)
    gain_shape = jax.ShapeDtypeStruct((HEADS, head), F32)
    token_shape = jax.ShapeDtypeStruct((8, head), F32)
    whole = pltpu.VMEM((features, head), HALF)
    gain_row = gain.reshape(1, features)

    pieces = call(
        part(state_kernel, head, group),
        [piece] * group,
        [pltpu.with_memory_space_constraint(a, pltpu.HBM) for a in (k, v)],
        1,
        [whole]
        + [pltpu.VMEM((rows, features), HALF)] * 2
        + [pltpu.SemaphoreType.DMA((2,))],
        ins={0: HBM, 1: HBM},
    )
    scores, intra = call(part(local_kernel, head), [scores_shape, wide], [q, k, v], 2)
    prefix, _ = exclusive_scan(pieces, CROSSED, width, False, intra)
    message = jax.ShapeDtypeStruct((width + 2 * HEADS, head), HALF)
    sources = [q, intra, gain_row, cot]
    early, squares, inner = call(
        part(early_norm_kernel, head, CROSSED),
        [wide, square, square],
        sources + prefix[:-1],
        1,
    )
    late, inverse, grad, *pieces = call(
        part(norm_kernel, head, group, (CROSSED, DIAGONAL_FIRST), lax.axis_size("dp")),
        [jax.ShapeDtypeStruct((rows, width), F32), square, half] + [message] * group,
        sources + [early, squares, inner, prefix[-1]],
        2,
        [pltpu.VMEM((1, features), F32), pltpu.VMEM((HEADS, head), F32)],
    )
    output, grad_query, key_part, value_part, token = call(
        part(backward_kernel, head, group),
        [half, half, wide, wide, token_shape],
        [q, k, v, scores, grad, early, late, inverse, gain_row] + prefix,
        5,
        [whole],
    )
    suffix, gain_grad = exclusive_scan(pieces, DIAGONAL_FIRST, width, True, token)
    gains = summed_over("dp", 1, gain_grad)
    inputs = [k, v, key_part, value_part]
    outs = []
    for slots in ((0, 1, 2), (3,)):
        last = group - 1 in slots
        at = len(inputs) + len(slots)
        results = call(
            part(final_kernel, head, slots, last),
            [half, half] + [gain_shape] * last,
            inputs + [suffix[slot] for slot in slots] + outs + (gains if last else []),
            1,
            [pltpu.VMEM((len(slots), rows, width), HALF)] * 2
            + [pltpu.SemaphoreType.DMA((2, len(slots)))]
            + [pltpu.VMEM((HEADS, head), F32), pltpu.SemaphoreType.DMA(())] * last,
            ins={at + i: HBM for i in range(len(outs))},
            out_specs={0: HBM, 1: HBM, 2: HBM},
            aliases={at + i: i for i in range(len(outs))},
        )
        outs = list(results[:2])
    grad_key, grad_value, gain_grad = results
    return (
        output[None],
        grad_query[None],
        grad_key[None],
        grad_value[None],
        gain_grad.reshape(features),
    )


def solution(mesh):
    spec = P("dp", "seq", None)
    return jax.shard_map(
        per_device,
        mesh=mesh,
        in_specs=(spec, spec, spec, P(), spec),
        out_specs=(spec, spec, spec, spec, P()),
        check_vma=False,
    )
```

```python
import functools

import jax
import jax.numpy as jnp
from jax import lax
from jax.experimental import pallas as pl
from jax.experimental.pallas import tpu as pltpu
from jax.sharding import PartitionSpec as P

HEADS = 16

EPSILON = 1e-06

F32 = jnp.float32
HALF = jnp.bfloat16


def dot(lhs, rhs, lhs_dim, rhs_dim):
    return lax.dot_general(
        lhs, rhs, (((lhs_dim,), (rhs_dim,)), ((), ())), preferred_element_type=F32
    )


def causal(size):
    rows = lax.broadcasted_iota(jnp.int32, (size, size), 0)
    columns = lax.broadcasted_iota(jnp.int32, (size, size), 1)
    return rows >= columns


def member_of(group):
    return lax.rem(lax.axis_index("seq"), group)


STATE_ORDERS = (((0, 1, 2, 3), (0, 2, 1, 3)), ((0, 1, 2, 3), (0, 2, 1, 3)))
GRAD_ORDERS = (((0, 3, 1, 2), (0, 3, 1, 2)), ((0, 1, 3, 2), (0, 3, 1, 2)))
NORM_ORDERS = (STATE_ORDERS[1], GRAD_ORDERS[0])


def partner_of(order, slot):
    even, odd = order[0][slot], order[1][slot]
    offset = even
    if even != odd:
        offset = jnp.where(lax.rem(lax.axis_index("dp"), 2) == 1, odd, even)
    return member_of(len(order[0])) ^ offset


def block_at(index, size):
    return pl.ds(pl.multiple_of(index * size, size), size)


def gathered(order, piece_refs, size, whole_ref):
    for j, ref in enumerate(piece_refs):
        whole_ref[block_at(partner_of(order, j), size), :] = ref[0:size, :]


def columns(first, count):
    return slice(first, first + count)


def first_state_kernel(head, slot, k_ref, v_ref, piece_ref, k_buffer, v_buffer, arrived):
    width = piece_ref.shape[0]
    source = block_at(partner_of(STATE_ORDERS[0], slot), width)
    copies = [
        pltpu.make_async_copy(k_ref.at[:, source], k_buffer, arrived.at[0]),
        pltpu.make_async_copy(v_ref.at[:, source], v_buffer, arrived.at[1]),
    ]
    for copy in copies:
        copy.start()
    for copy in copies:
        copy.wait()
    for i in range(width // head):
        part = columns(i * head, head)
        piece_ref[part, :] = dot(k_buffer[:, part], v_buffer[:, part], 0, 0).astype(HALF)


def state_kernel(head, slots, k_ref, v_ref, token_ref, *piece_refs):
    del token_ref
    for slot, piece_ref in zip(slots, piece_refs):
        width = piece_ref.shape[0]
        for i in range(width // head):
            part = features_at(STATE_ORDERS[0], slot, i, width, head)
            piece_ref[columns(i * head, head), :] = dot(
                k_ref[:, part], v_ref[:, part], 0, 0
            ).astype(HALF)


def local_kernel(head, q_ref, k_ref, v_ref, scores_ref, intra_ref):
    rows = q_ref.shape[0]
    mask = causal(rows)
    scaling = head ** (-0.5)
    for h in range(HEADS):
        part = columns(h * head, head)
        scores = dot(q_ref[:, part], k_ref[:, part], 1, 1) * scaling
        scores = jnp.where(mask, scores, 0.0).astype(HALF)
        scores_ref[columns(h * rows, rows), :] = scores
        intra_ref[:, part] = dot(scores, v_ref[:, part], 1, 0)


def features_at(order, slot, i, width, head):
    start = partner_of(order, slot) * width + i * head
    return pl.ds(pl.multiple_of(start, head), head)


def attend(head, order, slot, refs, prefix_ref, attended_ref, at, squares, inner):
    q_ref, intra_ref, gain_ref, cot_ref = refs
    scaling = head ** (-0.5)
    width = prefix_ref.shape[0]
    for i in range(width // head):
        part = features_at(order, slot, i, width, head)
        prefix = prefix_ref[columns(i * head, head), :]
        attended = intra_ref[:, part] + scaling * dot(q_ref[:, part], prefix, 1, 0)
        attended_ref[:, part if at is None else columns(i * head, head)] = attended
        scaled = cot_ref[:, part].astype(F32) * gain_ref[:, part]
        squares += attended * attended
        inner += scaled * attended
    return squares, inner


def early_norm_kernel(head, order, *refs):
    prefix_refs, (attended_ref, squares_ref, inner_ref) = refs[4:-3], refs[-3:]
    squares = jnp.zeros(squares_ref.shape, F32)
    inner = jnp.zeros(squares_ref.shape, F32)
    for slot, prefix_ref in enumerate(prefix_refs):
        squares, inner = attend(
            head, order, slot, refs[:4], prefix_ref, attended_ref, None, squares, inner
        )
    squares_ref[...] = squares
    inner_ref[...] = inner


def norm_kernel(head, group, orders, replicas, *refs):
    q_ref, _, gain_ref, cot_ref = refs[:4]
    early_ref, squares_ref, inner_ref, prefix_ref = refs[4:8]
    late_ref, inverse_ref, grad_ref = refs[8:11]
    piece_refs = refs[11 : 11 + group]
    gain_grad_ref, gain_rows_ref = refs[11 + group :]
    features = q_ref.shape[1]
    width = features // group
    last = orders[0][0][group - 1]
    squares, inner = attend(
        head,
        orders[0],
        group - 1,
        refs[:4],
        prefix_ref,
        late_ref,
        0,
        squares_ref[...],
        inner_ref[...],
    )
    inverse = lax.rsqrt(
        jnp.sum(squares, axis=1, keepdims=True) * (1.0 / features) + EPSILON
    )
    inner_mean = jnp.sum(inner, axis=1, keepdims=True) * (1.0 / features) * inverse
    inverse_ref[...] = jnp.broadcast_to(inverse, inverse_ref.shape)
    scaling = head ** (-0.5)
    for slot in range(group):
        for i in range(width // head):
            part = features_at(orders[1], slot, i, width, head)
            local = columns(i * head, head)
            if orders[1][0][slot] == last:
                attended = late_ref[:, local]
            else:
                attended = early_ref[:, part]
            normalized = attended * inverse
            upstream = cot_ref[:, part].astype(F32)
            gain_grad_ref[:, part] = jnp.sum(
                upstream * normalized, axis=0, keepdims=True
            ) * (1.0 / replicas)
            scaled = upstream * gain_ref[:, part]
            grad = ((scaled - normalized * inner_mean) * inverse).astype(HALF)
            grad_ref[:, part] = grad
            piece_refs[slot][local, :] = (
                scaling * dot(q_ref[:, part], grad, 0, 0)
            ).astype(HALF)
    for h in range(HEADS):
        gain_rows_ref[h : h + 1, :] = gain_grad_ref[:, columns(h * head, head)]
    for ref in piece_refs:
        put_wide_rows(ref, width, gain_rows_ref[...])


def backward_kernel(head, group, *refs):
    q_ref, k_ref, v_ref, scores_ref, grad_ref = refs[:5]
    early_ref, late_ref, inverse_ref, gain_ref = refs[5:9]
    prefix_refs = refs[9 : 9 + group]
    out_ref, grad_query_ref, key_part_ref, value_part_ref, token_ref = refs[
        9 + group : 14 + group
    ]
    whole_ref = refs[14 + group]
    rows = q_ref.shape[0]
    mask = causal(rows)
    scaling = head ** (-0.5)
    gathered(STATE_ORDERS[1], prefix_refs, prefix_refs[0].shape[0], whole_ref)
    inverse = inverse_ref[...]
    width = late_ref.shape[1]
    for slot in range(group):
        for i in range(width // head):
            part = features_at(STATE_ORDERS[1], slot, i, width, head)
            if slot == group - 1:
                attended = late_ref[:, columns(i * head, head)]
            else:
                attended = early_ref[:, part]
            out_ref[:, part] = (gain_ref[:, part] * (attended * inverse)).astype(HALF)
    for h in range(HEADS):
        part = columns(h * head, head)
        grad = grad_ref[:, part]
        grad_scores = dot(grad, v_ref[:, part], 1, 1)
        grad_scores = jnp.where(mask, grad_scores, 0.0).astype(HALF)
        grad_query = dot(grad_scores, k_ref[:, part], 1, 0) + dot(
            grad, whole_ref[part, :], 1, 1
        )
        grad_query_ref[:, part] = (scaling * grad_query).astype(HALF)
        key_part_ref[:, part] = scaling * dot(grad_scores, q_ref[:, part], 0, 0)
        value_part_ref[:, part] = dot(
            scores_ref[columns(h * rows, rows), :], grad, 0, 0
        )
    token_ref[...] = jnp.zeros_like(token_ref)


def final_kernel(head, slots, last, *refs):
    k_ref, v_ref, key_part_ref, value_part_ref = refs[:4]
    suffix_refs = refs[4 : 4 + len(slots)]
    refs = refs[4 + len(slots) :]
    copies = []
    if last:
        gain_grad_ref, total_ref, gain_written = refs[-6], refs[-2], refs[-1]
        total_ref[...] = tree_sum([ref[...] for ref in refs[2:-8]])
        copies.append(pltpu.make_async_copy(total_ref, gain_grad_ref, gain_written))
        copies[0].start()
        out_refs, refs = refs[-8:-6], refs[-5:-2]
    else:
        out_refs, refs = refs[:2], refs[2:]
    key_buffer, value_buffer, written = refs
    width = key_buffer.shape[2]
    for n, slot in enumerate(slots):
        for i in range(width // head):
            part = features_at(GRAD_ORDERS[1], slot, i, width, head)
            local = columns(i * head, head)
            suffix = suffix_refs[n][local, :]
            key_buffer[n, :, local] = (
                key_part_ref[:, part] + dot(v_ref[:, part], suffix, 1, 1)
            ).astype(HALF)
            value_buffer[n, :, local] = (
                value_part_ref[:, part] + dot(k_ref[:, part], suffix, 1, 0)
            ).astype(HALF)
        for i, buffer in enumerate((key_buffer, value_buffer)):
            copy = pltpu.make_async_copy(
                buffer.at[n],
                out_refs[i].at[:, block_at(partner_of(GRAD_ORDERS[1], slot), width)],
                written.at[i, n],
            )
            copy.start()
            copies.append(copy)
    for copy in copies:
        copy.wait()


def tree_sum(terms):
    while len(terms) > 1:
        terms = [a + b for a, b in zip(terms[::2], terms[1::2])]
    return terms[0]


def wide_rows(ref, start):
    rows = (ref.shape[0] - start) // 2
    high = ref[columns(start, rows), :].astype(F32)
    return high + ref[columns(start + rows, rows), :].astype(F32)


def put_wide_rows(ref, start, value):
    rows = value.shape[0]
    high = value.astype(HALF)
    ref[columns(start, rows), :] = high
    ref[columns(start + rows, rows), :] = (value - high.astype(F32)).astype(HALF)


def total_kernel(size, *refs):
    out_ref = refs[-1]
    total = refs[0][0:size, :].astype(F32)
    for ref in refs[1:-1]:
        total += ref[0:size, :].astype(F32)
    out_ref[0:size, :] = total.astype(HALF)
    if out_ref.shape[0] > size:
        put_wide_rows(out_ref, size, tree_sum([wide_rows(ref, size) for ref in refs[:-1]]))


def group_flag(group, reverse, distance):
    index = lax.axis_index("seq") // group
    last = lax.axis_size("seq") // group - 1
    known = index + distance <= last if reverse else index >= distance
    return jnp.where(known, 1.0, 0.0)


def carry_kernel(group, reverse, distance, first, own_ref, moved_ref, out_ref):
    own = own_ref[...].astype(F32)
    if first:
        own = own * group_flag(group, reverse, 1)
    moved = moved_ref[...].astype(F32) * group_flag(group, reverse, distance)
    out_ref[...] = (own + moved).astype(HALF)


def scan_kernel(group, orders, reverse, masked, size, riding, *refs):
    sources = [partner_of(orders[0], j) for j in range(group)]
    targets = [partner_of(orders[1], j) for j in range(group)]
    carry = refs[0][0:size, :].astype(F32)
    if masked:
        carry = carry * group_flag(group, reverse, 1)
    blocks = [ref[0:size, :].astype(F32) for ref in refs[1 : 1 + group]]
    out_refs = refs[-group - riding :][:group]
    for j in range(group):
        total = carry
        for i in range(group):
            earlier = sources[i] < targets[j]
            later = sources[i] > targets[j]
            total += jnp.where(later if reverse else earlier, 1.0, 0.0) * blocks[i]
        out_refs[j][...] = total.astype(HALF)
    if riding:
        refs[-1][...] = wide_rows(refs[0], size) + wide_rows(refs[1 + group], size)


VMEM = pl.BlockSpec(memory_space=pltpu.VMEM)
ANY = pl.BlockSpec(memory_space=pl.ANY)
HBM = pl.BlockSpec(memory_space=pltpu.HBM)


def call(kernel, outs, args, matmuls, scratch=(), ins=None, out_specs=None, aliases=None):
    size = sum(a.size * a.dtype.itemsize for a in args)
    size += sum(o.size * o.dtype.itemsize for o in outs)
    ins = ins or {}
    out_specs = out_specs or {}
    return pl.pallas_call(
        kernel,
        out_shape=tuple(outs),
        in_specs=[ins.get(i, VMEM) for i in range(len(args))],
        out_specs=tuple(out_specs.get(i, VMEM) for i in range(len(outs))),
        scratch_shapes=list(scratch),
        input_output_aliases=aliases or {},
        compiler_params=pltpu.CompilerParams(vmem_limit_bytes=16 * 1024 * 1024),
        cost_estimate=pl.CostEstimate(
            flops=2 * 128 * 128 * 128 * HEADS * matmuls,
            bytes_accessed=size,
            transcendentals=0,
        ),
    )(*args)


def swap(array, axis, offset):
    count = lax.axis_size(axis)
    return lax.ppermute(array, axis, [(i, i ^ offset) for i in range(count)])


def own_and_swapped(pieces, order):
    count = lax.axis_size("seq")
    results = [pieces[0]]
    for slot in range(1, len(pieces)):
        pairs = []
        for row in range(lax.axis_size("dp")):
            offset = order[row % 2][slot]
            pairs += [(row * count + i, row * count + (i ^ offset)) for i in range(count)]
        results.append(lax.ppermute(pieces[slot], ("dp", "seq"), pairs))
    return results


def exclusive_scan(pieces, orders, size, reverse, token):
    group = len(pieces)
    count = lax.axis_size("seq")
    groups = count // group
    part = functools.partial
    lanes = pieces[0].shape[1]
    extra = pieces[0].shape[0] - size
    piece = jax.ShapeDtypeStruct((size, lanes), HALF)
    gain_shape = jax.ShapeDtypeStruct((extra // 2, lanes), F32)

    def shifted(array, distance):
        step = -distance if reverse else distance
        pairs = [(i, (i + step) % count) for i in range(count)]
        return lax.ppermute(array, "seq", pairs)

    received = own_and_swapped(pieces, orders[0])
    (total,) = call(
        part(total_kernel, size),
        [jax.ShapeDtypeStruct(pieces[0].shape, HALF)],
        received,
        0,
    )
    riding = int(extra > 0 and groups == 2)
    gain = None
    if extra and not riding:
        gain = total[size : size + extra // 2].astype(F32) + total[size + extra // 2 :]
        gain = tree_sum(summed_over("seq", group, gain))
        total = total[:size]
    carry = shifted(total, group)
    distance = 1
    while distance < groups - 1:
        moved = shifted(carry, distance * group)
        kernel = part(
            carry_kernel, group, reverse, distance + (distance == 1), distance == 1
        )
        (carry,) = call(kernel, [piece], [carry, moved], 0)
        distance *= 2
    inputs = [carry] + received + ([total] if riding else []) + [token]
    sums = call(
        part(scan_kernel, group, orders, reverse, groups <= 2, size, riding),
        [piece] * group + [gain_shape] * riding,
        inputs,
        0,
        ins={len(inputs) - 1: ANY},
    )
    results = own_and_swapped(sums[:group], orders[1])
    return results, (sums[-1] if riding else gain)


def summed_over(axis, stride, array):
    count = lax.axis_size(axis)
    terms = [array]
    while stride < count:
        array = tree_sum(terms)
        width = 4 if count // stride % 4 == 0 else 2
        order = sorted(range(1, width), key=lambda i: i % 2)
        moved = {i: swap(array, axis, i * stride) for i in order}
        terms = [array] + [moved[i] for i in range(1, width)]
        stride *= width
    return terms


def per_device(queries, keys, values, gain, cotangent):
    q, k, v, cot = queries[0], keys[0], values[0], cotangent[0]
    rows, features = q.shape
    head = features // HEADS
    group = 4
    width = features // group
    part = functools.partial
    wide = jax.ShapeDtypeStruct((rows, features), F32)
    half = jax.ShapeDtypeStruct((rows, features), HALF)
    square = jax.ShapeDtypeStruct((rows, head), F32)
    piece = jax.ShapeDtypeStruct((width, head), HALF)
    scores_shape = jax.ShapeDtypeStruct((HEADS * rows, rows), HALF)
    gain_shape = jax.ShapeDtypeStruct((HEADS, head), F32)
    token_shape = jax.ShapeDtypeStruct((8, head), F32)
    whole = pltpu.VMEM((features, head), HALF)
    gain_row = gain.reshape(1, features)

    (first,) = call(
        part(first_state_kernel, head, 1),
        [piece],
        [pltpu.with_memory_space_constraint(a, pltpu.HBM) for a in (k, v)],
        1,
        [pltpu.VMEM((rows, width), HALF)] * 2 + [pltpu.SemaphoreType.DMA((2,))],
        ins={0: HBM, 1: HBM},
    )
    slots = (2, 3, 0)
    rest = call(
        part(state_kernel, head, slots), [piece] * 3, [k, v, first], 1, ins={2: ANY}
    )
    pieces = dict(zip(slots, rest))
    pieces[1] = first
    pieces = [pieces[slot] for slot in range(group)]
    scores, intra = call(part(local_kernel, head), [scores_shape, wide], [q, k, v], 2)
    prefix, _ = exclusive_scan(pieces, STATE_ORDERS, width, False, intra)
    message = jax.ShapeDtypeStruct((width + 2 * HEADS, head), HALF)
    sources = [q, intra, gain_row, cot]
    early, squares, inner = call(
        part(early_norm_kernel, head, STATE_ORDERS[1]),
        [wide, square, square],
        sources + prefix[:-1],
        1,
    )
    late, inverse, grad, *pieces = call(
        part(norm_kernel, head, group, NORM_ORDERS, lax.axis_size("dp")),
        [jax.ShapeDtypeStruct((rows, width), F32), square, half] + [message] * group,
        sources + [early, squares, inner, prefix[-1]],
        2,
        [pltpu.VMEM((1, features), F32), pltpu.VMEM((HEADS, head), F32)],
    )
    output, grad_query, key_part, value_part, token = call(
        part(backward_kernel, head, group),
        [half, half, wide, wide, token_shape],
        [q, k, v, scores, grad, early, late, inverse, gain_row] + prefix,
        5,
        [whole],
    )
    suffix, gain_grad = exclusive_scan(pieces, GRAD_ORDERS, width, True, token)
    gains = summed_over("dp", 1, gain_grad)
    inputs = [k, v, key_part, value_part]
    outs = []
    for slots in ((0, 1, 2), (3,)):
        last = group - 1 in slots
        at = len(inputs) + len(slots)
        results = call(
            part(final_kernel, head, slots, last),
            [half, half] + [gain_shape] * last,
            inputs + [suffix[slot] for slot in slots] + outs + (gains if last else []),
            1,
            [pltpu.VMEM((len(slots), rows, width), HALF)] * 2
            + [pltpu.SemaphoreType.DMA((2, len(slots)))]
            + [pltpu.VMEM((HEADS, head), F32), pltpu.SemaphoreType.DMA(())] * last,
            ins={at + i: HBM for i in range(len(outs))},
            out_specs={0: HBM, 1: HBM, 2: HBM},
            aliases={at + i: i for i in range(len(outs))},
        )
        outs = list(results[:2])
    grad_key, grad_value, gain_grad = results
    return (
        output[None],
        grad_query[None],
        grad_key[None],
        grad_value[None],
        gain_grad.reshape(features),
    )


def solution(mesh):
    spec = P("dp", "seq", None)
    return jax.shard_map(
        per_device,
        mesh=mesh,
        in_specs=(spec, spec, spec, P(), spec),
        out_specs=(spec, spec, spec, spec, P()),
        check_vma=False,
    )
```

```python
import functools

import jax
import jax.numpy as jnp
from jax import lax
from jax.experimental import pallas as pl
from jax.experimental.pallas import tpu as pltpu
from jax.sharding import PartitionSpec as P

HEADS = 16

EPSILON = 1e-06

F32 = jnp.float32
HALF = jnp.bfloat16


def dot(lhs, rhs, lhs_dim, rhs_dim):
    return lax.dot_general(
        lhs, rhs, (((lhs_dim,), (rhs_dim,)), ((), ())), preferred_element_type=F32
    )


def causal(size):
    rows = lax.broadcasted_iota(jnp.int32, (size, size), 0)
    columns = lax.broadcasted_iota(jnp.int32, (size, size), 1)
    return rows >= columns


def member_of(group):
    return lax.rem(lax.axis_index("seq"), group)


STATE_ORDERS = (((0, 1, 2, 3), (0, 2, 1, 3)), ((0, 2, 1, 3), (0, 1, 2, 3)))
GRAD_ORDERS = (((0, 3, 1, 2), (0, 3, 1, 2)), ((0, 1, 2, 3), (0, 2, 1, 3)))
NORM_ORDERS = (STATE_ORDERS[1], GRAD_ORDERS[0])


def partner_of(order, slot):
    even, odd = order[0][slot], order[1][slot]
    offset = even
    if even != odd:
        offset = jnp.where(lax.rem(lax.axis_index("dp"), 2) == 1, odd, even)
    return member_of(len(order[0])) ^ offset


def block_at(index, size):
    return pl.ds(pl.multiple_of(index * size, size), size)


def gathered(order, piece_refs, size, whole_ref):
    for j, ref in enumerate(piece_refs):
        whole_ref[block_at(partner_of(order, j), size), :] = ref[0:size, :]


def columns(first, count):
    return slice(first, first + count)


def first_state_kernel(head, slot, k_ref, v_ref, piece_ref, k_buffer, v_buffer, arrived):
    width = piece_ref.shape[0]
    source = block_at(partner_of(STATE_ORDERS[0], slot), width)
    copies = [
        pltpu.make_async_copy(k_ref.at[:, source], k_buffer, arrived.at[0]),
        pltpu.make_async_copy(v_ref.at[:, source], v_buffer, arrived.at[1]),
    ]
    for copy in copies:
        copy.start()
    for copy in copies:
        copy.wait()
    for i in range(width // head):
        part = columns(i * head, head)
        piece_ref[part, :] = dot(k_buffer[:, part], v_buffer[:, part], 0, 0).astype(HALF)


def state_kernel(head, slots, k_ref, v_ref, token_ref, *piece_refs):
    del token_ref
    for slot, piece_ref in zip(slots, piece_refs):
        width = piece_ref.shape[0]
        for i in range(width // head):
            part = features_at(STATE_ORDERS[0], slot, i, width, head)
            piece_ref[columns(i * head, head), :] = dot(
                k_ref[:, part], v_ref[:, part], 0, 0
            ).astype(HALF)


def local_kernel(head, q_ref, k_ref, v_ref, scores_ref, intra_ref):
    rows = q_ref.shape[0]
    mask = causal(rows)
    scaling = head ** (-0.5)
    for h in range(HEADS):
        part = columns(h * head, head)
        scores = dot(q_ref[:, part], k_ref[:, part], 1, 1) * scaling
        scores = jnp.where(mask, scores, 0.0).astype(HALF)
        scores_ref[columns(h * rows, rows), :] = scores
        intra_ref[:, part] = dot(scores, v_ref[:, part], 1, 0)


def features_at(order, slot, i, width, head):
    start = partner_of(order, slot) * width + i * head
    return pl.ds(pl.multiple_of(start, head), head)


def attend(head, order, slot, refs, prefix_ref, attended_ref, at, squares, inner):
    q_ref, intra_ref, gain_ref, cot_ref = refs
    scaling = head ** (-0.5)
    width = prefix_ref.shape[0]
    for i in range(width // head):
        part = features_at(order, slot, i, width, head)
        prefix = prefix_ref[columns(i * head, head), :]
        attended = intra_ref[:, part] + scaling * dot(q_ref[:, part], prefix, 1, 0)
        attended_ref[:, part if at is None else columns(i * head, head)] = attended
        scaled = cot_ref[:, part].astype(F32) * gain_ref[:, part]
        squares += attended * attended
        inner += scaled * attended
    return squares, inner


def early_norm_kernel(head, order, *refs):
    prefix_refs, (attended_ref, squares_ref, inner_ref) = refs[4:-3], refs[-3:]
    squares = jnp.zeros(squares_ref.shape, F32)
    inner = jnp.zeros(squares_ref.shape, F32)
    for slot, prefix_ref in enumerate(prefix_refs):
        squares, inner = attend(
            head, order, slot, refs[:4], prefix_ref, attended_ref, None, squares, inner
        )
    squares_ref[...] = squares
    inner_ref[...] = inner


def norm_kernel(head, group, orders, replicas, *refs):
    q_ref, _, gain_ref, cot_ref = refs[:4]
    early_ref, squares_ref, inner_ref, prefix_ref = refs[4:8]
    late_ref, inverse_ref, grad_ref = refs[8:11]
    piece_refs = refs[11 : 11 + group]
    gain_grad_ref, gain_rows_ref = refs[11 + group :]
    features = q_ref.shape[1]
    width = features // group
    last = orders[0][0][group - 1]
    odd = lax.rem(lax.axis_index("dp"), 2) == 1
    squares, inner = attend(
        head,
        orders[0],
        group - 1,
        refs[:4],
        prefix_ref,
        late_ref,
        0,
        squares_ref[...],
        inner_ref[...],
    )
    inverse = lax.rsqrt(
        jnp.sum(squares, axis=1, keepdims=True) * (1.0 / features) + EPSILON
    )
    inner_mean = jnp.sum(inner, axis=1, keepdims=True) * (1.0 / features) * inverse
    inverse_ref[...] = jnp.broadcast_to(inverse, inverse_ref.shape)
    scaling = head ** (-0.5)
    for slot in range(group):
        for i in range(width // head):
            part = features_at(orders[1], slot, i, width, head)
            local = columns(i * head, head)
            late = [order[slot] == last for order in orders[1]]
            attended = late_ref[:, local] if late[0] else early_ref[:, part]
            if late[0] != late[1]:
                other = late_ref[:, local] if late[1] else early_ref[:, part]
                attended = jnp.where(odd, other, attended)
            normalized = attended * inverse
            upstream = cot_ref[:, part].astype(F32)
            gain_grad_ref[:, part] = jnp.sum(
                upstream * normalized, axis=0, keepdims=True
            ) * (1.0 / replicas)
            scaled = upstream * gain_ref[:, part]
            grad = ((scaled - normalized * inner_mean) * inverse).astype(HALF)
            grad_ref[:, part] = grad
            piece_refs[slot][local, :] = (
                scaling * dot(q_ref[:, part], grad, 0, 0)
            ).astype(HALF)
    for h in range(HEADS):
        gain_rows_ref[h : h + 1, :] = gain_grad_ref[:, columns(h * head, head)]
    for ref in piece_refs:
        put_wide_rows(ref, width, gain_rows_ref[...])


def backward_kernel(head, group, *refs):
    q_ref, k_ref, v_ref, scores_ref, grad_ref = refs[:5]
    early_ref, late_ref, inverse_ref, gain_ref = refs[5:9]
    prefix_refs = refs[9 : 9 + group]
    out_ref, grad_query_ref, key_part_ref, value_part_ref, token_ref = refs[
        9 + group : 14 + group
    ]
    whole_ref = refs[14 + group]
    rows = q_ref.shape[0]
    mask = causal(rows)
    scaling = head ** (-0.5)
    gathered(STATE_ORDERS[1], prefix_refs, prefix_refs[0].shape[0], whole_ref)
    inverse = inverse_ref[...]
    width = late_ref.shape[1]
    for slot in range(group):
        for i in range(width // head):
            part = features_at(STATE_ORDERS[1], slot, i, width, head)
            if slot == group - 1:
                attended = late_ref[:, columns(i * head, head)]
            else:
                attended = early_ref[:, part]
            out_ref[:, part] = (gain_ref[:, part] * (attended * inverse)).astype(HALF)
    for h in range(HEADS):
        part = columns(h * head, head)
        grad = grad_ref[:, part]
        grad_scores = dot(grad, v_ref[:, part], 1, 1)
        grad_scores = jnp.where(mask, grad_scores, 0.0).astype(HALF)
        grad_query = dot(grad_scores, k_ref[:, part], 1, 0) + dot(
            grad, whole_ref[part, :], 1, 1
        )
        grad_query_ref[:, part] = (scaling * grad_query).astype(HALF)
        key_part_ref[:, part] = scaling * dot(grad_scores, q_ref[:, part], 0, 0)
        value_part_ref[:, part] = dot(
            scores_ref[columns(h * rows, rows), :], grad, 0, 0
        )
    token_ref[...] = jnp.zeros_like(token_ref)


def final_kernel(head, slots, last, *refs):
    k_ref, v_ref, key_part_ref, value_part_ref = refs[:4]
    suffix_refs = refs[4 : 4 + len(slots)]
    refs = refs[4 + len(slots) :]
    copies = []
    if last:
        gain_grad_ref, total_ref, gain_written = refs[-6], refs[-2], refs[-1]
        total_ref[...] = tree_sum([ref[...] for ref in refs[2:-8]])
        copies.append(pltpu.make_async_copy(total_ref, gain_grad_ref, gain_written))
        copies[0].start()
        out_refs, refs = refs[-8:-6], refs[-5:-2]
    else:
        out_refs, refs = refs[:2], refs[2:]
    key_buffer, value_buffer, written = refs
    width = key_buffer.shape[2]
    for n, slot in enumerate(slots):
        for i in range(width // head):
            part = features_at(GRAD_ORDERS[1], slot, i, width, head)
            local = columns(i * head, head)
            suffix = suffix_refs[n][local, :]
            key_buffer[n, :, local] = (
                key_part_ref[:, part] + dot(v_ref[:, part], suffix, 1, 1)
            ).astype(HALF)
            value_buffer[n, :, local] = (
                value_part_ref[:, part] + dot(k_ref[:, part], suffix, 1, 0)
            ).astype(HALF)
        for i, buffer in enumerate((key_buffer, value_buffer)):
            copy = pltpu.make_async_copy(
                buffer.at[n],
                out_refs[i].at[:, block_at(partner_of(GRAD_ORDERS[1], slot), width)],
                written.at[i, n],
            )
            copy.start()
            copies.append(copy)
    for copy in copies:
        copy.wait()


def tree_sum(terms):
    while len(terms) > 1:
        terms = [a + b for a, b in zip(terms[::2], terms[1::2])]
    return terms[0]


def wide_rows(ref, start):
    rows = (ref.shape[0] - start) // 2
    high = ref[columns(start, rows), :].astype(F32)
    return high + ref[columns(start + rows, rows), :].astype(F32)


def put_wide_rows(ref, start, value):
    rows = value.shape[0]
    high = value.astype(HALF)
    ref[columns(start, rows), :] = high
    ref[columns(start + rows, rows), :] = (value - high.astype(F32)).astype(HALF)


def total_kernel(size, count, *refs):
    refs, out_refs = refs[:count], refs[count + 1 :]
    total = refs[0][0:size, :].astype(F32)
    for ref in refs[1:]:
        total += ref[0:size, :].astype(F32)
    out_refs[0][0:size, :] = total.astype(HALF)
    if len(out_refs) > 1:
        gain = tree_sum([wide_rows(ref, size) for ref in refs])
        put_wide_rows(out_refs[0], size, gain)
        out_refs[1][...] = wide_rows(out_refs[0], size)


def group_flag(group, reverse, distance):
    index = lax.axis_index("seq") // group
    last = lax.axis_size("seq") // group - 1
    known = index + distance <= last if reverse else index >= distance
    return jnp.where(known, 1.0, 0.0)


def carry_kernel(group, reverse, distance, first, own_ref, moved_ref, out_ref):
    own = own_ref[...].astype(F32)
    if first:
        own = own * group_flag(group, reverse, 1)
    moved = moved_ref[...].astype(F32) * group_flag(group, reverse, distance)
    out_ref[...] = (own + moved).astype(HALF)


def scan_kernel(group, orders, slots, reverse, masked, size, riding, *refs):
    sources = [partner_of(orders[0], j) for j in range(group)]
    carry = refs[0][0:size, :].astype(F32)
    if masked:
        carry = carry * group_flag(group, reverse, 1)
    blocks = [ref[0:size, :].astype(F32) for ref in refs[1 : 1 + group]]
    out_refs = refs[-len(slots) - riding :][: len(slots)]
    for slot, out_ref in zip(slots, out_refs):
        target = partner_of(orders[1], slot)
        total = carry
        for i in range(group):
            known = sources[i] > target if reverse else sources[i] < target
            total += jnp.where(known, 1.0, 0.0) * blocks[i]
        out_ref[...] = total.astype(HALF)
    if riding:
        refs[-1][...] = refs[1 + group][...] + wide_rows(refs[0], size)


VMEM = pl.BlockSpec(memory_space=pltpu.VMEM)
ANY = pl.BlockSpec(memory_space=pl.ANY)
HBM = pl.BlockSpec(memory_space=pltpu.HBM)


def call(kernel, outs, args, matmuls, scratch=(), ins=None, out_specs=None, aliases=None):
    size = sum(a.size * a.dtype.itemsize for a in args)
    size += sum(o.size * o.dtype.itemsize for o in outs)
    ins = ins or {}
    out_specs = out_specs or {}
    return pl.pallas_call(
        kernel,
        out_shape=tuple(outs),
        in_specs=[ins.get(i, VMEM) for i in range(len(args))],
        out_specs=tuple(out_specs.get(i, VMEM) for i in range(len(outs))),
        scratch_shapes=list(scratch),
        input_output_aliases=aliases or {},
        compiler_params=pltpu.CompilerParams(vmem_limit_bytes=16 * 1024 * 1024),
        cost_estimate=pl.CostEstimate(
            flops=2 * 128 * 128 * 128 * HEADS * matmuls,
            bytes_accessed=size,
            transcendentals=0,
        ),
    )(*args)


def swap(array, axis, offset):
    count = lax.axis_size(axis)
    return lax.ppermute(array, axis, [(i, i ^ offset) for i in range(count)])


def own_and_swapped(pieces, order):
    count = lax.axis_size("seq")
    results = [pieces[0]]
    for slot in range(1, len(pieces)):
        pairs = []
        for row in range(lax.axis_size("dp")):
            offset = order[row % 2][slot]
            pairs += [(row * count + i, row * count + (i ^ offset)) for i in range(count)]
        results.append(lax.ppermute(pieces[slot], ("dp", "seq"), pairs))
    return results


def exclusive_scan(pieces, orders, size, reverse, token):
    group = len(pieces)
    count, rows = lax.axis_size("seq"), lax.axis_size("dp")
    groups = count // group
    part = functools.partial
    lanes = pieces[0].shape[1]
    extra = pieces[0].shape[0] - size
    piece = jax.ShapeDtypeStruct((size, lanes), HALF)
    gain_shape = jax.ShapeDtypeStruct((extra // 2, lanes), F32)

    def shifted(array, distance):
        step = -distance if reverse else distance
        pairs = [(i, (i + step) % count) for i in range(count)]
        return lax.ppermute(array, "seq", pairs)

    received = own_and_swapped(pieces, orders[0])
    totals = call(
        part(total_kernel, size, group),
        [jax.ShapeDtypeStruct(pieces[0].shape, HALF)] + [gain_shape] * (extra > 0),
        received + [token],
        0,
        ins={group: ANY},
    )
    total, gains = totals[0], list(totals[1:])
    riding = int(extra > 0 and groups == 2 and rows == 4)
    carry = shifted(total if riding else total[:size], group)
    if riding:
        for offset in (0, group):
            pairs = [
                (row * count + i, (row ^ 2) * count + (i ^ offset))
                for row in range(rows)
                for i in range(count)
            ]
            gains.append(lax.ppermute(gains[0], ("dp", "seq"), pairs))
    elif extra:
        gains = [tree_sum(summed_over("seq", group, gains[0]))]
        gains = [tree_sum(summed_over("dp", 2, gains[0]))]
    distance = 1
    while distance < groups - 1:
        moved = shifted(carry, distance * group)
        kernel = part(
            carry_kernel, group, reverse, distance + (distance == 1), distance == 1
        )
        (carry,) = call(kernel, [piece], [carry, moved], 0)
        distance *= 2
    pieces, after = {}, []
    for slots in ((1,), (2,), (3, 0)):
        adding = riding if 0 in slots else 0
        inputs = [carry] + received + gains[:adding] + after
        sums = call(
            part(scan_kernel, group, orders, slots, reverse, groups <= 2, size, adding),
            [piece] * len(slots) + [gain_shape] * adding,
            inputs,
            0,
            ins={len(inputs) - 1: ANY} if after else {},
        )
        pieces.update(zip(slots, sums))
        after = [sums[0]]
    results = own_and_swapped([pieces[slot] for slot in range(group)], orders[1])
    if riding:
        gains = [sums[-1] + (gains[1] + gains[2])]
    return results, (gains[0] if gains else None)


def summed_over(axis, stride, array):
    count = lax.axis_size(axis)
    terms = [array]
    while stride < count:
        array = tree_sum(terms)
        width = 4 if count // stride % 4 == 0 else 2
        order = sorted(range(1, width), key=lambda i: i % 2)
        moved = {i: swap(array, axis, i * stride) for i in order}
        terms = [array] + [moved[i] for i in range(1, width)]
        stride *= width
    return terms


def per_device(queries, keys, values, gain, cotangent):
    q, k, v, cot = queries[0], keys[0], values[0], cotangent[0]
    rows, features = q.shape
    head = features // HEADS
    group = 4
    width = features // group
    part = functools.partial
    wide = jax.ShapeDtypeStruct((rows, features), F32)
    half = jax.ShapeDtypeStruct((rows, features), HALF)
    square = jax.ShapeDtypeStruct((rows, head), F32)
    piece = jax.ShapeDtypeStruct((width, head), HALF)
    scores_shape = jax.ShapeDtypeStruct((HEADS * rows, rows), HALF)
    gain_shape = jax.ShapeDtypeStruct((HEADS, head), F32)
    token_shape = jax.ShapeDtypeStruct((8, head), F32)
    whole = pltpu.VMEM((features, head), HALF)
    gain_row = gain.reshape(1, features)

    (first,) = call(
        part(first_state_kernel, head, 1),
        [piece],
        [pltpu.with_memory_space_constraint(a, pltpu.HBM) for a in (k, v)],
        1,
        [pltpu.VMEM((rows, width), HALF)] * 2 + [pltpu.SemaphoreType.DMA((2,))],
        ins={0: HBM, 1: HBM},
    )
    slots = (2, 3, 0)
    rest = call(
        part(state_kernel, head, slots), [piece] * 3, [k, v, first], 1, ins={2: ANY}
    )
    pieces = dict(zip(slots, rest))
    pieces[1] = first
    pieces = [pieces[slot] for slot in range(group)]
    scores, intra = call(part(local_kernel, head), [scores_shape, wide], [q, k, v], 2)
    prefix, _ = exclusive_scan(pieces, STATE_ORDERS, width, False, intra)
    message = jax.ShapeDtypeStruct((width + 2 * HEADS, head), HALF)
    sources = [q, intra, gain_row, cot]
    early, squares, inner = call(
        part(early_norm_kernel, head, STATE_ORDERS[1]),
        [wide, square, square],
        sources + prefix[:-1],
        1,
    )
    late, inverse, grad, *pieces = call(
        part(norm_kernel, head, group, NORM_ORDERS, lax.axis_size("dp")),
        [jax.ShapeDtypeStruct((rows, width), F32), square, half] + [message] * group,
        sources + [early, squares, inner, prefix[-1]],
        2,
        [pltpu.VMEM((1, features), F32), pltpu.VMEM((HEADS, head), F32)],
    )
    output, grad_query, key_part, value_part, token = call(
        part(backward_kernel, head, group),
        [half, half, wide, wide, token_shape],
        [q, k, v, scores, grad, early, late, inverse, gain_row] + prefix,
        5,
        [whole],
    )
    suffix, gain_grad = exclusive_scan(pieces, GRAD_ORDERS, width, True, token)
    gains = [gain_grad, swap(gain_grad, "dp", 1)]
    inputs = [k, v, key_part, value_part]
    outs = []
    for slots in ((0, 1, 2), (3,)):
        last = group - 1 in slots
        at = len(inputs) + len(slots)
        results = call(
            part(final_kernel, head, slots, last),
            [half, half] + [gain_shape] * last,
            inputs + [suffix[slot] for slot in slots] + outs + (gains if last else []),
            1,
            [pltpu.VMEM((len(slots), rows, width), HALF)] * 2
            + [pltpu.SemaphoreType.DMA((2, len(slots)))]
            + [pltpu.VMEM((HEADS, head), F32), pltpu.SemaphoreType.DMA(())] * last,
            ins={at + i: HBM for i in range(len(outs))},
            out_specs={0: HBM, 1: HBM, 2: HBM},
            aliases={at + i: i for i in range(len(outs))},
        )
        outs = list(results[:2])
    grad_key, grad_value, gain_grad = results
    return (
        output[None],
        grad_query[None],
        grad_key[None],
        grad_value[None],
        gain_grad.reshape(features),
    )


def solution(mesh):
    spec = P("dp", "seq", None)
    return jax.shard_map(
        per_device,
        mesh=mesh,
        in_specs=(spec, spec, spec, P(), spec),
        out_specs=(spec, spec, spec, spec, P()),
        check_vma=False,
    )
```

```python
import functools

import jax
import jax.numpy as jnp
from jax import lax
from jax.experimental import pallas as pl
from jax.experimental.pallas import tpu as pltpu
from jax.sharding import PartitionSpec as P

HEADS = 16

EPSILON = 1e-06

F32 = jnp.float32
HALF = jnp.bfloat16


def dot(lhs, rhs, lhs_dim, rhs_dim):
    return lax.dot_general(
        lhs, rhs, (((lhs_dim,), (rhs_dim,)), ((), ())), preferred_element_type=F32
    )


def causal(size):
    rows = lax.broadcasted_iota(jnp.int32, (size, size), 0)
    columns = lax.broadcasted_iota(jnp.int32, (size, size), 1)
    return rows >= columns


def member_of(group):
    return lax.rem(lax.axis_index("seq"), group)


STATE_ORDERS = (((0, 1, 2, 3), (0, 2, 1, 3)), ((0, 2, 1, 3), (0, 1, 2, 3)))
GRAD_ORDERS = (((0, 3, 1, 2), (0, 3, 1, 2)), ((0, 3, 1, 2), (0, 1, 2, 3)))
NORM_ORDERS = (STATE_ORDERS[1], GRAD_ORDERS[0])


def partner_of(order, slot):
    even, odd = order[0][slot], order[1][slot]
    offset = even
    if even != odd:
        offset = jnp.where(lax.rem(lax.axis_index("dp"), 2) == 1, odd, even)
    return member_of(len(order[0])) ^ offset


def block_at(index, size):
    return pl.ds(pl.multiple_of(index * size, size), size)


def gathered(order, piece_refs, size, whole_ref):
    for j, ref in enumerate(piece_refs):
        whole_ref[block_at(partner_of(order, j), size), :] = ref[0:size, :]


def columns(first, count):
    return slice(first, first + count)


def first_state_kernel(head, slot, k_ref, v_ref, piece_ref, k_buffer, v_buffer, arrived):
    width = piece_ref.shape[0]
    source = block_at(partner_of(STATE_ORDERS[0], slot), width)
    copies = [
        pltpu.make_async_copy(k_ref.at[:, source], k_buffer, arrived.at[0]),
        pltpu.make_async_copy(v_ref.at[:, source], v_buffer, arrived.at[1]),
    ]
    for copy in copies:
        copy.start()
    for copy in copies:
        copy.wait()
    for i in range(width // head):
        part = columns(i * head, head)
        piece_ref[part, :] = dot(k_buffer[:, part], v_buffer[:, part], 0, 0).astype(HALF)


def state_kernel(head, slots, k_ref, v_ref, token_ref, *piece_refs):
    del token_ref
    for slot, piece_ref in zip(slots, piece_refs):
        width = piece_ref.shape[0]
        for i in range(width // head):
            part = features_at(STATE_ORDERS[0], slot, i, width, head)
            piece_ref[columns(i * head, head), :] = dot(
                k_ref[:, part], v_ref[:, part], 0, 0
            ).astype(HALF)


def local_kernel(head, q_ref, k_ref, v_ref, scores_ref, intra_ref):
    rows = q_ref.shape[0]
    mask = causal(rows)
    scaling = head ** (-0.5)
    for h in range(HEADS):
        part = columns(h * head, head)
        scores = dot(q_ref[:, part], k_ref[:, part], 1, 1) * scaling
        scores = jnp.where(mask, scores, 0.0).astype(HALF)
        scores_ref[columns(h * rows, rows), :] = scores
        intra_ref[:, part] = dot(scores, v_ref[:, part], 1, 0)


def features_at(order, slot, i, width, head):
    start = partner_of(order, slot) * width + i * head
    return pl.ds(pl.multiple_of(start, head), head)


def attend(head, order, slot, refs, prefix_ref, attended_ref, at, squares, inner):
    q_ref, intra_ref, gain_ref, cot_ref = refs
    scaling = head ** (-0.5)
    width = prefix_ref.shape[0]
    for i in range(width // head):
        part = features_at(order, slot, i, width, head)
        prefix = prefix_ref[columns(i * head, head), :]
        attended = intra_ref[:, part] + scaling * dot(q_ref[:, part], prefix, 1, 0)
        attended_ref[:, part if at is None else columns(i * head, head)] = attended
        scaled = cot_ref[:, part].astype(F32) * gain_ref[:, part]
        squares += attended * attended
        inner += scaled * attended
    return squares, inner


def early_norm_kernel(head, order, *refs):
    prefix_refs, (attended_ref, squares_ref, inner_ref) = refs[4:-3], refs[-3:]
    squares = jnp.zeros(squares_ref.shape, F32)
    inner = jnp.zeros(squares_ref.shape, F32)
    for slot, prefix_ref in enumerate(prefix_refs):
        squares, inner = attend(
            head, order, slot, refs[:4], prefix_ref, attended_ref, None, squares, inner
        )
    squares_ref[...] = squares
    inner_ref[...] = inner


def norm_kernel(head, group, orders, replicas, *refs):
    q_ref, _, gain_ref, cot_ref = refs[:4]
    early_ref, squares_ref, inner_ref, prefix_ref = refs[4:8]
    late_ref, inverse_ref, grad_ref = refs[8:11]
    piece_refs = refs[11 : 11 + group]
    gain_grad_ref, gain_rows_ref = refs[11 + group :]
    features = q_ref.shape[1]
    width = features // group
    last = orders[0][0][group - 1]
    odd = lax.rem(lax.axis_index("dp"), 2) == 1
    squares, inner = attend(
        head,
        orders[0],
        group - 1,
        refs[:4],
        prefix_ref,
        late_ref,
        0,
        squares_ref[...],
        inner_ref[...],
    )
    inverse = lax.rsqrt(
        jnp.sum(squares, axis=1, keepdims=True) * (1.0 / features) + EPSILON
    )
    inner_mean = jnp.sum(inner, axis=1, keepdims=True) * (1.0 / features) * inverse
    inverse_ref[...] = jnp.broadcast_to(inverse, inverse_ref.shape)
    scaling = head ** (-0.5)
    for slot in range(group):
        for i in range(width // head):
            part = features_at(orders[1], slot, i, width, head)
            local = columns(i * head, head)
            late = [order[slot] == last for order in orders[1]]
            attended = late_ref[:, local] if late[0] else early_ref[:, part]
            if late[0] != late[1]:
                other = late_ref[:, local] if late[1] else early_ref[:, part]
                attended = jnp.where(odd, other, attended)
            normalized = attended * inverse
            upstream = cot_ref[:, part].astype(F32)
            gain_grad_ref[:, part] = jnp.sum(
                upstream * normalized, axis=0, keepdims=True
            ) * (1.0 / replicas)
            scaled = upstream * gain_ref[:, part]
            grad = ((scaled - normalized * inner_mean) * inverse).astype(HALF)
            grad_ref[:, part] = grad
            piece_refs[slot][local, :] = (
                scaling * dot(q_ref[:, part], grad, 0, 0)
            ).astype(HALF)
    for h in range(HEADS):
        gain_rows_ref[h : h + 1, :] = gain_grad_ref[:, columns(h * head, head)]
    for ref in piece_refs:
        put_wide_rows(ref, width, gain_rows_ref[...])


def backward_kernel(head, group, *refs):
    q_ref, k_ref, v_ref, scores_ref, grad_ref = refs[:5]
    early_ref, late_ref, inverse_ref, gain_ref = refs[5:9]
    prefix_refs = refs[9 : 9 + group]
    out_ref, grad_query_ref, key_part_ref, value_part_ref, token_ref = refs[
        9 + group : 14 + group
    ]
    whole_ref = refs[14 + group]
    rows = q_ref.shape[0]
    mask = causal(rows)
    scaling = head ** (-0.5)
    gathered(STATE_ORDERS[1], prefix_refs, prefix_refs[0].shape[0], whole_ref)
    inverse = inverse_ref[...]
    width = late_ref.shape[1]
    for slot in range(group):
        for i in range(width // head):
            part = features_at(STATE_ORDERS[1], slot, i, width, head)
            if slot == group - 1:
                attended = late_ref[:, columns(i * head, head)]
            else:
                attended = early_ref[:, part]
            out_ref[:, part] = (gain_ref[:, part] * (attended * inverse)).astype(HALF)
    for h in range(HEADS):
        part = columns(h * head, head)
        grad = grad_ref[:, part]
        grad_scores = dot(grad, v_ref[:, part], 1, 1)
        grad_scores = jnp.where(mask, grad_scores, 0.0).astype(HALF)
        grad_query = dot(grad_scores, k_ref[:, part], 1, 0) + dot(
            grad, whole_ref[part, :], 1, 1
        )
        grad_query_ref[:, part] = (scaling * grad_query).astype(HALF)
        key_part_ref[:, part] = scaling * dot(grad_scores, q_ref[:, part], 0, 0)
        value_part_ref[:, part] = dot(
            scores_ref[columns(h * rows, rows), :], grad, 0, 0
        )
    token_ref[...] = jnp.zeros_like(token_ref)


def final_kernel(head, slots, last, *refs):
    k_ref, v_ref, key_part_ref, value_part_ref = refs[:4]
    suffix_refs = refs[4 : 4 + len(slots)]
    refs = refs[4 + len(slots) :]
    copies = []
    if last:
        gain_grad_ref, total_ref, gain_written = refs[-6], refs[-2], refs[-1]
        total_ref[...] = tree_sum([ref[...] for ref in refs[2:-8]])
        copies.append(pltpu.make_async_copy(total_ref, gain_grad_ref, gain_written))
        copies[0].start()
        out_refs, refs = refs[-8:-6], refs[-5:-2]
    else:
        out_refs, refs = refs[:2], refs[2:]
    key_buffer, value_buffer, written = refs
    width = key_buffer.shape[2]
    for n, slot in enumerate(slots):
        for i in range(width // head):
            part = features_at(GRAD_ORDERS[1], slot, i, width, head)
            local = columns(i * head, head)
            suffix = suffix_refs[n][local, :]
            key_buffer[n, :, local] = (
                key_part_ref[:, part] + dot(v_ref[:, part], suffix, 1, 1)
            ).astype(HALF)
            value_buffer[n, :, local] = (
                value_part_ref[:, part] + dot(k_ref[:, part], suffix, 1, 0)
            ).astype(HALF)
        for i, buffer in enumerate((key_buffer, value_buffer)):
            copy = pltpu.make_async_copy(
                buffer.at[n],
                out_refs[i].at[:, block_at(partner_of(GRAD_ORDERS[1], slot), width)],
                written.at[i, n],
            )
            copy.start()
            copies.append(copy)
    for copy in copies:
        copy.wait()


def tree_sum(terms):
    while len(terms) > 1:
        terms = [a + b for a, b in zip(terms[::2], terms[1::2])]
    return terms[0]


def wide_rows(ref, start):
    rows = (ref.shape[0] - start) // 2
    high = ref[columns(start, rows), :].astype(F32)
    return high + ref[columns(start + rows, rows), :].astype(F32)


def put_wide_rows(ref, start, value):
    rows = value.shape[0]
    high = value.astype(HALF)
    ref[columns(start, rows), :] = high
    ref[columns(start + rows, rows), :] = (value - high.astype(F32)).astype(HALF)


def total_kernel(size, count, *refs):
    refs, out_refs = refs[:count], refs[count + 1 :]
    total = refs[0][0:size, :].astype(F32)
    for ref in refs[1:]:
        total += ref[0:size, :].astype(F32)
    out_refs[0][0:size, :] = total.astype(HALF)
    if len(out_refs) > 1:
        gain = tree_sum([wide_rows(ref, size) for ref in refs])
        put_wide_rows(out_refs[0], size, gain)
        out_refs[1][...] = wide_rows(out_refs[0], size)


def group_flag(group, reverse, distance):
    index = lax.axis_index("seq") // group
    last = lax.axis_size("seq") // group - 1
    known = index + distance <= last if reverse else index >= distance
    return jnp.where(known, 1.0, 0.0)


def carry_kernel(group, reverse, distance, first, own_ref, moved_ref, out_ref):
    own = own_ref[...].astype(F32)
    if first:
        own = own * group_flag(group, reverse, 1)
    moved = moved_ref[...].astype(F32) * group_flag(group, reverse, distance)
    out_ref[...] = (own + moved).astype(HALF)


def scan_kernel(group, orders, slots, reverse, masked, size, riding, *refs):
    sources = [partner_of(orders[0], j) for j in range(group)]
    carry = refs[0][0:size, :].astype(F32)
    if masked:
        carry = carry * group_flag(group, reverse, 1)
    blocks = [ref[0:size, :].astype(F32) for ref in refs[1 : 1 + group]]
    out_refs = refs[-len(slots) - riding :][: len(slots)]
    for slot, out_ref in zip(slots, out_refs):
        target = partner_of(orders[1], slot)
        total = carry
        for i in range(group):
            known = sources[i] > target if reverse else sources[i] < target
            total += jnp.where(known, 1.0, 0.0) * blocks[i]
        out_ref[...] = total.astype(HALF)
    if riding:
        refs[-1][...] = refs[1 + group][...] + wide_rows(refs[0], size)


VMEM = pl.BlockSpec(memory_space=pltpu.VMEM)
ANY = pl.BlockSpec(memory_space=pl.ANY)
HBM = pl.BlockSpec(memory_space=pltpu.HBM)


def call(kernel, outs, args, matmuls, scratch=(), ins=None, out_specs=None, aliases=None):
    size = sum(a.size * a.dtype.itemsize for a in args)
    size += sum(o.size * o.dtype.itemsize for o in outs)
    ins = ins or {}
    out_specs = out_specs or {}
    return pl.pallas_call(
        kernel,
        out_shape=tuple(outs),
        in_specs=[ins.get(i, VMEM) for i in range(len(args))],
        out_specs=tuple(out_specs.get(i, VMEM) for i in range(len(outs))),
        scratch_shapes=list(scratch),
        input_output_aliases=aliases or {},
        compiler_params=pltpu.CompilerParams(vmem_limit_bytes=16 * 1024 * 1024),
        cost_estimate=pl.CostEstimate(
            flops=2 * 128 * 128 * 128 * HEADS * matmuls,
            bytes_accessed=size,
            transcendentals=0,
        ),
    )(*args)


def swap(array, axis, offset):
    count = lax.axis_size(axis)
    return lax.ppermute(array, axis, [(i, i ^ offset) for i in range(count)])


def own_and_swapped(pieces, order):
    count = lax.axis_size("seq")
    results = [pieces[0]]
    for slot in range(1, len(pieces)):
        pairs = []
        for row in range(lax.axis_size("dp")):
            offset = order[row % 2][slot]
            pairs += [(row * count + i, row * count + (i ^ offset)) for i in range(count)]
        results.append(lax.ppermute(pieces[slot], ("dp", "seq"), pairs))
    return results


def exclusive_scan(pieces, orders, size, reverse, token):
    group = len(pieces)
    count, rows = lax.axis_size("seq"), lax.axis_size("dp")
    groups = count // group
    part = functools.partial
    lanes = pieces[0].shape[1]
    extra = pieces[0].shape[0] - size
    piece = jax.ShapeDtypeStruct((size, lanes), HALF)
    gain_shape = jax.ShapeDtypeStruct((extra // 2, lanes), F32)

    def shifted(array, distance):
        step = -distance if reverse else distance
        pairs = [(i, (i + step) % count) for i in range(count)]
        return lax.ppermute(array, "seq", pairs)

    received = own_and_swapped(pieces, orders[0])
    totals = call(
        part(total_kernel, size, group),
        [jax.ShapeDtypeStruct(pieces[0].shape, HALF)] + [gain_shape] * (extra > 0),
        received + [token],
        0,
        ins={group: ANY},
    )
    total, gains = totals[0], list(totals[1:])
    riding = int(extra > 0 and groups == 2 and rows == 4)
    carry = shifted(total if riding else total[:size], group)
    if riding:
        for offset in (0, group):
            pairs = [
                (row * count + i, (row ^ 2) * count + (i ^ offset))
                for row in range(rows)
                for i in range(count)
            ]
            gains.append(lax.ppermute(gains[0], ("dp", "seq"), pairs))
    elif extra:
        gains = [tree_sum(summed_over("seq", group, gains[0]))]
        gains = [tree_sum(summed_over("dp", 2, gains[0]))]
    distance = 1
    while distance < groups - 1:
        moved = shifted(carry, distance * group)
        kernel = part(
            carry_kernel, group, reverse, distance + (distance == 1), distance == 1
        )
        (carry,) = call(kernel, [piece], [carry, moved], 0)
        distance *= 2
    pieces, after = {}, []
    for slots in ((1,), (2,), (3, 0)):
        adding = riding if 0 in slots else 0
        inputs = [carry] + received + gains[:adding] + after
        sums = call(
            part(scan_kernel, group, orders, slots, reverse, groups <= 2, size, adding),
            [piece] * len(slots) + [gain_shape] * adding,
            inputs,
            0,
            ins={len(inputs) - 1: ANY} if after else {},
        )
        pieces.update(zip(slots, sums))
        after = [sums[0]]
    results = own_and_swapped([pieces[slot] for slot in range(group)], orders[1])
    if riding:
        gains = [sums[-1] + (gains[1] + gains[2])]
    return results, (gains[0] if gains else None)


def summed_over(axis, stride, array):
    count = lax.axis_size(axis)
    terms = [array]
    while stride < count:
        array = tree_sum(terms)
        width = 4 if count // stride % 4 == 0 else 2
        order = sorted(range(1, width), key=lambda i: i % 2)
        moved = {i: swap(array, axis, i * stride) for i in order}
        terms = [array] + [moved[i] for i in range(1, width)]
        stride *= width
    return terms


def per_device(queries, keys, values, gain, cotangent):
    q, k, v, cot = queries[0], keys[0], values[0], cotangent[0]
    rows, features = q.shape
    head = features // HEADS
    group = 4
    width = features // group
    part = functools.partial
    wide = jax.ShapeDtypeStruct((rows, features), F32)
    half = jax.ShapeDtypeStruct((rows, features), HALF)
    square = jax.ShapeDtypeStruct((rows, head), F32)
    piece = jax.ShapeDtypeStruct((width, head), HALF)
    scores_shape = jax.ShapeDtypeStruct((HEADS * rows, rows), HALF)
    gain_shape = jax.ShapeDtypeStruct((HEADS, head), F32)
    token_shape = jax.ShapeDtypeStruct((8, head), F32)
    whole = pltpu.VMEM((features, head), HALF)
    gain_row = gain.reshape(1, features)

    (first,) = call(
        part(first_state_kernel, head, 1),
        [piece],
        [pltpu.with_memory_space_constraint(a, pltpu.HBM) for a in (k, v)],
        1,
        [pltpu.VMEM((rows, width), HALF)] * 2 + [pltpu.SemaphoreType.DMA((2,))],
        ins={0: HBM, 1: HBM},
    )
    slots = (2, 3, 0)
    rest = call(
        part(state_kernel, head, slots), [piece] * 3, [k, v, first], 1, ins={2: ANY}
    )
    pieces = dict(zip(slots, rest))
    pieces[1] = first
    pieces = [pieces[slot] for slot in range(group)]
    scores, intra = call(part(local_kernel, head), [scores_shape, wide], [q, k, v], 2)
    prefix, _ = exclusive_scan(pieces, STATE_ORDERS, width, False, intra)
    message = jax.ShapeDtypeStruct((width + 2 * HEADS, head), HALF)
    sources = [q, intra, gain_row, cot]
    early, squares, inner = call(
        part(early_norm_kernel, head, STATE_ORDERS[1]),
        [wide, square, square],
        sources + prefix[:-1],
        1,
    )
    late, inverse, grad, *pieces = call(
        part(norm_kernel, head, group, NORM_ORDERS, lax.axis_size("dp")),
        [jax.ShapeDtypeStruct((rows, width), F32), square, half] + [message] * group,
        sources + [early, squares, inner, prefix[-1]],
        2,
        [pltpu.VMEM((1, features), F32), pltpu.VMEM((HEADS, head), F32)],
    )
    output, grad_query, key_part, value_part, token = call(
        part(backward_kernel, head, group),
        [half, half, wide, wide, token_shape],
        [q, k, v, scores, grad, early, late, inverse, gain_row] + prefix,
        5,
        [whole],
    )
    suffix, gain_grad = exclusive_scan(pieces, GRAD_ORDERS, width, True, token)
    gains = [gain_grad, swap(gain_grad, "dp", 1)]
    inputs = [k, v, key_part, value_part]
    outs = []
    for slots in ((0, 1, 2), (3,)):
        last = group - 1 in slots
        at = len(inputs) + len(slots)
        results = call(
            part(final_kernel, head, slots, last),
            [half, half] + [gain_shape] * last,
            inputs + [suffix[slot] for slot in slots] + outs + (gains if last else []),
            1,
            [pltpu.VMEM((len(slots), rows, width), HALF)] * 2
            + [pltpu.SemaphoreType.DMA((2, len(slots)))]
            + [pltpu.VMEM((HEADS, head), F32), pltpu.SemaphoreType.DMA(())] * last,
            ins={at + i: HBM for i in range(len(outs))},
            out_specs={0: HBM, 1: HBM, 2: HBM},
            aliases={at + i: i for i in range(len(outs))},
        )
        outs = list(results[:2])
    grad_key, grad_value, gain_grad = results
    return (
        output[None],
        grad_query[None],
        grad_key[None],
        grad_value[None],
        gain_grad.reshape(features),
    )


def solution(mesh):
    spec = P("dp", "seq", None)
    return jax.shard_map(
        per_device,
        mesh=mesh,
        in_specs=(spec, spec, spec, P(), spec),
        out_specs=(spec, spec, spec, spec, P()),
        check_vma=False,
    )
```

```python
import functools

import jax
import jax.numpy as jnp
from jax import lax
from jax.experimental import pallas as pl
from jax.experimental.pallas import tpu as pltpu
from jax.sharding import PartitionSpec as P

HEADS = 16

EPSILON = 1e-06

F32 = jnp.float32
HALF = jnp.bfloat16


def dot(lhs, rhs, lhs_dim, rhs_dim):
    return lax.dot_general(
        lhs, rhs, (((lhs_dim,), (rhs_dim,)), ((), ())), preferred_element_type=F32
    )


def causal(size):
    rows = lax.broadcasted_iota(jnp.int32, (size, size), 0)
    columns = lax.broadcasted_iota(jnp.int32, (size, size), 1)
    return rows >= columns


def member_of(group):
    return lax.rem(lax.axis_index("seq"), group)


STATE_ORDERS = (((0, 1, 3, 2), (0, 2, 3, 1)), ((0, 3, 1, 2), (0, 3, 2, 1)))
GRAD_ORDERS = (((0, 3, 1, 2), (0, 3, 1, 2)), ((0, 3, 1, 2), (0, 1, 2, 3)))
NORM_ORDERS = (STATE_ORDERS[1], GRAD_ORDERS[0])


def partner_of(order, slot):
    even, odd = order[0][slot], order[1][slot]
    offset = even
    if even != odd:
        offset = jnp.where(lax.rem(lax.axis_index("dp"), 2) == 1, odd, even)
    return member_of(len(order[0])) ^ offset


def block_at(index, size):
    return pl.ds(pl.multiple_of(index * size, size), size)


def gathered(order, piece_refs, size, whole_ref):
    for j, ref in enumerate(piece_refs):
        whole_ref[block_at(partner_of(order, j), size), :] = ref[0:size, :]


def columns(first, count):
    return slice(first, first + count)


def first_state_kernel(head, slot, k_ref, v_ref, piece_ref, k_buffer, v_buffer, arrived):
    width = piece_ref.shape[0]
    source = block_at(partner_of(STATE_ORDERS[0], slot), width)
    copies = [
        pltpu.make_async_copy(k_ref.at[:, source], k_buffer, arrived.at[0]),
        pltpu.make_async_copy(v_ref.at[:, source], v_buffer, arrived.at[1]),
    ]
    for copy in copies:
        copy.start()
    for copy in copies:
        copy.wait()
    for i in range(width // head):
        part = columns(i * head, head)
        piece_ref[part, :] = dot(k_buffer[:, part], v_buffer[:, part], 0, 0).astype(HALF)


def state_kernel(head, slots, k_ref, v_ref, token_ref, *piece_refs):
    del token_ref
    for slot, piece_ref in zip(slots, piece_refs):
        width = piece_ref.shape[0]
        for i in range(width // head):
            part = features_at(STATE_ORDERS[0], slot, i, width, head)
            piece_ref[columns(i * head, head), :] = dot(
                k_ref[:, part], v_ref[:, part], 0, 0
            ).astype(HALF)


def local_kernel(head, q_ref, k_ref, v_ref, scores_ref, intra_ref):
    rows = q_ref.shape[0]
    mask = causal(rows)
    scaling = head ** (-0.5)
    for h in range(HEADS):
        part = columns(h * head, head)
        scores = dot(q_ref[:, part], k_ref[:, part], 1, 1) * scaling
        scores = jnp.where(mask, scores, 0.0).astype(HALF)
        scores_ref[columns(h * rows, rows), :] = scores
        intra_ref[:, part] = dot(scores, v_ref[:, part], 1, 0)


def features_at(order, slot, i, width, head):
    start = partner_of(order, slot) * width + i * head
    return pl.ds(pl.multiple_of(start, head), head)


def attend(head, order, slot, refs, prefix_ref, attended_ref, at, squares, inner):
    q_ref, intra_ref, gain_ref, cot_ref = refs
    scaling = head ** (-0.5)
    width = prefix_ref.shape[0]
    for i in range(width // head):
        part = features_at(order, slot, i, width, head)
        prefix = prefix_ref[columns(i * head, head), :]
        attended = intra_ref[:, part] + scaling * dot(q_ref[:, part], prefix, 1, 0)
        attended_ref[:, part if at is None else columns(i * head, head)] = attended
        scaled = cot_ref[:, part].astype(F32) * gain_ref[:, part]
        squares += attended * attended
        inner += scaled * attended
    return squares, inner


def early_norm_kernel(head, order, *refs):
    prefix_refs, (attended_ref, squares_ref, inner_ref) = refs[4:-3], refs[-3:]
    squares = jnp.zeros(squares_ref.shape, F32)
    inner = jnp.zeros(squares_ref.shape, F32)
    for slot, prefix_ref in enumerate(prefix_refs):
        squares, inner = attend(
            head, order, slot, refs[:4], prefix_ref, attended_ref, None, squares, inner
        )
    squares_ref[...] = squares
    inner_ref[...] = inner


def norm_kernel(head, group, orders, replicas, *refs):
    q_ref, _, gain_ref, cot_ref = refs[:4]
    early_ref, squares_ref, inner_ref, prefix_ref = refs[4:8]
    late_ref, inverse_ref, grad_ref = refs[8:11]
    piece_refs = refs[11 : 11 + group]
    gain_grad_ref, gain_rows_ref = refs[11 + group :]
    features = q_ref.shape[1]
    width = features // group
    odd = lax.rem(lax.axis_index("dp"), 2) == 1
    squares, inner = attend(
        head,
        orders[0],
        group - 1,
        refs[:4],
        prefix_ref,
        late_ref,
        0,
        squares_ref[...],
        inner_ref[...],
    )
    inverse = lax.rsqrt(
        jnp.sum(squares, axis=1, keepdims=True) * (1.0 / features) + EPSILON
    )
    inner_mean = jnp.sum(inner, axis=1, keepdims=True) * (1.0 / features) * inverse
    inverse_ref[...] = jnp.broadcast_to(inverse, inverse_ref.shape)
    scaling = head ** (-0.5)
    for slot in range(group):
        for i in range(width // head):
            part = features_at(orders[1], slot, i, width, head)
            local = columns(i * head, head)
            late = [order[slot] == before[-1] for before, order in zip(*orders)]
            attended = late_ref[:, local] if late[0] else early_ref[:, part]
            if late[0] != late[1]:
                other = late_ref[:, local] if late[1] else early_ref[:, part]
                attended = jnp.where(odd, other, attended)
            normalized = attended * inverse
            upstream = cot_ref[:, part].astype(F32)
            gain_grad_ref[:, part] = jnp.sum(
                upstream * normalized, axis=0, keepdims=True
            ) * (1.0 / replicas)
            scaled = upstream * gain_ref[:, part]
            grad = ((scaled - normalized * inner_mean) * inverse).astype(HALF)
            grad_ref[:, part] = grad
            piece_refs[slot][local, :] = (
                scaling * dot(q_ref[:, part], grad, 0, 0)
            ).astype(HALF)
    for h in range(HEADS):
        gain_rows_ref[h : h + 1, :] = gain_grad_ref[:, columns(h * head, head)]
    for ref in piece_refs:
        put_wide_rows(ref, width, gain_rows_ref[...])


def backward_kernel(head, group, *refs):
    q_ref, k_ref, v_ref, scores_ref, grad_ref = refs[:5]
    early_ref, late_ref, inverse_ref, gain_ref = refs[5:9]
    prefix_refs = refs[9 : 9 + group]
    out_ref, grad_query_ref, key_part_ref, value_part_ref, token_ref = refs[
        9 + group : 14 + group
    ]
    whole_ref = refs[14 + group]
    rows = q_ref.shape[0]
    mask = causal(rows)
    scaling = head ** (-0.5)
    gathered(STATE_ORDERS[1], prefix_refs, prefix_refs[0].shape[0], whole_ref)
    inverse = inverse_ref[...]
    width = late_ref.shape[1]
    for slot in range(group):
        for i in range(width // head):
            part = features_at(STATE_ORDERS[1], slot, i, width, head)
            if slot == group - 1:
                attended = late_ref[:, columns(i * head, head)]
            else:
                attended = early_ref[:, part]
            out_ref[:, part] = (gain_ref[:, part] * (attended * inverse)).astype(HALF)
    for h in range(HEADS):
        part = columns(h * head, head)
        grad = grad_ref[:, part]
        grad_scores = dot(grad, v_ref[:, part], 1, 1)
        grad_scores = jnp.where(mask, grad_scores, 0.0).astype(HALF)
        grad_query = dot(grad_scores, k_ref[:, part], 1, 0) + dot(
            grad, whole_ref[part, :], 1, 1
        )
        grad_query_ref[:, part] = (scaling * grad_query).astype(HALF)
        key_part_ref[:, part] = scaling * dot(grad_scores, q_ref[:, part], 0, 0)
        value_part_ref[:, part] = dot(
            scores_ref[columns(h * rows, rows), :], grad, 0, 0
        )
    token_ref[...] = jnp.zeros_like(token_ref)


def final_kernel(head, slots, last, *refs):
    k_ref, v_ref, key_part_ref, value_part_ref = refs[:4]
    suffix_refs = refs[4 : 4 + len(slots)]
    refs = refs[4 + len(slots) :]
    copies = []
    if last:
        gain_grad_ref, total_ref, gain_written = refs[-6], refs[-2], refs[-1]
        total_ref[...] = tree_sum([ref[...] for ref in refs[2:-8]])
        copies.append(pltpu.make_async_copy(total_ref, gain_grad_ref, gain_written))
        copies[0].start()
        out_refs, refs = refs[-8:-6], refs[-5:-2]
    else:
        out_refs, refs = refs[-5:-3], refs[-3:]
    key_buffer, value_buffer, written = refs
    width = key_buffer.shape[2]
    for n, slot in enumerate(slots):
        for i in range(width // head):
            part = features_at(GRAD_ORDERS[1], slot, i, width, head)
            local = columns(i * head, head)
            suffix = suffix_refs[n][local, :]
            key_buffer[n, :, local] = (
                key_part_ref[:, part] + dot(v_ref[:, part], suffix, 1, 1)
            ).astype(HALF)
            value_buffer[n, :, local] = (
                value_part_ref[:, part] + dot(k_ref[:, part], suffix, 1, 0)
            ).astype(HALF)
        for i, buffer in enumerate((key_buffer, value_buffer)):
            copy = pltpu.make_async_copy(
                buffer.at[n],
                out_refs[i].at[:, block_at(partner_of(GRAD_ORDERS[1], slot), width)],
                written.at[i, n],
            )
            copy.start()
            copies.append(copy)
    for copy in copies:
        copy.wait()


def tree_sum(terms):
    while len(terms) > 1:
        terms = [a + b for a, b in zip(terms[::2], terms[1::2])]
    return terms[0]


def wide_rows(ref, start):
    rows = (ref.shape[0] - start) // 2
    high = ref[columns(start, rows), :].astype(F32)
    return high + ref[columns(start + rows, rows), :].astype(F32)


def put_wide_rows(ref, start, value):
    rows = value.shape[0]
    high = value.astype(HALF)
    ref[columns(start, rows), :] = high
    ref[columns(start + rows, rows), :] = (value - high.astype(F32)).astype(HALF)


def total_kernel(size, count, *refs):
    refs, out_refs = refs[:count], refs[count + 1 :]
    total = refs[0][0:size, :].astype(F32)
    for ref in refs[1:]:
        total += ref[0:size, :].astype(F32)
    out_refs[0][0:size, :] = total.astype(HALF)
    if len(out_refs) > 1:
        gain = tree_sum([wide_rows(ref, size) for ref in refs])
        put_wide_rows(out_refs[0], size, gain)
        out_refs[1][...] = wide_rows(out_refs[0], size)


def group_flag(group, reverse, distance):
    index = lax.axis_index("seq") // group
    last = lax.axis_size("seq") // group - 1
    known = index + distance <= last if reverse else index >= distance
    return jnp.where(known, 1.0, 0.0)


def carry_kernel(group, reverse, distance, first, own_ref, moved_ref, out_ref):
    own = own_ref[...].astype(F32)
    if first:
        own = own * group_flag(group, reverse, 1)
    moved = moved_ref[...].astype(F32) * group_flag(group, reverse, distance)
    out_ref[...] = (own + moved).astype(HALF)


def scan_kernel(group, orders, slots, reverse, masked, size, riding, *refs):
    sources = [partner_of(orders[0], j) for j in range(group)]
    carry = refs[0][0:size, :].astype(F32)
    if masked:
        carry = carry * group_flag(group, reverse, 1)
    blocks = [ref[0:size, :].astype(F32) for ref in refs[1 : 1 + group]]
    out_refs = refs[-len(slots) - riding :][: len(slots)]
    for slot, out_ref in zip(slots, out_refs):
        target = partner_of(orders[1], slot)
        total = carry
        for i in range(group):
            known = sources[i] > target if reverse else sources[i] < target
            total += jnp.where(known, 1.0, 0.0) * blocks[i]
        out_ref[...] = total.astype(HALF)
    if riding:
        refs[-1][...] = refs[1 + group][...] + wide_rows(refs[0], size)


VMEM = pl.BlockSpec(memory_space=pltpu.VMEM)
ANY = pl.BlockSpec(memory_space=pl.ANY)
HBM = pl.BlockSpec(memory_space=pltpu.HBM)


def call(kernel, outs, args, matmuls, scratch=(), ins=None, out_specs=None, aliases=None):
    size = sum(a.size * a.dtype.itemsize for a in args)
    size += sum(o.size * o.dtype.itemsize for o in outs)
    ins = ins or {}
    out_specs = out_specs or {}
    return pl.pallas_call(
        kernel,
        out_shape=tuple(outs),
        in_specs=[ins.get(i, VMEM) for i in range(len(args))],
        out_specs=tuple(out_specs.get(i, VMEM) for i in range(len(outs))),
        scratch_shapes=list(scratch),
        input_output_aliases=aliases or {},
        compiler_params=pltpu.CompilerParams(vmem_limit_bytes=16 * 1024 * 1024),
        cost_estimate=pl.CostEstimate(
            flops=2 * 128 * 128 * 128 * HEADS * matmuls,
            bytes_accessed=size,
            transcendentals=0,
        ),
    )(*args)


def swap(array, axis, offset):
    count = lax.axis_size(axis)
    return lax.ppermute(array, axis, [(i, i ^ offset) for i in range(count)])


def own_and_swapped(pieces, order):
    count = lax.axis_size("seq")
    results = [pieces[0]]
    for slot in range(1, len(pieces)):
        pairs = []
        for row in range(lax.axis_size("dp")):
            offset = order[row % 2][slot]
            pairs += [(row * count + i, row * count + (i ^ offset)) for i in range(count)]
        results.append(lax.ppermute(pieces[slot], ("dp", "seq"), pairs))
    return results


def exclusive_scan(pieces, orders, size, reverse, token):
    group = len(pieces)
    count, rows = lax.axis_size("seq"), lax.axis_size("dp")
    groups = count // group
    part = functools.partial
    lanes = pieces[0].shape[1]
    extra = pieces[0].shape[0] - size
    piece = jax.ShapeDtypeStruct((size, lanes), HALF)
    gain_shape = jax.ShapeDtypeStruct((extra // 2, lanes), F32)

    def shifted(array, distance):
        step = -distance if reverse else distance
        pairs = [(i, (i + step) % count) for i in range(count)]
        return lax.ppermute(array, "seq", pairs)

    received = own_and_swapped(pieces, orders[0])
    totals = call(
        part(total_kernel, size, group),
        [jax.ShapeDtypeStruct(pieces[0].shape, HALF)] + [gain_shape] * (extra > 0),
        received + [token],
        0,
        ins={group: ANY},
    )
    total, gains = totals[0], list(totals[1:])
    riding = int(extra > 0 and groups == 2 and rows == 4)
    carry = shifted(total if riding else total[:size], group)
    if riding:
        for offset in (0, group):
            pairs = [
                (row * count + i, (row ^ 2) * count + (i ^ offset))
                for row in range(rows)
                for i in range(count)
            ]
            gains.append(lax.ppermute(gains[0], ("dp", "seq"), pairs))
    elif extra:
        gains = [tree_sum(summed_over("seq", group, gains[0]))]
        gains = [tree_sum(summed_over("dp", 2, gains[0]))]
    distance = 1
    while distance < groups - 1:
        moved = shifted(carry, distance * group)
        kernel = part(
            carry_kernel, group, reverse, distance + (distance == 1), distance == 1
        )
        (carry,) = call(kernel, [piece], [carry, moved], 0)
        distance *= 2
    pieces, after = {}, []
    for slots in ((1,), (2,), (3, 0)):
        adding = riding if 0 in slots else 0
        inputs = [carry] + received + gains[:adding] + after
        sums = call(
            part(scan_kernel, group, orders, slots, reverse, groups <= 2, size, adding),
            [piece] * len(slots) + [gain_shape] * adding,
            inputs,
            0,
            ins={len(inputs) - 1: ANY} if after else {},
        )
        pieces.update(zip(slots, sums))
        after = [sums[0]]
    results = own_and_swapped([pieces[slot] for slot in range(group)], orders[1])
    if riding:
        gains = [sums[-1] + (gains[1] + gains[2])]
    return results, (gains[0] if gains else None)


def summed_over(axis, stride, array):
    count = lax.axis_size(axis)
    terms = [array]
    while stride < count:
        array = tree_sum(terms)
        width = 4 if count // stride % 4 == 0 else 2
        order = sorted(range(1, width), key=lambda i: i % 2)
        moved = {i: swap(array, axis, i * stride) for i in order}
        terms = [array] + [moved[i] for i in range(1, width)]
        stride *= width
    return terms


def per_device(queries, keys, values, gain, cotangent):
    q, k, v, cot = queries[0], keys[0], values[0], cotangent[0]
    rows, features = q.shape
    head = features // HEADS
    group = 4
    width = features // group
    part = functools.partial
    wide = jax.ShapeDtypeStruct((rows, features), F32)
    half = jax.ShapeDtypeStruct((rows, features), HALF)
    square = jax.ShapeDtypeStruct((rows, head), F32)
    piece = jax.ShapeDtypeStruct((width, head), HALF)
    scores_shape = jax.ShapeDtypeStruct((HEADS * rows, rows), HALF)
    gain_shape = jax.ShapeDtypeStruct((HEADS, head), F32)
    token_shape = jax.ShapeDtypeStruct((8, head), F32)
    whole = pltpu.VMEM((features, head), HALF)
    gain_row = gain.reshape(1, features)

    (first,) = call(
        part(first_state_kernel, head, 1),
        [piece],
        [pltpu.with_memory_space_constraint(a, pltpu.HBM) for a in (k, v)],
        1,
        [pltpu.VMEM((rows, width), HALF)] * 2 + [pltpu.SemaphoreType.DMA((2,))],
        ins={0: HBM, 1: HBM},
    )
    slots = (2, 3, 0)
    rest = call(
        part(state_kernel, head, slots), [piece] * 3, [k, v, first], 1, ins={2: ANY}
    )
    pieces = dict(zip(slots, rest))
    pieces[1] = first
    pieces = [pieces[slot] for slot in range(group)]
    scores, intra = call(part(local_kernel, head), [scores_shape, wide], [q, k, v], 2)
    prefix, _ = exclusive_scan(pieces, STATE_ORDERS, width, False, intra)
    message = jax.ShapeDtypeStruct((width + 2 * HEADS, head), HALF)
    sources = [q, intra, gain_row, cot]
    early, squares, inner = call(
        part(early_norm_kernel, head, STATE_ORDERS[1]),
        [wide, square, square],
        sources + prefix[:-1],
        1,
    )
    late, inverse, grad, *pieces = call(
        part(norm_kernel, head, group, NORM_ORDERS, lax.axis_size("dp")),
        [jax.ShapeDtypeStruct((rows, width), F32), square, half] + [message] * group,
        sources + [early, squares, inner, prefix[-1]],
        2,
        [pltpu.VMEM((1, features), F32), pltpu.VMEM((HEADS, head), F32)],
    )
    output, grad_query, key_part, value_part, token = call(
        part(backward_kernel, head, group),
        [half, half, wide, wide, token_shape],
        [q, k, v, scores, grad, early, late, inverse, gain_row] + prefix,
        5,
        [whole],
    )
    suffix, gain_grad = exclusive_scan(pieces, GRAD_ORDERS, width, True, token)
    gains = [gain_grad, swap(gain_grad, "dp", 1)]
    inputs = [k, v, key_part, value_part]
    outs = []
    for slots in ((0, 1), (2,), (3,)):
        last = group - 1 in slots
        at = len(inputs) + len(slots)
        results = call(
            part(final_kernel, head, slots, last),
            [half, half] + [gain_shape] * last,
            inputs + [suffix[slot] for slot in slots] + outs + (gains if last else []),
            1,
            [pltpu.VMEM((len(slots), rows, width), HALF)] * 2
            + [pltpu.SemaphoreType.DMA((2, len(slots)))]
            + [pltpu.VMEM((HEADS, head), F32), pltpu.SemaphoreType.DMA(())] * last,
            ins={at + i: HBM for i in range(len(outs))},
            out_specs={0: HBM, 1: HBM, 2: HBM},
            aliases={at + i: i for i in range(len(outs))},
        )
        outs = list(results[:2])
    grad_key, grad_value, gain_grad = results
    return (
        output[None],
        grad_query[None],
        grad_key[None],
        grad_value[None],
        gain_grad.reshape(features),
    )


def solution(mesh):
    spec = P("dp", "seq", None)
    return jax.shard_map(
        per_device,
        mesh=mesh,
        in_specs=(spec, spec, spec, P(), spec),
        out_specs=(spec, spec, spec, spec, P()),
        check_vma=False,
    )
```

```python
import functools

import jax
import jax.numpy as jnp
from jax import lax
from jax.experimental import pallas as pl
from jax.experimental.pallas import tpu as pltpu
from jax.sharding import PartitionSpec as P

HEADS = 16

EPSILON = 1e-06

F32 = jnp.float32
HALF = jnp.bfloat16


def dot(lhs, rhs, lhs_dim, rhs_dim):
    return lax.dot_general(
        lhs, rhs, (((lhs_dim,), (rhs_dim,)), ((), ())), preferred_element_type=F32
    )


def causal(size):
    rows = lax.broadcasted_iota(jnp.int32, (size, size), 0)
    columns = lax.broadcasted_iota(jnp.int32, (size, size), 1)
    return rows >= columns


def member_of(group):
    return lax.rem(lax.axis_index("seq"), group)


STATE_ORDERS = (((0, 1, 2, 3), (0, 2, 1, 3)), ((0, 2, 1, 3), (0, 1, 2, 3)))
GRAD_ORDERS = (((0, 3, 1, 2), (0, 3, 1, 2)), ((0, 3, 1, 2), (0, 1, 2, 3)))
NORM_ORDERS = (STATE_ORDERS[1], GRAD_ORDERS[0])


def partner_of(order, slot):
    even, odd = order[0][slot], order[1][slot]
    offset = even
    if even != odd:
        offset = jnp.where(lax.rem(lax.axis_index("dp"), 2) == 1, odd, even)
    return member_of(len(order[0])) ^ offset


def block_at(index, size):
    return pl.ds(pl.multiple_of(index * size, size), size)


def gathered(order, piece_refs, size, whole_ref):
    for j, ref in enumerate(piece_refs):
        whole_ref[block_at(partner_of(order, j), size), :] = ref[0:size, :]


def columns(first, count):
    return slice(first, first + count)


def first_state_kernel(head, slot, k_ref, v_ref, piece_ref, k_buffer, v_buffer, arrived):
    width = piece_ref.shape[0]
    source = block_at(partner_of(STATE_ORDERS[0], slot), width)
    copies = [
        pltpu.make_async_copy(k_ref.at[:, source], k_buffer, arrived.at[0]),
        pltpu.make_async_copy(v_ref.at[:, source], v_buffer, arrived.at[1]),
    ]
    for copy in copies:
        copy.start()
    for copy in copies:
        copy.wait()
    for i in range(width // head):
        part = columns(i * head, head)
        piece_ref[part, :] = dot(k_buffer[:, part], v_buffer[:, part], 0, 0).astype(HALF)


def state_kernel(head, slots, k_ref, v_ref, token_ref, *piece_refs):
    del token_ref
    for slot, piece_ref in zip(slots, piece_refs):
        width = piece_ref.shape[0]
        for i in range(width // head):
            part = features_at(STATE_ORDERS[0], slot, i, width, head)
            piece_ref[columns(i * head, head), :] = dot(
                k_ref[:, part], v_ref[:, part], 0, 0
            ).astype(HALF)


def local_kernel(head, q_ref, k_ref, v_ref, scores_ref, intra_ref):
    rows = q_ref.shape[0]
    mask = causal(rows)
    scaling = head ** (-0.5)
    for h in range(HEADS):
        part = columns(h * head, head)
        scores = dot(q_ref[:, part], k_ref[:, part], 1, 1) * scaling
        scores = jnp.where(mask, scores, 0.0).astype(HALF)
        scores_ref[columns(h * rows, rows), :] = scores
        intra_ref[:, part] = dot(scores, v_ref[:, part], 1, 0)


def features_at(order, slot, i, width, head):
    start = partner_of(order, slot) * width + i * head
    return pl.ds(pl.multiple_of(start, head), head)


def attend(head, order, slot, refs, prefix_ref, attended_ref, at, squares, inner):
    q_ref, intra_ref, gain_ref, cot_ref = refs
    scaling = head ** (-0.5)
    width = prefix_ref.shape[0]
    for i in range(width // head):
        part = features_at(order, slot, i, width, head)
        prefix = prefix_ref[columns(i * head, head), :]
        attended = intra_ref[:, part] + scaling * dot(q_ref[:, part], prefix, 1, 0)
        attended_ref[:, part if at is None else columns(i * head, head)] = attended
        scaled = cot_ref[:, part].astype(F32) * gain_ref[:, part]
        squares += attended * attended
        inner += scaled * attended
    return squares, inner


def early_norm_kernel(head, order, *refs):
    prefix_refs, (attended_ref, squares_ref, inner_ref) = refs[4:-3], refs[-3:]
    squares = jnp.zeros(squares_ref.shape, F32)
    inner = jnp.zeros(squares_ref.shape, F32)
    for slot, prefix_ref in enumerate(prefix_refs):
        squares, inner = attend(
            head, order, slot, refs[:4], prefix_ref, attended_ref, None, squares, inner
        )
    squares_ref[...] = squares
    inner_ref[...] = inner


def norm_kernel(head, group, orders, replicas, *refs):
    q_ref, _, gain_ref, cot_ref = refs[:4]
    early_ref, squares_ref, inner_ref, prefix_ref = refs[4:8]
    late_ref, inverse_ref, grad_ref = refs[8:11]
    piece_refs = refs[11 : 11 + group]
    gain_grad_ref, gain_rows_ref = refs[11 + group :]
    features = q_ref.shape[1]
    width = features // group
    odd = lax.rem(lax.axis_index("dp"), 2) == 1
    squares, inner = attend(
        head,
        orders[0],
        group - 1,
        refs[:4],
        prefix_ref,
        late_ref,
        0,
        squares_ref[...],
        inner_ref[...],
    )
    inverse = lax.rsqrt(
        jnp.sum(squares, axis=1, keepdims=True) * (1.0 / features) + EPSILON
    )
    inner_mean = jnp.sum(inner, axis=1, keepdims=True) * (1.0 / features) * inverse
    inverse_ref[...] = jnp.broadcast_to(inverse, inverse_ref.shape)
    scaling = head ** (-0.5)
    for slot in range(group):
        for i in range(width // head):
            part = features_at(orders[1], slot, i, width, head)
            local = columns(i * head, head)
            late = [order[slot] == before[-1] for before, order in zip(*orders)]
            attended = late_ref[:, local] if late[0] else early_ref[:, part]
            if late[0] != late[1]:
                other = late_ref[:, local] if late[1] else early_ref[:, part]
                attended = jnp.where(odd, other, attended)
            normalized = attended * inverse
            upstream = cot_ref[:, part].astype(F32)
            gain_grad_ref[:, part] = jnp.sum(
                upstream * normalized, axis=0, keepdims=True
            ) * (1.0 / replicas)
            scaled = upstream * gain_ref[:, part]
            grad = ((scaled - normalized * inner_mean) * inverse).astype(HALF)
            grad_ref[:, part] = grad
            piece_refs[slot][local, :] = (
                scaling * dot(q_ref[:, part], grad, 0, 0)
            ).astype(HALF)
    for h in range(HEADS):
        gain_rows_ref[h : h + 1, :] = gain_grad_ref[:, columns(h * head, head)]
    for ref in piece_refs:
        put_wide_rows(ref, width, gain_rows_ref[...])


def backward_kernel(head, group, *refs):
    q_ref, k_ref, v_ref, scores_ref, grad_ref = refs[:5]
    early_ref, late_ref, inverse_ref, gain_ref = refs[5:9]
    prefix_refs = refs[9 : 9 + group]
    out_ref, grad_query_ref, key_part_ref, value_part_ref, token_ref = refs[
        9 + group : 14 + group
    ]
    whole_ref = refs[14 + group]
    rows = q_ref.shape[0]
    mask = causal(rows)
    scaling = head ** (-0.5)
    gathered(STATE_ORDERS[1], prefix_refs, prefix_refs[0].shape[0], whole_ref)
    inverse = inverse_ref[...]
    width = late_ref.shape[1]
    for slot in range(group):
        for i in range(width // head):
            part = features_at(STATE_ORDERS[1], slot, i, width, head)
            if slot == group - 1:
                attended = late_ref[:, columns(i * head, head)]
            else:
                attended = early_ref[:, part]
            out_ref[:, part] = (gain_ref[:, part] * (attended * inverse)).astype(HALF)
    for h in range(HEADS):
        part = columns(h * head, head)
        grad = grad_ref[:, part]
        grad_scores = dot(grad, v_ref[:, part], 1, 1)
        grad_scores = jnp.where(mask, grad_scores, 0.0).astype(HALF)
        grad_query = dot(grad_scores, k_ref[:, part], 1, 0) + dot(
            grad, whole_ref[part, :], 1, 1
        )
        grad_query_ref[:, part] = (scaling * grad_query).astype(HALF)
        key_part_ref[:, part] = scaling * dot(grad_scores, q_ref[:, part], 0, 0)
        value_part_ref[:, part] = dot(
            scores_ref[columns(h * rows, rows), :], grad, 0, 0
        )
    token_ref[...] = jnp.zeros_like(token_ref)


def final_kernel(head, slots, last, *refs):
    k_ref, v_ref, key_part_ref, value_part_ref = refs[:4]
    suffix_refs = refs[4 : 4 + len(slots)]
    refs = refs[4 + len(slots) :]
    copies = []
    if last:
        gain_grad_ref, total_ref, gain_written = refs[-6], refs[-2], refs[-1]
        total_ref[...] = tree_sum([ref[...] for ref in refs[2:-8]])
        copies.append(pltpu.make_async_copy(total_ref, gain_grad_ref, gain_written))
        copies[0].start()
        out_refs, refs = refs[-8:-6], refs[-5:-2]
    else:
        out_refs, refs = refs[-5:-3], refs[-3:]
    key_buffer, value_buffer, written = refs
    width = key_buffer.shape[2]
    for n, slot in enumerate(slots):
        for i in range(width // head):
            part = features_at(GRAD_ORDERS[1], slot, i, width, head)
            local = columns(i * head, head)
            suffix = suffix_refs[n][local, :]
            key_buffer[n, :, local] = (
                key_part_ref[:, part] + dot(v_ref[:, part], suffix, 1, 1)
            ).astype(HALF)
            value_buffer[n, :, local] = (
                value_part_ref[:, part] + dot(k_ref[:, part], suffix, 1, 0)
            ).astype(HALF)
        for i, buffer in enumerate((key_buffer, value_buffer)):
            copy = pltpu.make_async_copy(
                buffer.at[n],
                out_refs[i].at[:, block_at(partner_of(GRAD_ORDERS[1], slot), width)],
                written.at[i, n],
            )
            copy.start()
            copies.append(copy)
    for copy in copies:
        copy.wait()


def tree_sum(terms):
    while len(terms) > 1:
        terms = [a + b for a, b in zip(terms[::2], terms[1::2])]
    return terms[0]


def wide_rows(ref, start):
    rows = (ref.shape[0] - start) // 2
    high = ref[columns(start, rows), :].astype(F32)
    return high + ref[columns(start + rows, rows), :].astype(F32)


def put_wide_rows(ref, start, value):
    rows = value.shape[0]
    high = value.astype(HALF)
    ref[columns(start, rows), :] = high
    ref[columns(start + rows, rows), :] = (value - high.astype(F32)).astype(HALF)


def total_kernel(size, count, *refs):
    refs, out_refs = refs[:count], refs[count + 1 :]
    total = refs[0][0:size, :].astype(F32)
    for ref in refs[1:]:
        total += ref[0:size, :].astype(F32)
    out_refs[0][0:size, :] = total.astype(HALF)
    if len(out_refs) > 1:
        gain = tree_sum([wide_rows(ref, size) for ref in refs])
        put_wide_rows(out_refs[0], size, gain)
        out_refs[1][...] = wide_rows(out_refs[0], size)


def group_flag(group, reverse, distance):
    index = lax.axis_index("seq") // group
    last = lax.axis_size("seq") // group - 1
    known = index + distance <= last if reverse else index >= distance
    return jnp.where(known, 1.0, 0.0)


def carry_kernel(group, reverse, distance, first, own_ref, moved_ref, out_ref):
    own = own_ref[...].astype(F32)
    if first:
        own = own * group_flag(group, reverse, 1)
    moved = moved_ref[...].astype(F32) * group_flag(group, reverse, distance)
    out_ref[...] = (own + moved).astype(HALF)


def scan_kernel(group, orders, slots, reverse, masked, size, riding, *refs):
    sources = [partner_of(orders[0], j) for j in range(group)]
    carry = refs[0][0:size, :].astype(F32)
    if masked:
        carry = carry * group_flag(group, reverse, 1)
    blocks = [ref[0:size, :].astype(F32) for ref in refs[1 : 1 + group]]
    out_refs = refs[-len(slots) - riding :][: len(slots)]
    for slot, out_ref in zip(slots, out_refs):
        target = partner_of(orders[1], slot)
        total = carry
        for i in range(group):
            known = sources[i] > target if reverse else sources[i] < target
            total += jnp.where(known, 1.0, 0.0) * blocks[i]
        out_ref[...] = total.astype(HALF)
    if riding:
        refs[-1][...] = refs[1 + group][...] + wide_rows(refs[0], size)


VMEM = pl.BlockSpec(memory_space=pltpu.VMEM)
ANY = pl.BlockSpec(memory_space=pl.ANY)
HBM = pl.BlockSpec(memory_space=pltpu.HBM)


def call(kernel, outs, args, matmuls, scratch=(), ins=None, out_specs=None, aliases=None):
    size = sum(a.size * a.dtype.itemsize for a in args)
    size += sum(o.size * o.dtype.itemsize for o in outs)
    ins = ins or {}
    out_specs = out_specs or {}
    return pl.pallas_call(
        kernel,
        out_shape=tuple(outs),
        in_specs=[ins.get(i, VMEM) for i in range(len(args))],
        out_specs=tuple(out_specs.get(i, VMEM) for i in range(len(outs))),
        scratch_shapes=list(scratch),
        input_output_aliases=aliases or {},
        compiler_params=pltpu.CompilerParams(vmem_limit_bytes=16 * 1024 * 1024),
        cost_estimate=pl.CostEstimate(
            flops=2 * 128 * 128 * 128 * HEADS * matmuls,
            bytes_accessed=size,
            transcendentals=0,
        ),
    )(*args)


def swap(array, axis, offset):
    count = lax.axis_size(axis)
    return lax.ppermute(array, axis, [(i, i ^ offset) for i in range(count)])


def own_and_swapped(pieces, order):
    count = lax.axis_size("seq")
    results = [pieces[0]]
    for slot in range(1, len(pieces)):
        pairs = []
        for row in range(lax.axis_size("dp")):
            offset = order[row % 2][slot]
            pairs += [(row * count + i, row * count + (i ^ offset)) for i in range(count)]
        results.append(lax.ppermute(pieces[slot], ("dp", "seq"), pairs))
    return results


def exclusive_scan(pieces, orders, size, reverse, token):
    group = len(pieces)
    count, rows = lax.axis_size("seq"), lax.axis_size("dp")
    groups = count // group
    part = functools.partial
    lanes = pieces[0].shape[1]
    extra = pieces[0].shape[0] - size
    piece = jax.ShapeDtypeStruct((size, lanes), HALF)
    gain_shape = jax.ShapeDtypeStruct((extra // 2, lanes), F32)

    def shifted(array, distance):
        step = -distance if reverse else distance
        pairs = [(i, (i + step) % count) for i in range(count)]
        return lax.ppermute(array, "seq", pairs)

    received = own_and_swapped(pieces, orders[0])
    totals = call(
        part(total_kernel, size, group),
        [jax.ShapeDtypeStruct(pieces[0].shape, HALF)] + [gain_shape] * (extra > 0),
        received + [token],
        0,
        ins={group: ANY},
    )
    total, gains = totals[0], list(totals[1:])
    riding = int(extra > 0 and groups == 2 and rows == 4)
    carry = shifted(total if riding else total[:size], group)
    if riding:
        for offset in (0, group):
            pairs = [
                (row * count + i, (row ^ 2) * count + (i ^ offset))
                for row in range(rows)
                for i in range(count)
            ]
            gains.append(lax.ppermute(gains[0], ("dp", "seq"), pairs))
    elif extra:
        gains = [tree_sum(summed_over("seq", group, gains[0]))]
        gains = [tree_sum(summed_over("dp", 2, gains[0]))]
    distance = 1
    while distance < groups - 1:
        moved = shifted(carry, distance * group)
        kernel = part(
            carry_kernel, group, reverse, distance + (distance == 1), distance == 1
        )
        (carry,) = call(kernel, [piece], [carry, moved], 0)
        distance *= 2
    pieces, after = {}, []
    for slots in ((1,), (2,), (3, 0)):
        adding = riding if 0 in slots else 0
        inputs = [carry] + received + gains[:adding] + after
        sums = call(
            part(scan_kernel, group, orders, slots, reverse, groups <= 2, size, adding),
            [piece] * len(slots) + [gain_shape] * adding,
            inputs,
            0,
            ins={len(inputs) - 1: ANY} if after else {},
        )
        pieces.update(zip(slots, sums))
        after = [sums[0]]
    results = own_and_swapped([pieces[slot] for slot in range(group)], orders[1])
    if riding:
        gains = [sums[-1] + (gains[1] + gains[2])]
    return results, (gains[0] if gains else None)


def summed_over(axis, stride, array):
    count = lax.axis_size(axis)
    terms = [array]
    while stride < count:
        array = tree_sum(terms)
        width = 4 if count // stride % 4 == 0 else 2
        order = sorted(range(1, width), key=lambda i: i % 2)
        moved = {i: swap(array, axis, i * stride) for i in order}
        terms = [array] + [moved[i] for i in range(1, width)]
        stride *= width
    return terms


def per_device(queries, keys, values, gain, cotangent):
    q, k, v, cot = queries[0], keys[0], values[0], cotangent[0]
    rows, features = q.shape
    head = features // HEADS
    group = 4
    width = features // group
    part = functools.partial
    wide = jax.ShapeDtypeStruct((rows, features), F32)
    half = jax.ShapeDtypeStruct((rows, features), HALF)
    square = jax.ShapeDtypeStruct((rows, head), F32)
    piece = jax.ShapeDtypeStruct((width, head), HALF)
    scores_shape = jax.ShapeDtypeStruct((HEADS * rows, rows), HALF)
    gain_shape = jax.ShapeDtypeStruct((HEADS, head), F32)
    token_shape = jax.ShapeDtypeStruct((8, head), F32)
    whole = pltpu.VMEM((features, head), HALF)
    gain_row = gain.reshape(1, features)

    (first,) = call(
        part(first_state_kernel, head, 1),
        [piece],
        [pltpu.with_memory_space_constraint(a, pltpu.HBM) for a in (k, v)],
        1,
        [pltpu.VMEM((rows, width), HALF)] * 2 + [pltpu.SemaphoreType.DMA((2,))],
        ins={0: HBM, 1: HBM},
    )
    slots = (2, 3, 0)
    rest = call(
        part(state_kernel, head, slots), [piece] * 3, [k, v, first], 1, ins={2: ANY}
    )
    pieces = dict(zip(slots, rest))
    pieces[1] = first
    pieces = [pieces[slot] for slot in range(group)]
    scores, intra = call(part(local_kernel, head), [scores_shape, wide], [q, k, v], 2)
    prefix, _ = exclusive_scan(pieces, STATE_ORDERS, width, False, intra)
    message = jax.ShapeDtypeStruct((width + 2 * HEADS, head), HALF)
    sources = [q, intra, gain_row, cot]
    early, squares, inner = call(
        part(early_norm_kernel, head, STATE_ORDERS[1]),
        [wide, square, square],
        sources + prefix[:-1],
        1,
    )
    late, inverse, grad, *pieces = call(
        part(norm_kernel, head, group, NORM_ORDERS, lax.axis_size("dp")),
        [jax.ShapeDtypeStruct((rows, width), F32), square, half] + [message] * group,
        sources + [early, squares, inner, prefix[-1]],
        2,
        [pltpu.VMEM((1, features), F32), pltpu.VMEM((HEADS, head), F32)],
    )
    output, grad_query, key_part, value_part, token = call(
        part(backward_kernel, head, group),
        [half, half, wide, wide, token_shape],
        [q, k, v, scores, grad, early, late, inverse, gain_row] + prefix,
        5,
        [whole],
    )
    suffix, gain_grad = exclusive_scan(pieces, GRAD_ORDERS, width, True, token)
    gains = [gain_grad, swap(gain_grad, "dp", 1)]
    inputs = [k, v, key_part, value_part]
    outs = []
    for slots in ((0, 1), (2,), (3,)):
        last = group - 1 in slots
        at = len(inputs) + len(slots)
        results = call(
            part(final_kernel, head, slots, last),
            [half, half] + [gain_shape] * last,
            inputs + [suffix[slot] for slot in slots] + outs + (gains if last else []),
            1,
            [pltpu.VMEM((len(slots), rows, width), HALF)] * 2
            + [pltpu.SemaphoreType.DMA((2, len(slots)))]
            + [pltpu.VMEM((HEADS, head), F32), pltpu.SemaphoreType.DMA(())] * last,
            ins={at + i: HBM for i in range(len(outs))},
            out_specs={0: HBM, 1: HBM, 2: HBM},
            aliases={at + i: i for i in range(len(outs))},
        )
        outs = list(results[:2])
    grad_key, grad_value, gain_grad = results
    return (
        output[None],
        grad_query[None],
        grad_key[None],
        grad_value[None],
        gain_grad.reshape(features),
    )


def solution(mesh):
    spec = P("dp", "seq", None)
    return jax.shard_map(
        per_device,
        mesh=mesh,
        in_specs=(spec, spec, spec, P(), spec),
        out_specs=(spec, spec, spec, spec, P()),
        check_vma=False,
    )
```

```python
import functools

import jax
import jax.numpy as jnp
from jax import lax
from jax.experimental import pallas as pl
from jax.experimental.pallas import tpu as pltpu
from jax.sharding import PartitionSpec as P

HEADS = 16

EPSILON = 1e-06

F32 = jnp.float32
HALF = jnp.bfloat16


def dot(lhs, rhs, lhs_dim, rhs_dim):
    return lax.dot_general(
        lhs, rhs, (((lhs_dim,), (rhs_dim,)), ((), ())), preferred_element_type=F32
    )


def causal(size):
    rows = lax.broadcasted_iota(jnp.int32, (size, size), 0)
    columns = lax.broadcasted_iota(jnp.int32, (size, size), 1)
    return rows >= columns


def member_of(group):
    return lax.rem(lax.axis_index("seq"), group)


STATE_ORDERS = (
    (((0, 1, 2, 3), (0, 2, 1, 3)), ((0, 1, 2, 3), (0, 2, 1, 3))),
    (((0, 2, 1, 3), (0, 1, 2, 3)), ((0, 2, 1, 3), (0, 1, 2, 3))),
)
GRAD_ORDERS = (
    (((0, 1, 2, 3), (0, 2, 1, 3)), ((0, 3, 1, 2), (0, 3, 1, 2))),
    (((0, 3, 1, 2), (0, 1, 2, 3)), ((0, 3, 1, 2), (0, 1, 2, 3))),
)
NORM_ORDERS = (STATE_ORDERS[1], GRAD_ORDERS[0])


def picked(table, group):
    (first, second), (third, fourth) = table
    if first == second == third == fourth:
        return first
    odd = lax.rem(lax.axis_index("dp"), 2) == 1
    odd_group = lax.rem(lax.axis_index("seq") // group, 2) == 1
    return jnp.where(
        odd_group, jnp.where(odd, fourth, third), jnp.where(odd, second, first)
    )


def partner_of(order, slot):
    group = len(order[0][0])
    offset = picked([[row[slot] for row in rows] for rows in order], group)
    return member_of(group) ^ offset


def block_at(index, size):
    return pl.ds(pl.multiple_of(index * size, size), size)


def gathered(order, piece_refs, size, whole_ref):
    for j, ref in enumerate(piece_refs):
        whole_ref[block_at(partner_of(order, j), size), :] = ref[0:size, :]


def columns(first, count):
    return slice(first, first + count)


def first_state_kernel(head, slot, k_ref, v_ref, piece_ref, k_buffer, v_buffer, arrived):
    width = piece_ref.shape[0]
    source = block_at(partner_of(STATE_ORDERS[0], slot), width)
    copies = [
        pltpu.make_async_copy(k_ref.at[:, source], k_buffer, arrived.at[0]),
        pltpu.make_async_copy(v_ref.at[:, source], v_buffer, arrived.at[1]),
    ]
    for copy in copies:
        copy.start()
    for copy in copies:
        copy.wait()
    for i in range(width // head):
        part = columns(i * head, head)
        piece_ref[part, :] = dot(k_buffer[:, part], v_buffer[:, part], 0, 0).astype(HALF)


def state_kernel(head, slots, k_ref, v_ref, token_ref, *piece_refs):
    del token_ref
    for slot, piece_ref in zip(slots, piece_refs):
        width = piece_ref.shape[0]
        for i in range(width // head):
            part = features_at(STATE_ORDERS[0], slot, i, width, head)
            piece_ref[columns(i * head, head), :] = dot(
                k_ref[:, part], v_ref[:, part], 0, 0
            ).astype(HALF)


def local_kernel(head, q_ref, k_ref, v_ref, scores_ref, intra_ref):
    rows = q_ref.shape[0]
    mask = causal(rows)
    scaling = head ** (-0.5)
    for h in range(HEADS):
        part = columns(h * head, head)
        scores = dot(q_ref[:, part], k_ref[:, part], 1, 1) * scaling
        scores = jnp.where(mask, scores, 0.0).astype(HALF)
        scores_ref[columns(h * rows, rows), :] = scores
        intra_ref[:, part] = dot(scores, v_ref[:, part], 1, 0)


def features_at(order, slot, i, width, head):
    start = partner_of(order, slot) * width + i * head
    return pl.ds(pl.multiple_of(start, head), head)


def attend(head, order, slot, refs, prefix_ref, attended_ref, at, squares, inner):
    q_ref, intra_ref, gain_ref, cot_ref = refs
    scaling = head ** (-0.5)
    width = prefix_ref.shape[0]
    for i in range(width // head):
        part = features_at(order, slot, i, width, head)
        prefix = prefix_ref[columns(i * head, head), :]
        attended = intra_ref[:, part] + scaling * dot(q_ref[:, part], prefix, 1, 0)
        attended_ref[:, part if at is None else columns(i * head, head)] = attended
        scaled = cot_ref[:, part].astype(F32) * gain_ref[:, part]
        squares += attended * attended
        inner += scaled * attended
    return squares, inner


def early_norm_kernel(head, order, *refs):
    prefix_refs, (attended_ref, squares_ref, inner_ref) = refs[4:-3], refs[-3:]
    squares = jnp.zeros(squares_ref.shape, F32)
    inner = jnp.zeros(squares_ref.shape, F32)
    for slot, prefix_ref in enumerate(prefix_refs):
        squares, inner = attend(
            head, order, slot, refs[:4], prefix_ref, attended_ref, None, squares, inner
        )
    squares_ref[...] = squares
    inner_ref[...] = inner


def norm_kernel(head, group, orders, replicas, *refs):
    q_ref, _, gain_ref, cot_ref = refs[:4]
    early_ref, squares_ref, inner_ref, prefix_ref = refs[4:8]
    late_ref, inverse_ref, grad_ref = refs[8:11]
    piece_refs = refs[11 : 11 + group]
    gain_grad_ref, gain_rows_ref = refs[11 + group :]
    features = q_ref.shape[1]
    width = features // group
    squares, inner = attend(
        head,
        orders[0],
        group - 1,
        refs[:4],
        prefix_ref,
        late_ref,
        0,
        squares_ref[...],
        inner_ref[...],
    )
    inverse = lax.rsqrt(
        jnp.sum(squares, axis=1, keepdims=True) * (1.0 / features) + EPSILON
    )
    inner_mean = jnp.sum(inner, axis=1, keepdims=True) * (1.0 / features) * inverse
    inverse_ref[...] = jnp.broadcast_to(inverse, inverse_ref.shape)
    scaling = head ** (-0.5)
    for slot in range(group):
        for i in range(width // head):
            part = features_at(orders[1], slot, i, width, head)
            local = columns(i * head, head)
            late = [
                [int(row[slot] == before[-1]) for before, row in zip(*rows)]
                for rows in zip(*orders)
            ]
            if sum(late[0] + late[1]) in (0, 4):
                attended = late_ref[:, local] if late[0][0] else early_ref[:, part]
            else:
                attended = jnp.where(
                    picked(late, group) == 1, late_ref[:, local], early_ref[:, part]
                )
            normalized = attended * inverse
            upstream = cot_ref[:, part].astype(F32)
            gain_grad_ref[:, part] = jnp.sum(
                upstream * normalized, axis=0, keepdims=True
            ) * (1.0 / replicas)
            scaled = upstream * gain_ref[:, part]
            grad = ((scaled - normalized * inner_mean) * inverse).astype(HALF)
            grad_ref[:, part] = grad
            piece_refs[slot][local, :] = (
                scaling * dot(q_ref[:, part], grad, 0, 0)
            ).astype(HALF)
    for h in range(HEADS):
        gain_rows_ref[h : h + 1, :] = gain_grad_ref[:, columns(h * head, head)]
    for ref in piece_refs:
        put_wide_rows(ref, width, gain_rows_ref[...])


def backward_kernel(head, group, *refs):
    q_ref, k_ref, v_ref, scores_ref, grad_ref = refs[:5]
    early_ref, late_ref, inverse_ref, gain_ref = refs[5:9]
    prefix_refs = refs[9 : 9 + group]
    out_ref, grad_query_ref, key_part_ref, value_part_ref, token_ref = refs[
        9 + group : 14 + group
    ]
    whole_ref = refs[14 + group]
    rows = q_ref.shape[0]
    mask = causal(rows)
    scaling = head ** (-0.5)
    gathered(STATE_ORDERS[1], prefix_refs, prefix_refs[0].shape[0], whole_ref)
    inverse = inverse_ref[...]
    width = late_ref.shape[1]
    for slot in range(group):
        for i in range(width // head):
            part = features_at(STATE_ORDERS[1], slot, i, width, head)
            if slot == group - 1:
                attended = late_ref[:, columns(i * head, head)]
            else:
                attended = early_ref[:, part]
            out_ref[:, part] = (gain_ref[:, part] * (attended * inverse)).astype(HALF)
    for h in range(HEADS):
        part = columns(h * head, head)
        grad = grad_ref[:, part]
        grad_scores = dot(grad, v_ref[:, part], 1, 1)
        grad_scores = jnp.where(mask, grad_scores, 0.0).astype(HALF)
        grad_query = dot(grad_scores, k_ref[:, part], 1, 0) + dot(
            grad, whole_ref[part, :], 1, 1
        )
        grad_query_ref[:, part] = (scaling * grad_query).astype(HALF)
        key_part_ref[:, part] = scaling * dot(grad_scores, q_ref[:, part], 0, 0)
        value_part_ref[:, part] = dot(
            scores_ref[columns(h * rows, rows), :], grad, 0, 0
        )
    token_ref[...] = jnp.zeros_like(token_ref)


def final_kernel(head, slots, last, *refs):
    k_ref, v_ref, key_part_ref, value_part_ref = refs[:4]
    suffix_refs = refs[4 : 4 + len(slots)]
    refs = refs[4 + len(slots) :]
    copies = []
    if last:
        gain_grad_ref, total_ref, gain_written = refs[-6], refs[-2], refs[-1]
        total_ref[...] = tree_sum([ref[...] for ref in refs[2:-8]])
        copies.append(pltpu.make_async_copy(total_ref, gain_grad_ref, gain_written))
        copies[0].start()
        out_refs, refs = refs[-8:-6], refs[-5:-2]
    else:
        out_refs, refs = refs[-5:-3], refs[-3:]
    key_buffer, value_buffer, written = refs
    width = key_buffer.shape[2]
    for n, slot in enumerate(slots):
        for i in range(width // head):
            part = features_at(GRAD_ORDERS[1], slot, i, width, head)
            local = columns(i * head, head)
            suffix = suffix_refs[n][local, :]
            key_buffer[n, :, local] = (
                key_part_ref[:, part] + dot(v_ref[:, part], suffix, 1, 1)
            ).astype(HALF)
            value_buffer[n, :, local] = (
                value_part_ref[:, part] + dot(k_ref[:, part], suffix, 1, 0)
            ).astype(HALF)
        for i, buffer in enumerate((key_buffer, value_buffer)):
            copy = pltpu.make_async_copy(
                buffer.at[n],
                out_refs[i].at[:, block_at(partner_of(GRAD_ORDERS[1], slot), width)],
                written.at[i, n],
            )
            copy.start()
            copies.append(copy)
    for copy in copies:
        copy.wait()


def tree_sum(terms):
    while len(terms) > 1:
        terms = [a + b for a, b in zip(terms[::2], terms[1::2])]
    return terms[0]


def wide_rows(ref, start):
    rows = (ref.shape[0] - start) // 2
    high = ref[columns(start, rows), :].astype(F32)
    return high + ref[columns(start + rows, rows), :].astype(F32)


def put_wide_rows(ref, start, value):
    rows = value.shape[0]
    high = value.astype(HALF)
    ref[columns(start, rows), :] = high
    ref[columns(start + rows, rows), :] = (value - high.astype(F32)).astype(HALF)


def total_kernel(size, count, *refs):
    refs, out_refs = refs[:count], refs[count + 1 :]
    total = refs[0][0:size, :].astype(F32)
    for ref in refs[1:]:
        total += ref[0:size, :].astype(F32)
    out_refs[0][0:size, :] = total.astype(HALF)
    if len(out_refs) > 1:
        gain = tree_sum([wide_rows(ref, size) for ref in refs])
        put_wide_rows(out_refs[0], size, gain)
        out_refs[1][...] = wide_rows(out_refs[0], size)


def group_flag(group, reverse, distance):
    index = lax.axis_index("seq") // group
    last = lax.axis_size("seq") // group - 1
    known = index + distance <= last if reverse else index >= distance
    return jnp.where(known, 1.0, 0.0)


def carry_kernel(group, reverse, distance, first, own_ref, moved_ref, out_ref):
    own = own_ref[...].astype(F32)
    if first:
        own = own * group_flag(group, reverse, 1)
    moved = moved_ref[...].astype(F32) * group_flag(group, reverse, distance)
    out_ref[...] = (own + moved).astype(HALF)


def scan_kernel(group, orders, slots, reverse, masked, size, riding, *refs):
    sources = [partner_of(orders[0], j) for j in range(group)]
    carry = refs[0][0:size, :].astype(F32)
    if masked:
        carry = carry * group_flag(group, reverse, 1)
    blocks = [ref[0:size, :].astype(F32) for ref in refs[1 : 1 + group]]
    out_refs = refs[-len(slots) - riding :][: len(slots)]
    for slot, out_ref in zip(slots, out_refs):
        target = partner_of(orders[1], slot)
        total = carry
        for i in range(group):
            known = sources[i] > target if reverse else sources[i] < target
            total += jnp.where(known, 1.0, 0.0) * blocks[i]
        out_ref[...] = total.astype(HALF)
    if riding:
        refs[-1][...] = refs[1 + group][...] + wide_rows(refs[0], size)


VMEM = pl.BlockSpec(memory_space=pltpu.VMEM)
ANY = pl.BlockSpec(memory_space=pl.ANY)
HBM = pl.BlockSpec(memory_space=pltpu.HBM)


def call(kernel, outs, args, matmuls, scratch=(), ins=None, out_specs=None, aliases=None):
    size = sum(a.size * a.dtype.itemsize for a in args)
    size += sum(o.size * o.dtype.itemsize for o in outs)
    ins = ins or {}
    out_specs = out_specs or {}
    return pl.pallas_call(
        kernel,
        out_shape=tuple(outs),
        in_specs=[ins.get(i, VMEM) for i in range(len(args))],
        out_specs=tuple(out_specs.get(i, VMEM) for i in range(len(outs))),
        scratch_shapes=list(scratch),
        input_output_aliases=aliases or {},
        compiler_params=pltpu.CompilerParams(vmem_limit_bytes=16 * 1024 * 1024),
        cost_estimate=pl.CostEstimate(
            flops=2 * 128 * 128 * 128 * HEADS * matmuls,
            bytes_accessed=size,
            transcendentals=0,
        ),
    )(*args)


def swap(array, axis, offset):
    count = lax.axis_size(axis)
    return lax.ppermute(array, axis, [(i, i ^ offset) for i in range(count)])


def own_and_swapped(pieces, order):
    count, group = lax.axis_size("seq"), len(pieces)
    results = [pieces[0]]
    for slot in range(1, group):
        pairs = []
        for row in range(lax.axis_size("dp")):
            for i in range(count):
                offset = order[i // group % 2][row % 2][slot]
                pairs.append((row * count + i, row * count + (i ^ offset)))
        results.append(lax.ppermute(pieces[slot], ("dp", "seq"), pairs))
    return results


def exclusive_scan(pieces, orders, size, reverse, token):
    group = len(pieces)
    count, rows = lax.axis_size("seq"), lax.axis_size("dp")
    groups = count // group
    part = functools.partial
    lanes = pieces[0].shape[1]
    extra = pieces[0].shape[0] - size
    piece = jax.ShapeDtypeStruct((size, lanes), HALF)
    gain_shape = jax.ShapeDtypeStruct((extra // 2, lanes), F32)

    def shifted(array, distance):
        step = -distance if reverse else distance
        pairs = [(i, (i + step) % count) for i in range(count)]
        return lax.ppermute(array, "seq", pairs)

    received = own_and_swapped(pieces, orders[0])
    totals = call(
        part(total_kernel, size, group),
        [jax.ShapeDtypeStruct(pieces[0].shape, HALF)] + [gain_shape] * (extra > 0),
        received + [token],
        0,
        ins={group: ANY},
    )
    total, gains = totals[0], list(totals[1:])
    riding = int(extra > 0 and groups == 2 and rows == 4)
    carry = shifted(total if riding else total[:size], group)
    if riding:
        for offset in (0, group):
            pairs = [
                (row * count + i, (row ^ 2) * count + (i ^ offset))
                for row in range(rows)
                for i in range(count)
            ]
            gains.append(lax.ppermute(gains[0], ("dp", "seq"), pairs))
    elif extra:
        gains = [tree_sum(summed_over("seq", group, gains[0]))]
        gains = [tree_sum(summed_over("dp", 2, gains[0]))]
    distance = 1
    while distance < groups - 1:
        moved = shifted(carry, distance * group)
        kernel = part(
            carry_kernel, group, reverse, distance + (distance == 1), distance == 1
        )
        (carry,) = call(kernel, [piece], [carry, moved], 0)
        distance *= 2
    pieces, after = {}, []
    for slots in ((1,), (2,), (3, 0)):
        adding = riding if 0 in slots else 0
        inputs = [carry] + received + gains[:adding] + after
        sums = call(
            part(scan_kernel, group, orders, slots, reverse, groups <= 2, size, adding),
            [piece] * len(slots) + [gain_shape] * adding,
            inputs,
            0,
            ins={len(inputs) - 1: ANY} if after else {},
        )
        pieces.update(zip(slots, sums))
        after = [sums[0]]
    results = own_and_swapped([pieces[slot] for slot in range(group)], orders[1])
    if riding:
        gains = [sums[-1] + (gains[1] + gains[2])]
    return results, (gains[0] if gains else None)


def summed_over(axis, stride, array):
    count = lax.axis_size(axis)
    terms = [array]
    while stride < count:
        array = tree_sum(terms)
        width = 4 if count // stride % 4 == 0 else 2
        order = sorted(range(1, width), key=lambda i: i % 2)
        moved = {i: swap(array, axis, i * stride) for i in order}
        terms = [array] + [moved[i] for i in range(1, width)]
        stride *= width
    return terms


def per_device(queries, keys, values, gain, cotangent):
    q, k, v, cot = queries[0], keys[0], values[0], cotangent[0]
    rows, features = q.shape
    head = features // HEADS
    group = 4
    width = features // group
    part = functools.partial
    wide = jax.ShapeDtypeStruct((rows, features), F32)
    half = jax.ShapeDtypeStruct((rows, features), HALF)
    square = jax.ShapeDtypeStruct((rows, head), F32)
    piece = jax.ShapeDtypeStruct((width, head), HALF)
    scores_shape = jax.ShapeDtypeStruct((HEADS * rows, rows), HALF)
    gain_shape = jax.ShapeDtypeStruct((HEADS, head), F32)
    token_shape = jax.ShapeDtypeStruct((8, head), F32)
    whole = pltpu.VMEM((features, head), HALF)
    gain_row = gain.reshape(1, features)

    (first,) = call(
        part(first_state_kernel, head, 1),
        [piece],
        [pltpu.with_memory_space_constraint(a, pltpu.HBM) for a in (k, v)],
        1,
        [pltpu.VMEM((rows, width), HALF)] * 2 + [pltpu.SemaphoreType.DMA((2,))],
        ins={0: HBM, 1: HBM},
    )
    slots = (2, 3, 0)
    rest = call(
        part(state_kernel, head, slots), [piece] * 3, [k, v, first], 1, ins={2: ANY}
    )
    pieces = dict(zip(slots, rest))
    pieces[1] = first
    pieces = [pieces[slot] for slot in range(group)]
    scores, intra = call(part(local_kernel, head), [scores_shape, wide], [q, k, v], 2)
    prefix, _ = exclusive_scan(pieces, STATE_ORDERS, width, False, intra)
    message = jax.ShapeDtypeStruct((width + 2 * HEADS, head), HALF)
    sources = [q, intra, gain_row, cot]
    early, squares, inner = call(
        part(early_norm_kernel, head, STATE_ORDERS[1]),
        [wide, square, square],
        sources + prefix[:-1],
        1,
    )
    late, inverse, grad, *pieces = call(
        part(norm_kernel, head, group, NORM_ORDERS, lax.axis_size("dp")),
        [jax.ShapeDtypeStruct((rows, width), F32), square, half] + [message] * group,
        sources + [early, squares, inner, prefix[-1]],
        2,
        [pltpu.VMEM((1, features), F32), pltpu.VMEM((HEADS, head), F32)],
    )
    output, grad_query, key_part, value_part, token = call(
        part(backward_kernel, head, group),
        [half, half, wide, wide, token_shape],
        [q, k, v, scores, grad, early, late, inverse, gain_row] + prefix,
        5,
        [whole],
    )
    suffix, gain_grad = exclusive_scan(pieces, GRAD_ORDERS, width, True, token)
    gains = [gain_grad, swap(gain_grad, "dp", 1)]
    inputs = [k, v, key_part, value_part]
    outs = []
    for slots in ((0, 1), (2,), (3,)):
        last = group - 1 in slots
        at = len(inputs) + len(slots)
        results = call(
            part(final_kernel, head, slots, last),
            [half, half] + [gain_shape] * last,
            inputs + [suffix[slot] for slot in slots] + outs + (gains if last else []),
            1,
            [pltpu.VMEM((len(slots), rows, width), HALF)] * 2
            + [pltpu.SemaphoreType.DMA((2, len(slots)))]
            + [pltpu.VMEM((HEADS, head), F32), pltpu.SemaphoreType.DMA(())] * last,
            ins={at + i: HBM for i in range(len(outs))},
            out_specs={0: HBM, 1: HBM, 2: HBM},
            aliases={at + i: i for i in range(len(outs))},
        )
        outs = list(results[:2])
    grad_key, grad_value, gain_grad = results
    return (
        output[None],
        grad_query[None],
        grad_key[None],
        grad_value[None],
        gain_grad.reshape(features),
    )


def solution(mesh):
    spec = P("dp", "seq", None)
    return jax.shard_map(
        per_device,
        mesh=mesh,
        in_specs=(spec, spec, spec, P(), spec),
        out_specs=(spec, spec, spec, spec, P()),
        check_vma=False,
    )
```

```python
import functools

import jax
import jax.numpy as jnp
from jax import lax
from jax.experimental import pallas as pl
from jax.experimental.pallas import tpu as pltpu
from jax.sharding import PartitionSpec as P

HEADS = 16

EPSILON = 1e-06

F32 = jnp.float32
HALF = jnp.bfloat16


def dot(lhs, rhs, lhs_dim, rhs_dim):
    return lax.dot_general(
        lhs, rhs, (((lhs_dim,), (rhs_dim,)), ((), ())), preferred_element_type=F32
    )


def causal(size):
    rows = lax.broadcasted_iota(jnp.int32, (size, size), 0)
    columns = lax.broadcasted_iota(jnp.int32, (size, size), 1)
    return rows >= columns


def member_of(group):
    return lax.rem(lax.axis_index("seq"), group)


STATE_ORDERS = (
    (((0, 1, 2, 3), (0, 2, 1, 3)), ((0, 1, 2, 3), (0, 2, 1, 3))),
    (((0, 2, 1, 3), (0, 1, 2, 3)), ((0, 2, 1, 3), (0, 1, 2, 3))),
)
GRAD_ORDERS = (
    (((0, 3, 1, 2), (0, 3, 1, 2)), ((0, 3, 1, 2), (0, 3, 1, 2))),
    (((0, 3, 1, 2), (0, 1, 2, 3)), ((0, 3, 1, 2), (0, 1, 2, 3))),
)
NORM_ORDERS = (STATE_ORDERS[1], GRAD_ORDERS[0])


def picked(table, group):
    (first, second), (third, fourth) = table
    if first == second == third == fourth:
        return first
    odd = lax.rem(lax.axis_index("dp"), 2) == 1
    odd_group = lax.rem(lax.axis_index("seq") // group, 2) == 1
    return jnp.where(
        odd_group, jnp.where(odd, fourth, third), jnp.where(odd, second, first)
    )


def partner_of(order, slot):
    group = len(order[0][0])
    offset = picked([[row[slot] for row in rows] for rows in order], group)
    return member_of(group) ^ offset


def block_at(index, size):
    return pl.ds(pl.multiple_of(index * size, size), size)


def gathered(order, piece_refs, size, whole_ref):
    for j, ref in enumerate(piece_refs):
        whole_ref[block_at(partner_of(order, j), size), :] = ref[0:size, :]


def columns(first, count):
    return slice(first, first + count)


def first_state_kernel(head, slot, k_ref, v_ref, piece_ref, k_buffer, v_buffer, arrived):
    width = piece_ref.shape[0]
    source = block_at(partner_of(STATE_ORDERS[0], slot), width)
    copies = [
        pltpu.make_async_copy(k_ref.at[:, source], k_buffer, arrived.at[0]),
        pltpu.make_async_copy(v_ref.at[:, source], v_buffer, arrived.at[1]),
    ]
    for copy in copies:
        copy.start()
    for copy in copies:
        copy.wait()
    for i in range(width // head):
        part = columns(i * head, head)
        piece_ref[part, :] = dot(k_buffer[:, part], v_buffer[:, part], 0, 0).astype(HALF)


def state_kernel(head, slots, k_ref, v_ref, token_ref, *piece_refs):
    del token_ref
    for slot, piece_ref in zip(slots, piece_refs):
        width = piece_ref.shape[0]
        for i in range(width // head):
            part = features_at(STATE_ORDERS[0], slot, i, width, head)
            piece_ref[columns(i * head, head), :] = dot(
                k_ref[:, part], v_ref[:, part], 0, 0
            ).astype(HALF)


def local_kernel(head, q_ref, k_ref, v_ref, scores_ref, intra_ref):
    rows = q_ref.shape[0]
    mask = causal(rows)
    scaling = head ** (-0.5)
    for h in range(HEADS):
        part = columns(h * head, head)
        scores = dot(q_ref[:, part], k_ref[:, part], 1, 1) * scaling
        scores = jnp.where(mask, scores, 0.0).astype(HALF)
        scores_ref[columns(h * rows, rows), :] = scores
        intra_ref[:, part] = dot(scores, v_ref[:, part], 1, 0)


def features_at(order, slot, i, width, head):
    start = partner_of(order, slot) * width + i * head
    return pl.ds(pl.multiple_of(start, head), head)


def attend(head, order, slot, refs, prefix_ref, attended_ref, at, squares, inner):
    q_ref, intra_ref, gain_ref, cot_ref = refs
    scaling = head ** (-0.5)
    width = prefix_ref.shape[0]
    for i in range(width // head):
        part = features_at(order, slot, i, width, head)
        prefix = prefix_ref[columns(i * head, head), :]
        attended = intra_ref[:, part] + scaling * dot(q_ref[:, part], prefix, 1, 0)
        attended_ref[:, part if at is None else columns(i * head, head)] = attended
        scaled = cot_ref[:, part].astype(F32) * gain_ref[:, part]
        squares += attended * attended
        inner += scaled * attended
    return squares, inner


def early_norm_kernel(head, order, *refs):
    prefix_refs, (attended_ref, squares_ref, inner_ref) = refs[4:-3], refs[-3:]
    squares = jnp.zeros(squares_ref.shape, F32)
    inner = jnp.zeros(squares_ref.shape, F32)
    for slot, prefix_ref in enumerate(prefix_refs):
        squares, inner = attend(
            head, order, slot, refs[:4], prefix_ref, attended_ref, None, squares, inner
        )
    squares_ref[...] = squares
    inner_ref[...] = inner


def norm_kernel(head, group, orders, replicas, *refs):
    q_ref, _, gain_ref, cot_ref = refs[:4]
    early_ref, squares_ref, inner_ref, prefix_ref = refs[4:8]
    late_ref, inverse_ref, grad_ref = refs[8:11]
    piece_refs = refs[11 : 11 + group]
    gain_grad_ref, gain_rows_ref = refs[11 + group :]
    features = q_ref.shape[1]
    width = features // group
    squares, inner = attend(
        head,
        orders[0],
        group - 1,
        refs[:4],
        prefix_ref,
        late_ref,
        0,
        squares_ref[...],
        inner_ref[...],
    )
    inverse = lax.rsqrt(
        jnp.sum(squares, axis=1, keepdims=True) * (1.0 / features) + EPSILON
    )
    inner_mean = jnp.sum(inner, axis=1, keepdims=True) * (1.0 / features) * inverse
    inverse_ref[...] = jnp.broadcast_to(inverse, inverse_ref.shape)
    scaling = head ** (-0.5)
    for slot in range(group):
        for i in range(width // head):
            part = features_at(orders[1], slot, i, width, head)
            local = columns(i * head, head)
            late = [
                [int(row[slot] == before[-1]) for before, row in zip(*rows)]
                for rows in zip(*orders)
            ]
            if sum(late[0] + late[1]) in (0, 4):
                attended = late_ref[:, local] if late[0][0] else early_ref[:, part]
            else:
                attended = jnp.where(
                    picked(late, group) == 1, late_ref[:, local], early_ref[:, part]
                )
            normalized = attended * inverse
            upstream = cot_ref[:, part].astype(F32)
            gain_grad_ref[:, part] = jnp.sum(
                upstream * normalized, axis=0, keepdims=True
            ) * (1.0 / replicas)
            scaled = upstream * gain_ref[:, part]
            grad = ((scaled - normalized * inner_mean) * inverse).astype(HALF)
            grad_ref[:, part] = grad
            piece_refs[slot][local, :] = (
                scaling * dot(q_ref[:, part], grad, 0, 0)
            ).astype(HALF)
    for h in range(HEADS):
        gain_rows_ref[h : h + 1, :] = gain_grad_ref[:, columns(h * head, head)]
    for ref in piece_refs:
        put_wide_rows(ref, width, gain_rows_ref[...])


def backward_kernel(head, group, *refs):
    q_ref, k_ref, v_ref, scores_ref, grad_ref = refs[:5]
    early_ref, late_ref, inverse_ref, gain_ref = refs[5:9]
    prefix_refs = refs[9 : 9 + group]
    out_ref, grad_query_ref, key_part_ref, value_part_ref, token_ref = refs[
        9 + group : 14 + group
    ]
    whole_ref = refs[14 + group]
    rows = q_ref.shape[0]
    mask = causal(rows)
    scaling = head ** (-0.5)
    gathered(STATE_ORDERS[1], prefix_refs, prefix_refs[0].shape[0], whole_ref)
    inverse = inverse_ref[...]
    width = late_ref.shape[1]
    for slot in range(group):
        for i in range(width // head):
            part = features_at(STATE_ORDERS[1], slot, i, width, head)
            if slot == group - 1:
                attended = late_ref[:, columns(i * head, head)]
            else:
                attended = early_ref[:, part]
            out_ref[:, part] = (gain_ref[:, part] * (attended * inverse)).astype(HALF)
    for h in range(HEADS):
        part = columns(h * head, head)
        grad = grad_ref[:, part]
        grad_scores = dot(grad, v_ref[:, part], 1, 1)
        grad_scores = jnp.where(mask, grad_scores, 0.0).astype(HALF)
        grad_query = dot(grad_scores, k_ref[:, part], 1, 0) + dot(
            grad, whole_ref[part, :], 1, 1
        )
        grad_query_ref[:, part] = (scaling * grad_query).astype(HALF)
        key_part_ref[:, part] = scaling * dot(grad_scores, q_ref[:, part], 0, 0)
        value_part_ref[:, part] = dot(
            scores_ref[columns(h * rows, rows), :], grad, 0, 0
        )
    token_ref[...] = jnp.zeros_like(token_ref)


def final_kernel(head, slots, last, *refs):
    k_ref, v_ref, key_part_ref, value_part_ref = refs[:4]
    suffix_refs = refs[4 : 4 + len(slots)]
    refs = refs[4 + len(slots) :]
    copies = []
    if last:
        gain_grad_ref, total_ref, gain_written = refs[-6], refs[-2], refs[-1]
        total_ref[...] = tree_sum([ref[...] for ref in refs[2:-8]])
        copies.append(pltpu.make_async_copy(total_ref, gain_grad_ref, gain_written))
        copies[0].start()
        out_refs, refs = refs[-8:-6], refs[-5:-2]
    else:
        out_refs, refs = refs[-5:-3], refs[-3:]
    key_buffer, value_buffer, written = refs
    width = key_buffer.shape[2]
    for n, slot in enumerate(slots):
        for i in range(width // head):
            part = features_at(GRAD_ORDERS[1], slot, i, width, head)
            local = columns(i * head, head)
            suffix = suffix_refs[n][local, :]
            key_buffer[n, :, local] = (
                key_part_ref[:, part] + dot(v_ref[:, part], suffix, 1, 1)
            ).astype(HALF)
            value_buffer[n, :, local] = (
                value_part_ref[:, part] + dot(k_ref[:, part], suffix, 1, 0)
            ).astype(HALF)
        for i, buffer in enumerate((key_buffer, value_buffer)):
            copy = pltpu.make_async_copy(
                buffer.at[n],
                out_refs[i].at[:, block_at(partner_of(GRAD_ORDERS[1], slot), width)],
                written.at[i, n],
            )
            copy.start()
            copies.append(copy)
    for copy in copies:
        copy.wait()


def tree_sum(terms):
    while len(terms) > 1:
        terms = [a + b for a, b in zip(terms[::2], terms[1::2])]
    return terms[0]


def wide_rows(ref, start):
    rows = (ref.shape[0] - start) // 2
    high = ref[columns(start, rows), :].astype(F32)
    return high + ref[columns(start + rows, rows), :].astype(F32)


def put_wide_rows(ref, start, value):
    rows = value.shape[0]
    high = value.astype(HALF)
    ref[columns(start, rows), :] = high
    ref[columns(start + rows, rows), :] = (value - high.astype(F32)).astype(HALF)


def total_kernel(size, count, *refs):
    refs, out_refs = refs[:count], refs[count + 1 :]
    total = refs[0][0:size, :].astype(F32)
    for ref in refs[1:]:
        total += ref[0:size, :].astype(F32)
    out_refs[0][0:size, :] = total.astype(HALF)
    if len(out_refs) > 1:
        gain = tree_sum([wide_rows(ref, size) for ref in refs])
        put_wide_rows(out_refs[0], size, gain)
        out_refs[1][...] = wide_rows(out_refs[0], size)


def group_flag(group, reverse, distance):
    index = lax.axis_index("seq") // group
    last = lax.axis_size("seq") // group - 1
    known = index + distance <= last if reverse else index >= distance
    return jnp.where(known, 1.0, 0.0)


def carry_kernel(group, reverse, distance, first, own_ref, moved_ref, out_ref):
    own = own_ref[...].astype(F32)
    if first:
        own = own * group_flag(group, reverse, 1)
    moved = moved_ref[...].astype(F32) * group_flag(group, reverse, distance)
    out_ref[...] = (own + moved).astype(HALF)


def scan_kernel(group, orders, slots, reverse, masked, size, riding, *refs):
    sources = [partner_of(orders[0], j) for j in range(group)]
    carry = refs[0][0:size, :].astype(F32)
    if masked:
        carry = carry * group_flag(group, reverse, 1)
    blocks = [ref[0:size, :].astype(F32) for ref in refs[1 : 1 + group]]
    out_refs = refs[-len(slots) - riding :][: len(slots)]
    for slot, out_ref in zip(slots, out_refs):
        target = partner_of(orders[1], slot)
        total = carry
        for i in range(group):
            known = sources[i] > target if reverse else sources[i] < target
            total += jnp.where(known, 1.0, 0.0) * blocks[i]
        out_ref[...] = total.astype(HALF)
    if riding:
        refs[-1][...] = refs[1 + group][...] + wide_rows(refs[0], size)


VMEM = pl.BlockSpec(memory_space=pltpu.VMEM)
ANY = pl.BlockSpec(memory_space=pl.ANY)
HBM = pl.BlockSpec(memory_space=pltpu.HBM)


def call(kernel, outs, args, matmuls, scratch=(), ins=None, out_specs=None, aliases=None):
    size = sum(a.size * a.dtype.itemsize for a in args)
    size += sum(o.size * o.dtype.itemsize for o in outs)
    ins = ins or {}
    out_specs = out_specs or {}
    return pl.pallas_call(
        kernel,
        out_shape=tuple(outs),
        in_specs=[ins.get(i, VMEM) for i in range(len(args))],
        out_specs=tuple(out_specs.get(i, VMEM) for i in range(len(outs))),
        scratch_shapes=list(scratch),
        input_output_aliases=aliases or {},
        compiler_params=pltpu.CompilerParams(vmem_limit_bytes=16 * 1024 * 1024),
        cost_estimate=pl.CostEstimate(
            flops=2 * 128 * 128 * 128 * HEADS * matmuls,
            bytes_accessed=size,
            transcendentals=0,
        ),
    )(*args)


def swap(array, axis, offset):
    count = lax.axis_size(axis)
    return lax.ppermute(array, axis, [(i, i ^ offset) for i in range(count)])


def own_and_swapped(pieces, order):
    count, group = lax.axis_size("seq"), len(pieces)
    results = [pieces[0]]
    for slot in range(1, group):
        pairs = []
        for row in range(lax.axis_size("dp")):
            for i in range(count):
                offset = order[i // group % 2][row % 2][slot]
                pairs.append((row * count + i, row * count + (i ^ offset)))
        results.append(lax.ppermute(pieces[slot], ("dp", "seq"), pairs))
    return results


def exclusive_scan(pieces, orders, size, reverse, token):
    group = len(pieces)
    count, rows = lax.axis_size("seq"), lax.axis_size("dp")
    groups = count // group
    part = functools.partial
    lanes = pieces[0].shape[1]
    extra = pieces[0].shape[0] - size
    piece = jax.ShapeDtypeStruct((size, lanes), HALF)
    gain_shape = jax.ShapeDtypeStruct((extra // 2, lanes), F32)

    def shifted(array, distance):
        step = -distance if reverse else distance
        pairs = [(i, (i + step) % count) for i in range(count)]
        return lax.ppermute(array, "seq", pairs)

    received = own_and_swapped(pieces, orders[0])
    totals = call(
        part(total_kernel, size, group),
        [jax.ShapeDtypeStruct(pieces[0].shape, HALF)] + [gain_shape] * (extra > 0),
        received + [token],
        0,
        ins={group: ANY},
    )
    total, gains = totals[0], list(totals[1:])
    riding = int(extra > 0 and groups == 2 and rows == 4)
    carry = shifted(total if riding else total[:size], group)
    if riding:
        for offset in (0, group):
            pairs = [
                (row * count + i, (row ^ 2) * count + (i ^ offset))
                for row in range(rows)
                for i in range(count)
            ]
            gains.append(lax.ppermute(gains[0], ("dp", "seq"), pairs))
    elif extra:
        gains = [tree_sum(summed_over("seq", group, gains[0]))]
        gains = [tree_sum(summed_over("dp", 2, gains[0]))]
    distance = 1
    while distance < groups - 1:
        moved = shifted(carry, distance * group)
        kernel = part(
            carry_kernel, group, reverse, distance + (distance == 1), distance == 1
        )
        (carry,) = call(kernel, [piece], [carry, moved], 0)
        distance *= 2
    pieces, after = {}, []
    for slots in ((1,), (2,), (3,), (0,)):
        adding = riding if 0 in slots else 0
        inputs = [carry] + received + gains[:adding] + after
        sums = call(
            part(scan_kernel, group, orders, slots, reverse, groups <= 2, size, adding),
            [piece] * len(slots) + [gain_shape] * adding,
            inputs,
            0,
            ins={len(inputs) - 1: ANY} if after else {},
        )
        pieces.update(zip(slots, sums))
        after = [sums[0]]
    results = own_and_swapped([pieces[slot] for slot in range(group)], orders[1])
    if riding:
        gains = [sums[-1] + (gains[1] + gains[2])]
    return results, (gains[0] if gains else None)


def summed_over(axis, stride, array):
    count = lax.axis_size(axis)
    terms = [array]
    while stride < count:
        array = tree_sum(terms)
        width = 4 if count // stride % 4 == 0 else 2
        order = sorted(range(1, width), key=lambda i: i % 2)
        moved = {i: swap(array, axis, i * stride) for i in order}
        terms = [array] + [moved[i] for i in range(1, width)]
        stride *= width
    return terms


def per_device(queries, keys, values, gain, cotangent):
    q, k, v, cot = queries[0], keys[0], values[0], cotangent[0]
    rows, features = q.shape
    head = features // HEADS
    group = 4
    width = features // group
    part = functools.partial
    wide = jax.ShapeDtypeStruct((rows, features), F32)
    half = jax.ShapeDtypeStruct((rows, features), HALF)
    square = jax.ShapeDtypeStruct((rows, head), F32)
    piece = jax.ShapeDtypeStruct((width, head), HALF)
    scores_shape = jax.ShapeDtypeStruct((HEADS * rows, rows), HALF)
    gain_shape = jax.ShapeDtypeStruct((HEADS, head), F32)
    token_shape = jax.ShapeDtypeStruct((8, head), F32)
    whole = pltpu.VMEM((features, head), HALF)
    gain_row = gain.reshape(1, features)

    (first,) = call(
        part(first_state_kernel, head, 1),
        [piece],
        [pltpu.with_memory_space_constraint(a, pltpu.HBM) for a in (k, v)],
        1,
        [pltpu.VMEM((rows, width), HALF)] * 2 + [pltpu.SemaphoreType.DMA((2,))],
        ins={0: HBM, 1: HBM},
    )
    slots = (2, 3, 0)
    rest = call(
        part(state_kernel, head, slots), [piece] * 3, [k, v, first], 1, ins={2: ANY}
    )
    pieces = dict(zip(slots, rest))
    pieces[1] = first
    pieces = [pieces[slot] for slot in range(group)]
    scores, intra = call(part(local_kernel, head), [scores_shape, wide], [q, k, v], 2)
    prefix, _ = exclusive_scan(pieces, STATE_ORDERS, width, False, intra)
    message = jax.ShapeDtypeStruct((width + 2 * HEADS, head), HALF)
    sources = [q, intra, gain_row, cot]
    early, squares, inner = call(
        part(early_norm_kernel, head, STATE_ORDERS[1]),
        [wide, square, square],
        sources + prefix[:-1],
        1,
    )
    late, inverse, grad, *pieces = call(
        part(norm_kernel, head, group, NORM_ORDERS, lax.axis_size("dp")),
        [jax.ShapeDtypeStruct((rows, width), F32), square, half] + [message] * group,
        sources + [early, squares, inner, prefix[-1]],
        2,
        [pltpu.VMEM((1, features), F32), pltpu.VMEM((HEADS, head), F32)],
    )
    output, grad_query, key_part, value_part, token = call(
        part(backward_kernel, head, group),
        [half, half, wide, wide, token_shape],
        [q, k, v, scores, grad, early, late, inverse, gain_row] + prefix,
        5,
        [whole],
    )
    suffix, gain_grad = exclusive_scan(pieces, GRAD_ORDERS, width, True, token)
    gains = [gain_grad, swap(gain_grad, "dp", 1)]
    inputs = [k, v, key_part, value_part]
    outs = []
    for slots in ((0, 1), (2, 3)):
        last = group - 1 in slots
        at = len(inputs) + len(slots)
        results = call(
            part(final_kernel, head, slots, last),
            [half, half] + [gain_shape] * last,
            inputs + [suffix[slot] for slot in slots] + outs + (gains if last else []),
            1,
            [pltpu.VMEM((len(slots), rows, width), HALF)] * 2
            + [pltpu.SemaphoreType.DMA((2, len(slots)))]
            + [pltpu.VMEM((HEADS, head), F32), pltpu.SemaphoreType.DMA(())] * last,
            ins={at + i: HBM for i in range(len(outs))},
            out_specs={0: HBM, 1: HBM, 2: HBM},
            aliases={at + i: i for i in range(len(outs))},
        )
        outs = list(results[:2])
    grad_key, grad_value, gain_grad = results
    return (
        output[None],
        grad_query[None],
        grad_key[None],
        grad_value[None],
        gain_grad.reshape(features),
    )


def solution(mesh):
    spec = P("dp", "seq", None)
    return jax.shard_map(
        per_device,
        mesh=mesh,
        in_specs=(spec, spec, spec, P(), spec),
        out_specs=(spec, spec, spec, spec, P()),
        check_vma=False,
    )
```

```python
import functools

import jax
import jax.numpy as jnp
from jax import lax
from jax.experimental import pallas as pl
from jax.experimental.pallas import tpu as pltpu
from jax.sharding import PartitionSpec as P

HEADS = 16

EPSILON = 1e-06

F32 = jnp.float32
HALF = jnp.bfloat16


def dot(lhs, rhs, lhs_dim, rhs_dim):
    return lax.dot_general(
        lhs, rhs, (((lhs_dim,), (rhs_dim,)), ((), ())), preferred_element_type=F32
    )


def causal(size):
    rows = lax.broadcasted_iota(jnp.int32, (size, size), 0)
    columns = lax.broadcasted_iota(jnp.int32, (size, size), 1)
    return rows >= columns


def member_of(group):
    return lax.rem(lax.axis_index("seq"), group)


STATE_ORDERS = (((0, 1, 2, 3), (0, 2, 1, 3)), ((0, 2, 1, 3), (0, 1, 2, 3)))
GRAD_ORDERS = (((0, 3, 1, 2), (0, 3, 1, 2)), ((0, 3, 1, 2), (0, 1, 2, 3)))
NORM_ORDERS = (STATE_ORDERS[1], GRAD_ORDERS[0])


def partner_of(order, slot):
    even, odd = order[0][slot], order[1][slot]
    offset = even
    if even != odd:
        offset = jnp.where(lax.rem(lax.axis_index("dp"), 2) == 1, odd, even)
    return member_of(len(order[0])) ^ offset


def block_at(index, size):
    return pl.ds(pl.multiple_of(index * size, size), size)


def gathered(order, piece_refs, size, whole_ref):
    for j, ref in enumerate(piece_refs):
        whole_ref[block_at(partner_of(order, j), size), :] = ref[0:size, :]


def columns(first, count):
    return slice(first, first + count)


def first_state_kernel(head, slot, k_ref, v_ref, piece_ref, k_buffer, v_buffer, arrived):
    width = piece_ref.shape[0]
    source = block_at(partner_of(STATE_ORDERS[0], slot), width)
    copies = [
        pltpu.make_async_copy(k_ref.at[:, source], k_buffer, arrived.at[0]),
        pltpu.make_async_copy(v_ref.at[:, source], v_buffer, arrived.at[1]),
    ]
    for copy in copies:
        copy.start()
    for copy in copies:
        copy.wait()
    for i in range(width // head):
        part = columns(i * head, head)
        piece_ref[part, :] = dot(k_buffer[:, part], v_buffer[:, part], 0, 0).astype(HALF)


def state_kernel(head, slots, k_ref, v_ref, token_ref, *piece_refs):
    del token_ref
    for slot, piece_ref in zip(slots, piece_refs):
        width = piece_ref.shape[0]
        for i in range(width // head):
            part = features_at(STATE_ORDERS[0], slot, i, width, head)
            piece_ref[columns(i * head, head), :] = dot(
                k_ref[:, part], v_ref[:, part], 0, 0
            ).astype(HALF)


def local_kernel(head, q_ref, k_ref, v_ref, scores_ref, intra_ref):
    rows = q_ref.shape[0]
    mask = causal(rows)
    scaling = head ** (-0.5)
    for h in range(HEADS):
        part = columns(h * head, head)
        scores = dot(q_ref[:, part], k_ref[:, part], 1, 1) * scaling
        scores = jnp.where(mask, scores, 0.0).astype(HALF)
        scores_ref[columns(h * rows, rows), :] = scores
        intra_ref[:, part] = dot(scores, v_ref[:, part], 1, 0)


def features_at(order, slot, i, width, head):
    start = partner_of(order, slot) * width + i * head
    return pl.ds(pl.multiple_of(start, head), head)


def attend(head, order, slot, refs, prefix_ref, attended_ref, at, squares, inner):
    q_ref, intra_ref, gain_ref, cot_ref = refs
    scaling = head ** (-0.5)
    width = prefix_ref.shape[0]
    for i in range(width // head):
        part = features_at(order, slot, i, width, head)
        prefix = prefix_ref[columns(i * head, head), :]
        attended = intra_ref[:, part] + scaling * dot(q_ref[:, part], prefix, 1, 0)
        attended_ref[:, part if at is None else columns(i * head, head)] = attended
        scaled = cot_ref[:, part].astype(F32) * gain_ref[:, part]
        squares += attended * attended
        inner += scaled * attended
    return squares, inner


def early_norm_kernel(head, order, *refs):
    prefix_refs, (attended_ref, squares_ref, inner_ref) = refs[4:-3], refs[-3:]
    squares = jnp.zeros(squares_ref.shape, F32)
    inner = jnp.zeros(squares_ref.shape, F32)
    for slot, prefix_ref in enumerate(prefix_refs):
        squares, inner = attend(
            head, order, slot, refs[:4], prefix_ref, attended_ref, None, squares, inner
        )
    squares_ref[...] = squares
    inner_ref[...] = inner


def norm_kernel(head, group, orders, replicas, *refs):
    q_ref, _, gain_ref, cot_ref = refs[:4]
    early_ref, squares_ref, inner_ref, prefix_ref = refs[4:8]
    late_ref, inverse_ref, grad_ref = refs[8:11]
    piece_refs = refs[11 : 11 + group]
    gain_grad_ref, gain_rows_ref = refs[11 + group :]
    features = q_ref.shape[1]
    width = features // group
    odd = lax.rem(lax.axis_index("dp"), 2) == 1
    squares, inner = attend(
        head,
        orders[0],
        group - 1,
        refs[:4],
        prefix_ref,
        late_ref,
        0,
        squares_ref[...],
        inner_ref[...],
    )
    inverse = lax.rsqrt(
        jnp.sum(squares, axis=1, keepdims=True) * (1.0 / features) + EPSILON
    )
    inner_mean = jnp.sum(inner, axis=1, keepdims=True) * (1.0 / features) * inverse
    inverse_ref[...] = jnp.broadcast_to(inverse, inverse_ref.shape)
    scaling = head ** (-0.5)
    for slot in range(group):
        for i in range(width // head):
            part = features_at(orders[1], slot, i, width, head)
            local = columns(i * head, head)
            late = [order[slot] == before[-1] for before, order in zip(*orders)]
            attended = late_ref[:, local] if late[0] else early_ref[:, part]
            if late[0] != late[1]:
                other = late_ref[:, local] if late[1] else early_ref[:, part]
                attended = jnp.where(odd, other, attended)
            normalized = attended * inverse
            upstream = cot_ref[:, part].astype(F32)
            gain_grad_ref[:, part] = jnp.sum(
                upstream * normalized, axis=0, keepdims=True
            ) * (1.0 / replicas)
            scaled = upstream * gain_ref[:, part]
            grad = ((scaled - normalized * inner_mean) * inverse).astype(HALF)
            grad_ref[:, part] = grad
            piece_refs[slot][local, :] = (
                scaling * dot(q_ref[:, part], grad, 0, 0)
            ).astype(HALF)
    for h in range(HEADS):
        gain_rows_ref[h : h + 1, :] = gain_grad_ref[:, columns(h * head, head)]
    for ref in piece_refs:
        put_wide_rows(ref, width, gain_rows_ref[...])


def backward_kernel(head, group, *refs):
    q_ref, k_ref, v_ref, scores_ref, grad_ref = refs[:5]
    early_ref, late_ref, inverse_ref, gain_ref = refs[5:9]
    prefix_refs = refs[9 : 9 + group]
    out_ref, grad_query_ref, key_part_ref, value_part_ref, token_ref = refs[
        9 + group : 14 + group
    ]
    whole_ref = refs[14 + group]
    rows = q_ref.shape[0]
    mask = causal(rows)
    scaling = head ** (-0.5)
    gathered(STATE_ORDERS[1], prefix_refs, prefix_refs[0].shape[0], whole_ref)
    inverse = inverse_ref[...]
    width = late_ref.shape[1]
    for slot in range(group):
        for i in range(width // head):
            part = features_at(STATE_ORDERS[1], slot, i, width, head)
            if slot == group - 1:
                attended = late_ref[:, columns(i * head, head)]
            else:
                attended = early_ref[:, part]
            out_ref[:, part] = (gain_ref[:, part] * (attended * inverse)).astype(HALF)
    for h in range(HEADS):
        part = columns(h * head, head)
        grad = grad_ref[:, part]
        grad_scores = dot(grad, v_ref[:, part], 1, 1)
        grad_scores = jnp.where(mask, grad_scores, 0.0).astype(HALF)
        grad_query = dot(grad_scores, k_ref[:, part], 1, 0) + dot(
            grad, whole_ref[part, :], 1, 1
        )
        grad_query_ref[:, part] = (scaling * grad_query).astype(HALF)
        key_part_ref[:, part] = scaling * dot(grad_scores, q_ref[:, part], 0, 0)
        value_part_ref[:, part] = dot(
            scores_ref[columns(h * rows, rows), :], grad, 0, 0
        )
    token_ref[...] = jnp.zeros_like(token_ref)


def final_kernel(head, slots, last, *refs):
    k_ref, v_ref, key_part_ref, value_part_ref = refs[:4]
    suffix_refs = refs[4 : 4 + len(slots)]
    refs = refs[4 + len(slots) :]
    copies = []
    if last:
        gain_grad_ref, total_ref, gain_written = refs[-6], refs[-2], refs[-1]
        total_ref[...] = tree_sum([ref[...] for ref in refs[2:-8]])
        copies.append(pltpu.make_async_copy(total_ref, gain_grad_ref, gain_written))
        copies[0].start()
        out_refs, refs = refs[-8:-6], refs[-5:-2]
    else:
        out_refs, refs = refs[-5:-3], refs[-3:]
    key_buffer, value_buffer, written = refs
    width = key_buffer.shape[2]
    for n, slot in enumerate(slots):
        for i in range(width // head):
            part = features_at(GRAD_ORDERS[1], slot, i, width, head)
            local = columns(i * head, head)
            suffix = suffix_refs[n][local, :]
            key_buffer[n, :, local] = (
                key_part_ref[:, part] + dot(v_ref[:, part], suffix, 1, 1)
            ).astype(HALF)
            value_buffer[n, :, local] = (
                value_part_ref[:, part] + dot(k_ref[:, part], suffix, 1, 0)
            ).astype(HALF)
        for i, buffer in enumerate((key_buffer, value_buffer)):
            copy = pltpu.make_async_copy(
                buffer.at[n],
                out_refs[i].at[:, block_at(partner_of(GRAD_ORDERS[1], slot), width)],
                written.at[i, n],
            )
            copy.start()
            copies.append(copy)
    for copy in copies:
        copy.wait()


def tree_sum(terms):
    while len(terms) > 1:
        terms = [a + b for a, b in zip(terms[::2], terms[1::2])]
    return terms[0]


def wide_rows(ref, start):
    rows = (ref.shape[0] - start) // 2
    high = ref[columns(start, rows), :].astype(F32)
    return high + ref[columns(start + rows, rows), :].astype(F32)


def put_wide_rows(ref, start, value):
    rows = value.shape[0]
    high = value.astype(HALF)
    ref[columns(start, rows), :] = high
    ref[columns(start + rows, rows), :] = (value - high.astype(F32)).astype(HALF)


def total_kernel(size, count, *refs):
    refs, out_refs = refs[:count], refs[count + 1 :]
    total = refs[0][0:size, :].astype(F32)
    for ref in refs[1:]:
        total += ref[0:size, :].astype(F32)
    out_refs[0][0:size, :] = total.astype(HALF)
    if len(out_refs) > 1:
        gain = tree_sum([wide_rows(ref, size) for ref in refs])
        put_wide_rows(out_refs[0], size, gain)
        out_refs[1][...] = wide_rows(out_refs[0], size)


def group_flag(group, reverse, distance):
    index = lax.axis_index("seq") // group
    last = lax.axis_size("seq") // group - 1
    known = index + distance <= last if reverse else index >= distance
    return jnp.where(known, 1.0, 0.0)


def carry_kernel(group, reverse, distance, first, own_ref, moved_ref, out_ref):
    own = own_ref[...].astype(F32)
    if first:
        own = own * group_flag(group, reverse, 1)
    moved = moved_ref[...].astype(F32) * group_flag(group, reverse, distance)
    out_ref[...] = (own + moved).astype(HALF)


def scan_kernel(group, orders, slots, reverse, masked, size, riding, *refs):
    sources = [partner_of(orders[0], j) for j in range(group)]
    carry = refs[0][0:size, :].astype(F32)
    if masked:
        carry = carry * group_flag(group, reverse, 1)
    blocks = [ref[0:size, :].astype(F32) for ref in refs[1 : 1 + group]]
    out_refs = refs[-len(slots) - riding :][: len(slots)]
    for slot, out_ref in zip(slots, out_refs):
        target = partner_of(orders[1], slot)
        total = carry
        for i in range(group):
            known = sources[i] > target if reverse else sources[i] < target
            total += jnp.where(known, 1.0, 0.0) * blocks[i]
        out_ref[...] = total.astype(HALF)
    if riding:
        refs[-1][...] = refs[1 + group][...] + wide_rows(refs[0], size)


VMEM = pl.BlockSpec(memory_space=pltpu.VMEM)
ANY = pl.BlockSpec(memory_space=pl.ANY)
HBM = pl.BlockSpec(memory_space=pltpu.HBM)


def call(kernel, outs, args, matmuls, scratch=(), ins=None, out_specs=None, aliases=None):
    size = sum(a.size * a.dtype.itemsize for a in args)
    size += sum(o.size * o.dtype.itemsize for o in outs)
    ins = ins or {}
    out_specs = out_specs or {}
    return pl.pallas_call(
        kernel,
        out_shape=tuple(outs),
        in_specs=[ins.get(i, VMEM) for i in range(len(args))],
        out_specs=tuple(out_specs.get(i, VMEM) for i in range(len(outs))),
        scratch_shapes=list(scratch),
        input_output_aliases=aliases or {},
        compiler_params=pltpu.CompilerParams(vmem_limit_bytes=16 * 1024 * 1024),
        cost_estimate=pl.CostEstimate(
            flops=2 * 128 * 128 * 128 * HEADS * matmuls,
            bytes_accessed=size,
            transcendentals=0,
        ),
    )(*args)


def swap(array, axis, offset):
    count = lax.axis_size(axis)
    return lax.ppermute(array, axis, [(i, i ^ offset) for i in range(count)])


def own_and_swapped(pieces, order):
    count = lax.axis_size("seq")
    results = [pieces[0]]
    for slot in range(1, len(pieces)):
        pairs = []
        for row in range(lax.axis_size("dp")):
            offset = order[row % 2][slot]
            pairs += [(row * count + i, row * count + (i ^ offset)) for i in range(count)]
        results.append(lax.ppermute(pieces[slot], ("dp", "seq"), pairs))
    return results


def exclusive_scan(pieces, orders, size, reverse, token):
    group = len(pieces)
    count, rows = lax.axis_size("seq"), lax.axis_size("dp")
    groups = count // group
    part = functools.partial
    lanes = pieces[0].shape[1]
    extra = pieces[0].shape[0] - size
    piece = jax.ShapeDtypeStruct((size, lanes), HALF)
    gain_shape = jax.ShapeDtypeStruct((extra // 2, lanes), F32)

    def shifted(array, distance):
        step = -distance if reverse else distance
        pairs = [(i, (i + step) % count) for i in range(count)]
        return lax.ppermute(array, "seq", pairs)

    received = own_and_swapped(pieces, orders[0])
    totals = call(
        part(total_kernel, size, group),
        [jax.ShapeDtypeStruct(pieces[0].shape, HALF)] + [gain_shape] * (extra > 0),
        received + [token],
        0,
        ins={group: ANY},
    )
    total, gains = totals[0], list(totals[1:])
    riding = int(extra > 0 and groups == 2 and rows == 4)
    carry = shifted(total if riding else total[:size], group)
    if riding:
        for offset in (0, group):
            pairs = [
                (row * count + i, (row ^ 2) * count + (i ^ offset))
                for row in range(rows)
                for i in range(count)
            ]
            gains.append(lax.ppermute(gains[0], ("dp", "seq"), pairs))
    elif extra:
        gains = [tree_sum(summed_over("seq", group, gains[0]))]
        gains = [tree_sum(summed_over("dp", 2, gains[0]))]
    distance = 1
    while distance < groups - 1:
        moved = shifted(carry, distance * group)
        kernel = part(
            carry_kernel, group, reverse, distance + (distance == 1), distance == 1
        )
        (carry,) = call(kernel, [piece], [carry, moved], 0)
        distance *= 2
    pieces, after = {}, []
    for slots in ((1,), (2,), (3, 0)):
        adding = riding if 0 in slots else 0
        inputs = [carry] + received + gains[:adding] + after
        sums = call(
            part(scan_kernel, group, orders, slots, reverse, groups <= 2, size, adding),
            [piece] * len(slots) + [gain_shape] * adding,
            inputs,
            0,
            ins={len(inputs) - 1: ANY} if after else {},
        )
        pieces.update(zip(slots, sums))
        after = [sums[0]]
    results = own_and_swapped([pieces[slot] for slot in range(group)], orders[1])
    if riding:
        gains = [sums[-1] + (gains[1] + gains[2])]
    return results, (gains[0] if gains else None)


def summed_over(axis, stride, array):
    count = lax.axis_size(axis)
    terms = [array]
    while stride < count:
        array = tree_sum(terms)
        width = 4 if count // stride % 4 == 0 else 2
        order = sorted(range(1, width), key=lambda i: i % 2)
        moved = {i: swap(array, axis, i * stride) for i in order}
        terms = [array] + [moved[i] for i in range(1, width)]
        stride *= width
    return terms


def per_device(queries, keys, values, gain, cotangent):
    q, k, v, cot = queries[0], keys[0], values[0], cotangent[0]
    rows, features = q.shape
    head = features // HEADS
    group = 4
    width = features // group
    part = functools.partial
    wide = jax.ShapeDtypeStruct((rows, features), F32)
    half = jax.ShapeDtypeStruct((rows, features), HALF)
    square = jax.ShapeDtypeStruct((rows, head), F32)
    piece = jax.ShapeDtypeStruct((width, head), HALF)
    scores_shape = jax.ShapeDtypeStruct((HEADS * rows, rows), HALF)
    gain_shape = jax.ShapeDtypeStruct((HEADS, head), F32)
    token_shape = jax.ShapeDtypeStruct((8, head), F32)
    whole = pltpu.VMEM((features, head), HALF)
    gain_row = gain.reshape(1, features)

    (first,) = call(
        part(first_state_kernel, head, 1),
        [piece],
        [pltpu.with_memory_space_constraint(a, pltpu.HBM) for a in (k, v)],
        1,
        [pltpu.VMEM((rows, width), HALF)] * 2 + [pltpu.SemaphoreType.DMA((2,))],
        ins={0: HBM, 1: HBM},
    )
    slots = (2, 3, 0)
    rest = call(
        part(state_kernel, head, slots), [piece] * 3, [k, v, first], 1, ins={2: ANY}
    )
    pieces = dict(zip(slots, rest))
    pieces[1] = first
    pieces = [pieces[slot] for slot in range(group)]
    scores, intra = call(part(local_kernel, head), [scores_shape, wide], [q, k, v], 2)
    prefix, _ = exclusive_scan(pieces, STATE_ORDERS, width, False, intra)
    message = jax.ShapeDtypeStruct((width + 2 * HEADS, head), HALF)
    sources = [q, intra, gain_row, cot]
    early, squares, inner = call(
        part(early_norm_kernel, head, STATE_ORDERS[1]),
        [wide, square, square],
        sources + prefix[:-1],
        1,
    )
    late, inverse, grad, *pieces = call(
        part(norm_kernel, head, group, NORM_ORDERS, lax.axis_size("dp")),
        [jax.ShapeDtypeStruct((rows, width), F32), square, half] + [message] * group,
        sources + [early, squares, inner, prefix[-1]],
        2,
        [pltpu.VMEM((1, features), F32), pltpu.VMEM((HEADS, head), F32)],
    )
    output, grad_query, key_part, value_part, token = call(
        part(backward_kernel, head, group),
        [half, half, wide, wide, token_shape],
        [q, k, v, scores, grad, early, late, inverse, gain_row] + prefix,
        5,
        [whole],
    )
    suffix, gain_grad = exclusive_scan(pieces, GRAD_ORDERS, width, True, token)
    gains = [gain_grad, swap(gain_grad, "dp", 1)]
    inputs = [k, v, key_part, value_part]
    outs = []
    for slots in ((0, 1), (2, 3)):
        last = group - 1 in slots
        at = len(inputs) + len(slots)
        results = call(
            part(final_kernel, head, slots, last),
            [half, half] + [gain_shape] * last,
            inputs + [suffix[slot] for slot in slots] + outs + (gains if last else []),
            1,
            [pltpu.VMEM((len(slots), rows, width), HALF)] * 2
            + [pltpu.SemaphoreType.DMA((2, len(slots)))]
            + [pltpu.VMEM((HEADS, head), F32), pltpu.SemaphoreType.DMA(())] * last,
            ins={at + i: HBM for i in range(len(outs))},
            out_specs={0: HBM, 1: HBM, 2: HBM},
            aliases={at + i: i for i in range(len(outs))},
        )
        outs = list(results[:2])
    grad_key, grad_value, gain_grad = results
    return (
        output[None],
        grad_query[None],
        grad_key[None],
        grad_value[None],
        gain_grad.reshape(features),
    )


def solution(mesh):
    spec = P("dp", "seq", None)
    return jax.shard_map(
        per_device,
        mesh=mesh,
        in_specs=(spec, spec, spec, P(), spec),
        out_specs=(spec, spec, spec, spec, P()),
        check_vma=False,
    )
```

```python
import functools

import jax
import jax.numpy as jnp
from jax import lax
from jax.experimental import pallas as pl
from jax.experimental.pallas import tpu as pltpu
from jax.sharding import PartitionSpec as P

HEADS = 16

EPSILON = 1e-06

F32 = jnp.float32
HALF = jnp.bfloat16


def dot(lhs, rhs, lhs_dim, rhs_dim):
    return lax.dot_general(
        lhs, rhs, (((lhs_dim,), (rhs_dim,)), ((), ())), preferred_element_type=F32
    )


def causal(size):
    rows = lax.broadcasted_iota(jnp.int32, (size, size), 0)
    columns = lax.broadcasted_iota(jnp.int32, (size, size), 1)
    return rows >= columns


def member_of(group):
    return lax.rem(lax.axis_index("seq"), group)


STATE_ORDERS = (((0, 1, 2, 3), (0, 2, 1, 3)), ((0, 2, 1, 3), (0, 1, 2, 3)))
GRAD_ORDERS = (((0, 3, 1, 2), (0, 3, 1, 2)), ((0, 1, 3, 2), (0, 1, 2, 3)))
NORM_ORDERS = (STATE_ORDERS[1], GRAD_ORDERS[0])


def partner_of(order, slot):
    even, odd = order[0][slot], order[1][slot]
    offset = even
    if even != odd:
        offset = jnp.where(lax.rem(lax.axis_index("dp"), 2) == 1, odd, even)
    return member_of(len(order[0])) ^ offset


def block_at(index, size):
    return pl.ds(pl.multiple_of(index * size, size), size)


def gathered(order, piece_refs, size, whole_ref):
    for j, ref in enumerate(piece_refs):
        whole_ref[block_at(partner_of(order, j), size), :] = ref[0:size, :]


def columns(first, count):
    return slice(first, first + count)


def first_state_kernel(head, slot, k_ref, v_ref, piece_ref, k_buffer, v_buffer, arrived):
    width = piece_ref.shape[0]
    source = block_at(partner_of(STATE_ORDERS[0], slot), width)
    copies = [
        pltpu.make_async_copy(k_ref.at[:, source], k_buffer, arrived.at[0]),
        pltpu.make_async_copy(v_ref.at[:, source], v_buffer, arrived.at[1]),
    ]
    for copy in copies:
        copy.start()
    for copy in copies:
        copy.wait()
    for i in range(width // head):
        part = columns(i * head, head)
        piece_ref[part, :] = dot(k_buffer[:, part], v_buffer[:, part], 0, 0).astype(HALF)


def state_kernel(head, slots, k_ref, v_ref, token_ref, *piece_refs):
    del token_ref
    for slot, piece_ref in zip(slots, piece_refs):
        width = piece_ref.shape[0]
        for i in range(width // head):
            part = features_at(STATE_ORDERS[0], slot, i, width, head)
            piece_ref[columns(i * head, head), :] = dot(
                k_ref[:, part], v_ref[:, part], 0, 0
            ).astype(HALF)


def local_kernel(head, q_ref, k_ref, v_ref, scores_ref, intra_ref):
    rows = q_ref.shape[0]
    mask = causal(rows)
    scaling = head ** (-0.5)
    for h in range(HEADS):
        part = columns(h * head, head)
        scores = dot(q_ref[:, part], k_ref[:, part], 1, 1) * scaling
        scores = jnp.where(mask, scores, 0.0).astype(HALF)
        scores_ref[columns(h * rows, rows), :] = scores
        intra_ref[:, part] = dot(scores, v_ref[:, part], 1, 0)


def features_at(order, slot, i, width, head):
    start = partner_of(order, slot) * width + i * head
    return pl.ds(pl.multiple_of(start, head), head)


def attend(head, order, slot, refs, prefix_ref, attended_ref, at, squares, inner):
    q_ref, intra_ref, gain_ref, cot_ref = refs
    scaling = head ** (-0.5)
    width = prefix_ref.shape[0]
    for i in range(width // head):
        part = features_at(order, slot, i, width, head)
        prefix = prefix_ref[columns(i * head, head), :]
        attended = intra_ref[:, part] + scaling * dot(q_ref[:, part], prefix, 1, 0)
        attended_ref[:, part if at is None else columns(i * head, head)] = attended
        scaled = cot_ref[:, part].astype(F32) * gain_ref[:, part]
        squares += attended * attended
        inner += scaled * attended
    return squares, inner


def early_norm_kernel(head, order, *refs):
    prefix_refs, (attended_ref, squares_ref, inner_ref) = refs[4:-3], refs[-3:]
    squares = jnp.zeros(squares_ref.shape, F32)
    inner = jnp.zeros(squares_ref.shape, F32)
    for slot, prefix_ref in enumerate(prefix_refs):
        squares, inner = attend(
            head, order, slot, refs[:4], prefix_ref, attended_ref, None, squares, inner
        )
    squares_ref[...] = squares
    inner_ref[...] = inner


def norm_kernel(head, group, orders, replicas, *refs):
    q_ref, _, gain_ref, cot_ref = refs[:4]
    early_ref, squares_ref, inner_ref, prefix_ref = refs[4:8]
    late_ref, inverse_ref, grad_ref = refs[8:11]
    piece_refs = refs[11 : 11 + group]
    gain_grad_ref, gain_rows_ref = refs[11 + group :]
    features = q_ref.shape[1]
    width = features // group
    odd = lax.rem(lax.axis_index("dp"), 2) == 1
    squares, inner = attend(
        head,
        orders[0],
        group - 1,
        refs[:4],
        prefix_ref,
        late_ref,
        0,
        squares_ref[...],
        inner_ref[...],
    )
    inverse = lax.rsqrt(
        jnp.sum(squares, axis=1, keepdims=True) * (1.0 / features) + EPSILON
    )
    inner_mean = jnp.sum(inner, axis=1, keepdims=True) * (1.0 / features) * inverse
    inverse_ref[...] = jnp.broadcast_to(inverse, inverse_ref.shape)
    scaling = head ** (-0.5)
    for slot in range(group):
        for i in range(width // head):
            part = features_at(orders[1], slot, i, width, head)
            local = columns(i * head, head)
            late = [order[slot] == before[-1] for before, order in zip(*orders)]
            attended = late_ref[:, local] if late[0] else early_ref[:, part]
            if late[0] != late[1]:
                other = late_ref[:, local] if late[1] else early_ref[:, part]
                attended = jnp.where(odd, other, attended)
            normalized = attended * inverse
            upstream = cot_ref[:, part].astype(F32)
            gain_grad_ref[:, part] = jnp.sum(
                upstream * normalized, axis=0, keepdims=True
            ) * (1.0 / replicas)
            scaled = upstream * gain_ref[:, part]
            grad = ((scaled - normalized * inner_mean) * inverse).astype(HALF)
            grad_ref[:, part] = grad
            piece_refs[slot][local, :] = (
                scaling * dot(q_ref[:, part], grad, 0, 0)
            ).astype(HALF)
    for h in range(HEADS):
        gain_rows_ref[h : h + 1, :] = gain_grad_ref[:, columns(h * head, head)]
    for ref in piece_refs:
        put_wide_rows(ref, width, gain_rows_ref[...])


def backward_kernel(head, group, *refs):
    q_ref, k_ref, v_ref, scores_ref, grad_ref = refs[:5]
    early_ref, late_ref, inverse_ref, gain_ref = refs[5:9]
    prefix_refs = refs[9 : 9 + group]
    out_ref, grad_query_ref, key_part_ref, value_part_ref, token_ref = refs[
        9 + group : 14 + group
    ]
    whole_ref = refs[14 + group]
    rows = q_ref.shape[0]
    mask = causal(rows)
    scaling = head ** (-0.5)
    gathered(STATE_ORDERS[1], prefix_refs, prefix_refs[0].shape[0], whole_ref)
    inverse = inverse_ref[...]
    width = late_ref.shape[1]
    for slot in range(group):
        for i in range(width // head):
            part = features_at(STATE_ORDERS[1], slot, i, width, head)
            if slot == group - 1:
                attended = late_ref[:, columns(i * head, head)]
            else:
                attended = early_ref[:, part]
            out_ref[:, part] = (gain_ref[:, part] * (attended * inverse)).astype(HALF)
    for h in range(HEADS):
        part = columns(h * head, head)
        grad = grad_ref[:, part]
        grad_scores = dot(grad, v_ref[:, part], 1, 1)
        grad_scores = jnp.where(mask, grad_scores, 0.0).astype(HALF)
        grad_query = dot(grad_scores, k_ref[:, part], 1, 0) + dot(
            grad, whole_ref[part, :], 1, 1
        )
        grad_query_ref[:, part] = (scaling * grad_query).astype(HALF)
        key_part_ref[:, part] = scaling * dot(grad_scores, q_ref[:, part], 0, 0)
        value_part_ref[:, part] = dot(
            scores_ref[columns(h * rows, rows), :], grad, 0, 0
        )
    token_ref[...] = jnp.zeros_like(token_ref)


def final_kernel(head, slots, last, *refs):
    k_ref, v_ref, key_part_ref, value_part_ref = refs[:4]
    suffix_refs = refs[4 : 4 + len(slots)]
    refs = refs[4 + len(slots) :]
    copies = []
    if last:
        gain_grad_ref, total_ref, gain_written = refs[-6], refs[-2], refs[-1]
        total_ref[...] = tree_sum([ref[...] for ref in refs[2:-8]])
        copies.append(pltpu.make_async_copy(total_ref, gain_grad_ref, gain_written))
        copies[0].start()
        out_refs, refs = refs[-8:-6], refs[-5:-2]
    else:
        out_refs, refs = refs[-5:-3], refs[-3:]
    key_buffer, value_buffer, written = refs
    width = key_buffer.shape[2]
    for n, slot in enumerate(slots):
        for i in range(width // head):
            part = features_at(GRAD_ORDERS[1], slot, i, width, head)
            local = columns(i * head, head)
            suffix = suffix_refs[n][local, :]
            key_buffer[n, :, local] = (
                key_part_ref[:, part] + dot(v_ref[:, part], suffix, 1, 1)
            ).astype(HALF)
            value_buffer[n, :, local] = (
                value_part_ref[:, part] + dot(k_ref[:, part], suffix, 1, 0)
            ).astype(HALF)
        for i, buffer in enumerate((key_buffer, value_buffer)):
            copy = pltpu.make_async_copy(
                buffer.at[n],
                out_refs[i].at[:, block_at(partner_of(GRAD_ORDERS[1], slot), width)],
                written.at[i, n],
            )
            copy.start()
            copies.append(copy)
    for copy in copies:
        copy.wait()


def tree_sum(terms):
    while len(terms) > 1:
        terms = [a + b for a, b in zip(terms[::2], terms[1::2])]
    return terms[0]


def wide_rows(ref, start):
    rows = (ref.shape[0] - start) // 2
    high = ref[columns(start, rows), :].astype(F32)
    return high + ref[columns(start + rows, rows), :].astype(F32)


def put_wide_rows(ref, start, value):
    rows = value.shape[0]
    high = value.astype(HALF)
    ref[columns(start, rows), :] = high
    ref[columns(start + rows, rows), :] = (value - high.astype(F32)).astype(HALF)


def total_kernel(size, count, *refs):
    refs, out_refs = refs[:count], refs[count + 1 :]
    total = refs[0][0:size, :].astype(F32)
    for ref in refs[1:]:
        total += ref[0:size, :].astype(F32)
    out_refs[0][0:size, :] = total.astype(HALF)
    if len(out_refs) > 1:
        gain = tree_sum([wide_rows(ref, size) for ref in refs])
        put_wide_rows(out_refs[0], size, gain)
        out_refs[1][...] = wide_rows(out_refs[0], size)


def group_flag(group, reverse, distance):
    index = lax.axis_index("seq") // group
    last = lax.axis_size("seq") // group - 1
    known = index + distance <= last if reverse else index >= distance
    return jnp.where(known, 1.0, 0.0)


def carry_kernel(group, reverse, distance, first, own_ref, moved_ref, out_ref):
    own = own_ref[...].astype(F32)
    if first:
        own = own * group_flag(group, reverse, 1)
    moved = moved_ref[...].astype(F32) * group_flag(group, reverse, distance)
    out_ref[...] = (own + moved).astype(HALF)


def scan_kernel(group, orders, slots, reverse, masked, size, riding, *refs):
    sources = [partner_of(orders[0], j) for j in range(group)]
    carry = refs[0][0:size, :].astype(F32)
    if masked:
        carry = carry * group_flag(group, reverse, 1)
    blocks = [ref[0:size, :].astype(F32) for ref in refs[1 : 1 + group]]
    out_refs = refs[-len(slots) - riding :][: len(slots)]
    for slot, out_ref in zip(slots, out_refs):
        target = partner_of(orders[1], slot)
        total = carry
        for i in range(group):
            known = sources[i] > target if reverse else sources[i] < target
            total += jnp.where(known, 1.0, 0.0) * blocks[i]
        out_ref[...] = total.astype(HALF)
    if riding:
        refs[-1][...] = refs[1 + group][...] + wide_rows(refs[0], size)


VMEM = pl.BlockSpec(memory_space=pltpu.VMEM)
ANY = pl.BlockSpec(memory_space=pl.ANY)
HBM = pl.BlockSpec(memory_space=pltpu.HBM)


def call(kernel, outs, args, matmuls, scratch=(), ins=None, out_specs=None, aliases=None):
    size = sum(a.size * a.dtype.itemsize for a in args)
    size += sum(o.size * o.dtype.itemsize for o in outs)
    ins = ins or {}
    out_specs = out_specs or {}
    return pl.pallas_call(
        kernel,
        out_shape=tuple(outs),
        in_specs=[ins.get(i, VMEM) for i in range(len(args))],
        out_specs=tuple(out_specs.get(i, VMEM) for i in range(len(outs))),
        scratch_shapes=list(scratch),
        input_output_aliases=aliases or {},
        compiler_params=pltpu.CompilerParams(vmem_limit_bytes=16 * 1024 * 1024),
        cost_estimate=pl.CostEstimate(
            flops=2 * 128 * 128 * 128 * HEADS * matmuls,
            bytes_accessed=size,
            transcendentals=0,
        ),
    )(*args)


def swap(array, axis, offset):
    count = lax.axis_size(axis)
    return lax.ppermute(array, axis, [(i, i ^ offset) for i in range(count)])


def own_and_swapped(pieces, order):
    count = lax.axis_size("seq")
    results = [pieces[0]]
    for slot in range(1, len(pieces)):
        pairs = []
        for row in range(lax.axis_size("dp")):
            offset = order[row % 2][slot]
            pairs += [(row * count + i, row * count + (i ^ offset)) for i in range(count)]
        results.append(lax.ppermute(pieces[slot], ("dp", "seq"), pairs))
    return results


def exclusive_scan(pieces, orders, size, reverse, token):
    group = len(pieces)
    count, rows = lax.axis_size("seq"), lax.axis_size("dp")
    groups = count // group
    part = functools.partial
    lanes = pieces[0].shape[1]
    extra = pieces[0].shape[0] - size
    piece = jax.ShapeDtypeStruct((size, lanes), HALF)
    gain_shape = jax.ShapeDtypeStruct((extra // 2, lanes), F32)

    def shifted(array, distance):
        step = -distance if reverse else distance
        pairs = [(i, (i + step) % count) for i in range(count)]
        return lax.ppermute(array, "seq", pairs)

    received = own_and_swapped(pieces, orders[0])
    totals = call(
        part(total_kernel, size, group),
        [jax.ShapeDtypeStruct(pieces[0].shape, HALF)] + [gain_shape] * (extra > 0),
        received + [token],
        0,
        ins={group: ANY},
    )
    total, gains = totals[0], list(totals[1:])
    riding = int(extra > 0 and groups == 2 and rows == 4)
    carry = shifted(total if riding else total[:size], group)
    if riding:
        for offset in (0, group):
            pairs = [
                (row * count + i, (row ^ 2) * count + (i ^ offset))
                for row in range(rows)
                for i in range(count)
            ]
            gains.append(lax.ppermute(gains[0], ("dp", "seq"), pairs))
    elif extra:
        gains = [tree_sum(summed_over("seq", group, gains[0]))]
        gains = [tree_sum(summed_over("dp", 2, gains[0]))]
    distance = 1
    while distance < groups - 1:
        moved = shifted(carry, distance * group)
        kernel = part(
            carry_kernel, group, reverse, distance + (distance == 1), distance == 1
        )
        (carry,) = call(kernel, [piece], [carry, moved], 0)
        distance *= 2
    pieces, after = {}, []
    for slots in ((1,), (2,), (3, 0)):
        adding = riding if 0 in slots else 0
        inputs = [carry] + received + gains[:adding] + after
        sums = call(
            part(scan_kernel, group, orders, slots, reverse, groups <= 2, size, adding),
            [piece] * len(slots) + [gain_shape] * adding,
            inputs,
            0,
            ins={len(inputs) - 1: ANY} if after else {},
        )
        pieces.update(zip(slots, sums))
        after = [sums[0]]
    results = own_and_swapped([pieces[slot] for slot in range(group)], orders[1])
    if riding:
        gains = [sums[-1] + (gains[1] + gains[2])]
    return results, (gains[0] if gains else None)


def summed_over(axis, stride, array):
    count = lax.axis_size(axis)
    terms = [array]
    while stride < count:
        array = tree_sum(terms)
        width = 4 if count // stride % 4 == 0 else 2
        order = sorted(range(1, width), key=lambda i: i % 2)
        moved = {i: swap(array, axis, i * stride) for i in order}
        terms = [array] + [moved[i] for i in range(1, width)]
        stride *= width
    return terms


def per_device(queries, keys, values, gain, cotangent):
    q, k, v, cot = queries[0], keys[0], values[0], cotangent[0]
    rows, features = q.shape
    head = features // HEADS
    group = 4
    width = features // group
    part = functools.partial
    wide = jax.ShapeDtypeStruct((rows, features), F32)
    half = jax.ShapeDtypeStruct((rows, features), HALF)
    square = jax.ShapeDtypeStruct((rows, head), F32)
    piece = jax.ShapeDtypeStruct((width, head), HALF)
    scores_shape = jax.ShapeDtypeStruct((HEADS * rows, rows), HALF)
    gain_shape = jax.ShapeDtypeStruct((HEADS, head), F32)
    token_shape = jax.ShapeDtypeStruct((8, head), F32)
    whole = pltpu.VMEM((features, head), HALF)
    gain_row = gain.reshape(1, features)

    (first,) = call(
        part(first_state_kernel, head, 1),
        [piece],
        [pltpu.with_memory_space_constraint(a, pltpu.HBM) for a in (k, v)],
        1,
        [pltpu.VMEM((rows, width), HALF)] * 2 + [pltpu.SemaphoreType.DMA((2,))],
        ins={0: HBM, 1: HBM},
    )
    slots = (2, 3, 0)
    rest = call(
        part(state_kernel, head, slots), [piece] * 3, [k, v, first], 1, ins={2: ANY}
    )
    pieces = dict(zip(slots, rest))
    pieces[1] = first
    pieces = [pieces[slot] for slot in range(group)]
    scores, intra = call(part(local_kernel, head), [scores_shape, wide], [q, k, v], 2)
    prefix, _ = exclusive_scan(pieces, STATE_ORDERS, width, False, intra)
    message = jax.ShapeDtypeStruct((width + 2 * HEADS, head), HALF)
    sources = [q, intra, gain_row, cot]
    early, squares, inner = call(
        part(early_norm_kernel, head, STATE_ORDERS[1]),
        [wide, square, square],
        sources + prefix[:-1],
        1,
    )
    late, inverse, grad, *pieces = call(
        part(norm_kernel, head, group, NORM_ORDERS, lax.axis_size("dp")),
        [jax.ShapeDtypeStruct((rows, width), F32), square, half] + [message] * group,
        sources + [early, squares, inner, prefix[-1]],
        2,
        [pltpu.VMEM((1, features), F32), pltpu.VMEM((HEADS, head), F32)],
    )
    output, grad_query, key_part, value_part, token = call(
        part(backward_kernel, head, group),
        [half, half, wide, wide, token_shape],
        [q, k, v, scores, grad, early, late, inverse, gain_row] + prefix,
        5,
        [whole],
    )
    suffix, gain_grad = exclusive_scan(pieces, GRAD_ORDERS, width, True, token)
    gains = [gain_grad, swap(gain_grad, "dp", 1)]
    inputs = [k, v, key_part, value_part]
    outs = []
    for slots in ((0, 1), (2, 3)):
        last = group - 1 in slots
        at = len(inputs) + len(slots)
        results = call(
            part(final_kernel, head, slots, last),
            [half, half] + [gain_shape] * last,
            inputs + [suffix[slot] for slot in slots] + outs + (gains if last else []),
            1,
            [pltpu.VMEM((len(slots), rows, width), HALF)] * 2
            + [pltpu.SemaphoreType.DMA((2, len(slots)))]
            + [pltpu.VMEM((HEADS, head), F32), pltpu.SemaphoreType.DMA(())] * last,
            ins={at + i: HBM for i in range(len(outs))},
            out_specs={0: HBM, 1: HBM, 2: HBM},
            aliases={at + i: i for i in range(len(outs))},
        )
        outs = list(results[:2])
    grad_key, grad_value, gain_grad = results
    return (
        output[None],
        grad_query[None],
        grad_key[None],
        grad_value[None],
        gain_grad.reshape(features),
    )


def solution(mesh):
    spec = P("dp", "seq", None)
    return jax.shard_map(
        per_device,
        mesh=mesh,
        in_specs=(spec, spec, spec, P(), spec),
        out_specs=(spec, spec, spec, spec, P()),
        check_vma=False,
    )
```

```python
import functools

import jax
import jax.numpy as jnp
from jax import lax
from jax.experimental import pallas as pl
from jax.experimental.pallas import tpu as pltpu
from jax.sharding import PartitionSpec as P

HEADS = 16

EPSILON = 1e-06

F32 = jnp.float32
HALF = jnp.bfloat16


def dot(lhs, rhs, lhs_dim, rhs_dim):
    return lax.dot_general(
        lhs, rhs, (((lhs_dim,), (rhs_dim,)), ((), ())), preferred_element_type=F32
    )


def causal(size):
    rows = lax.broadcasted_iota(jnp.int32, (size, size), 0)
    columns = lax.broadcasted_iota(jnp.int32, (size, size), 1)
    return rows >= columns


def member_of(group):
    return lax.rem(lax.axis_index("seq"), group)


STATE_ORDERS = (((0, 1, 2, 3), (0, 2, 1, 3)), ((0, 2, 1, 3), (0, 1, 2, 3)))
GRAD_ORDERS = (((0, 3, 1, 2), (0, 3, 1, 2)), ((0, 3, 2, 1), (0, 1, 2, 3)))
NORM_ORDERS = (STATE_ORDERS[1], GRAD_ORDERS[0])


def partner_of(order, slot):
    even, odd = order[0][slot], order[1][slot]
    offset = even
    if even != odd:
        offset = jnp.where(lax.rem(lax.axis_index("dp"), 2) == 1, odd, even)
    return member_of(len(order[0])) ^ offset


def block_at(index, size):
    return pl.ds(pl.multiple_of(index * size, size), size)


def gathered(order, piece_refs, size, whole_ref):
    for j, ref in enumerate(piece_refs):
        whole_ref[block_at(partner_of(order, j), size), :] = ref[0:size, :]


def columns(first, count):
    return slice(first, first + count)


def first_state_kernel(head, slot, k_ref, v_ref, piece_ref, k_buffer, v_buffer, arrived):
    width = piece_ref.shape[0]
    source = block_at(partner_of(STATE_ORDERS[0], slot), width)
    copies = [
        pltpu.make_async_copy(k_ref.at[:, source], k_buffer, arrived.at[0]),
        pltpu.make_async_copy(v_ref.at[:, source], v_buffer, arrived.at[1]),
    ]
    for copy in copies:
        copy.start()
    for copy in copies:
        copy.wait()
    for i in range(width // head):
        part = columns(i * head, head)
        piece_ref[part, :] = dot(k_buffer[:, part], v_buffer[:, part], 0, 0).astype(HALF)


def state_kernel(head, slots, k_ref, v_ref, token_ref, *piece_refs):
    del token_ref
    for slot, piece_ref in zip(slots, piece_refs):
        width = piece_ref.shape[0]
        for i in range(width // head):
            part = features_at(STATE_ORDERS[0], slot, i, width, head)
            piece_ref[columns(i * head, head), :] = dot(
                k_ref[:, part], v_ref[:, part], 0, 0
            ).astype(HALF)


def local_kernel(head, q_ref, k_ref, v_ref, scores_ref, intra_ref):
    rows = q_ref.shape[0]
    mask = causal(rows)
    scaling = head ** (-0.5)
    for h in range(HEADS):
        part = columns(h * head, head)
        scores = dot(q_ref[:, part], k_ref[:, part], 1, 1) * scaling
        scores = jnp.where(mask, scores, 0.0).astype(HALF)
        scores_ref[columns(h * rows, rows), :] = scores
        intra_ref[:, part] = dot(scores, v_ref[:, part], 1, 0)


def features_at(order, slot, i, width, head):
    start = partner_of(order, slot) * width + i * head
    return pl.ds(pl.multiple_of(start, head), head)


def attend(head, order, slot, refs, prefix_ref, attended_ref, at, squares, inner):
    q_ref, intra_ref, gain_ref, cot_ref = refs
    scaling = head ** (-0.5)
    width = prefix_ref.shape[0]
    for i in range(width // head):
        part = features_at(order, slot, i, width, head)
        prefix = prefix_ref[columns(i * head, head), :]
        attended = intra_ref[:, part] + scaling * dot(q_ref[:, part], prefix, 1, 0)
        attended_ref[:, part if at is None else columns(i * head, head)] = attended
        scaled = cot_ref[:, part].astype(F32) * gain_ref[:, part]
        squares += attended * attended
        inner += scaled * attended
    return squares, inner


def early_norm_kernel(head, order, *refs):
    prefix_refs, (attended_ref, squares_ref, inner_ref) = refs[4:-3], refs[-3:]
    squares = jnp.zeros(squares_ref.shape, F32)
    inner = jnp.zeros(squares_ref.shape, F32)
    for slot, prefix_ref in enumerate(prefix_refs):
        squares, inner = attend(
            head, order, slot, refs[:4], prefix_ref, attended_ref, None, squares, inner
        )
    squares_ref[...] = squares
    inner_ref[...] = inner


def norm_kernel(head, group, orders, replicas, *refs):
    q_ref, _, gain_ref, cot_ref = refs[:4]
    early_ref, squares_ref, inner_ref, prefix_ref = refs[4:8]
    late_ref, inverse_ref, grad_ref = refs[8:11]
    piece_refs = refs[11 : 11 + group]
    gain_grad_ref, gain_rows_ref = refs[11 + group :]
    features = q_ref.shape[1]
    width = features // group
    odd = lax.rem(lax.axis_index("dp"), 2) == 1
    squares, inner = attend(
        head,
        orders[0],
        group - 1,
        refs[:4],
        prefix_ref,
        late_ref,
        0,
        squares_ref[...],
        inner_ref[...],
    )
    inverse = lax.rsqrt(
        jnp.sum(squares, axis=1, keepdims=True) * (1.0 / features) + EPSILON
    )
    inner_mean = jnp.sum(inner, axis=1, keepdims=True) * (1.0 / features) * inverse
    inverse_ref[...] = jnp.broadcast_to(inverse, inverse_ref.shape)
    scaling = head ** (-0.5)
    for slot in range(group):
        for i in range(width // head):
            part = features_at(orders[1], slot, i, width, head)
            local = columns(i * head, head)
            late = [order[slot] == before[-1] for before, order in zip(*orders)]
            attended = late_ref[:, local] if late[0] else early_ref[:, part]
            if late[0] != late[1]:
                other = late_ref[:, local] if late[1] else early_ref[:, part]
                attended = jnp.where(odd, other, attended)
            normalized = attended * inverse
            upstream = cot_ref[:, part].astype(F32)
            gain_grad_ref[:, part] = jnp.sum(
                upstream * normalized, axis=0, keepdims=True
            ) * (1.0 / replicas)
            scaled = upstream * gain_ref[:, part]
            grad = ((scaled - normalized * inner_mean) * inverse).astype(HALF)
            grad_ref[:, part] = grad
            piece_refs[slot][local, :] = (
                scaling * dot(q_ref[:, part], grad, 0, 0)
            ).astype(HALF)
    for h in range(HEADS):
        gain_rows_ref[h : h + 1, :] = gain_grad_ref[:, columns(h * head, head)]
    for ref in piece_refs:
        put_wide_rows(ref, width, gain_rows_ref[...])


def backward_kernel(head, group, *refs):
    q_ref, k_ref, v_ref, scores_ref, grad_ref = refs[:5]
    early_ref, late_ref, inverse_ref, gain_ref = refs[5:9]
    prefix_refs = refs[9 : 9 + group]
    out_ref, grad_query_ref, key_part_ref, value_part_ref, token_ref = refs[
        9 + group : 14 + group
    ]
    whole_ref = refs[14 + group]
    rows = q_ref.shape[0]
    mask = causal(rows)
    scaling = head ** (-0.5)
    gathered(STATE_ORDERS[1], prefix_refs, prefix_refs[0].shape[0], whole_ref)
    inverse = inverse_ref[...]
    width = late_ref.shape[1]
    for slot in range(group):
        for i in range(width // head):
            part = features_at(STATE_ORDERS[1], slot, i, width, head)
            if slot == group - 1:
                attended = late_ref[:, columns(i * head, head)]
            else:
                attended = early_ref[:, part]
            out_ref[:, part] = (gain_ref[:, part] * (attended * inverse)).astype(HALF)
    for h in range(HEADS):
        part = columns(h * head, head)
        grad = grad_ref[:, part]
        grad_scores = dot(grad, v_ref[:, part], 1, 1)
        grad_scores = jnp.where(mask, grad_scores, 0.0).astype(HALF)
        grad_query = dot(grad_scores, k_ref[:, part], 1, 0) + dot(
            grad, whole_ref[part, :], 1, 1
        )
        grad_query_ref[:, part] = (scaling * grad_query).astype(HALF)
        key_part_ref[:, part] = scaling * dot(grad_scores, q_ref[:, part], 0, 0)
        value_part_ref[:, part] = dot(
            scores_ref[columns(h * rows, rows), :], grad, 0, 0
        )
    token_ref[...] = jnp.zeros_like(token_ref)


def final_kernel(head, slots, last, *refs):
    k_ref, v_ref, key_part_ref, value_part_ref = refs[:4]
    suffix_refs = refs[4 : 4 + len(slots)]
    refs = refs[4 + len(slots) :]
    copies = []
    if last:
        gain_grad_ref, total_ref, gain_written = refs[-6], refs[-2], refs[-1]
        total_ref[...] = tree_sum([ref[...] for ref in refs[2:-8]])
        copies.append(pltpu.make_async_copy(total_ref, gain_grad_ref, gain_written))
        copies[0].start()
        out_refs, refs = refs[-8:-6], refs[-5:-2]
    else:
        out_refs, refs = refs[-5:-3], refs[-3:]
    key_buffer, value_buffer, written = refs
    width = key_buffer.shape[2]
    for n, slot in enumerate(slots):
        for i in range(width // head):
            part = features_at(GRAD_ORDERS[1], slot, i, width, head)
            local = columns(i * head, head)
            suffix = suffix_refs[n][local, :]
            key_buffer[n, :, local] = (
                key_part_ref[:, part] + dot(v_ref[:, part], suffix, 1, 1)
            ).astype(HALF)
            value_buffer[n, :, local] = (
                value_part_ref[:, part] + dot(k_ref[:, part], suffix, 1, 0)
            ).astype(HALF)
        for i, buffer in enumerate((key_buffer, value_buffer)):
            copy = pltpu.make_async_copy(
                buffer.at[n],
                out_refs[i].at[:, block_at(partner_of(GRAD_ORDERS[1], slot), width)],
                written.at[i, n],
            )
            copy.start()
            copies.append(copy)
    for copy in copies:
        copy.wait()


def tree_sum(terms):
    while len(terms) > 1:
        terms = [a + b for a, b in zip(terms[::2], terms[1::2])]
    return terms[0]


def wide_rows(ref, start):
    rows = (ref.shape[0] - start) // 2
    high = ref[columns(start, rows), :].astype(F32)
    return high + ref[columns(start + rows, rows), :].astype(F32)


def put_wide_rows(ref, start, value):
    rows = value.shape[0]
    high = value.astype(HALF)
    ref[columns(start, rows), :] = high
    ref[columns(start + rows, rows), :] = (value - high.astype(F32)).astype(HALF)


def total_kernel(size, count, *refs):
    refs, out_refs = refs[:count], refs[count + 1 :]
    total = refs[0][0:size, :].astype(F32)
    for ref in refs[1:]:
        total += ref[0:size, :].astype(F32)
    out_refs[0][0:size, :] = total.astype(HALF)
    if len(out_refs) > 1:
        gain = tree_sum([wide_rows(ref, size) for ref in refs])
        put_wide_rows(out_refs[0], size, gain)
        out_refs[1][...] = wide_rows(out_refs[0], size)


def group_flag(group, reverse, distance):
    index = lax.axis_index("seq") // group
    last = lax.axis_size("seq") // group - 1
    known = index + distance <= last if reverse else index >= distance
    return jnp.where(known, 1.0, 0.0)


def carry_kernel(group, reverse, distance, first, own_ref, moved_ref, out_ref):
    own = own_ref[...].astype(F32)
    if first:
        own = own * group_flag(group, reverse, 1)
    moved = moved_ref[...].astype(F32) * group_flag(group, reverse, distance)
    out_ref[...] = (own + moved).astype(HALF)


def scan_kernel(group, orders, slots, reverse, masked, size, riding, *refs):
    sources = [partner_of(orders[0], j) for j in range(group)]
    carry = refs[0][0:size, :].astype(F32)
    if masked:
        carry = carry * group_flag(group, reverse, 1)
    blocks = [ref[0:size, :].astype(F32) for ref in refs[1 : 1 + group]]
    out_refs = refs[-len(slots) - riding :][: len(slots)]
    for slot, out_ref in zip(slots, out_refs):
        target = partner_of(orders[1], slot)
        total = carry
        for i in range(group):
            known = sources[i] > target if reverse else sources[i] < target
            total += jnp.where(known, 1.0, 0.0) * blocks[i]
        out_ref[...] = total.astype(HALF)
    if riding:
        refs[-1][...] = refs[1 + group][...] + wide_rows(refs[0], size)


VMEM = pl.BlockSpec(memory_space=pltpu.VMEM)
ANY = pl.BlockSpec(memory_space=pl.ANY)
HBM = pl.BlockSpec(memory_space=pltpu.HBM)


def call(kernel, outs, args, matmuls, scratch=(), ins=None, out_specs=None, aliases=None):
    size = sum(a.size * a.dtype.itemsize for a in args)
    size += sum(o.size * o.dtype.itemsize for o in outs)
    ins = ins or {}
    out_specs = out_specs or {}
    return pl.pallas_call(
        kernel,
        out_shape=tuple(outs),
        in_specs=[ins.get(i, VMEM) for i in range(len(args))],
        out_specs=tuple(out_specs.get(i, VMEM) for i in range(len(outs))),
        scratch_shapes=list(scratch),
        input_output_aliases=aliases or {},
        compiler_params=pltpu.CompilerParams(vmem_limit_bytes=16 * 1024 * 1024),
        cost_estimate=pl.CostEstimate(
            flops=2 * 128 * 128 * 128 * HEADS * matmuls,
            bytes_accessed=size,
            transcendentals=0,
        ),
    )(*args)


def swap(array, axis, offset):
    count = lax.axis_size(axis)
    return lax.ppermute(array, axis, [(i, i ^ offset) for i in range(count)])


def own_and_swapped(pieces, order):
    count = lax.axis_size("seq")
    results = [pieces[0]]
    for slot in range(1, len(pieces)):
        pairs = []
        for row in range(lax.axis_size("dp")):
            offset = order[row % 2][slot]
            pairs += [(row * count + i, row * count + (i ^ offset)) for i in range(count)]
        results.append(lax.ppermute(pieces[slot], ("dp", "seq"), pairs))
    return results


def exclusive_scan(pieces, orders, size, reverse, token):
    group = len(pieces)
    count, rows = lax.axis_size("seq"), lax.axis_size("dp")
    groups = count // group
    part = functools.partial
    lanes = pieces[0].shape[1]
    extra = pieces[0].shape[0] - size
    piece = jax.ShapeDtypeStruct((size, lanes), HALF)
    gain_shape = jax.ShapeDtypeStruct((extra // 2, lanes), F32)

    def shifted(array, distance):
        step = -distance if reverse else distance
        pairs = [(i, (i + step) % count) for i in range(count)]
        return lax.ppermute(array, "seq", pairs)

    received = own_and_swapped(pieces, orders[0])
    totals = call(
        part(total_kernel, size, group),
        [jax.ShapeDtypeStruct(pieces[0].shape, HALF)] + [gain_shape] * (extra > 0),
        received + [token],
        0,
        ins={group: ANY},
    )
    total, gains = totals[0], list(totals[1:])
    riding = int(extra > 0 and groups == 2 and rows == 4)
    carry = shifted(total if riding else total[:size], group)
    if riding:
        for offset in (0, group):
            pairs = [
                (row * count + i, (row ^ 2) * count + (i ^ offset))
                for row in range(rows)
                for i in range(count)
            ]
            gains.append(lax.ppermute(gains[0], ("dp", "seq"), pairs))
    elif extra:
        gains = [tree_sum(summed_over("seq", group, gains[0]))]
        gains = [tree_sum(summed_over("dp", 2, gains[0]))]
    distance = 1
    while distance < groups - 1:
        moved = shifted(carry, distance * group)
        kernel = part(
            carry_kernel, group, reverse, distance + (distance == 1), distance == 1
        )
        (carry,) = call(kernel, [piece], [carry, moved], 0)
        distance *= 2
    pieces, after = {}, []
    for slots in ((1,), (2,), (3, 0)):
        adding = riding if 0 in slots else 0
        inputs = [carry] + received + gains[:adding] + after
        sums = call(
            part(scan_kernel, group, orders, slots, reverse, groups <= 2, size, adding),
            [piece] * len(slots) + [gain_shape] * adding,
            inputs,
            0,
            ins={len(inputs) - 1: ANY} if after else {},
        )
        pieces.update(zip(slots, sums))
        after = [sums[0]]
    results = own_and_swapped([pieces[slot] for slot in range(group)], orders[1])
    if riding:
        gains = [sums[-1] + (gains[1] + gains[2])]
    return results, (gains[0] if gains else None)


def summed_over(axis, stride, array):
    count = lax.axis_size(axis)
    terms = [array]
    while stride < count:
        array = tree_sum(terms)
        width = 4 if count // stride % 4 == 0 else 2
        order = sorted(range(1, width), key=lambda i: i % 2)
        moved = {i: swap(array, axis, i * stride) for i in order}
        terms = [array] + [moved[i] for i in range(1, width)]
        stride *= width
    return terms


def per_device(queries, keys, values, gain, cotangent):
    q, k, v, cot = queries[0], keys[0], values[0], cotangent[0]
    rows, features = q.shape
    head = features // HEADS
    group = 4
    width = features // group
    part = functools.partial
    wide = jax.ShapeDtypeStruct((rows, features), F32)
    half = jax.ShapeDtypeStruct((rows, features), HALF)
    square = jax.ShapeDtypeStruct((rows, head), F32)
    piece = jax.ShapeDtypeStruct((width, head), HALF)
    scores_shape = jax.ShapeDtypeStruct((HEADS * rows, rows), HALF)
    gain_shape = jax.ShapeDtypeStruct((HEADS, head), F32)
    token_shape = jax.ShapeDtypeStruct((8, head), F32)
    whole = pltpu.VMEM((features, head), HALF)
    gain_row = gain.reshape(1, features)

    (first,) = call(
        part(first_state_kernel, head, 1),
        [piece],
        [pltpu.with_memory_space_constraint(a, pltpu.HBM) for a in (k, v)],
        1,
        [pltpu.VMEM((rows, width), HALF)] * 2 + [pltpu.SemaphoreType.DMA((2,))],
        ins={0: HBM, 1: HBM},
    )
    slots = (2, 3, 0)
    rest = call(
        part(state_kernel, head, slots), [piece] * 3, [k, v, first], 1, ins={2: ANY}
    )
    pieces = dict(zip(slots, rest))
    pieces[1] = first
    pieces = [pieces[slot] for slot in range(group)]
    scores, intra = call(part(local_kernel, head), [scores_shape, wide], [q, k, v], 2)
    prefix, _ = exclusive_scan(pieces, STATE_ORDERS, width, False, intra)
    message = jax.ShapeDtypeStruct((width + 2 * HEADS, head), HALF)
    sources = [q, intra, gain_row, cot]
    early, squares, inner = call(
        part(early_norm_kernel, head, STATE_ORDERS[1]),
        [wide, square, square],
        sources + prefix[:-1],
        1,
    )
    late, inverse, grad, *pieces = call(
        part(norm_kernel, head, group, NORM_ORDERS, lax.axis_size("dp")),
        [jax.ShapeDtypeStruct((rows, width), F32), square, half] + [message] * group,
        sources + [early, squares, inner, prefix[-1]],
        2,
        [pltpu.VMEM((1, features), F32), pltpu.VMEM((HEADS, head), F32)],
    )
    output, grad_query, key_part, value_part, token = call(
        part(backward_kernel, head, group),
        [half, half, wide, wide, token_shape],
        [q, k, v, scores, grad, early, late, inverse, gain_row] + prefix,
        5,
        [whole],
    )
    suffix, gain_grad = exclusive_scan(pieces, GRAD_ORDERS, width, True, token)
    gains = [gain_grad, swap(gain_grad, "dp", 1)]
    inputs = [k, v, key_part, value_part]
    outs = []
    for slots in ((0, 1), (2, 3)):
        last = group - 1 in slots
        at = len(inputs) + len(slots)
        results = call(
            part(final_kernel, head, slots, last),
            [half, half] + [gain_shape] * last,
            inputs + [suffix[slot] for slot in slots] + outs + (gains if last else []),
            1,
            [pltpu.VMEM((len(slots), rows, width), HALF)] * 2
            + [pltpu.SemaphoreType.DMA((2, len(slots)))]
            + [pltpu.VMEM((HEADS, head), F32), pltpu.SemaphoreType.DMA(())] * last,
            ins={at + i: HBM for i in range(len(outs))},
            out_specs={0: HBM, 1: HBM, 2: HBM},
            aliases={at + i: i for i in range(len(outs))},
        )
        outs = list(results[:2])
    grad_key, grad_value, gain_grad = results
    return (
        output[None],
        grad_query[None],
        grad_key[None],
        grad_value[None],
        gain_grad.reshape(features),
    )


def solution(mesh):
    spec = P("dp", "seq", None)
    return jax.shard_map(
        per_device,
        mesh=mesh,
        in_specs=(spec, spec, spec, P(), spec),
        out_specs=(spec, spec, spec, spec, P()),
        check_vma=False,
    )
```

```python
import functools

import jax
import jax.numpy as jnp
from jax import lax
from jax.experimental import pallas as pl
from jax.experimental.pallas import tpu as pltpu
from jax.sharding import PartitionSpec as P

HEADS = 16

EPSILON = 1e-06

F32 = jnp.float32
HALF = jnp.bfloat16


def dot(lhs, rhs, lhs_dim, rhs_dim):
    return lax.dot_general(
        lhs, rhs, (((lhs_dim,), (rhs_dim,)), ((), ())), preferred_element_type=F32
    )


def causal(size):
    rows = lax.broadcasted_iota(jnp.int32, (size, size), 0)
    columns = lax.broadcasted_iota(jnp.int32, (size, size), 1)
    return rows >= columns


def member_of(group):
    return lax.rem(lax.axis_index("seq"), group)


STATE_ORDERS = (((0, 1, 2, 3), (0, 2, 1, 3)), ((0, 2, 1, 3), (0, 1, 2, 3)))
GRAD_ORDERS = (((0, 3, 1, 2), (0, 3, 1, 2)), ((0, 3, 1, 2), (0, 1, 2, 3)))
NORM_ORDERS = (STATE_ORDERS[1], GRAD_ORDERS[0])


def partner_of(order, slot):
    even, odd = order[0][slot], order[1][slot]
    offset = even
    if even != odd:
        offset = jnp.where(lax.rem(lax.axis_index("dp"), 2) == 1, odd, even)
    return member_of(len(order[0])) ^ offset


def block_at(index, size):
    return pl.ds(pl.multiple_of(index * size, size), size)


def gathered(order, piece_refs, size, whole_ref):
    for j, ref in enumerate(piece_refs):
        whole_ref[block_at(partner_of(order, j), size), :] = ref[0:size, :]


def columns(first, count):
    return slice(first, first + count)


def first_state_kernel(head, slot, k_ref, v_ref, piece_ref, k_buffer, v_buffer, arrived):
    width = piece_ref.shape[0]
    source = block_at(partner_of(STATE_ORDERS[0], slot), width)
    step = k_buffer.shape[0] // arrived.shape[1]
    copies = []
    for i in range(arrived.shape[1]):
        part = columns(i * step, step)
        for n, (ref, buffer) in enumerate(((k_ref, k_buffer), (v_ref, v_buffer))):
            copies.append(
                pltpu.make_async_copy(
                    ref.at[part, source], buffer.at[part, :], arrived.at[n, i]
                )
            )
    for copy in copies:
        copy.start()
    for copy in copies:
        copy.wait()
    for i in range(width // head):
        part = columns(i * head, head)
        piece_ref[part, :] = dot(k_buffer[:, part], v_buffer[:, part], 0, 0).astype(HALF)


def state_kernel(head, slots, k_ref, v_ref, token_ref, *piece_refs):
    del token_ref
    for slot, piece_ref in zip(slots, piece_refs):
        width = piece_ref.shape[0]
        for i in range(width // head):
            part = features_at(STATE_ORDERS[0], slot, i, width, head)
            piece_ref[columns(i * head, head), :] = dot(
                k_ref[:, part], v_ref[:, part], 0, 0
            ).astype(HALF)


def local_kernel(head, q_ref, k_ref, v_ref, scores_ref, intra_ref):
    rows = q_ref.shape[0]
    mask = causal(rows)
    scaling = head ** (-0.5)
    for h in range(HEADS):
        part = columns(h * head, head)
        scores = dot(q_ref[:, part], k_ref[:, part], 1, 1) * scaling
        scores = jnp.where(mask, scores, 0.0).astype(HALF)
        scores_ref[columns(h * rows, rows), :] = scores
        intra_ref[:, part] = dot(scores, v_ref[:, part], 1, 0)


def features_at(order, slot, i, width, head):
    start = partner_of(order, slot) * width + i * head
    return pl.ds(pl.multiple_of(start, head), head)


def attend(head, order, slot, refs, prefix_ref, attended_ref, at, squares, inner):
    q_ref, intra_ref, gain_ref, cot_ref = refs
    scaling = head ** (-0.5)
    width = prefix_ref.shape[0]
    for i in range(width // head):
        part = features_at(order, slot, i, width, head)
        prefix = prefix_ref[columns(i * head, head), :]
        attended = intra_ref[:, part] + scaling * dot(q_ref[:, part], prefix, 1, 0)
        attended_ref[:, part if at is None else columns(i * head, head)] = attended
        scaled = cot_ref[:, part].astype(F32) * gain_ref[:, part]
        squares += attended * attended
        inner += scaled * attended
    return squares, inner


def early_norm_kernel(head, order, *refs):
    prefix_refs, (attended_ref, squares_ref, inner_ref) = refs[4:-3], refs[-3:]
    squares = jnp.zeros(squares_ref.shape, F32)
    inner = jnp.zeros(squares_ref.shape, F32)
    for slot, prefix_ref in enumerate(prefix_refs):
        squares, inner = attend(
            head, order, slot, refs[:4], prefix_ref, attended_ref, None, squares, inner
        )
    squares_ref[...] = squares
    inner_ref[...] = inner


def norm_kernel(head, group, orders, replicas, *refs):
    q_ref, _, gain_ref, cot_ref = refs[:4]
    early_ref, squares_ref, inner_ref, prefix_ref = refs[4:8]
    late_ref, inverse_ref, grad_ref = refs[8:11]
    piece_refs = refs[11 : 11 + group]
    gain_grad_ref, gain_rows_ref = refs[11 + group :]
    features = q_ref.shape[1]
    width = features // group
    odd = lax.rem(lax.axis_index("dp"), 2) == 1
    squares, inner = attend(
        head,
        orders[0],
        group - 1,
        refs[:4],
        prefix_ref,
        late_ref,
        0,
        squares_ref[...],
        inner_ref[...],
    )
    inverse = lax.rsqrt(
        jnp.sum(squares, axis=1, keepdims=True) * (1.0 / features) + EPSILON
    )
    inner_mean = jnp.sum(inner, axis=1, keepdims=True) * (1.0 / features) * inverse
    inverse_ref[...] = jnp.broadcast_to(inverse, inverse_ref.shape)
    scaling = head ** (-0.5)
    for slot in range(group):
        for i in range(width // head):
            part = features_at(orders[1], slot, i, width, head)
            local = columns(i * head, head)
            late = [order[slot] == before[-1] for before, order in zip(*orders)]
            attended = late_ref[:, local] if late[0] else early_ref[:, part]
            if late[0] != late[1]:
                other = late_ref[:, local] if late[1] else early_ref[:, part]
                attended = jnp.where(odd, other, attended)
            normalized = attended * inverse
            upstream = cot_ref[:, part].astype(F32)
            gain_grad_ref[:, part] = jnp.sum(
                upstream * normalized, axis=0, keepdims=True
            ) * (1.0 / replicas)
            scaled = upstream * gain_ref[:, part]
            grad = ((scaled - normalized * inner_mean) * inverse).astype(HALF)
            grad_ref[:, part] = grad
            piece_refs[slot][local, :] = (
                scaling * dot(q_ref[:, part], grad, 0, 0)
            ).astype(HALF)
    for h in range(HEADS):
        gain_rows_ref[h : h + 1, :] = gain_grad_ref[:, columns(h * head, head)]
    for ref in piece_refs:
        put_wide_rows(ref, width, gain_rows_ref[...])


def backward_kernel(head, group, *refs):
    q_ref, k_ref, v_ref, scores_ref, grad_ref = refs[:5]
    early_ref, late_ref, inverse_ref, gain_ref = refs[5:9]
    prefix_refs = refs[9 : 9 + group]
    out_ref, grad_query_ref, key_part_ref, value_part_ref, token_ref = refs[
        9 + group : 14 + group
    ]
    whole_ref = refs[14 + group]
    rows = q_ref.shape[0]
    mask = causal(rows)
    scaling = head ** (-0.5)
    gathered(STATE_ORDERS[1], prefix_refs, prefix_refs[0].shape[0], whole_ref)
    inverse = inverse_ref[...]
    width = late_ref.shape[1]
    for slot in range(group):
        for i in range(width // head):
            part = features_at(STATE_ORDERS[1], slot, i, width, head)
            if slot == group - 1:
                attended = late_ref[:, columns(i * head, head)]
            else:
                attended = early_ref[:, part]
            out_ref[:, part] = (gain_ref[:, part] * (attended * inverse)).astype(HALF)
    for h in range(HEADS):
        part = columns(h * head, head)
        grad = grad_ref[:, part]
        grad_scores = dot(grad, v_ref[:, part], 1, 1)
        grad_scores = jnp.where(mask, grad_scores, 0.0).astype(HALF)
        grad_query = dot(grad_scores, k_ref[:, part], 1, 0) + dot(
            grad, whole_ref[part, :], 1, 1
        )
        grad_query_ref[:, part] = (scaling * grad_query).astype(HALF)
        key_part_ref[:, part] = scaling * dot(grad_scores, q_ref[:, part], 0, 0)
        value_part_ref[:, part] = dot(
            scores_ref[columns(h * rows, rows), :], grad, 0, 0
        )
    token_ref[...] = jnp.zeros_like(token_ref)


def final_kernel(head, slots, last, *refs):
    k_ref, v_ref, key_part_ref, value_part_ref = refs[:4]
    suffix_refs = refs[4 : 4 + len(slots)]
    refs = refs[4 + len(slots) :]
    copies = []
    if last:
        gain_grad_ref, total_ref, gain_written = refs[-6], refs[-2], refs[-1]
        total_ref[...] = tree_sum([ref[...] for ref in refs[2:-8]])
        copies.append(pltpu.make_async_copy(total_ref, gain_grad_ref, gain_written))
        copies[0].start()
        out_refs, refs = refs[-8:-6], refs[-5:-2]
    else:
        out_refs, refs = refs[-5:-3], refs[-3:]
    key_buffer, value_buffer, written = refs
    width = key_buffer.shape[2]
    for n, slot in enumerate(slots):
        for i in range(width // head):
            part = features_at(GRAD_ORDERS[1], slot, i, width, head)
            local = columns(i * head, head)
            suffix = suffix_refs[n][local, :]
            key_buffer[n, :, local] = (
                key_part_ref[:, part] + dot(v_ref[:, part], suffix, 1, 1)
            ).astype(HALF)
            value_buffer[n, :, local] = (
                value_part_ref[:, part] + dot(k_ref[:, part], suffix, 1, 0)
            ).astype(HALF)
        for i, buffer in enumerate((key_buffer, value_buffer)):
            copy = pltpu.make_async_copy(
                buffer.at[n],
                out_refs[i].at[:, block_at(partner_of(GRAD_ORDERS[1], slot), width)],
                written.at[i, n],
            )
            copy.start()
            copies.append(copy)
    for copy in copies:
        copy.wait()


def tree_sum(terms):
    while len(terms) > 1:
        terms = [a + b for a, b in zip(terms[::2], terms[1::2])]
    return terms[0]


def wide_rows(ref, start):
    rows = (ref.shape[0] - start) // 2
    high = ref[columns(start, rows), :].astype(F32)
    return high + ref[columns(start + rows, rows), :].astype(F32)


def put_wide_rows(ref, start, value):
    rows = value.shape[0]
    high = value.astype(HALF)
    ref[columns(start, rows), :] = high
    ref[columns(start + rows, rows), :] = (value - high.astype(F32)).astype(HALF)


def total_kernel(size, count, *refs):
    refs, out_refs = refs[:count], refs[count + 1 :]
    total = refs[0][0:size, :].astype(F32)
    for ref in refs[1:]:
        total += ref[0:size, :].astype(F32)
    out_refs[0][0:size, :] = total.astype(HALF)
    if len(out_refs) > 1:
        gain = tree_sum([wide_rows(ref, size) for ref in refs])
        put_wide_rows(out_refs[0], size, gain)
        out_refs[1][...] = wide_rows(out_refs[0], size)


def group_flag(group, reverse, distance):
    index = lax.axis_index("seq") // group
    last = lax.axis_size("seq") // group - 1
    known = index + distance <= last if reverse else index >= distance
    return jnp.where(known, 1.0, 0.0)


def carry_kernel(group, reverse, distance, first, own_ref, moved_ref, out_ref):
    own = own_ref[...].astype(F32)
    if first:
        own = own * group_flag(group, reverse, 1)
    moved = moved_ref[...].astype(F32) * group_flag(group, reverse, distance)
    out_ref[...] = (own + moved).astype(HALF)


def scan_kernel(group, orders, slots, reverse, masked, size, riding, *refs):
    sources = [partner_of(orders[0], j) for j in range(group)]
    carry = refs[0][0:size, :].astype(F32)
    if masked:
        carry = carry * group_flag(group, reverse, 1)
    blocks = [ref[0:size, :].astype(F32) for ref in refs[1 : 1 + group]]
    out_refs = refs[-len(slots) - riding :][: len(slots)]
    for slot, out_ref in zip(slots, out_refs):
        target = partner_of(orders[1], slot)
        total = carry
        for i in range(group):
            known = sources[i] > target if reverse else sources[i] < target
            total += jnp.where(known, 1.0, 0.0) * blocks[i]
        out_ref[...] = total.astype(HALF)
    if riding:
        refs[-1][...] = refs[1 + group][...] + wide_rows(refs[0], size)


VMEM = pl.BlockSpec(memory_space=pltpu.VMEM)
ANY = pl.BlockSpec(memory_space=pl.ANY)
HBM = pl.BlockSpec(memory_space=pltpu.HBM)


def call(kernel, outs, args, matmuls, scratch=(), ins=None, out_specs=None, aliases=None):
    size = sum(a.size * a.dtype.itemsize for a in args)
    size += sum(o.size * o.dtype.itemsize for o in outs)
    ins = ins or {}
    out_specs = out_specs or {}
    return pl.pallas_call(
        kernel,
        out_shape=tuple(outs),
        in_specs=[ins.get(i, VMEM) for i in range(len(args))],
        out_specs=tuple(out_specs.get(i, VMEM) for i in range(len(outs))),
        scratch_shapes=list(scratch),
        input_output_aliases=aliases or {},
        compiler_params=pltpu.CompilerParams(vmem_limit_bytes=16 * 1024 * 1024),
        cost_estimate=pl.CostEstimate(
            flops=2 * 128 * 128 * 128 * HEADS * matmuls,
            bytes_accessed=size,
            transcendentals=0,
        ),
    )(*args)


def swap(array, axis, offset):
    count = lax.axis_size(axis)
    return lax.ppermute(array, axis, [(i, i ^ offset) for i in range(count)])


def own_and_swapped(pieces, order):
    count = lax.axis_size("seq")
    results = [pieces[0]]
    for slot in range(1, len(pieces)):
        pairs = []
        for row in range(lax.axis_size("dp")):
            offset = order[row % 2][slot]
            pairs += [(row * count + i, row * count + (i ^ offset)) for i in range(count)]
        results.append(lax.ppermute(pieces[slot], ("dp", "seq"), pairs))
    return results


def exclusive_scan(pieces, orders, size, reverse, token):
    group = len(pieces)
    count, rows = lax.axis_size("seq"), lax.axis_size("dp")
    groups = count // group
    part = functools.partial
    lanes = pieces[0].shape[1]
    extra = pieces[0].shape[0] - size
    piece = jax.ShapeDtypeStruct((size, lanes), HALF)
    gain_shape = jax.ShapeDtypeStruct((extra // 2, lanes), F32)

    def shifted(array, distance):
        step = -distance if reverse else distance
        pairs = [(i, (i + step) % count) for i in range(count)]
        return lax.ppermute(array, "seq", pairs)

    received = own_and_swapped(pieces, orders[0])
    totals = call(
        part(total_kernel, size, group),
        [jax.ShapeDtypeStruct(pieces[0].shape, HALF)] + [gain_shape] * (extra > 0),
        received + [token],
        0,
        ins={group: ANY},
    )
    total, gains = totals[0], list(totals[1:])
    riding = int(extra > 0 and groups == 2 and rows == 4)
    carry = shifted(total if riding else total[:size], group)
    if riding:
        for offset in (0, group):
            pairs = [
                (row * count + i, (row ^ 2) * count + (i ^ offset))
                for row in range(rows)
                for i in range(count)
            ]
            gains.append(lax.ppermute(gains[0], ("dp", "seq"), pairs))
    elif extra:
        gains = [tree_sum(summed_over("seq", group, gains[0]))]
        gains = [tree_sum(summed_over("dp", 2, gains[0]))]
    distance = 1
    while distance < groups - 1:
        moved = shifted(carry, distance * group)
        kernel = part(
            carry_kernel, group, reverse, distance + (distance == 1), distance == 1
        )
        (carry,) = call(kernel, [piece], [carry, moved], 0)
        distance *= 2
    pieces, after = {}, []
    for slots in ((1,), (2,), (3, 0)):
        adding = riding if 0 in slots else 0
        inputs = [carry] + received + gains[:adding] + after
        sums = call(
            part(scan_kernel, group, orders, slots, reverse, groups <= 2, size, adding),
            [piece] * len(slots) + [gain_shape] * adding,
            inputs,
            0,
            ins={len(inputs) - 1: ANY} if after else {},
        )
        pieces.update(zip(slots, sums))
        after = [sums[0]]
    results = own_and_swapped([pieces[slot] for slot in range(group)], orders[1])
    if riding:
        gains = [sums[-1] + (gains[1] + gains[2])]
    return results, (gains[0] if gains else None)


def summed_over(axis, stride, array):
    count = lax.axis_size(axis)
    terms = [array]
    while stride < count:
        array = tree_sum(terms)
        width = 4 if count // stride % 4 == 0 else 2
        order = sorted(range(1, width), key=lambda i: i % 2)
        moved = {i: swap(array, axis, i * stride) for i in order}
        terms = [array] + [moved[i] for i in range(1, width)]
        stride *= width
    return terms


def per_device(queries, keys, values, gain, cotangent):
    q, k, v, cot = queries[0], keys[0], values[0], cotangent[0]
    rows, features = q.shape
    head = features // HEADS
    group = 4
    width = features // group
    part = functools.partial
    wide = jax.ShapeDtypeStruct((rows, features), F32)
    half = jax.ShapeDtypeStruct((rows, features), HALF)
    square = jax.ShapeDtypeStruct((rows, head), F32)
    piece = jax.ShapeDtypeStruct((width, head), HALF)
    scores_shape = jax.ShapeDtypeStruct((HEADS * rows, rows), HALF)
    gain_shape = jax.ShapeDtypeStruct((HEADS, head), F32)
    token_shape = jax.ShapeDtypeStruct((8, head), F32)
    whole = pltpu.VMEM((features, head), HALF)
    gain_row = gain.reshape(1, features)

    (first,) = call(
        part(first_state_kernel, head, 1),
        [piece],
        [pltpu.with_memory_space_constraint(a, pltpu.HBM) for a in (k, v)],
        1,
        [pltpu.VMEM((rows, width), HALF)] * 2 + [pltpu.SemaphoreType.DMA((2, 2))],
        ins={0: HBM, 1: HBM},
    )
    slots = (2, 3, 0)
    rest = call(
        part(state_kernel, head, slots), [piece] * 3, [k, v, first], 1, ins={2: ANY}
    )
    pieces = dict(zip(slots, rest))
    pieces[1] = first
    pieces = [pieces[slot] for slot in range(group)]
    scores, intra = call(part(local_kernel, head), [scores_shape, wide], [q, k, v], 2)
    prefix, _ = exclusive_scan(pieces, STATE_ORDERS, width, False, intra)
    message = jax.ShapeDtypeStruct((width + 2 * HEADS, head), HALF)
    sources = [q, intra, gain_row, cot]
    early, squares, inner = call(
        part(early_norm_kernel, head, STATE_ORDERS[1]),
        [wide, square, square],
        sources + prefix[:-1],
        1,
    )
    late, inverse, grad, *pieces = call(
        part(norm_kernel, head, group, NORM_ORDERS, lax.axis_size("dp")),
        [jax.ShapeDtypeStruct((rows, width), F32), square, half] + [message] * group,
        sources + [early, squares, inner, prefix[-1]],
        2,
        [pltpu.VMEM((1, features), F32), pltpu.VMEM((HEADS, head), F32)],
    )
    output, grad_query, key_part, value_part, token = call(
        part(backward_kernel, head, group),
        [half, half, wide, wide, token_shape],
        [q, k, v, scores, grad, early, late, inverse, gain_row] + prefix,
        5,
        [whole],
    )
    suffix, gain_grad = exclusive_scan(pieces, GRAD_ORDERS, width, True, token)
    gains = [gain_grad, swap(gain_grad, "dp", 1)]
    inputs = [k, v, key_part, value_part]
    outs = []
    for slots in ((0, 1), (2, 3)):
        last = group - 1 in slots
        at = len(inputs) + len(slots)
        results = call(
            part(final_kernel, head, slots, last),
            [half, half] + [gain_shape] * last,
            inputs + [suffix[slot] for slot in slots] + outs + (gains if last else []),
            1,
            [pltpu.VMEM((len(slots), rows, width), HALF)] * 2
            + [pltpu.SemaphoreType.DMA((2, len(slots)))]
            + [pltpu.VMEM((HEADS, head), F32), pltpu.SemaphoreType.DMA(())] * last,
            ins={at + i: HBM for i in range(len(outs))},
            out_specs={0: HBM, 1: HBM, 2: HBM},
            aliases={at + i: i for i in range(len(outs))},
        )
        outs = list(results[:2])
    grad_key, grad_value, gain_grad = results
    return (
        output[None],
        grad_query[None],
        grad_key[None],
        grad_value[None],
        gain_grad.reshape(features),
    )


def solution(mesh):
    spec = P("dp", "seq", None)
    return jax.shard_map(
        per_device,
        mesh=mesh,
        in_specs=(spec, spec, spec, P(), spec),
        out_specs=(spec, spec, spec, spec, P()),
        check_vma=False,
    )
```

```python
import functools

import jax
import jax.numpy as jnp
from jax import lax
from jax.experimental import pallas as pl
from jax.experimental.pallas import tpu as pltpu
from jax.sharding import PartitionSpec as P

HEADS = 16

EPSILON = 1e-06

F32 = jnp.float32
HALF = jnp.bfloat16


def dot(lhs, rhs, lhs_dim, rhs_dim):
    return lax.dot_general(
        lhs, rhs, (((lhs_dim,), (rhs_dim,)), ((), ())), preferred_element_type=F32
    )


def causal(size):
    rows = lax.broadcasted_iota(jnp.int32, (size, size), 0)
    columns = lax.broadcasted_iota(jnp.int32, (size, size), 1)
    return rows >= columns


def member_of(group):
    return lax.rem(lax.axis_index("seq"), group)


STATE_ORDERS = (((0, 1, 2, 3), (0, 2, 1, 3)), ((0, 2, 1, 3), (0, 1, 2, 3)))
GRAD_ORDERS = (((0, 3, 1, 2), (0, 3, 1, 2)), ((0, 3, 1, 2), (0, 1, 2, 3)))
NORM_ORDERS = (STATE_ORDERS[1], GRAD_ORDERS[0])


def partner_of(order, slot):
    even, odd = order[0][slot], order[1][slot]
    offset = even
    if even != odd:
        offset = jnp.where(lax.rem(lax.axis_index("dp"), 2) == 1, odd, even)
    return member_of(len(order[0])) ^ offset


def block_at(index, size):
    return pl.ds(pl.multiple_of(index * size, size), size)


def gathered(order, piece_refs, size, whole_ref):
    for j, ref in enumerate(piece_refs):
        whole_ref[block_at(partner_of(order, j), size), :] = ref[0:size, :]


def columns(first, count):
    return slice(first, first + count)


def first_state_kernel(head, slot, k_ref, v_ref, piece_ref, k_buffer, v_buffer, arrived):
    width = piece_ref.shape[0]
    source = block_at(partner_of(STATE_ORDERS[0], slot), width)
    copies = [
        pltpu.make_async_copy(k_ref.at[:, source], k_buffer, arrived.at[0]),
        pltpu.make_async_copy(v_ref.at[:, source], v_buffer, arrived.at[1]),
    ]
    for copy in copies:
        copy.start()
    for copy in copies:
        copy.wait()
    for i in range(width // head):
        part = columns(i * head, head)
        piece_ref[part, :] = dot(k_buffer[:, part], v_buffer[:, part], 0, 0).astype(HALF)


def state_kernel(head, slots, k_ref, v_ref, token_ref, *piece_refs):
    del token_ref
    for slot, piece_ref in zip(slots, piece_refs):
        width = piece_ref.shape[0]
        for i in range(width // head):
            part = features_at(STATE_ORDERS[0], slot, i, width, head)
            piece_ref[columns(i * head, head), :] = dot(
                k_ref[:, part], v_ref[:, part], 0, 0
            ).astype(HALF)


def local_kernel(head, q_ref, k_ref, v_ref, scores_ref, intra_ref):
    rows = q_ref.shape[0]
    mask = causal(rows)
    scaling = head ** (-0.5)
    for h in range(HEADS):
        part = columns(h * head, head)
        scores = dot(q_ref[:, part], k_ref[:, part], 1, 1) * scaling
        scores = jnp.where(mask, scores, 0.0).astype(HALF)
        scores_ref[columns(h * rows, rows), :] = scores
        intra_ref[:, part] = dot(scores, v_ref[:, part], 1, 0)


def features_at(order, slot, i, width, head):
    start = partner_of(order, slot) * width + i * head
    return pl.ds(pl.multiple_of(start, head), head)


def attend(head, order, slot, refs, prefix_ref, attended_ref, at, squares, inner):
    q_ref, intra_ref, gain_ref, cot_ref = refs
    scaling = head ** (-0.5)
    width = prefix_ref.shape[0]
    for i in range(width // head):
        part = features_at(order, slot, i, width, head)
        prefix = prefix_ref[columns(i * head, head), :]
        attended = intra_ref[:, part] + scaling * dot(q_ref[:, part], prefix, 1, 0)
        attended_ref[:, part if at is None else columns(i * head, head)] = attended
        scaled = cot_ref[:, part].astype(F32) * gain_ref[:, part]
        squares += attended * attended
        inner += scaled * attended
    return squares, inner


def early_norm_kernel(head, order, *refs):
    prefix_refs, (attended_ref, squares_ref, inner_ref) = refs[4:-3], refs[-3:]
    squares = jnp.zeros(squares_ref.shape, F32)
    inner = jnp.zeros(squares_ref.shape, F32)
    for slot, prefix_ref in enumerate(prefix_refs):
        squares, inner = attend(
            head, order, slot, refs[:4], prefix_ref, attended_ref, None, squares, inner
        )
    squares_ref[...] = squares
    inner_ref[...] = inner


def norm_kernel(head, group, orders, replicas, *refs):
    q_ref, _, gain_ref, cot_ref = refs[:4]
    early_ref, squares_ref, inner_ref, prefix_ref = refs[4:8]
    late_ref, inverse_ref, grad_ref = refs[8:11]
    piece_refs = refs[11 : 11 + group]
    gain_grad_ref, gain_rows_ref = refs[11 + group :]
    features = q_ref.shape[1]
    width = features // group
    odd = lax.rem(lax.axis_index("dp"), 2) == 1
    squares, inner = attend(
        head,
        orders[0],
        group - 1,
        refs[:4],
        prefix_ref,
        late_ref,
        0,
        squares_ref[...],
        inner_ref[...],
    )
    inverse = lax.rsqrt(
        jnp.sum(squares, axis=1, keepdims=True) * (1.0 / features) + EPSILON
    )
    inner_mean = jnp.sum(inner, axis=1, keepdims=True) * (1.0 / features) * inverse
    inverse_ref[...] = jnp.broadcast_to(inverse, inverse_ref.shape)
    scaling = head ** (-0.5)
    for slot in range(group):
        for i in range(width // head):
            part = features_at(orders[1], slot, i, width, head)
            local = columns(i * head, head)
            late = [order[slot] == before[-1] for before, order in zip(*orders)]
            attended = late_ref[:, local] if late[0] else early_ref[:, part]
            if late[0] != late[1]:
                other = late_ref[:, local] if late[1] else early_ref[:, part]
                attended = jnp.where(odd, other, attended)
            normalized = attended * inverse
            upstream = cot_ref[:, part].astype(F32)
            gain_grad_ref[:, part] = jnp.sum(
                upstream * normalized, axis=0, keepdims=True
            ) * (1.0 / replicas)
            scaled = upstream * gain_ref[:, part]
            grad = ((scaled - normalized * inner_mean) * inverse).astype(HALF)
            grad_ref[:, part] = grad
            piece_refs[slot][local, :] = (
                scaling * dot(q_ref[:, part], grad, 0, 0)
            ).astype(HALF)
    for h in range(HEADS):
        gain_rows_ref[h : h + 1, :] = gain_grad_ref[:, columns(h * head, head)]
    for ref in piece_refs:
        put_wide_rows(ref, width, gain_rows_ref[...])


def backward_kernel(head, group, *refs):
    q_ref, k_ref, v_ref, scores_ref, grad_ref = refs[:5]
    early_ref, late_ref, inverse_ref, gain_ref = refs[5:9]
    prefix_refs = refs[9 : 9 + group]
    out_ref, grad_query_ref, key_part_ref, value_part_ref, token_ref = refs[
        9 + group : 14 + group
    ]
    whole_ref = refs[14 + group]
    rows = q_ref.shape[0]
    mask = causal(rows)
    scaling = head ** (-0.5)
    gathered(STATE_ORDERS[1], prefix_refs, prefix_refs[0].shape[0], whole_ref)
    inverse = inverse_ref[...]
    width = late_ref.shape[1]
    for slot in range(group):
        for i in range(width // head):
            part = features_at(STATE_ORDERS[1], slot, i, width, head)
            if slot == group - 1:
                attended = late_ref[:, columns(i * head, head)]
            else:
                attended = early_ref[:, part]
            out_ref[:, part] = (gain_ref[:, part] * (attended * inverse)).astype(HALF)
    for h in range(HEADS):
        part = columns(h * head, head)
        grad = grad_ref[:, part]
        grad_scores = dot(grad, v_ref[:, part], 1, 1)
        grad_scores = jnp.where(mask, grad_scores, 0.0).astype(HALF)
        grad_query = dot(grad_scores, k_ref[:, part], 1, 0) + dot(
            grad, whole_ref[part, :], 1, 1
        )
        grad_query_ref[:, part] = (scaling * grad_query).astype(HALF)
        key_part_ref[:, part] = scaling * dot(grad_scores, q_ref[:, part], 0, 0)
        value_part_ref[:, part] = dot(
            scores_ref[columns(h * rows, rows), :], grad, 0, 0
        )
    token_ref[...] = jnp.zeros_like(token_ref)


def final_kernel(head, slots, last, *refs):
    k_ref, v_ref, key_part_ref, value_part_ref = refs[:4]
    suffix_refs = refs[4 : 4 + len(slots)]
    refs = refs[4 + len(slots) :]
    copies = []
    if last:
        gain_grad_ref, total_ref, gain_written = refs[-6], refs[-2], refs[-1]
        total_ref[...] = tree_sum([ref[...] for ref in refs[2:-8]])
        copies.append(pltpu.make_async_copy(total_ref, gain_grad_ref, gain_written))
        copies[0].start()
        out_refs, refs = refs[-8:-6], refs[-5:-2]
    else:
        out_refs, refs = refs[-5:-3], refs[-3:]
    key_buffer, value_buffer, written = refs
    width = key_buffer.shape[2]
    for n, slot in enumerate(slots):
        for i in range(width // head):
            part = features_at(GRAD_ORDERS[1], slot, i, width, head)
            local = columns(i * head, head)
            suffix = suffix_refs[n][local, :]
            key_buffer[n, :, local] = (
                key_part_ref[:, part] + dot(v_ref[:, part], suffix, 1, 1)
            ).astype(HALF)
            value_buffer[n, :, local] = (
                value_part_ref[:, part] + dot(k_ref[:, part], suffix, 1, 0)
            ).astype(HALF)
        for i, buffer in enumerate((key_buffer, value_buffer)):
            copy = pltpu.make_async_copy(
                buffer.at[n],
                out_refs[i].at[:, block_at(partner_of(GRAD_ORDERS[1], slot), width)],
                written.at[i, n],
            )
            copy.start()
            copies.append(copy)
    for copy in copies:
        copy.wait()


def tree_sum(terms):
    while len(terms) > 1:
        terms = [a + b for a, b in zip(terms[::2], terms[1::2])]
    return terms[0]


def wide_rows(ref, start):
    rows = (ref.shape[0] - start) // 2
    high = ref[columns(start, rows), :].astype(F32)
    return high + ref[columns(start + rows, rows), :].astype(F32)


def put_wide_rows(ref, start, value):
    rows = value.shape[0]
    high = value.astype(HALF)
    ref[columns(start, rows), :] = high
    ref[columns(start + rows, rows), :] = (value - high.astype(F32)).astype(HALF)


def total_kernel(size, count, *refs):
    refs, out_refs = refs[:count], refs[count + 1 :]
    total = refs[0][0:size, :].astype(F32)
    for ref in refs[1:]:
        total += ref[0:size, :].astype(F32)
    out_refs[0][0:size, :] = total.astype(HALF)
    if len(out_refs) > 1:
        gain = tree_sum([wide_rows(ref, size) for ref in refs])
        put_wide_rows(out_refs[0], size, gain)
        out_refs[1][...] = wide_rows(out_refs[0], size)


def group_flag(group, reverse, distance):
    index = lax.axis_index("seq") // group
    last = lax.axis_size("seq") // group - 1
    known = index + distance <= last if reverse else index >= distance
    return jnp.where(known, 1.0, 0.0)


def carry_kernel(group, reverse, distance, first, own_ref, moved_ref, out_ref):
    own = own_ref[...].astype(F32)
    if first:
        own = own * group_flag(group, reverse, 1)
    moved = moved_ref[...].astype(F32) * group_flag(group, reverse, distance)
    out_ref[...] = (own + moved).astype(HALF)


def scan_kernel(group, orders, slots, reverse, masked, size, riding, *refs):
    sources = [partner_of(orders[0], j) for j in range(group)]
    carry = refs[0][0:size, :].astype(F32)
    if masked:
        carry = carry * group_flag(group, reverse, 1)
    blocks = [ref[0:size, :].astype(F32) for ref in refs[1 : 1 + group]]
    out_refs = refs[-len(slots) - riding :][: len(slots)]
    for slot, out_ref in zip(slots, out_refs):
        target = partner_of(orders[1], slot)
        total = carry
        for i in range(group):
            known = sources[i] > target if reverse else sources[i] < target
            total += jnp.where(known, 1.0, 0.0) * blocks[i]
        out_ref[...] = total.astype(HALF)
    if riding:
        refs[-1][...] = refs[1 + group][...] + wide_rows(refs[0], size)


VMEM = pl.BlockSpec(memory_space=pltpu.VMEM)
ANY = pl.BlockSpec(memory_space=pl.ANY)
HBM = pl.BlockSpec(memory_space=pltpu.HBM)


def call(kernel, outs, args, matmuls, scratch=(), ins=None, out_specs=None, aliases=None):
    size = sum(a.size * a.dtype.itemsize for a in args)
    size += sum(o.size * o.dtype.itemsize for o in outs)
    ins = ins or {}
    out_specs = out_specs or {}
    return pl.pallas_call(
        kernel,
        out_shape=tuple(outs),
        in_specs=[ins.get(i, VMEM) for i in range(len(args))],
        out_specs=tuple(out_specs.get(i, VMEM) for i in range(len(outs))),
        scratch_shapes=list(scratch),
        input_output_aliases=aliases or {},
        compiler_params=pltpu.CompilerParams(vmem_limit_bytes=16 * 1024 * 1024),
        cost_estimate=pl.CostEstimate(
            flops=2 * 128 * 128 * 128 * HEADS * matmuls,
            bytes_accessed=size,
            transcendentals=0,
        ),
    )(*args)


def swap(array, axis, offset):
    count = lax.axis_size(axis)
    return lax.ppermute(array, axis, [(i, i ^ offset) for i in range(count)])


def own_and_swapped(pieces, order):
    count = lax.axis_size("seq")
    results = [pieces[0]]
    for slot in range(1, len(pieces)):
        pairs = []
        for row in range(lax.axis_size("dp")):
            offset = order[row % 2][slot]
            pairs += [(row * count + i, row * count + (i ^ offset)) for i in range(count)]
        results.append(lax.ppermute(pieces[slot], ("dp", "seq"), pairs))
    return results


def exclusive_scan(pieces, orders, size, reverse, token):
    group = len(pieces)
    count, rows = lax.axis_size("seq"), lax.axis_size("dp")
    groups = count // group
    part = functools.partial
    lanes = pieces[0].shape[1]
    extra = pieces[0].shape[0] - size
    piece = jax.ShapeDtypeStruct((size, lanes), HALF)
    gain_shape = jax.ShapeDtypeStruct((extra // 2, lanes), F32)

    def shifted(array, distance):
        step = -distance if reverse else distance
        pairs = [(i, (i + step) % count) for i in range(count)]
        return lax.ppermute(array, "seq", pairs)

    received = own_and_swapped(pieces, orders[0])
    totals = call(
        part(total_kernel, size, group),
        [jax.ShapeDtypeStruct(pieces[0].shape, HALF)] + [gain_shape] * (extra > 0),
        received + [token],
        0,
        ins={group: ANY},
    )
    total, gains = totals[0], list(totals[1:])
    riding = int(extra > 0 and groups == 2 and rows == 4)
    carry = shifted(total if riding else total[:size], group)
    if riding:
        for offset in (0, group):
            pairs = [
                (row * count + i, (row ^ 2) * count + (i ^ offset))
                for row in range(rows)
                for i in range(count)
            ]
            gains.append(lax.ppermute(gains[0], ("dp", "seq"), pairs))
    elif extra:
        gains = [tree_sum(summed_over("seq", group, gains[0]))]
        gains = [tree_sum(summed_over("dp", 2, gains[0]))]
    distance = 1
    while distance < groups - 1:
        moved = shifted(carry, distance * group)
        kernel = part(
            carry_kernel, group, reverse, distance + (distance == 1), distance == 1
        )
        (carry,) = call(kernel, [piece], [carry, moved], 0)
        distance *= 2
    pieces, after = {}, []
    for slots in ((1,), (2,), (3, 0)):
        adding = riding if 0 in slots else 0
        inputs = [carry] + received + gains[:adding] + after
        sums = call(
            part(scan_kernel, group, orders, slots, reverse, groups <= 2, size, adding),
            [piece] * len(slots) + [gain_shape] * adding,
            inputs,
            0,
            ins={len(inputs) - 1: ANY} if after else {},
        )
        pieces.update(zip(slots, sums))
        after = [sums[0]]
    results = own_and_swapped([pieces[slot] for slot in range(group)], orders[1])
    if riding:
        gains = [sums[-1] + (gains[1] + gains[2])]
    return results, (gains[0] if gains else None)


def summed_over(axis, stride, array):
    count = lax.axis_size(axis)
    terms = [array]
    while stride < count:
        array = tree_sum(terms)
        width = 4 if count // stride % 4 == 0 else 2
        order = sorted(range(1, width), key=lambda i: i % 2)
        moved = {i: swap(array, axis, i * stride) for i in order}
        terms = [array] + [moved[i] for i in range(1, width)]
        stride *= width
    return terms


def per_device(queries, keys, values, gain, cotangent):
    q, k, v, cot = queries[0], keys[0], values[0], cotangent[0]
    rows, features = q.shape
    head = features // HEADS
    group = 4
    width = features // group
    part = functools.partial
    wide = jax.ShapeDtypeStruct((rows, features), F32)
    half = jax.ShapeDtypeStruct((rows, features), HALF)
    square = jax.ShapeDtypeStruct((rows, head), F32)
    piece = jax.ShapeDtypeStruct((width, head), HALF)
    scores_shape = jax.ShapeDtypeStruct((HEADS * rows, rows), HALF)
    gain_shape = jax.ShapeDtypeStruct((HEADS, head), F32)
    token_shape = jax.ShapeDtypeStruct((8, head), F32)
    whole = pltpu.VMEM((features, head), HALF)
    gain_row = gain.reshape(1, features)

    (first,) = call(
        part(first_state_kernel, head, 1),
        [piece],
        [pltpu.with_memory_space_constraint(a, pltpu.HBM) for a in (k, v)],
        1,
        [pltpu.VMEM((rows, width), HALF)] * 2 + [pltpu.SemaphoreType.DMA((2,))],
        ins={0: HBM, 1: HBM},
    )
    slots = (2, 3, 0)
    rest = call(
        part(state_kernel, head, slots), [piece] * 3, [k, v, first], 1, ins={2: ANY}
    )
    pieces = dict(zip(slots, rest))
    pieces[1] = first
    pieces = [pieces[slot] for slot in range(group)]
    scores, intra = call(part(local_kernel, head), [scores_shape, wide], [q, k, v], 2)
    prefix, _ = exclusive_scan(pieces, STATE_ORDERS, width, False, intra)
    message = jax.ShapeDtypeStruct((width + 2 * HEADS, head), HALF)
    sources = [q, intra, gain_row, cot]
    early, squares, inner = call(
        part(early_norm_kernel, head, STATE_ORDERS[1]),
        [wide, square, square],
        sources + prefix[:-1],
        1,
    )
    late, inverse, grad, *pieces = call(
        part(norm_kernel, head, group, NORM_ORDERS, lax.axis_size("dp")),
        [jax.ShapeDtypeStruct((rows, width), F32), square, half] + [message] * group,
        sources + [early, squares, inner, prefix[-1]],
        2,
        [pltpu.VMEM((1, features), F32), pltpu.VMEM((HEADS, head), F32)],
    )
    output, grad_query, key_part, value_part, token = call(
        part(backward_kernel, head, group),
        [half, half, wide, wide, token_shape],
        [q, k, v, scores, grad, early, late, inverse, gain_row] + prefix,
        5,
        [whole],
    )
    suffix, gain_grad = exclusive_scan(pieces, GRAD_ORDERS, width, True, token)
    gains = [gain_grad, swap(gain_grad, "dp", 1)]
    inputs = [k, v, key_part, value_part]
    outs = []
    for slots in ((0,), (1, 2, 3)):
        last = group - 1 in slots
        at = len(inputs) + len(slots)
        results = call(
            part(final_kernel, head, slots, last),
            [half, half] + [gain_shape] * last,
            inputs + [suffix[slot] for slot in slots] + outs + (gains if last else []),
            1,
            [pltpu.VMEM((len(slots), rows, width), HALF)] * 2
            + [pltpu.SemaphoreType.DMA((2, len(slots)))]
            + [pltpu.VMEM((HEADS, head), F32), pltpu.SemaphoreType.DMA(())] * last,
            ins={at + i: HBM for i in range(len(outs))},
            out_specs={0: HBM, 1: HBM, 2: HBM},
            aliases={at + i: i for i in range(len(outs))},
        )
        outs = list(results[:2])
    grad_key, grad_value, gain_grad = results
    return (
        output[None],
        grad_query[None],
        grad_key[None],
        grad_value[None],
        gain_grad.reshape(features),
    )


def solution(mesh):
    spec = P("dp", "seq", None)
    return jax.shard_map(
        per_device,
        mesh=mesh,
        in_specs=(spec, spec, spec, P(), spec),
        out_specs=(spec, spec, spec, spec, P()),
        check_vma=False,
    )
```

```python
import functools

import jax
import jax.numpy as jnp
from jax import lax
from jax.experimental import pallas as pl
from jax.experimental.pallas import tpu as pltpu
from jax.sharding import PartitionSpec as P

HEADS = 16

EPSILON = 1e-06

F32 = jnp.float32
HALF = jnp.bfloat16


def dot(lhs, rhs, lhs_dim, rhs_dim):
    return lax.dot_general(
        lhs, rhs, (((lhs_dim,), (rhs_dim,)), ((), ())), preferred_element_type=F32
    )


def causal(size):
    rows = lax.broadcasted_iota(jnp.int32, (size, size), 0)
    columns = lax.broadcasted_iota(jnp.int32, (size, size), 1)
    return rows >= columns


def member_of(group):
    return lax.rem(lax.axis_index("seq"), group)


STATE_ORDERS = (((0, 1, 2, 3), (0, 2, 1, 3)), ((0, 2, 1, 3), (0, 1, 2, 3)))
GRAD_ORDERS = (((0, 3, 1, 2), (0, 3, 1, 2)), ((0, 3, 1, 2), (0, 1, 2, 3)))
NORM_ORDERS = (STATE_ORDERS[1], GRAD_ORDERS[0])


def partner_of(order, slot):
    even, odd = order[0][slot], order[1][slot]
    offset = even
    if even != odd:
        offset = jnp.where(lax.rem(lax.axis_index("dp"), 2) == 1, odd, even)
    return member_of(len(order[0])) ^ offset


def block_at(index, size):
    return pl.ds(pl.multiple_of(index * size, size), size)


def gathered(order, piece_refs, size, whole_ref):
    for j, ref in enumerate(piece_refs):
        whole_ref[block_at(partner_of(order, j), size), :] = ref[0:size, :]


def columns(first, count):
    return slice(first, first + count)


def first_state_kernel(head, slot, k_ref, v_ref, piece_ref, k_buffer, v_buffer, arrived):
    width = piece_ref.shape[0]
    source = block_at(partner_of(STATE_ORDERS[0], slot), width)
    copies = [
        pltpu.make_async_copy(k_ref.at[:, source], k_buffer, arrived.at[0]),
        pltpu.make_async_copy(v_ref.at[:, source], v_buffer, arrived.at[1]),
    ]
    for copy in copies:
        copy.start()
    for copy in copies:
        copy.wait()
    for i in range(width // head):
        part = columns(i * head, head)
        piece_ref[part, :] = dot(k_buffer[:, part], v_buffer[:, part], 0, 0).astype(HALF)


def state_kernel(head, slots, k_ref, v_ref, token_ref, *piece_refs):
    del token_ref
    for slot, piece_ref in zip(slots, piece_refs):
        width = piece_ref.shape[0]
        for i in range(width // head):
            part = features_at(STATE_ORDERS[0], slot, i, width, head)
            piece_ref[columns(i * head, head), :] = dot(
                k_ref[:, part], v_ref[:, part], 0, 0
            ).astype(HALF)


def local_kernel(head, q_ref, k_ref, v_ref, scores_ref, intra_ref):
    rows = q_ref.shape[0]
    mask = causal(rows)
    scaling = head ** (-0.5)
    for h in range(HEADS):
        part = columns(h * head, head)
        scores = dot(q_ref[:, part], k_ref[:, part], 1, 1) * scaling
        scores = jnp.where(mask, scores, 0.0).astype(HALF)
        scores_ref[columns(h * rows, rows), :] = scores
        intra_ref[:, part] = dot(scores, v_ref[:, part], 1, 0)


def features_at(order, slot, i, width, head):
    start = partner_of(order, slot) * width + i * head
    return pl.ds(pl.multiple_of(start, head), head)


def attend(head, order, slot, refs, prefix_ref, attended_ref, at, squares, inner):
    q_ref, intra_ref, gain_ref, cot_ref = refs
    scaling = head ** (-0.5)
    width = prefix_ref.shape[0]
    for i in range(width // head):
        part = features_at(order, slot, i, width, head)
        prefix = prefix_ref[columns(i * head, head), :]
        attended = intra_ref[:, part] + scaling * dot(q_ref[:, part], prefix, 1, 0)
        attended_ref[:, part if at is None else columns(i * head, head)] = attended
        scaled = cot_ref[:, part].astype(F32) * gain_ref[:, part]
        squares += attended * attended
        inner += scaled * attended
    return squares, inner


def early_norm_kernel(head, order, *refs):
    prefix_refs, (attended_ref, squares_ref, inner_ref) = refs[4:-3], refs[-3:]
    squares = jnp.zeros(squares_ref.shape, F32)
    inner = jnp.zeros(squares_ref.shape, F32)
    for slot, prefix_ref in enumerate(prefix_refs):
        squares, inner = attend(
            head, order, slot, refs[:4], prefix_ref, attended_ref, None, squares, inner
        )
    squares_ref[...] = squares
    inner_ref[...] = inner


def norm_kernel(head, group, orders, replicas, *refs):
    q_ref, _, gain_ref, cot_ref = refs[:4]
    early_ref, squares_ref, inner_ref, prefix_ref = refs[4:8]
    late_ref, inverse_ref, grad_ref = refs[8:11]
    piece_refs = refs[11 : 11 + group]
    gain_grad_ref, gain_rows_ref = refs[11 + group :]
    features = q_ref.shape[1]
    width = features // group
    odd = lax.rem(lax.axis_index("dp"), 2) == 1
    squares, inner = attend(
        head,
        orders[0],
        group - 1,
        refs[:4],
        prefix_ref,
        late_ref,
        0,
        squares_ref[...],
        inner_ref[...],
    )
    inverse = lax.rsqrt(
        jnp.sum(squares, axis=1, keepdims=True) * (1.0 / features) + EPSILON
    )
    inner_mean = jnp.sum(inner, axis=1, keepdims=True) * (1.0 / features) * inverse
    inverse_ref[...] = jnp.broadcast_to(inverse, inverse_ref.shape)
    scaling = head ** (-0.5)
    for slot in range(group):
        for i in range(width // head):
            part = features_at(orders[1], slot, i, width, head)
            local = columns(i * head, head)
            late = [order[slot] == before[-1] for before, order in zip(*orders)]
            attended = late_ref[:, local] if late[0] else early_ref[:, part]
            if late[0] != late[1]:
                other = late_ref[:, local] if late[1] else early_ref[:, part]
                attended = jnp.where(odd, other, attended)
            normalized = attended * inverse
            upstream = cot_ref[:, part].astype(F32)
            gain_grad_ref[:, part] = jnp.sum(
                upstream * normalized, axis=0, keepdims=True
            ) * (1.0 / replicas)
            scaled = upstream * gain_ref[:, part]
            grad = ((scaled - normalized * inner_mean) * inverse).astype(HALF)
            grad_ref[:, part] = grad
            piece_refs[slot][local, :] = (
                scaling * dot(q_ref[:, part], grad, 0, 0)
            ).astype(HALF)
    for h in range(HEADS):
        gain_rows_ref[h : h + 1, :] = gain_grad_ref[:, columns(h * head, head)]
    for ref in piece_refs:
        put_wide_rows(ref, width, gain_rows_ref[...])


def backward_kernel(head, group, *refs):
    q_ref, k_ref, v_ref, scores_ref, grad_ref = refs[:5]
    early_ref, late_ref, inverse_ref, gain_ref = refs[5:9]
    prefix_refs = refs[9 : 9 + group]
    out_ref, grad_query_ref, key_part_ref, value_part_ref, token_ref = refs[
        9 + group : 14 + group
    ]
    whole_ref = refs[14 + group]
    rows = q_ref.shape[0]
    mask = causal(rows)
    scaling = head ** (-0.5)
    gathered(STATE_ORDERS[1], prefix_refs, prefix_refs[0].shape[0], whole_ref)
    inverse = inverse_ref[...]
    width = late_ref.shape[1]
    for slot in range(group):
        for i in range(width // head):
            part = features_at(STATE_ORDERS[1], slot, i, width, head)
            if slot == group - 1:
                attended = late_ref[:, columns(i * head, head)]
            else:
                attended = early_ref[:, part]
            out_ref[:, part] = (gain_ref[:, part] * (attended * inverse)).astype(HALF)
    for h in range(HEADS):
        part = columns(h * head, head)
        grad = grad_ref[:, part]
        grad_scores = dot(grad, v_ref[:, part], 1, 1)
        grad_scores = jnp.where(mask, grad_scores, 0.0).astype(HALF)
        grad_query = dot(grad_scores, k_ref[:, part], 1, 0) + dot(
            grad, whole_ref[part, :], 1, 1
        )
        grad_query_ref[:, part] = (scaling * grad_query).astype(HALF)
        key_part_ref[:, part] = scaling * dot(grad_scores, q_ref[:, part], 0, 0)
        value_part_ref[:, part] = dot(
            scores_ref[columns(h * rows, rows), :], grad, 0, 0
        )
    token_ref[...] = jnp.zeros_like(token_ref)


def final_kernel(head, slots, last, *refs):
    k_ref, v_ref, key_part_ref, value_part_ref = refs[:4]
    suffix_refs = refs[4 : 4 + len(slots)]
    refs = refs[4 + len(slots) :]
    copies = []
    if last:
        gain_grad_ref, total_ref, gain_written = refs[-6], refs[-2], refs[-1]
        total_ref[...] = tree_sum([ref[...] for ref in refs[2:-8]])
        copies.append(pltpu.make_async_copy(total_ref, gain_grad_ref, gain_written))
        copies[0].start()
        out_refs, refs = refs[-8:-6], refs[-5:-2]
    else:
        out_refs, refs = refs[-5:-3], refs[-3:]
    key_buffer, value_buffer, written = refs
    width = key_buffer.shape[2]
    for n, slot in enumerate(slots):
        for i in range(width // head):
            part = features_at(GRAD_ORDERS[1], slot, i, width, head)
            local = columns(i * head, head)
            suffix = suffix_refs[n][local, :]
            key_buffer[n, :, local] = (
                key_part_ref[:, part] + dot(v_ref[:, part], suffix, 1, 1)
            ).astype(HALF)
            value_buffer[n, :, local] = (
                value_part_ref[:, part] + dot(k_ref[:, part], suffix, 1, 0)
            ).astype(HALF)
        for i, buffer in enumerate((key_buffer, value_buffer)):
            copy = pltpu.make_async_copy(
                buffer.at[n],
                out_refs[i].at[:, block_at(partner_of(GRAD_ORDERS[1], slot), width)],
                written.at[i, n],
            )
            copy.start()
            copies.append(copy)
    for copy in copies:
        copy.wait()


def tree_sum(terms):
    while len(terms) > 1:
        terms = [a + b for a, b in zip(terms[::2], terms[1::2])]
    return terms[0]


def wide_rows(ref, start):
    rows = (ref.shape[0] - start) // 2
    high = ref[columns(start, rows), :].astype(F32)
    return high + ref[columns(start + rows, rows), :].astype(F32)


def put_wide_rows(ref, start, value):
    rows = value.shape[0]
    high = value.astype(HALF)
    ref[columns(start, rows), :] = high
    ref[columns(start + rows, rows), :] = (value - high.astype(F32)).astype(HALF)


def total_kernel(size, count, *refs):
    refs, out_refs = refs[:count], refs[count + 1 :]
    total = refs[0][0:size, :].astype(F32)
    for ref in refs[1:]:
        total += ref[0:size, :].astype(F32)
    out_refs[0][0:size, :] = total.astype(HALF)
    if len(out_refs) > 1:
        gain = tree_sum([wide_rows(ref, size) for ref in refs])
        put_wide_rows(out_refs[0], size, gain)
        out_refs[1][...] = wide_rows(out_refs[0], size)


def group_flag(group, reverse, distance):
    index = lax.axis_index("seq") // group
    last = lax.axis_size("seq") // group - 1
    known = index + distance <= last if reverse else index >= distance
    return jnp.where(known, 1.0, 0.0)


def carry_kernel(group, reverse, distance, first, own_ref, moved_ref, out_ref):
    own = own_ref[...].astype(F32)
    if first:
        own = own * group_flag(group, reverse, 1)
    moved = moved_ref[...].astype(F32) * group_flag(group, reverse, distance)
    out_ref[...] = (own + moved).astype(HALF)


def scan_kernel(group, orders, slots, reverse, masked, size, riding, *refs):
    sources = [partner_of(orders[0], j) for j in range(group)]
    carry = refs[0][0:size, :].astype(F32)
    if masked:
        carry = carry * group_flag(group, reverse, 1)
    blocks = [ref[0:size, :].astype(F32) for ref in refs[1 : 1 + group]]
    out_refs = refs[-len(slots) - riding :][: len(slots)]
    for slot, out_ref in zip(slots, out_refs):
        target = partner_of(orders[1], slot)
        total = carry
        for i in range(group):
            known = sources[i] > target if reverse else sources[i] < target
            total += jnp.where(known, 1.0, 0.0) * blocks[i]
        out_ref[...] = total.astype(HALF)
    if riding:
        refs[-1][...] = refs[1 + group][...] + wide_rows(refs[0], size)


VMEM = pl.BlockSpec(memory_space=pltpu.VMEM)
ANY = pl.BlockSpec(memory_space=pl.ANY)
HBM = pl.BlockSpec(memory_space=pltpu.HBM)


def call(kernel, outs, args, matmuls, scratch=(), ins=None, out_specs=None, aliases=None):
    size = sum(a.size * a.dtype.itemsize for a in args)
    size += sum(o.size * o.dtype.itemsize for o in outs)
    ins = ins or {}
    out_specs = out_specs or {}
    return pl.pallas_call(
        kernel,
        out_shape=tuple(outs),
        in_specs=[ins.get(i, VMEM) for i in range(len(args))],
        out_specs=tuple(out_specs.get(i, VMEM) for i in range(len(outs))),
        scratch_shapes=list(scratch),
        input_output_aliases=aliases or {},
        compiler_params=pltpu.CompilerParams(vmem_limit_bytes=16 * 1024 * 1024),
        cost_estimate=pl.CostEstimate(
            flops=2 * 128 * 128 * 128 * HEADS * matmuls,
            bytes_accessed=size,
            transcendentals=0,
        ),
    )(*args)


def swap(array, axis, offset):
    count = lax.axis_size(axis)
    return lax.ppermute(array, axis, [(i, i ^ offset) for i in range(count)])


def own_and_swapped(pieces, order):
    count = lax.axis_size("seq")
    results = [pieces[0]]
    for slot in range(1, len(pieces)):
        pairs = []
        for row in range(lax.axis_size("dp")):
            offset = order[row % 2][slot]
            pairs += [(row * count + i, row * count + (i ^ offset)) for i in range(count)]
        results.append(lax.ppermute(pieces[slot], ("dp", "seq"), pairs))
    return results


def exclusive_scan(pieces, orders, size, reverse, token):
    group = len(pieces)
    count, rows = lax.axis_size("seq"), lax.axis_size("dp")
    groups = count // group
    part = functools.partial
    lanes = pieces[0].shape[1]
    extra = pieces[0].shape[0] - size
    piece = jax.ShapeDtypeStruct((size, lanes), HALF)
    gain_shape = jax.ShapeDtypeStruct((extra // 2, lanes), F32)

    def shifted(array, distance):
        step = -distance if reverse else distance
        pairs = [(i, (i + step) % count) for i in range(count)]
        return lax.ppermute(array, "seq", pairs)

    received = own_and_swapped(pieces, orders[0])
    totals = call(
        part(total_kernel, size, group),
        [jax.ShapeDtypeStruct(pieces[0].shape, HALF)] + [gain_shape] * (extra > 0),
        received + [token],
        0,
        ins={group: ANY},
    )
    total, gains = totals[0], list(totals[1:])
    riding = int(extra > 0 and groups == 2 and rows == 4)
    carry = shifted(total if riding else total[:size], group)
    if riding:
        for offset in (0, group):
            pairs = [
                (row * count + i, (row ^ 2) * count + (i ^ offset))
                for row in range(rows)
                for i in range(count)
            ]
            gains.append(lax.ppermute(gains[0], ("dp", "seq"), pairs))
    elif extra:
        gains = [tree_sum(summed_over("seq", group, gains[0]))]
        gains = [tree_sum(summed_over("dp", 2, gains[0]))]
    distance = 1
    while distance < groups - 1:
        moved = shifted(carry, distance * group)
        kernel = part(
            carry_kernel, group, reverse, distance + (distance == 1), distance == 1
        )
        (carry,) = call(kernel, [piece], [carry, moved], 0)
        distance *= 2
    pieces, after = {}, []
    for slots in ((1,), (2,), (3, 0)):
        adding = riding if 0 in slots else 0
        inputs = [carry] + received + gains[:adding] + after
        sums = call(
            part(scan_kernel, group, orders, slots, reverse, groups <= 2, size, adding),
            [piece] * len(slots) + [gain_shape] * adding,
            inputs,
            0,
            ins={len(inputs) - 1: ANY} if after else {},
        )
        pieces.update(zip(slots, sums))
        after = [sums[0]]
    results = own_and_swapped([pieces[slot] for slot in range(group)], orders[1])
    if riding:
        gains = [sums[-1] + (gains[1] + gains[2])]
    return results, (gains[0] if gains else None)


def summed_over(axis, stride, array):
    count = lax.axis_size(axis)
    terms = [array]
    while stride < count:
        array = tree_sum(terms)
        width = 4 if count // stride % 4 == 0 else 2
        order = sorted(range(1, width), key=lambda i: i % 2)
        moved = {i: swap(array, axis, i * stride) for i in order}
        terms = [array] + [moved[i] for i in range(1, width)]
        stride *= width
    return terms


def per_device(queries, keys, values, gain, cotangent):
    q, k, v, cot = queries[0], keys[0], values[0], cotangent[0]
    rows, features = q.shape
    head = features // HEADS
    group = 4
    width = features // group
    part = functools.partial
    wide = jax.ShapeDtypeStruct((rows, features), F32)
    half = jax.ShapeDtypeStruct((rows, features), HALF)
    square = jax.ShapeDtypeStruct((rows, head), F32)
    piece = jax.ShapeDtypeStruct((width, head), HALF)
    scores_shape = jax.ShapeDtypeStruct((HEADS * rows, rows), HALF)
    gain_shape = jax.ShapeDtypeStruct((HEADS, head), F32)
    token_shape = jax.ShapeDtypeStruct((8, head), F32)
    whole = pltpu.VMEM((features, head), HALF)
    gain_row = gain.reshape(1, features)

    (first,) = call(
        part(first_state_kernel, head, 1),
        [piece],
        [pltpu.with_memory_space_constraint(a, pltpu.HBM) for a in (k, v)],
        1,
        [pltpu.VMEM((rows, width), HALF)] * 2 + [pltpu.SemaphoreType.DMA((2,))],
        ins={0: HBM, 1: HBM},
    )
    slots = (2, 3, 0)
    rest = call(
        part(state_kernel, head, slots), [piece] * 3, [k, v, first], 1, ins={2: ANY}
    )
    pieces = dict(zip(slots, rest))
    pieces[1] = first
    pieces = [pieces[slot] for slot in range(group)]
    scores, intra = call(part(local_kernel, head), [scores_shape, wide], [q, k, v], 2)
    prefix, _ = exclusive_scan(pieces, STATE_ORDERS, width, False, intra)
    message = jax.ShapeDtypeStruct((width + 2 * HEADS, head), HALF)
    sources = [q, intra, gain_row, cot]
    early, squares, inner = call(
        part(early_norm_kernel, head, STATE_ORDERS[1]),
        [wide, square, square],
        sources + prefix[:-1],
        1,
    )
    late, inverse, grad, *pieces = call(
        part(norm_kernel, head, group, NORM_ORDERS, lax.axis_size("dp")),
        [jax.ShapeDtypeStruct((rows, width), F32), square, half] + [message] * group,
        sources + [early, squares, inner, prefix[-1]],
        2,
        [pltpu.VMEM((1, features), F32), pltpu.VMEM((HEADS, head), F32)],
    )
    output, grad_query, key_part, value_part, token = call(
        part(backward_kernel, head, group),
        [half, half, wide, wide, token_shape],
        [q, k, v, scores, grad, early, late, inverse, gain_row] + prefix,
        5,
        [whole],
    )
    suffix, gain_grad = exclusive_scan(pieces, GRAD_ORDERS, width, True, token)
    gains = [gain_grad, swap(gain_grad, "dp", 1)]
    inputs = [k, v, key_part, value_part]
    outs = []
    for slots in ((0,), (1,), (2, 3)):
        last = group - 1 in slots
        at = len(inputs) + len(slots)
        results = call(
            part(final_kernel, head, slots, last),
            [half, half] + [gain_shape] * last,
            inputs + [suffix[slot] for slot in slots] + outs + (gains if last else []),
            1,
            [pltpu.VMEM((len(slots), rows, width), HALF)] * 2
            + [pltpu.SemaphoreType.DMA((2, len(slots)))]
            + [pltpu.VMEM((HEADS, head), F32), pltpu.SemaphoreType.DMA(())] * last,
            ins={at + i: HBM for i in range(len(outs))},
            out_specs={0: HBM, 1: HBM, 2: HBM},
            aliases={at + i: i for i in range(len(outs))},
        )
        outs = list(results[:2])
    grad_key, grad_value, gain_grad = results
    return (
        output[None],
        grad_query[None],
        grad_key[None],
        grad_value[None],
        gain_grad.reshape(features),
    )


def solution(mesh):
    spec = P("dp", "seq", None)
    return jax.shard_map(
        per_device,
        mesh=mesh,
        in_specs=(spec, spec, spec, P(), spec),
        out_specs=(spec, spec, spec, spec, P()),
        check_vma=False,
    )
```
